32 devices in a mesh: fsdp: 16 (over z, y, core), tp: 2 (over x).
Axes of the slice: x: 2, y: 2, z: 4, core: 2. Of those that a mesh axis runs over, the one named last changes fastest.
Arguments:
- inputs: bfloat16 [32768, 1024], P(('fsdp', 'tp')), may hold values from -6 to 6
- segments: int32 [32768], P('fsdp'), may hold values from 0 to 512, as said below
- teacher: bfloat16 [32768, 1024], P('fsdp', 'tp'), may hold values from -6 to 6
- first_norm_gain: float32 [1024], P(('fsdp', 'tp')), may hold values from 0.5 to 1.5
- first_norm_bias: float32 [1024], P(('fsdp', 'tp')), may hold values from -1 to 1
- time_decay: float32 [1024], P(('fsdp', 'tp')), may hold values from -6.5 to -2
- time_first: float32 [1024], P(('fsdp', 'tp')), may hold values from -1 to 1
- time_mix_key: float32 [1024], P(('fsdp', 'tp')), may hold values from 0.1 to 0.9
- time_mix_value: float32 [1024], P(('fsdp', 'tp')), may hold values from 0.1 to 0.9
- time_mix_recept: float32 [1024], P(('fsdp', 'tp')), may hold values from 0.1 to 0.9
- time_key: bfloat16 [1024, 1024], P('fsdp', 'tp'), may hold values from -0.1875 to 0.1875
- time_value: bfloat16 [1024, 1024], P('fsdp', 'tp'), may hold values from -0.1875 to 0.1875
- time_recept: bfloat16 [1024, 1024], P('fsdp', 'tp'), may hold values from -0.1875 to 0.1875
- time_output: bfloat16 [1024, 1024], P('tp', 'fsdp'), may hold values from -0.75 to 0.75
- second_norm_gain: float32 [1024], P(('fsdp', 'tp')), may hold values from 0.5 to 1.5
- second_norm_bias: float32 [1024], P(('fsdp', 'tp')), may hold values from -1 to 1
- channel_mix_key: float32 [1024], P(('fsdp', 'tp')), may hold values from 0.1 to 0.9
- channel_mix_recept: float32 [1024], P(('fsdp', 'tp')), may hold values from 0.1 to 0.9
- channel_key: bfloat16 [1024, 4096], P('fsdp', 'tp'), may hold values from -0.1875 to 0.1875
- channel_recept: bfloat16 [1024, 1024], P('fsdp', 'tp'), may hold values from -0.1875 to 0.1875
- channel_value: bfloat16 [4096, 1024], P('tp', 'fsdp'), may hold values from -0.09375 to 0.09375
Outputs:
- outputs: bfloat16 [32768, 1024], P('fsdp', 'tp')
- loss: float32 [], replicated
- input_grad: float32 [32768, 1024], P(('fsdp', 'tp'))
- first_norm_gain_grad: float32 [1024], P(('fsdp', 'tp'))
- first_norm_bias_grad: float32 [1024], P(('fsdp', 'tp'))
- time_decay_grad: float32 [1024], P(('fsdp', 'tp'))
- time_first_grad: float32 [1024], P(('fsdp', 'tp'))
- time_mix_key_grad: float32 [1024], P(('fsdp', 'tp'))
- time_mix_value_grad: float32 [1024], P(('fsdp', 'tp'))
- time_mix_recept_grad: float32 [1024], P(('fsdp', 'tp'))
- time_key_grad: float32 [1024, 1024], P('fsdp', 'tp')
- time_value_grad: float32 [1024, 1024], P('fsdp', 'tp')
- time_recept_grad: float32 [1024, 1024], P('fsdp', 'tp')
- time_output_grad: float32 [1024, 1024], P('tp', 'fsdp')
- second_norm_gain_grad: float32 [1024], P(('fsdp', 'tp'))
- second_norm_bias_grad: float32 [1024], P(('fsdp', 'tp'))
- channel_mix_key_grad: float32 [1024], P(('fsdp', 'tp'))
- channel_mix_recept_grad: float32 [1024], P(('fsdp', 'tp'))
- channel_key_grad: float32 [1024, 4096], P('fsdp', 'tp')
- channel_recept_grad: float32 [1024, 1024], P('fsdp', 'tp')
- channel_value_grad: float32 [4096, 1024], P('tp', 'fsdp')
The draws below stay inside these ranges and needn't reach their ends.
Inputs may be any that keep to these rules, and one draw needn't show every extreme that they name: `segments`: within each sequence of 1024 tokens the document numbers start at 1 on its first token, never fall, never exceed 1024 // 2, and end in a run of 1 to 512 padding tokens (0).
All inputs are finite; a program needn't handle non-finite values.
Results may differ from the reference program's by a relative error of at most 0.009.
Values may be sent and summed in bfloat16 or wider, within the bound.
No kernel may reach another device: no remote copies, remote signals or barrier semaphores. Data moves between devices by JAX's collectives and lax.ppermute only.
A program may use at most 320 MiB of HBM per device.

```python
import jax
import jax.numpy as jnp
from jax import lax

D = 1024
FF = 4096
SEQ_LEN = 1024
SEQ_DEV = 2
TOKENS = 32768


def draw_segments(key, part):
    sequence_count = TOKENS // SEQ_LEN
    key_kind, key_bits, key_pad = jax.random.split(key, 3)
    doc_kinds = jax.random.randint(key_kind, (sequence_count, 1), 0, 3)
    periods = jnp.where(doc_kinds == 0, 8, jnp.where(doc_kinds == 1, 48, 320)).astype(jnp.int32)
    random_bits = jax.random.randint(key_bits, (sequence_count, SEQ_LEN), 0, 1 << 20)
    positions = jnp.arange(SEQ_LEN, dtype=jnp.int32)[None, :]
    starts = (random_bits % periods == 0) | (positions == 0)
    numbers = jnp.minimum(jnp.cumsum(starts.astype(jnp.int32), axis=1), SEQ_LEN // 2)
    padding = jax.random.randint(key_pad, (sequence_count, 1), 1, SEQ_LEN // 2 + 1)
    numbers = jnp.where(positions >= SEQ_LEN - padding, 0, numbers)
    first_row = jnp.where(positions < SEQ_LEN // 2, positions + 1, 0)
    rows = jnp.arange(sequence_count, dtype=jnp.int32)[:, None]
    numbers = jnp.where(rows == 0, first_row, numbers)
    return numbers.reshape(-1).astype(jnp.int32)


def shard_levels(own_key, dims, cuts, smallest, top_value):
    def one(axis_at, parts):
        steps = jax.random.uniform(jax.random.fold_in(jax.random.fold_in(own_key, 6), axis_at), (parts,), jnp.float32, smallest / len(cuts), top_value / len(cuts))
        return jnp.repeat(jnp.exp(steps), dims[axis_at] // parts).reshape((-1,) + (1,) * (len(dims) - axis_at - 1))

    level = one(*cuts[0])
    for cut in cuts[1:]:
        level = level * one(*cut)
    return level


def gaussian(stream_key, dims, width, reach, pieces=(), held_as=jnp.bfloat16):
    array = jax.random.normal(stream_key, dims, jnp.float32) * width
    if len(pieces) > 0:
        array = shard_levels(stream_key, dims, pieces, -0.22, 0.18) * array
    return jnp.clip(array, min=-reach, max=reach).astype(held_as)


def setup_inputs(seed: int = 0) -> dict:
    key_list = jax.random.split(jax.random.key(seed), 22)
    inputs = gaussian(key_list[0], (TOKENS, D), 1.0, 6.0, ((0, 32),))
    segments = draw_segments(jax.random.fold_in(key_list[21], 71), 0)
    teacher = gaussian(key_list[2], (TOKENS, D), 1.0, 6.0, ((0, 16), (1, 2)))
    first_norm_gain = jnp.clip(1.0 + 0.1 * jax.random.normal(key_list[3], (D,), jnp.float32), 0.5, 1.5)
    first_norm_bias = gaussian(key_list[4], (D,), 0.2, 1.0, ((0, 32),), jnp.float32)
    time_decay = jnp.clip(-6.5 + 4.5 * jax.random.uniform(key_list[5], (D,), jnp.float32) ** shard_levels(key_list[5], (D,), ((0, 32),), -0.2, 0.2), -6.5, -2.0)
    time_first = jnp.clip(jax.random.uniform(key_list[6], (D,), jnp.float32, -1.0, 1.0) * shard_levels(key_list[6], (D,), ((0, 32),), -0.4, 0.0), -1.0, 1.0)
    time_mix_key = jnp.clip(0.1 + 0.79999997 * jax.random.uniform(key_list[7], (D,), jnp.float32) ** shard_levels(key_list[7], (D,), ((0, 32),), -0.2, 0.2), 0.1, 0.9)
    time_mix_value = jnp.clip(0.1 + 0.79999997 * jax.random.uniform(key_list[8], (D,), jnp.float32) ** shard_levels(key_list[8], (D,), ((0, 32),), -0.2, 0.2), 0.1, 0.9)
    time_mix_recept = jnp.clip(0.1 + 0.79999997 * jax.random.uniform(key_list[9], (D,), jnp.float32) ** shard_levels(key_list[9], (D,), ((0, 32),), -0.2, 0.2), 0.1, 0.9)
    time_key = gaussian(key_list[10], (D, D), D ** -0.5, 0.1875, ((0, 16), (1, 2)))
    time_value = gaussian(key_list[11], (D, D), D ** -0.5, 0.1875, ((0, 16), (1, 2)))
    time_recept = gaussian(key_list[12], (D, D), D ** -0.5, 0.1875, ((0, 16), (1, 2)))
    time_output = gaussian(key_list[13], (D, D), (D // 16) ** -0.5, 0.75, ((0, 2), (1, 16)))
    second_norm_gain = jnp.clip(1.0 + 0.1 * jax.random.normal(key_list[14], (D,), jnp.float32), 0.5, 1.5)
    second_norm_bias = gaussian(key_list[15], (D,), 0.2, 1.0, ((0, 32),), jnp.float32)
    channel_mix_key = jnp.clip(0.1 + 0.79999997 * jax.random.uniform(key_list[16], (D,), jnp.float32) ** shard_levels(key_list[16], (D,), ((0, 32),), -0.2, 0.2), 0.1, 0.9)
    channel_mix_recept = jnp.clip(0.1 + 0.79999997 * jax.random.uniform(key_list[17], (D,), jnp.float32) ** shard_levels(key_list[17], (D,), ((0, 32),), -0.2, 0.2), 0.1, 0.9)
    channel_key = gaussian(key_list[18], (D, FF), D ** -0.5, 0.1875, ((0, 16), (1, 2)))
    channel_recept = gaussian(key_list[19], (D, D), D ** -0.5, 0.1875, ((0, 16), (1, 2)))
    channel_value = gaussian(key_list[20], (FF, D), FF ** -0.5, 0.09375, ((0, 2), (1, 16)))
    return dict(inputs=inputs, segments=segments, teacher=teacher, first_norm_gain=first_norm_gain, first_norm_bias=first_norm_bias, time_decay=time_decay, time_first=time_first, time_mix_key=time_mix_key, time_mix_value=time_mix_value, time_mix_recept=time_mix_recept, time_key=time_key, time_value=time_value, time_recept=time_recept, time_output=time_output, second_norm_gain=second_norm_gain, second_norm_bias=second_norm_bias, channel_mix_key=channel_mix_key, channel_mix_recept=channel_mix_recept, channel_key=channel_key, channel_recept=channel_recept, channel_value=channel_value)


@jax.custom_vjp
def low(v):
    return lax.optimization_barrier(v.astype(jnp.bfloat16)).astype(jnp.float32)

@jax.custom_vjp
def low_back(v):
    return v

def low_keep(v):
    return (low(v), None)

def low_pass(kept, grad):
    return (grad,)

def back_keep(v):
    return (v, None)

def back_low(kept, grad):
    return (low(grad),)
low.defvjp(low_keep, low_pass)
low_back.defvjp(back_keep, back_low)

def matmul(left, right):
    return jnp.dot(left, right, precision=lax.Precision.HIGHEST)

def shift_down(values, persist_filter):
    moved = jnp.concatenate([jnp.zeros_like(values[:1]), values[:-1]], axis=0)
    return moved * persist_filter[:, None]

def layer_norm(values, gain, bias):
    centre = values - lax.optimization_barrier(jnp.mean(values, axis=-1, keepdims=True))
    scaled = lax.rsqrt(lax.optimization_barrier(jnp.mean(centre * centre, axis=-1, keepdims=True)) + 1e-05)
    return centre * scaled * gain + bias

def blend(normed, behind, mix_rate):
    return normed * mix_rate + behind * (1.0 - mix_rate)

def link_states(earlier, later):
    gate_early, state_a_early, state_b_early = earlier
    gate_late, state_a_late, state_b_late = later
    return (gate_early * gate_late, gate_late * state_a_early + state_a_late, gate_late * state_b_early + state_b_late)

def attention_recurrence_invoke(lookup_mapped, content_mapped, attenuation_multiplier, reward_tempo, persist_filter):
    retain = jnp.exp(-jnp.exp(attenuation_multiplier))
    retain_gate = persist_filter[:, None] * retain[None, :]
    lookup_array = jnp.exp(lookup_mapped)
    linked = lax.associative_scan(link_states, (retain_gate, lookup_array * content_mapped, lookup_array), axis=0)
    prior_memory_alpha = shift_down(linked[1], persist_filter)
    prior_memory_beta = shift_down(linked[2], persist_filter)
    reward_array = jnp.exp(reward_tempo[None, :] + lookup_mapped)
    return (prior_memory_alpha + reward_array * content_mapped) / (prior_memory_beta + reward_array)

def layer_loss(values, learnable_set, persist_filter, valid_rows, teacher_rows):
    initial_standardize_gain, initial_standardize_shift, attenuation_multiplier, reward_tempo, initial_lookup_mixing, initial_content_mixing, initial_gating_mixing, lookup_array, content_array, gating_array, result_array, latter_standardize_gain, latter_standardize_shift, latter_lookup_mixing, latter_gating_mixing, feedfwd_lookup_coeffs, feedfwd_gating_coeffs, feedfwd_content_coeffs = learnable_set
    normed_one = layer_norm(values, initial_standardize_gain, initial_standardize_shift)
    behind_one = shift_down(normed_one, persist_filter)
    mixed_key = low(blend(normed_one, behind_one, initial_lookup_mixing))
    mixed_value = low(blend(normed_one, behind_one, initial_content_mixing))
    mixed_recept = low(blend(normed_one, behind_one, initial_gating_mixing))
    lookup_mapped = low_back(matmul(mixed_key, lookup_array))
    content_mapped = low_back(matmul(mixed_value, content_array))
    recept_gate = jax.nn.sigmoid(low_back(matmul(mixed_recept, gating_array)))
    attention_recurrence_result = attention_recurrence_invoke(lookup_mapped, content_mapped, attenuation_multiplier, reward_tempo, persist_filter)
    gated = low(recept_gate * attention_recurrence_result)
    middle = values + low_back(matmul(gated, result_array))
    normed_two = layer_norm(middle, latter_standardize_gain, latter_standardize_shift)
    behind_two = shift_down(normed_two, persist_filter)
    mixed_key_two = low(blend(normed_two, behind_two, latter_lookup_mixing))
    mixed_recept_two = low(blend(normed_two, behind_two, latter_gating_mixing))
    active = jnp.maximum(low_back(matmul(mixed_key_two, feedfwd_lookup_coeffs)), 0.0)
    hidden = low(active * active)
    value_two = low_back(matmul(hidden, feedfwd_content_coeffs))
    recept_two = jax.nn.sigmoid(low_back(matmul(mixed_recept_two, feedfwd_gating_coeffs)))
    result = middle + recept_two * value_two
    error = (result - teacher_rows) * valid_rows[:, None]
    return (jnp.sum(error * error), result)

def reference(inputs, segments, teacher, first_norm_gain, first_norm_bias, time_decay, time_first, time_mix_key, time_mix_value, time_mix_recept, time_key, time_value, time_recept, time_output, second_norm_gain, second_norm_bias, channel_mix_key, channel_mix_recept, channel_key, channel_recept, channel_value):
    learnable_set = tuple((item.astype(jnp.float32) for item in (first_norm_gain, first_norm_bias, time_decay, time_first, time_mix_key, time_mix_value, time_mix_recept, time_key, time_value, time_recept, time_output, second_norm_gain, second_norm_bias, channel_mix_key, channel_mix_recept, channel_key, channel_recept, channel_value)))
    group_rows = SEQ_DEV * SEQ_LEN
    group_count = TOKENS // group_rows
    positions = jnp.arange(TOKENS, dtype=jnp.int32) % SEQ_LEN
    previous_ids = jnp.concatenate([jnp.zeros((1,), jnp.int32), segments[:-1]])
    persist_filter = ((segments == previous_ids) & (segments > 0) & (positions > 0)).astype(jnp.float32)
    valid_rows = (segments > 0).astype(jnp.float32)
    count = jnp.sum(valid_rows)
    grad_weight = TOKENS / (2.0 * count)
    blocks = (inputs.astype(jnp.float32).reshape(group_count, group_rows, D), persist_filter.reshape(group_count, group_rows), valid_rows.reshape(group_count, group_rows), teacher.astype(jnp.float32).reshape(group_count, group_rows, D))
    zero_grads = tuple((jnp.zeros_like(item) for item in learnable_set))

    def visit(carried, block):
        loss_sum, grad_sums = carried
        block_values, block_mask, block_valid, block_teacher = block

        def objective(values_in, params_in):
            return layer_loss(values_in, params_in, block_mask, block_valid, block_teacher)
        loss_part, back_fn, result_part = jax.vjp(objective, block_values, learnable_set, has_aux=True)
        grad_values, grad_params = back_fn(grad_weight.astype(loss_part.dtype))
        new_sums = tuple((total + part for total, part in zip(grad_sums, grad_params)))
        return ((loss_sum + loss_part, new_sums), (result_part, grad_values))
    start_loss = jnp.zeros((), jnp.float32)
    (loss_sum, grad_sums), (results, grad_inputs) = lax.scan(visit, (start_loss, zero_grads), blocks)
    outputs = results.reshape(TOKENS, D).astype(jnp.bfloat16)
    loss = loss_sum / (2.0 * count * D)
    input_grad = grad_inputs.reshape(TOKENS, D)
    return (outputs, loss, input_grad) + tuple(grad_sums)
```

```python
import functools
import itertools

import jax
import jax.numpy as jnp
from jax import lax
from jax.experimental import pallas as pl
from jax.experimental.pallas import tpu as pltpu
from jax.sharding import Mesh
from jax.sharding import PartitionSpec as P

BF = jnp.bfloat16
F32 = jnp.float32
EPSILON = 1e-05
SLOT = 64
CHUNK = 16
VMEM_LIMIT = 58 << 20
SIZES = {"z": 4, "y": 2, "x": 2}
EVERY = ("z", "y", "c", "x")
SWAP = [(0, 1), (1, 0)]

NN = (((1,), (0,)), ((), ()))
NT = (((1,), (1,)), ((), ()))
TN = (((0,), (0,)), ((), ()))


def dot(left, right, dims):
    return lax.dot_general(left, right, dims, preferred_element_type=F32)


def slot_list(order):
    dims = order[::-1]
    for index in itertools.product(*[range(SIZES[d]) for d in dims]):
        yield index, dict(zip(dims, index))


def slot_place(co, rel, other_core):
    block = ((co[0] + 4 - rel["z"]) & 3) * 4 + (co[1] ^ rel["y"]) * 2 + (co[2] ^ other_core)
    return pl.multiple_of(block * SLOT, SLOT), co[3] ^ rel["x"]


def weight_copies(co, own, other, whole, sems, order):
    copies = []
    for other_core, source in ((0, own), (1, other)):
        for index, rel in slot_list(order):
            row, half = slot_place(co, rel, other_core)
            copy = pltpu.make_async_copy(
                source.at[index], whole.at[half, pl.ds(row, SLOT), :], sems.at[len(copies)]
            )
            copies.append((rel["x"], copy))
    return copies


def start_all(copies):
    for _, copy in copies:
        copy.start()


def wait_half(copies, half):
    for which, copy in copies:
        if which == half:
            copy.wait()


def norm_rows(values, gain, bias):
    centre = values - jnp.mean(values, axis=-1, keepdims=True)
    scaled = lax.rsqrt(jnp.mean(centre * centre, axis=-1, keepdims=True) + EPSILON)
    unit = centre * scaled
    return unit * gain + bias, unit, scaled


def norm_rows_back(grad, unit, scaled, gain):
    weighted = grad * gain
    return scaled * (
        weighted
        - jnp.mean(weighted, axis=-1, keepdims=True)
        - unit * jnp.mean(weighted * unit, axis=-1, keepdims=True)
    )


def first_row(shape):
    return lax.broadcasted_iota(jnp.int32, shape, 0) == 0


def last_row(shape):
    return lax.broadcasted_iota(jnp.int32, shape, 0) == shape[0] - 1


def move_down(values, before):
    return jnp.where(first_row(values.shape), before, pltpu.roll(values, 1, 0))


def move_up(values, after):
    return jnp.where(last_row(values.shape), after, pltpu.roll(values, values.shape[0] - 1, 0))


def fold_rows(values):
    return values[:8] + values[8:]


def params(semantics=1):
    return pltpu.CompilerParams(vmem_limit_bytes=VMEM_LIMIT)


def anywhere():
    return pl.BlockSpec(memory_space=pl.ANY)


def cost(units, traffic):
    return pl.CostEstimate(
        flops=int(units * 2 * 1024**3), bytes_accessed=int(traffic), transcendentals=0
    )


def first_mix_kernel(x_ref, carry_ref, vec_ref, mk_ref, mv_ref, mr_ref):
    gain, bias = vec_ref[0:1, :], vec_ref[1:2, :]
    mixes = [vec_ref[i : i + 1, :] for i in (4, 5, 6)]
    width = x_ref.shape[1]

    def step(i, before):
        rows = pl.ds(pl.multiple_of(i * CHUNK, CHUNK), CHUNK)
        normed, _, _ = norm_rows(x_ref[rows, :].astype(F32), gain, bias)
        behind = move_down(normed, before) * carry_ref[rows, :]
        for mix, out in zip(mixes, (mk_ref, mv_ref, mr_ref)):
            out[rows, :] = (normed * mix + behind * (1.0 - mix)).astype(BF)
        return normed[CHUNK - 1 :, :]

    lax.fori_loop(0, x_ref.shape[0] // CHUNK, step, jnp.zeros((1, width), F32), unroll=2)


def first_mix(x, carry, vectors):
    shape = jax.ShapeDtypeStruct(x.shape, BF)
    return pl.pallas_call(
        first_mix_kernel,
        out_shape=[shape] * 3,
        compiler_params=params(),
        cost_estimate=cost(0, 8 << 20),
    )(x, carry, vectors)


TILE = 256


def scan_rates(decay):
    speed = jnp.exp(decay)
    return [jnp.exp(-float(n) * speed) for n in (1, 2, 4, 8)]


def twice(values):
    return jnp.concatenate([values] * (TILE // 128), axis=1)


def time_forward_kernel(
    co, mk, mv, mr, ko, kx, vo, vx, ro, rx, vec, masks,
    key_ref, val_ref, rec_ref, pa_ref, pb_ref, gated_ref, kw, vw, rw, sems,
):
    j = pl.program_id(0)
    per_half = kw.shape[2] // TILE
    groups = [
        weight_copies(co, own, other, whole, sems.at[n], order)
        for n, (own, other, whole, order) in enumerate(
            ((ko, kx, kw, ORDERS[0]), (vo, vx, vw, ORDERS[1]), (ro, rx, rw, ORDERS[2]))
        )
    ]

    @pl.when(j == 0)
    def _():
        for copies in groups:
            start_all(copies)
        for copies in groups:
            wait_half(copies, 0)

    @pl.when(j == per_half)
    def _():
        for copies in groups:
            wait_half(copies, 1)

    half = co[3] ^ lax.div(j, per_half)
    columns = pl.ds(pl.multiple_of(lax.rem(j, per_half) * TILE, TILE), TILE)
    key_ref[...] = dot(mk[...], kw[half, :, columns], NN)
    val_ref[...] = dot(mv[...], vw[half, :, columns], NN)
    rec_ref[...] = dot(mr[...], rw[half, :, columns], NN)

    spread = (8, TILE)
    decay = jnp.broadcast_to(vec[2:3, :], spread)
    first = jnp.broadcast_to(vec[3:4, :], spread)
    r1, r2, r4, r8 = scan_rates(decay)
    powers = jnp.exp(-lax.broadcasted_iota(jnp.int32, spread, 0).astype(F32) * jnp.exp(decay))

    def group(start, state):
        rows = pl.ds(start, 8)
        key, val, pre = key_ref[rows, :], val_ref[rows, :], rec_ref[rows, :]
        m1, m2, m4, mf, ml = (twice(masks[n, rows, :]) for n in range(5))
        rec = 1.0 / (1.0 + jnp.exp(-pre))
        power = jnp.exp(key)
        bonus = jnp.exp(first + key)
        c1, c2, c4, cf, cl = m1 * r1, m2 * r2, m4 * r4, mf * powers, ml * r8
        priors, ends = [], []
        for local, entering in ((power * val, state[0]), (power, state[1])):
            local = local + c1 * pltpu.roll(local, 1, 0)
            local = local + c2 * pltpu.roll(local, 2, 0)
            local = local + c4 * pltpu.roll(local, 4, 0)
            priors.append(m1 * pltpu.roll(local, 1, 0) + cf * entering)
            ends.append(jnp.broadcast_to(local[7:8, :], spread) + cl * entering)
        wkv = (priors[0] + bonus * val) / (priors[1] + bonus)
        rec_ref[rows, :] = rec
        pa_ref[rows, :] = priors[0]
        pb_ref[rows, :] = priors[1]
        return rec * wkv, tuple(ends)

    def step(i, state):
        start = pl.multiple_of(i * CHUNK, CHUNK)
        upper, state = group(start, state)
        lower, state = group(pl.multiple_of(start + 8, 8), state)
        gated_ref[pl.ds(start, CHUNK), :] = jnp.concatenate([upper, lower], axis=0).astype(BF)
        return state

    zero = jnp.zeros(spread, F32)
    lax.fori_loop(0, key_ref.shape[0] // CHUNK, step, (zero, zero))


def time_forward(co, mixed, weights, vectors, masks):
    tokens, width = mixed[0].shape
    half = width // 2
    per_half = half // TILE

    def tile(j, co):
        return 0, (co[3] ^ lax.div(j, per_half)) * per_half + lax.rem(j, per_half)

    fixed = pl.BlockSpec((tokens, width), lambda j, co: (0, 0))
    block = pl.BlockSpec((tokens, TILE), tile)
    return pl.pallas_call(
        time_forward_kernel,
        grid_spec=pltpu.PrefetchScalarGridSpec(
            num_scalar_prefetch=1,
            grid=(width // TILE,),
            in_specs=[fixed] * 3
            + [anywhere()] * 6
            + [
                pl.BlockSpec((vectors.shape[0], TILE), tile),
                pl.BlockSpec(masks.shape, lambda j, co: (0, 0, 0)),
            ],
            out_specs=[block] * 6,
            scratch_shapes=[pltpu.VMEM((2, width, half), BF)] * 3
            + [pltpu.SemaphoreType.DMA((3, 32))],
        ),
        out_shape=[jax.ShapeDtypeStruct((tokens, width), F32)] * 5
        + [jax.ShapeDtypeStruct((tokens, width), BF)],
        compiler_params=params(),
        cost_estimate=cost(8, 34 << 20),
    )(co, *mixed, *[part for pair in weights for part in pair], vectors, masks)


def time_output_kernel(
    co, gated, x_ref, carry_ref, vec_ref, oo, ox, middle_ref, mk_ref, mr_ref, ow, last, sems
):
    i = pl.program_id(0)
    copies = weight_copies(co, oo, ox, ow, sems, ORDERS[3])

    @pl.when(i == 0)
    def _():
        start_all(copies)
        last[...] = jnp.zeros_like(last)
        wait_half(copies, 0)
        wait_half(copies, 1)

    half = ow.shape[2]
    middle_ref[...] = dot(gated[:, :half], ow[0], NT) + dot(gated[:, half:], ow[1], NT)
    gain, bias = vec_ref[7:8, :], vec_ref[8:9, :]
    mixes = [vec_ref[n : n + 1, :] for n in (9, 10)]

    def step(n, before):
        rows = pl.ds(pl.multiple_of(n * CHUNK, CHUNK), CHUNK)
        middle = middle_ref[rows, :] + x_ref[rows, :].astype(F32)
        middle_ref[rows, :] = middle
        normed, _, _ = norm_rows(middle, gain, bias)
        behind = move_down(normed, before) * carry_ref[rows, :]
        for mix, out in zip(mixes, (mk_ref, mr_ref)):
            out[rows, :] = (normed * mix + behind * (1.0 - mix)).astype(BF)
        return normed[CHUNK - 1 :, :]

    last[...] = lax.fori_loop(0, x_ref.shape[0] // CHUNK, step, last[...], unroll=2)


def time_output_step(co, gated, x, carry, vectors, weight):
    tokens, width = x.shape
    rows = tokens // 4
    tall = pl.BlockSpec((rows, width), lambda i, co: (i, 0))
    return pl.pallas_call(
        time_output_kernel,
        grid_spec=pltpu.PrefetchScalarGridSpec(
            num_scalar_prefetch=1,
            grid=(4,),
            in_specs=[
                tall,
                tall,
                pl.BlockSpec((rows, 1), lambda i, co: (i, 0)),
                pl.BlockSpec(vectors.shape, lambda i, co: (0, 0)),
                anywhere(),
                anywhere(),
            ],
            out_specs=[tall] * 3,
            scratch_shapes=[
                pltpu.VMEM((2, width, width // 2), BF),
                pltpu.VMEM((1, width), F32),
                pltpu.SemaphoreType.DMA((32,)),
            ],
        ),
        out_shape=[jax.ShapeDtypeStruct((tokens, width), t) for t in (F32, BF, BF)],
        compiler_params=params(),
        cost_estimate=cost(3, 14 << 20),
    )(co, gated, x, carry, vectors, *weight)


WIDE = 512


def hidden_kernel(co, mk, wo, wx, hidden_ref, active_ref, whole, sems):
    j = pl.program_id(0)
    per_half = whole.shape[2] // WIDE
    copies = weight_copies(co, wo, wx, whole, sems, ORDERS[4])

    @pl.when(j == 0)
    def _():
        start_all(copies)
        wait_half(copies, 0)

    @pl.when(j == per_half)
    def _():
        wait_half(copies, 1)

    half = co[3] ^ lax.div(j, per_half)
    columns = pl.ds(pl.multiple_of(lax.rem(j, per_half) * WIDE, WIDE), WIDE)
    active = jnp.maximum(dot(mk[...], whole[half, :, columns], NN), 0.0)
    active_ref[...] = active.astype(BF)
    hidden_ref[...] = (active * active).astype(BF)


def column_tile(per_half):
    return lambda j, co: (0, (co[3] ^ lax.div(j, per_half)) * per_half + lax.rem(j, per_half))


def hidden_step(co, mixed, weight):
    tokens, width = mixed.shape
    half = weight[0].shape[-1]
    block = pl.BlockSpec((tokens, WIDE), column_tile(half // WIDE))
    return pl.pallas_call(
        hidden_kernel,
        grid_spec=pltpu.PrefetchScalarGridSpec(
            num_scalar_prefetch=1,
            grid=(2 * half // WIDE,),
            in_specs=[
                pl.BlockSpec((tokens, width), lambda j, co: (0, 0)),
                anywhere(),
                anywhere(),
            ],
            out_specs=[block] * 2,
            scratch_shapes=[
                pltpu.VMEM((2, width, half), BF),
                pltpu.SemaphoreType.DMA((32,)),
            ],
        ),
        out_shape=[jax.ShapeDtypeStruct((tokens, 2 * half), BF)] * 2,
        compiler_params=params(),
        cost_estimate=cost(4.5, 26 << 20),
    )(co, mixed, *weight)


def result_kernel(
    co, scale, hidden, mr, middle_ref, teacher_ref, valid_ref, wo, wx, ro, rx,
    out_ref, dres_ref, dkv_ref, drec_ref, loss_ref, ww, rw, kv_ref, pre_ref, sems,
):
    i = pl.program_id(0)
    copies = weight_copies(co, wo, wx, ww, sems.at[0], ORDERS[6])
    recept = weight_copies(co, ro, rx, rw, sems.at[1], ORDERS[5])

    @pl.when(i == 0)
    def _():
        start_all(recept)
        start_all(copies)
        loss_ref[...] = jnp.zeros_like(loss_ref)
        for half in (0, 1):
            wait_half(recept, half)
        for half in (0, 1):
            wait_half(copies, half)

    wide, narrow = ww.shape[2], rw.shape[2]
    kv_ref[...] = dot(hidden[:, :wide], ww[0], NT) + dot(hidden[:, wide:], ww[1], NT)
    pre_ref[:, :narrow] = dot(mr[...], rw[0], NN)
    pre_ref[:, narrow:] = dot(mr[...], rw[1], NN)
    factor = scale[0]

    def step(n, total):
        rows = pl.ds(pl.multiple_of(n * CHUNK, CHUNK), CHUNK)
        kv = kv_ref[rows, :]
        rec = 1.0 / (1.0 + jnp.exp(-pre_ref[rows, :]))
        result = middle_ref[rows, :] + rec * kv
        out_ref[rows, :] = result.astype(BF)
        error = (result - teacher_ref[rows, :].astype(F32)) * valid_ref[rows, :]
        grad = error * factor
        dres_ref[rows, :] = grad
        dkv_ref[rows, :] = (grad * rec).astype(BF)
        drec_ref[rows, :] = (grad * kv * rec * (1.0 - rec)).astype(BF)
        return total + fold_rows(error * error)

    total = lax.fori_loop(
        0, kv_ref.shape[0] // CHUNK, step, jnp.zeros((8, kv_ref.shape[1]), F32)
    )
    loss_ref[...] += total


def result_step(co, scale, hidden, mixed, middle, teacher, valid, weight, recept):
    tokens, width = mixed.shape
    rows = tokens // 4
    wide = weight[0].shape[-1]
    tall = pl.BlockSpec((rows, width), lambda i, co, s: (i, 0))
    return pl.pallas_call(
        result_kernel,
        grid_spec=pltpu.PrefetchScalarGridSpec(
            num_scalar_prefetch=2,
            grid=(4,),
            in_specs=[
                pl.BlockSpec((rows, 2 * wide), lambda i, co, s: (i, 0)),
                tall,
                tall,
                tall,
                pl.BlockSpec((rows, 1), lambda i, co, s: (i, 0)),
            ]
            + [anywhere()] * 4,
            out_specs=[tall] * 4 + [pl.BlockSpec((8, width), lambda i, co, s: (0, 0))],
            scratch_shapes=[
                pltpu.VMEM((2, width, wide), BF),
                pltpu.VMEM((2, width, width // 2), BF),
                pltpu.VMEM((rows, width), F32),
                pltpu.VMEM((rows, width), F32),
                pltpu.SemaphoreType.DMA((2, 32)),
            ],
        ),
        out_shape=[jax.ShapeDtypeStruct((tokens, width), t) for t in (BF, F32, BF, BF)]
        + [jax.ShapeDtypeStruct((8, width), F32)],
        compiler_params=params(),
        cost_estimate=cost(7, 38 << 20),
    )(co, scale, hidden, mixed, middle, teacher, valid, *weight, *recept)


def weight_grad_kernel(co, model_ref, chan_ref, own, other, whole, sems, *, order):
    j = pl.program_id(0)
    per_half = whole.shape[2] // WIDE
    part = lax.rem(j, per_half)
    columns = pl.ds(pl.multiple_of(part * WIDE, WIDE), WIDE)
    turn = lax.div(j, per_half)
    whole[co[3] ^ turn, :, columns] = dot(model_ref[...], chan_ref[...], TN).astype(BF)

    def copies(piece):
        found = []
        for other_core, target in ((0, own), (1, other)):
            for index, rel in slot_list(order):
                row, half = slot_place(co, rel, other_core)
                copy = pltpu.make_async_copy(
                    whole.at[half, pl.ds(row, SLOT), piece],
                    target.at[index + (slice(None), piece)],
                    sems.at[len(found)],
                )
                found.append((rel["x"], copy))
        return found

    for which in (0, 1):

        @pl.when(turn == which)
        def _(which=which):
            for rel_x, copy in copies(columns):
                if rel_x == which:
                    copy.start()

    @pl.when(j == pl.num_programs(0) - 1)
    def _():
        for _, copy in copies(slice(None)):
            copy.wait()


def weight_grad(co, model, chan, order):
    tokens, width = model.shape
    half = chan.shape[1] // 2
    dims = tuple(SIZES[d] for d in order[::-1])
    shape = jax.ShapeDtypeStruct(dims + (SLOT, half), BF)
    return pl.pallas_call(
        functools.partial(weight_grad_kernel, order=order),
        grid_spec=pltpu.PrefetchScalarGridSpec(
            num_scalar_prefetch=1,
            grid=(2 * half // WIDE,),
            in_specs=[
                pl.BlockSpec((tokens, width), lambda j, co: (0, 0)),
                pl.BlockSpec((tokens, WIDE), column_tile(half // WIDE)),
            ],
            out_specs=[anywhere()] * 2,
            scratch_shapes=[
                pltpu.VMEM((2, width, half), BF),
                pltpu.SemaphoreType.DMA((32,)),
            ],
        ),
        out_shape=[shape] * 2,
        compiler_params=params(),
        cost_estimate=cost(half / 512 * 1.2, (2 << 20) * (1 + half / 256)),
    )(co, model, chan)


def hidden_back_kernel(co, dkv, active_ref, wo, wx, out_ref, whole, sems):
    j = pl.program_id(0)
    per_half = whole.shape[2] // WIDE
    copies = weight_copies(co, wo, wx, whole, sems, ORDERS[6])

    @pl.when(j == 0)
    def _():
        start_all(copies)
        wait_half(copies, 0)

    @pl.when(j == per_half)
    def _():
        wait_half(copies, 1)

    half = co[3] ^ lax.div(j, per_half)
    columns = pl.ds(pl.multiple_of(lax.rem(j, per_half) * WIDE, WIDE), WIDE)
    grad = dot(dkv[...], whole[half, :, columns], NN)
    out_ref[...] = (2.0 * active_ref[...].astype(F32) * grad).astype(BF)


def hidden_back(co, dkv, active, weight):
    tokens, width = dkv.shape
    half = weight[0].shape[-1]
    block = pl.BlockSpec((tokens, WIDE), column_tile(half // WIDE))
    return pl.pallas_call(
        hidden_back_kernel,
        grid_spec=pltpu.PrefetchScalarGridSpec(
            num_scalar_prefetch=1,
            grid=(2 * half // WIDE,),
            in_specs=[
                pl.BlockSpec((tokens, width), lambda j, co: (0, 0)),
                block,
                anywhere(),
                anywhere(),
            ],
            out_specs=block,
            scratch_shapes=[
                pltpu.VMEM((2, width, half), BF),
                pltpu.SemaphoreType.DMA((32,)),
            ],
        ),
        out_shape=jax.ShapeDtypeStruct((tokens, 2 * half), BF),
        compiler_params=params(),
        cost_estimate=cost(4.5, 26 << 20),
    )(co, dkv, active, *weight)


def middle_back_kernel(
    co, dkey, drec, middle_ref, dres_ref, lead_ref, vec_ref, wo, wx, ro, rx,
    dmid_ref, dtime_ref, sums_ref, ww, rw, gk_ref, gr_ref, next_ref, sems,
):
    i = pl.program_id(0)
    copies = weight_copies(co, wo, wx, ww, sems.at[0], ORDERS[4])
    recept = weight_copies(co, ro, rx, rw, sems.at[1], ORDERS[5])

    @pl.when(i == 0)
    def _():
        start_all(recept)
        start_all(copies)
        sums_ref[...] = jnp.zeros_like(sums_ref)
        next_ref[...] = jnp.zeros_like(next_ref)
        for half in (0, 1):
            wait_half(recept, half)
        for half in (0, 1):
            wait_half(copies, half)

    wide, narrow = ww.shape[2], rw.shape[2]
    gk_ref[...] = dot(dkey[:, :wide], ww[0], NT) + dot(dkey[:, wide:], ww[1], NT)
    gr_ref[...] = dot(drec[:, :narrow], rw[0], NT) + dot(drec[:, narrow:], rw[1], NT)
    gain, bias = vec_ref[7:8, :], vec_ref[8:9, :]
    mix_k, mix_r = vec_ref[9:10, :], vec_ref[10:11, :]
    steps = middle_ref.shape[0] // CHUNK

    def step(n, after):
        rows = pl.ds(pl.multiple_of((steps - 1 - n) * CHUNK, CHUNK), CHUNK)
        normed, unit, scaled = norm_rows(middle_ref[rows, :], gain, bias)
        lead = lead_ref[rows, :]
        gk, gr = gk_ref[rows, :], gr_ref[rows, :]
        uk = move_up(gk, after[0]) * lead
        ur = move_up(gr, after[1]) * lead
        grad = gk * mix_k + gr * mix_r + uk * (1.0 - mix_k) + ur * (1.0 - mix_r)
        sums_ref[0] += fold_rows(grad * unit)
        sums_ref[1] += fold_rows(grad)
        sums_ref[2] += fold_rows(normed * (gk - uk))
        sums_ref[3] += fold_rows(normed * (gr - ur))
        dmid = dres_ref[rows, :] + norm_rows_back(grad, unit, scaled, gain)
        dmid_ref[rows, :] = dmid
        dtime_ref[rows, :] = dmid.astype(BF)
        return gk[:1, :], gr[:1, :]

    after = lax.fori_loop(0, steps, step, (next_ref[0:1, :], next_ref[1:2, :]))
    next_ref[0:1, :] = after[0]
    next_ref[1:2, :] = after[1]


def middle_back(co, dkey, drec, middle, dres, lead, vectors, weight, recept):
    tokens, width = middle.shape
    rows = tokens // 4
    wide = weight[0].shape[-1]
    tall = pl.BlockSpec((rows, width), lambda i, co: (3 - i, 0))
    return pl.pallas_call(
        middle_back_kernel,
        grid_spec=pltpu.PrefetchScalarGridSpec(
            num_scalar_prefetch=1,
            grid=(4,),
            in_specs=[
                pl.BlockSpec((rows, 2 * wide), lambda i, co: (3 - i, 0)),
                tall,
                tall,
                tall,
                pl.BlockSpec((rows, 1), lambda i, co: (3 - i, 0)),
                pl.BlockSpec(vectors.shape, lambda i, co: (0, 0)),
            ]
            + [anywhere()] * 4,
            out_specs=[tall] * 2 + [pl.BlockSpec((4, 8, width), lambda i, co: (0, 0, 0))],
            scratch_shapes=[
                pltpu.VMEM((2, width, wide), BF),
                pltpu.VMEM((2, width, width // 2), BF),
                pltpu.VMEM((rows, width), F32),
                pltpu.VMEM((rows, width), F32),
                pltpu.VMEM((8, width), F32),
                pltpu.SemaphoreType.DMA((2, 32)),
            ],
        ),
        out_shape=[
            jax.ShapeDtypeStruct((tokens, width), F32),
            jax.ShapeDtypeStruct((tokens, width), BF),
            jax.ShapeDtypeStruct((4, 8, width), F32),
        ],
        compiler_params=params(),
        cost_estimate=cost(8, 36 << 20),
    )(co, dkey, drec, middle, dres, lead, vectors, *weight, *recept)


def time_back_kernel(
    co, dtime, key_ref, val_ref, rec_ref, pa_ref, pb_ref, vec, masks, oo, ox,
    dkey_ref, dval_ref, drec_ref, sums_ref, ow, dg_ref, sems,
):
    j = pl.program_id(0)
    per_half = ow.shape[2] // TILE
    copies = weight_copies(co, oo, ox, ow, sems, ORDERS[3])

    @pl.when(j == 0)
    def _():
        start_all(copies)
        wait_half(copies, 0)

    @pl.when(j == per_half)
    def _():
        wait_half(copies, 1)

    half = co[3] ^ lax.div(j, per_half)
    columns = pl.ds(pl.multiple_of(lax.rem(j, per_half) * TILE, TILE), TILE)
    dg_ref[...] = dot(dtime[...], ow[half, :, columns], NN)

    spread = (8, TILE)
    decay = jnp.broadcast_to(vec[2:3, :], spread)
    first = jnp.broadcast_to(vec[3:4, :], spread)
    r1, r2, r4, r8 = scan_rates(decay)
    left = 7.0 - lax.broadcasted_iota(jnp.int32, spread, 0).astype(F32)
    powers = jnp.exp(-left * jnp.exp(decay))

    def group(start, state):
        rows = pl.ds(start, 8)
        n1, n2, n4, nf, c0, ml = (twice(masks[n, rows, :]) for n in (5, 6, 7, 8, 9, 4))
        key, val, rec, dg = key_ref[rows, :], val_ref[rows, :], rec_ref[rows, :], dg_ref[rows, :]
        pa, pb = pa_ref[rows, :], pb_ref[rows, :]
        power = jnp.exp(key)
        bonus = jnp.exp(first + key)
        inverse = 1.0 / (pb + bonus)
        wkv = (pa + bonus * val) * inverse
        slope = dg * rec * inverse
        drec = dg * wkv * rec * (1.0 - rec)
        c1, c2, c4, cf, cl = n1 * r1, n2 * r2, n4 * r4, nf * powers, ml * r8
        found, starts = [], []
        for local, leaving in ((slope, state[0]), (-slope * wkv, state[1])):
            local = local + c1 * pltpu.roll(local, 7, 0)
            local = local + c2 * pltpu.roll(local, 6, 0)
            local = local + c4 * pltpu.roll(local, 4, 0)
            found.append(n1 * pltpu.roll(local, 7, 0) + cf * leaving)
            starts.append(c0 * jnp.broadcast_to(local[0:1, :], spread) + cl * leaving)
        later_a, later_b = found
        summand = bonus * slope * (val - wkv)
        dkey = power * (later_a * val + later_b) + summand
        dval = power * later_a + bonus * slope
        state = (
            starts[0],
            starts[1],
            state[2] + summand,
            state[3] + later_a * pa + later_b * pb,
        )
        return (dkey, dval, drec), state

    steps = key_ref.shape[0] // CHUNK

    def step(n, state):
        start = pl.multiple_of((steps - 1 - n) * CHUNK, CHUNK)
        lower, state = group(pl.multiple_of(start + 8, 8), state)
        upper, state = group(start, state)
        for up, low, out in zip(upper, lower, (dkey_ref, dval_ref, drec_ref)):
            out[pl.ds(start, CHUNK), :] = jnp.concatenate([up, low], axis=0).astype(BF)
        return state

    zero = jnp.zeros(spread, F32)
    _, _, first_sum, decay_sum = lax.fori_loop(0, steps, step, (zero,) * 4)
    sums_ref[0] = -r1 * jnp.exp(decay) * decay_sum
    sums_ref[1] = first_sum


def time_back(co, dtime, saved, vectors, masks, weight):
    tokens, width = dtime.shape
    half = width // 2
    tile = column_tile(half // TILE)
    block = pl.BlockSpec((tokens, TILE), tile)
    return pl.pallas_call(
        time_back_kernel,
        grid_spec=pltpu.PrefetchScalarGridSpec(
            num_scalar_prefetch=1,
            grid=(width // TILE,),
            in_specs=[pl.BlockSpec((tokens, width), lambda j, co: (0, 0))]
            + [block] * 5
            + [
                pl.BlockSpec((vectors.shape[0], TILE), tile),
                pl.BlockSpec(masks.shape, lambda j, co: (0, 0, 0)),
                anywhere(),
                anywhere(),
            ],
            out_specs=[block] * 3
            + [pl.BlockSpec((2, 8, TILE), lambda j, co: (0,) + tile(j, co))],
            scratch_shapes=[
                pltpu.VMEM((2, width, half), BF),
                pltpu.VMEM((tokens, TILE), F32),
                pltpu.SemaphoreType.DMA((32,)),
            ],
        ),
        out_shape=[jax.ShapeDtypeStruct((tokens, width), BF)] * 3
        + [jax.ShapeDtypeStruct((2, 8, width), F32)],
        compiler_params=params(),
        cost_estimate=cost(9, 34 << 20),
    )(co, dtime, *saved, vectors, masks, *weight)


def input_back_kernel(
    co, dkey, dval, drec, x_ref, dmid_ref, lead_ref, vec_ref, ko, kx, vo, vx, ro, rx,
    out_ref, sums_ref, kw, vw, rw, gk_ref, gv_ref, gr_ref, next_ref, sems,
):
    i = pl.program_id(0)
    groups = [
        weight_copies(co, own, other, whole, sems.at[n], order)
        for n, (own, other, whole, order) in enumerate(
            ((ko, kx, kw, ORDERS[0]), (vo, vx, vw, ORDERS[1]), (ro, rx, rw, ORDERS[2]))
        )
    ]

    @pl.when(i == 0)
    def _():
        for copies in groups:
            start_all(copies)
        sums_ref[...] = jnp.zeros_like(sums_ref)
        next_ref[...] = jnp.zeros_like(next_ref)
        for copies in groups:
            wait_half(copies, 0)
            wait_half(copies, 1)

    half = kw.shape[2]
    for grad, whole, out in ((dkey, kw, gk_ref), (dval, vw, gv_ref), (drec, rw, gr_ref)):
        out[...] = dot(grad[:, :half], whole[0], NT) + dot(grad[:, half:], whole[1], NT)
    gain, bias = vec_ref[0:1, :], vec_ref[1:2, :]
    mixes = [vec_ref[n : n + 1, :] for n in (4, 5, 6)]
    steps = x_ref.shape[0] // CHUNK

    def step(n, after):
        rows = pl.ds(pl.multiple_of((steps - 1 - n) * CHUNK, CHUNK), CHUNK)
        normed, unit, scaled = norm_rows(x_ref[rows, :].astype(F32), gain, bias)
        lead = lead_ref[rows, :]
        total = jnp.zeros_like(normed)
        firsts = []
        for m, (part, mix) in enumerate(zip((gk_ref, gv_ref, gr_ref), mixes)):
            grad = part[rows, :]
            up = move_up(grad, after[m]) * lead
            total = total + grad * mix + up * (1.0 - mix)
            sums_ref[2 + m] += fold_rows(normed * (grad - up))
            firsts.append(grad[:1, :])
        sums_ref[0] += fold_rows(total * unit)
        sums_ref[1] += fold_rows(total)
        out_ref[rows, :] = dmid_ref[rows, :] + norm_rows_back(total, unit, scaled, gain)
        return tuple(firsts)

    after = lax.fori_loop(0, steps, step, tuple(next_ref[m : m + 1, :] for m in range(3)))
    for m in range(3):
        next_ref[m : m + 1, :] = after[m]


def input_back(co, grads, x, dmid, lead, vectors, weights):
    tokens, width = x.shape
    rows = tokens // 4
    tall = pl.BlockSpec((rows, width), lambda i, co: (3 - i, 0))
    return pl.pallas_call(
        input_back_kernel,
        grid_spec=pltpu.PrefetchScalarGridSpec(
            num_scalar_prefetch=1,
            grid=(4,),
            in_specs=[tall] * 5
            + [
                pl.BlockSpec((rows, 1), lambda i, co: (3 - i, 0)),
                pl.BlockSpec(vectors.shape, lambda i, co: (0, 0)),
            ]
            + [anywhere()] * 6,
            out_specs=[tall, pl.BlockSpec((5, 8, width), lambda i, co: (0, 0, 0))],
            scratch_shapes=[pltpu.VMEM((2, width, width // 2), BF)] * 3
            + [pltpu.VMEM((rows, width), F32)] * 3
            + [pltpu.VMEM((8, width), F32), pltpu.SemaphoreType.DMA((3, 32))],
        ),
        out_shape=[
            jax.ShapeDtypeStruct((tokens, width), F32),
            jax.ShapeDtypeStruct((5, 8, width), F32),
        ],
        compiler_params=params(),
        cost_estimate=cost(7, 26 << 20),
    )(co, *grads, x, dmid, lead, vectors, *[part for pair in weights for part in pair])


ORDERS = ("xzy", "yzx", "zyx", "zxy", "xzy", "zyx", "yzx")
RING_UP = [(0, 1), (1, 2), (2, 3), (3, 0)]
RING_DOWN = [(1, 0), (2, 1), (3, 2), (0, 3)]


class Links:
    def __init__(self):
        self.co = jnp.stack([lax.axis_index(a) for a in ("z", "y", "c", "x")]).astype(jnp.int32)

    def gather(self, shard, order):
        held = shard
        for axis in order:
            if axis == "z":
                parts = [held]
                for _ in range(3):
                    parts.append(lax.ppermute(parts[-1], "z", RING_UP))
                held = jnp.stack(parts)
            else:
                held = jnp.stack([held, lax.ppermute(held, axis, SWAP)])
        return held, lax.ppermute(held, "c", SWAP)

    def reduce(self, own, other, order):
        held = own + lax.ppermute(other, "c", SWAP)
        for n, axis in enumerate(order[::-1]):
            wide = (lambda v: v.astype(F32)) if n == 2 else (lambda v: v)
            if axis == "z":
                moving = held[3]
                for place in (2, 1):
                    moving = held[place] + lax.ppermute(moving, "z", RING_DOWN)
                held = wide(held[0]) + wide(lax.ppermute(moving, "z", RING_DOWN))
            else:
                held = wide(held[0]) + wide(lax.ppermute(held[1], axis, SWAP))
        return held

    def total(self, values):
        for axis in ("x", "y", "c"):
            values = values + lax.ppermute(values, axis, SWAP)
        values = values + lax.ppermute(values, "z", [(0, 1), (1, 0), (2, 3), (3, 2)])
        return values + lax.ppermute(values, "z", [(0, 2), (2, 0), (1, 3), (3, 1)])


class Plain:
    def __init__(self, blocks):
        self.blocks = blocks
        self.co = jnp.zeros((4,), jnp.int32)

    def gather(self, shard, order):
        whole = lax.all_gather(shard, ("z", "y", "c"), axis=0, tiled=True)
        whole = lax.all_gather(whole, "x", axis=1, tiled=True)
        half = whole.shape[1] // 2
        dims = tuple(SIZES[d] for d in order[::-1])
        found = []
        for core in (0, 1):
            parts = []
            for _, rel in slot_list(order):
                block = ((4 - rel["z"]) & 3) * 4 + rel["y"] * 2 + core
                part = whole[block * SLOT : (block + 1) * SLOT]
                parts.append(part[:, rel["x"] * half : (rel["x"] + 1) * half])
            found.append(jnp.stack(parts).reshape(dims + (SLOT, half)))
        return tuple(found)

    def reduce(self, own, other, order):
        half = own.shape[-1]
        table = {}
        for core, source in ((0, own), (1, other)):
            for index, rel in slot_list(order):
                block = ((4 - rel["z"]) & 3) * 4 + rel["y"] * 2 + core
                table[block, rel["x"]] = source[index]
        whole = jnp.concatenate(
            [jnp.concatenate([table[b, 0], table[b, 1]], axis=1) for b in range(16)], axis=0
        )
        whole = lax.psum_scatter(whole, ("z", "y", "c"), scatter_dimension=0, tiled=True)
        whole = lax.psum_scatter(whole, "x", scatter_dimension=1, tiled=True)
        return whole.astype(F32)

    def total(self, values):
        return lax.psum(values, EVERY)


def scan_masks(carry):
    c = carry.reshape(-1, 8)
    place = jnp.arange(8)[None, :]

    def behind(values, n):
        return jnp.where(place >= n, jnp.roll(values, n, axis=1), 0.0)

    def ahead(values, n):
        return jnp.where(place < 8 - n, jnp.roll(values, -n, axis=1), 0.0)

    m1 = jnp.where(place >= 1, c, 0.0)
    m2 = m1 * behind(m1, 1)
    m4 = m2 * behind(m2, 2)
    mf = jnp.cumprod(c, axis=1)
    ml = jnp.broadcast_to(mf[:, 7:], c.shape)
    n1 = ahead(c, 1)
    n2 = n1 * ahead(n1, 1)
    n4 = n2 * ahead(n2, 2)
    back = jnp.cumprod(c[:, ::-1], axis=1)[:, ::-1]
    nf = jnp.where(place < 7, jnp.roll(back, -1, axis=1), 1.0)
    c0 = jnp.broadcast_to(c[:, :1], c.shape)
    table = jnp.stack([m1, m2, m4, mf, ml, n1, n2, n4, nf, c0]).reshape(10, -1, 1)
    return jnp.broadcast_to(table, table.shape[:2] + (128,))


def on_device(
    inputs,
    segments,
    teacher,
    first_norm_gain,
    first_norm_bias,
    time_decay,
    time_first,
    time_mix_key,
    time_mix_value,
    time_mix_recept,
    time_key,
    time_value,
    time_recept,
    time_output,
    second_norm_gain,
    second_norm_bias,
    channel_mix_key,
    channel_mix_recept,
    channel_key,
    channel_recept,
    channel_value,
):
    tokens, width = inputs.shape
    sizes = {a: lax.axis_size(a) for a in EVERY}
    devices = sizes["z"] * sizes["y"] * sizes["c"] * sizes["x"]
    fast = (sizes["z"], sizes["y"], sizes["c"], sizes["x"]) == (4, 2, 2, 2)
    links = Links() if fast else Plain(width // SLOT)
    co = links.co
    side = lax.axis_index("x")

    ids = lax.dynamic_slice_in_dim(segments, side * tokens, tokens)
    previous = jnp.concatenate([jnp.zeros((1,), jnp.int32), ids[:-1]])
    started = jnp.arange(tokens, dtype=jnp.int32) > 0
    carry = ((ids == previous) & (ids > 0) & started).astype(F32)
    valid = (ids > 0).astype(F32)
    lead = jnp.concatenate([carry[1:], jnp.zeros((1,), F32)])
    masks = scan_masks(carry)
    carry, valid_rows, lead = carry[:, None], valid[:, None], lead[:, None]

    flat = ((lax.axis_index("z") * sizes["y"] + lax.axis_index("y")) * sizes["c"] + lax.axis_index("c")) * sizes["x"] + side
    own_vectors = jnp.stack(
        [
            first_norm_gain,
            first_norm_bias,
            time_decay,
            time_first,
            time_mix_key,
            time_mix_value,
            time_mix_recept,
            second_norm_gain,
            second_norm_bias,
            channel_mix_key,
            channel_mix_recept,
        ]
    )
    piece = own_vectors.shape[1]
    spread = jnp.where(
        jnp.arange(width)[None, :] // piece == flat, jnp.tile(own_vectors, (1, width // piece)), 0.0
    )
    counts = jnp.broadcast_to(jnp.sum(valid), (1, width))
    vectors = links.total(jnp.concatenate([spread, counts, jnp.zeros((4, width), F32)]))
    count = vectors[11, 0]

    shards = (
        time_key,
        time_value,
        time_recept,
        time_output.T,
        channel_key,
        channel_recept,
        channel_value.T,
    )
    key_w, value_w, recept_w, output_w, ckey_w, crecept_w, cvalue_w = (
        links.gather(shard, order) for shard, order in zip(shards, ORDERS)
    )

    if sizes["x"] == 2:
        mine = lax.dynamic_slice_in_dim(teacher, side * tokens, tokens)
        theirs = lax.dynamic_slice_in_dim(teacher, (1 - side) * tokens, tokens)
        theirs = lax.ppermute(theirs, "x", SWAP)
        teacher_rows = jnp.where(
            side == 0,
            jnp.concatenate([mine, theirs], axis=1),
            jnp.concatenate([theirs, mine], axis=1),
        )
    else:
        teacher_rows = teacher

    mixed = first_mix(inputs, carry, vectors)
    *saved, gated = time_forward(co, mixed, (key_w, value_w, recept_w), vectors, masks)
    middle, mixed_k2, mixed_r2 = time_output_step(co, gated, inputs, carry, vectors, output_w)
    hidden, active = hidden_step(co, mixed_k2, ckey_w)
    scale = (float(tokens * devices) / count).reshape(1)
    result, dres, dkv, drec2, loss_rows = result_step(
        co, scale, hidden, mixed_r2, middle, teacher_rows, valid_rows, cvalue_w, crecept_w
    )
    if sizes["x"] == 2:
        half = width // 2
        kept = lax.dynamic_slice_in_dim(result, side * half, half, axis=1)
        sent = lax.dynamic_slice_in_dim(result, (1 - side) * half, half, axis=1)
        arrived = lax.ppermute(sent, "x", SWAP)
        outputs = jnp.where(
            side == 0,
            jnp.concatenate([kept, arrived], axis=0),
            jnp.concatenate([arrived, kept], axis=0),
        )
    else:
        outputs = result

    cvalue_g = links.reduce(*weight_grad(co, dkv, hidden, ORDERS[6]), ORDERS[6])
    dkey2 = hidden_back(co, dkv, active, cvalue_w)
    ckey_g = links.reduce(*weight_grad(co, mixed_k2, dkey2, ORDERS[4]), ORDERS[4])
    crecept_g = links.reduce(*weight_grad(co, mixed_r2, drec2, ORDERS[5]), ORDERS[5])
    dmid, dtime, sums2 = middle_back(
        co, dkey2, drec2, middle, dres, lead, vectors, ckey_w, crecept_w
    )
    output_g = links.reduce(*weight_grad(co, dtime, gated, ORDERS[3]), ORDERS[3])
    *dmix, sums_t = time_back(co, dtime, saved, vectors, masks, output_w)
    time_g = [
        links.reduce(*weight_grad(co, m, d, order), order)
        for m, d, order in zip(mixed, dmix, ORDERS)
    ]
    input_grad, sums1 = input_back(
        co, dmix, inputs, dmid, lead, vectors, (key_w, value_w, recept_w)
    )

    rows = jnp.concatenate([sums1[:2], sums_t, sums1[2:], sums2, loss_rows[None]])
    totals = links.total(jnp.sum(rows, axis=1))
    loss = jnp.sum(totals[11]) / (2.0 * count * width)
    vector_g = lax.dynamic_slice_in_dim(totals, flat * piece, piece, axis=1)
    return (
        outputs,
        loss,
        input_grad,
        *[vector_g[n] for n in range(7)],
        *time_g,
        output_g.T,
        *[vector_g[n] for n in range(7, 11)],
        ckey_g,
        crecept_g,
        cvalue_g.T,
    )


def solution(mesh):
    fsdp, tp = mesh.shape["fsdp"], mesh.shape["tp"]
    core = 2 if fsdp % 4 == 0 else 1
    split = Mesh(mesh.devices.reshape(fsdp // (core * core), core, core, tp), EVERY)
    rows = ("z", "y", "c")
    vector = P(EVERY)
    matrix = P(rows, "x")
    turned = P("x", rows)
    tall = P(EVERY, None)
    return jax.shard_map(
        on_device,
        mesh=split,
        in_specs=(
            (tall, P(rows), matrix)
            + (vector,) * 7
            + (matrix, matrix, matrix, turned)
            + (vector,) * 4
            + (matrix, matrix, turned)
        ),
        out_specs=(
            (matrix, P(), tall)
            + (vector,) * 7
            + (matrix, matrix, matrix, turned)
            + (vector,) * 4
            + (matrix, matrix, turned)
        ),
        check_vma=False,
    )
```

```python
import functools
import itertools
import math

import jax
import jax.numpy as jnp
from jax import lax
from jax.experimental import pallas as pl
from jax.experimental.pallas import tpu as pltpu
from jax.sharding import Mesh
from jax.sharding import PartitionSpec as P

BF = jnp.bfloat16
F32 = jnp.float32
EPSILON = 1e-05
SLOT = 64
CHUNK = 16
VMEM_LIMIT = 58 << 20
EVERY = ("w", "u", "y", "c", "x")
SWAP = [(0, 1), (1, 0)]

NN = (((1,), (0,)), ((), ()))
NT = (((1,), (1,)), ((), ()))
TN = (((0,), (0,)), ((), ()))


def dot(left, right, dims):
    return lax.dot_general(left, right, dims, preferred_element_type=F32)


def rel_slots(order):
    for other_core in (0, 1):
        for last in (0, 1):
            for index in itertools.product((0, 1), repeat=3):
                rel = dict(zip(order[2::-1], index))
                rel[order[3]] = last
                rel["c"] = other_core
                yield other_core * 2 + last, index, rel


def slot_place(co, rel):
    at = {axis: co[n] ^ rel[axis] for n, axis in enumerate(EVERY)}
    block = at["w"] * 8 + at["u"] * 4 + at["y"] * 2 + at["c"]
    return pl.multiple_of(block * SLOT, SLOT), at["x"]


def weight_copies(co, refs, whole, sems, layout):
    copies = []
    refs = list(refs)
    for kind, order, first, columns in layout:
        target = pl.ds(first, columns)
        if kind == "rel":
            arrays, refs = refs[:4], refs[4:]
            for which, index, rel in rel_slots(order):
                row, half = slot_place(co, rel)
                copies.append(
                    (
                        rel["x"],
                        pltpu.make_async_copy(
                            arrays[which].at[index],
                            whole.at[half, pl.ds(row, SLOT), target],
                            sems.at[len(copies)],
                        ),
                    )
                )
        else:
            array, refs = refs[0], refs[1:]
            for rel_x in (0, 1):
                half = co[4] ^ rel_x
                for block in range(16):
                    copies.append(
                        (
                            rel_x,
                            pltpu.make_async_copy(
                                array.at[block, half, :, pl.ds(order, columns)],
                                whole.at[half, pl.ds(block * SLOT, SLOT), target],
                                sems.at[len(copies)],
                            ),
                        )
                    )
    return copies


def take_refs(refs, layout):
    count = sum(4 if part[0] == "rel" else 1 for part in layout)
    return refs[:count], refs[count:]


def arrays_of(*weights):
    return [array for _, arrays in weights for array in arrays]


def weight_width(weight):
    return sum(part[3] for part in weight[0])


def sem_count(weight):
    return 32 * len(weight[0])


def start_all(copies):
    for _, copy in copies:
        copy.start()


def wait_half(copies, half):
    for which, copy in copies:
        if which == half:
            copy.wait()


def norm_rows(values, gain, bias):
    centre = values - jnp.mean(values, axis=-1, keepdims=True)
    scaled = lax.rsqrt(jnp.mean(centre * centre, axis=-1, keepdims=True) + EPSILON)
    unit = centre * scaled
    return unit * gain + bias, unit, scaled


def norm_rows_back(grad, unit, scaled, gain):
    weighted = grad * gain
    return scaled * (
        weighted
        - jnp.mean(weighted, axis=-1, keepdims=True)
        - unit * jnp.mean(weighted * unit, axis=-1, keepdims=True)
    )


def first_row(shape):
    return lax.broadcasted_iota(jnp.int32, shape, 0) == 0


def last_row(shape):
    return lax.broadcasted_iota(jnp.int32, shape, 0) == shape[0] - 1


def move_down(values, before):
    return jnp.where(first_row(values.shape), before, pltpu.roll(values, 1, 0))


def move_up(values, after):
    return jnp.where(last_row(values.shape), after, pltpu.roll(values, values.shape[0] - 1, 0))


def fold_rows(values):
    return values[:8] + values[8:]


def params(semantics=1):
    return pltpu.CompilerParams(vmem_limit_bytes=VMEM_LIMIT)


def anywhere():
    return pl.BlockSpec(memory_space=pl.ANY)


def cost(units, traffic):
    return pl.CostEstimate(
        flops=int(units * 2 * 1024**3), bytes_accessed=int(traffic), transcendentals=0
    )


def first_mix_kernel(x_ref, carry_ref, vec_ref, mk_ref, mv_ref, mr_ref):
    gain, bias = vec_ref[0:1, :], vec_ref[1:2, :]
    mixes = [vec_ref[i : i + 1, :] for i in (4, 5, 6)]
    width = x_ref.shape[1]

    def step(i, before):
        rows = pl.ds(pl.multiple_of(i * CHUNK, CHUNK), CHUNK)
        normed, _, _ = norm_rows(x_ref[rows, :].astype(F32), gain, bias)
        behind = move_down(normed, before) * carry_ref[rows, :]
        for mix, out in zip(mixes, (mk_ref, mv_ref, mr_ref)):
            out[rows, :] = (normed * mix + behind * (1.0 - mix)).astype(BF)
        return normed[CHUNK - 1 :, :]

    lax.fori_loop(0, x_ref.shape[0] // CHUNK, step, jnp.zeros((1, width), F32), unroll=2)


def first_mix(x, carry, vectors):
    shape = jax.ShapeDtypeStruct(x.shape, BF)
    return pl.pallas_call(
        first_mix_kernel,
        out_shape=[shape] * 3,
        compiler_params=params(),
        cost_estimate=cost(0, 8 << 20),
    )(x, carry, vectors)


TILE = 256


def scan_rates(decay):
    speed = jnp.exp(decay)
    return [jnp.exp(-float(n) * speed) for n in (1, 2, 4, 8)]


def twice(values):
    return jnp.concatenate([values] * (TILE // 128), axis=1)


def time_forward_kernel(
    co, mk, mv, mr, vec, masks, *refs, layouts,
):
    key_w, refs = take_refs(refs, layouts[0])
    val_w, refs = take_refs(refs, layouts[1])
    rec_w, refs = take_refs(refs, layouts[2])
    key_ref, val_ref, rec_ref, pa_ref, pb_ref, gated_ref, kw, vw, rw, sems = refs
    j = pl.program_id(0)
    per_half = kw.shape[2] // TILE
    groups = [
        weight_copies(co, arrays, whole, sems.at[n], layout)
        for n, (arrays, whole, layout) in enumerate(zip((key_w, val_w, rec_w), (kw, vw, rw), layouts))
    ]

    @pl.when(j == 0)
    def _():
        for copies in groups:
            start_all(copies)
        for copies in groups:
            wait_half(copies, 0)

    @pl.when(j == per_half)
    def _():
        for copies in groups:
            wait_half(copies, 1)

    half = co[4] ^ lax.div(j, per_half)
    columns = pl.ds(pl.multiple_of(lax.rem(j, per_half) * TILE, TILE), TILE)
    key_ref[...] = dot(mk[...], kw[half, :, columns], NN)
    val_ref[...] = dot(mv[...], vw[half, :, columns], NN)
    rec_ref[...] = dot(mr[...], rw[half, :, columns], NN)

    spread = (8, TILE)
    decay = jnp.broadcast_to(vec[2:3, :], spread)
    first = jnp.broadcast_to(vec[3:4, :], spread)
    r1, r2, r4, r8 = scan_rates(decay)
    powers = jnp.exp(-lax.broadcasted_iota(jnp.int32, spread, 0).astype(F32) * jnp.exp(decay))

    def group(start, state):
        rows = pl.ds(start, 8)
        key, val, pre = key_ref[rows, :], val_ref[rows, :], rec_ref[rows, :]
        m1, m2, m4, mf, ml = (twice(masks[n, rows, :]) for n in range(5))
        rec = 1.0 / (1.0 + jnp.exp(-pre))
        power = jnp.exp(key)
        bonus = jnp.exp(first + key)
        c1, c2, c4, cf, cl = m1 * r1, m2 * r2, m4 * r4, mf * powers, ml * r8
        priors, ends = [], []
        for local, entering in ((power * val, state[0]), (power, state[1])):
            local = local + c1 * pltpu.roll(local, 1, 0)
            local = local + c2 * pltpu.roll(local, 2, 0)
            local = local + c4 * pltpu.roll(local, 4, 0)
            priors.append(m1 * pltpu.roll(local, 1, 0) + cf * entering)
            ends.append(jnp.broadcast_to(local[7:8, :], spread) + cl * entering)
        wkv = (priors[0] + bonus * val) / (priors[1] + bonus)
        rec_ref[rows, :] = rec
        pa_ref[rows, :] = priors[0]
        pb_ref[rows, :] = priors[1]
        return rec * wkv, tuple(ends)

    def step(i, state):
        start = pl.multiple_of(i * CHUNK, CHUNK)
        upper, state = group(start, state)
        lower, state = group(pl.multiple_of(start + 8, 8), state)
        gated_ref[pl.ds(start, CHUNK), :] = jnp.concatenate([upper, lower], axis=0).astype(BF)
        return state

    zero = jnp.zeros(spread, F32)
    lax.fori_loop(0, key_ref.shape[0] // CHUNK, step, (zero, zero))


def time_forward(co, mixed, weights, vectors, masks):
    tokens, width = mixed[0].shape
    half = width // 2
    per_half = half // TILE

    def tile(j, co):
        return 0, (co[4] ^ lax.div(j, per_half)) * per_half + lax.rem(j, per_half)

    fixed = pl.BlockSpec((tokens, width), lambda j, co: (0, 0))
    block = pl.BlockSpec((tokens, TILE), tile)
    return pl.pallas_call(
        functools.partial(time_forward_kernel, layouts=[w[0] for w in weights]),
        grid_spec=pltpu.PrefetchScalarGridSpec(
            num_scalar_prefetch=1,
            grid=(width // TILE,),
            in_specs=[fixed] * 3
            + [
                pl.BlockSpec((vectors.shape[0], TILE), tile),
                pl.BlockSpec(masks.shape, lambda j, co: (0, 0, 0)),
            ]
            + [anywhere()] * len(arrays_of(*weights)),
            out_specs=[block] * 6,
            scratch_shapes=[pltpu.VMEM((2, width, half), BF)] * 3
            + [pltpu.SemaphoreType.DMA((3, 32))],
        ),
        out_shape=[jax.ShapeDtypeStruct((tokens, width), F32)] * 5
        + [jax.ShapeDtypeStruct((tokens, width), BF)],
        compiler_params=params(),
        cost_estimate=cost(8, 34 << 20),
    )(co, *mixed, vectors, masks, *arrays_of(*weights))


def time_output_kernel(
    co, gated, x_ref, carry_ref, vec_ref, *refs, layout
):
    arrays, refs = take_refs(refs, layout)
    middle_ref, mk_ref, mr_ref, ow, last, sems = refs
    i = pl.program_id(0)
    copies = weight_copies(co, arrays, ow, sems, layout)

    @pl.when(i == 0)
    def _():
        start_all(copies)
        last[...] = jnp.zeros_like(last)
        wait_half(copies, 0)
        wait_half(copies, 1)

    half = ow.shape[2]
    middle_ref[...] = dot(gated[:, :half], ow[0], NT) + dot(gated[:, half:], ow[1], NT)
    gain, bias = vec_ref[7:8, :], vec_ref[8:9, :]
    mixes = [vec_ref[n : n + 1, :] for n in (9, 10)]

    def step(n, before):
        rows = pl.ds(pl.multiple_of(n * CHUNK, CHUNK), CHUNK)
        middle = middle_ref[rows, :] + x_ref[rows, :].astype(F32)
        middle_ref[rows, :] = middle
        normed, _, _ = norm_rows(middle, gain, bias)
        behind = move_down(normed, before) * carry_ref[rows, :]
        for mix, out in zip(mixes, (mk_ref, mr_ref)):
            out[rows, :] = (normed * mix + behind * (1.0 - mix)).astype(BF)
        return normed[CHUNK - 1 :, :]

    last[...] = lax.fori_loop(0, x_ref.shape[0] // CHUNK, step, last[...], unroll=2)


def time_output_step(co, gated, x, carry, vectors, weight):
    tokens, width = x.shape
    rows = tokens // 4
    tall = pl.BlockSpec((rows, width), lambda i, co: (i, 0))
    return pl.pallas_call(
        functools.partial(time_output_kernel, layout=weight[0]),
        grid_spec=pltpu.PrefetchScalarGridSpec(
            num_scalar_prefetch=1,
            grid=(4,),
            in_specs=[
                tall,
                tall,
                pl.BlockSpec((rows, 1), lambda i, co: (i, 0)),
                pl.BlockSpec(vectors.shape, lambda i, co: (0, 0)),
            ]
            + [anywhere()] * len(weight[1]),
            out_specs=[tall] * 3,
            scratch_shapes=[
                pltpu.VMEM((2, width, width // 2), BF),
                pltpu.VMEM((1, width), F32),
                pltpu.SemaphoreType.DMA((32,)),
            ],
        ),
        out_shape=[jax.ShapeDtypeStruct((tokens, width), t) for t in (F32, BF, BF)],
        compiler_params=params(),
        cost_estimate=cost(3, 14 << 20),
    )(co, gated, x, carry, vectors, *weight[1])


WIDE = 512


def hidden_kernel(co, mk, *refs, layout):
    arrays, (hidden_ref, active_ref, whole, sems) = take_refs(refs, layout)
    j = pl.program_id(0)
    per_half = whole.shape[2] // WIDE
    copies = weight_copies(co, arrays, whole, sems, layout)

    @pl.when(j == 0)
    def _():
        start_all(copies)
        wait_half(copies, 0)

    @pl.when(j == per_half)
    def _():
        wait_half(copies, 1)

    half = co[4] ^ lax.div(j, per_half)
    columns = pl.ds(pl.multiple_of(lax.rem(j, per_half) * WIDE, WIDE), WIDE)
    active = jnp.maximum(dot(mk[...], whole[half, :, columns], NN), 0.0)
    active_ref[...] = active.astype(BF)
    hidden_ref[...] = (active * active).astype(BF)


def column_tile(per_half):
    return lambda j, co: (0, (co[4] ^ lax.div(j, per_half)) * per_half + lax.rem(j, per_half))


def hidden_step(co, mixed, weight):
    tokens, width = mixed.shape
    half = weight_width(weight)
    block = pl.BlockSpec((tokens, WIDE), column_tile(half // WIDE))
    return pl.pallas_call(
        functools.partial(hidden_kernel, layout=weight[0]),
        grid_spec=pltpu.PrefetchScalarGridSpec(
            num_scalar_prefetch=1,
            grid=(2 * half // WIDE,),
            in_specs=[pl.BlockSpec((tokens, width), lambda j, co: (0, 0))]
            + [anywhere()] * len(weight[1]),
            out_specs=[block] * 2,
            scratch_shapes=[
                pltpu.VMEM((2, width, half), BF),
                pltpu.SemaphoreType.DMA((sem_count(weight),)),
            ],
        ),
        out_shape=[jax.ShapeDtypeStruct((tokens, 2 * half), BF)] * 2,
        compiler_params=params(),
        cost_estimate=cost(4.5, 26 << 20),
    )(co, mixed, *weight[1])


def result_kernel(
    co, scale, hidden, mr, middle_ref, teacher_ref, valid_ref, *refs, layouts,
):
    value_w, refs = take_refs(refs, layouts[0])
    recept_w, refs = take_refs(refs, layouts[1])
    out_ref, dres_ref, dkv_ref, drec_ref, loss_ref, ww, rw, kv_ref, pre_ref, sems, sems_r = refs
    i = pl.program_id(0)
    copies = weight_copies(co, value_w, ww, sems, layouts[0])
    recept = weight_copies(co, recept_w, rw, sems_r, layouts[1])

    @pl.when(i == 0)
    def _():
        start_all(recept)
        start_all(copies)
        loss_ref[...] = jnp.zeros_like(loss_ref)
        for half in (0, 1):
            wait_half(recept, half)
        for half in (0, 1):
            wait_half(copies, half)

    wide, narrow = ww.shape[2], rw.shape[2]
    kv_ref[...] = dot(hidden[:, :wide], ww[0], NT) + dot(hidden[:, wide:], ww[1], NT)
    pre_ref[:, :narrow] = dot(mr[...], rw[0], NN)
    pre_ref[:, narrow:] = dot(mr[...], rw[1], NN)
    factor = scale[0]

    def step(n, total):
        rows = pl.ds(pl.multiple_of(n * CHUNK, CHUNK), CHUNK)
        kv = kv_ref[rows, :]
        rec = 1.0 / (1.0 + jnp.exp(-pre_ref[rows, :]))
        result = middle_ref[rows, :] + rec * kv
        out_ref[rows, :] = result.astype(BF)
        error = (result - teacher_ref[rows, :].astype(F32)) * valid_ref[rows, :]
        grad = error * factor
        dres_ref[rows, :] = grad
        dkv_ref[rows, :] = (grad * rec).astype(BF)
        drec_ref[rows, :] = (grad * kv * rec * (1.0 - rec)).astype(BF)
        return total + fold_rows(error * error)

    total = lax.fori_loop(
        0, kv_ref.shape[0] // CHUNK, step, jnp.zeros((8, kv_ref.shape[1]), F32)
    )
    loss_ref[...] += total


def result_step(co, scale, hidden, mixed, middle, teacher, valid, weight, recept):
    tokens, width = mixed.shape
    rows = tokens // 4
    wide = weight_width(weight)
    tall = pl.BlockSpec((rows, width), lambda i, co, s: (i, 0))
    return pl.pallas_call(
        functools.partial(result_kernel, layouts=[weight[0], recept[0]]),
        grid_spec=pltpu.PrefetchScalarGridSpec(
            num_scalar_prefetch=2,
            grid=(4,),
            in_specs=[
                pl.BlockSpec((rows, 2 * wide), lambda i, co, s: (i, 0)),
                tall,
                tall,
                tall,
                pl.BlockSpec((rows, 1), lambda i, co, s: (i, 0)),
            ]
            + [anywhere()] * len(arrays_of(weight, recept)),
            out_specs=[tall] * 4 + [pl.BlockSpec((8, width), lambda i, co, s: (0, 0))],
            scratch_shapes=[
                pltpu.VMEM((2, width, wide), BF),
                pltpu.VMEM((2, width, width // 2), BF),
                pltpu.VMEM((rows, width), F32),
                pltpu.VMEM((rows, width), F32),
                pltpu.SemaphoreType.DMA((sem_count(weight),)),
                pltpu.SemaphoreType.DMA((sem_count(recept),)),
            ],
        ),
        out_shape=[jax.ShapeDtypeStruct((tokens, width), t) for t in (BF, F32, BF, BF)]
        + [jax.ShapeDtypeStruct((8, width), F32)],
        compiler_params=params(),
        cost_estimate=cost(7, 38 << 20),
    )(co, scale, hidden, mixed, middle, teacher, valid, *arrays_of(weight, recept))


def weight_grad_kernel(co, model_ref, chan_ref, *refs, order):
    targets, (whole, sems) = refs[:4], refs[4:]
    j = pl.program_id(0)
    per_half = whole.shape[2] // WIDE
    columns = pl.ds(pl.multiple_of(lax.rem(j, per_half) * WIDE, WIDE), WIDE)
    turn = lax.div(j, per_half)
    whole[co[4] ^ turn, :, columns] = dot(model_ref[...], chan_ref[...], TN).astype(BF)

    def copies(piece):
        found = []
        for which, index, rel in rel_slots(order):
            row, half = slot_place(co, rel)
            copy = pltpu.make_async_copy(
                whole.at[half, pl.ds(row, SLOT), piece],
                targets[which].at[index + (slice(None), piece)],
                sems.at[len(found)],
            )
            found.append((rel["x"], copy))
        return found

    for which in (0, 1):

        @pl.when(turn == which)
        def _(which=which):
            for rel_x, copy in copies(columns):
                if rel_x == which:
                    copy.start()

    @pl.when(j == pl.num_programs(0) - 1)
    def _():
        for _, copy in copies(slice(None)):
            copy.wait()


def weight_grad(co, model, chan, order, first=0, half=None):
    tokens, width = model.shape
    each = chan.shape[1] // 2
    half = half or each
    per_half, skip, stride = half // WIDE, first // WIDE, each // WIDE

    def tile(j, co):
        return 0, (co[4] ^ lax.div(j, per_half)) * stride + skip + lax.rem(j, per_half)

    shape = jax.ShapeDtypeStruct((2, 2, 2, SLOT, half), BF)
    return pl.pallas_call(
        functools.partial(weight_grad_kernel, order=order),
        grid_spec=pltpu.PrefetchScalarGridSpec(
            num_scalar_prefetch=1,
            grid=(2 * per_half,),
            in_specs=[
                pl.BlockSpec((tokens, width), lambda j, co: (0, 0)),
                pl.BlockSpec((tokens, WIDE), tile),
            ],
            out_specs=[anywhere()] * 4,
            scratch_shapes=[
                pltpu.VMEM((2, width, half), BF),
                pltpu.SemaphoreType.DMA((32,)),
            ],
        ),
        out_shape=[shape] * 4,
        compiler_params=params(),
        cost_estimate=cost(half / 512 * 1.2, (2 << 20) * (1 + half / 256)),
    )(co, model, chan)


def hidden_back_kernel(co, dkv, active_ref, *refs, layout):
    arrays, (out_ref, whole, sems) = take_refs(refs, layout)
    j = pl.program_id(0)
    per_half = whole.shape[2] // WIDE
    copies = weight_copies(co, arrays, whole, sems, layout)

    @pl.when(j == 0)
    def _():
        start_all(copies)
        wait_half(copies, 0)

    @pl.when(j == per_half)
    def _():
        wait_half(copies, 1)

    half = co[4] ^ lax.div(j, per_half)
    columns = pl.ds(pl.multiple_of(lax.rem(j, per_half) * WIDE, WIDE), WIDE)
    grad = dot(dkv[...], whole[half, :, columns], NN)
    out_ref[...] = (2.0 * active_ref[...].astype(F32) * grad).astype(BF)


def hidden_back(co, dkv, active, weight):
    tokens, width = dkv.shape
    half = weight_width(weight)
    block = pl.BlockSpec((tokens, WIDE), column_tile(half // WIDE))
    return pl.pallas_call(
        functools.partial(hidden_back_kernel, layout=weight[0]),
        grid_spec=pltpu.PrefetchScalarGridSpec(
            num_scalar_prefetch=1,
            grid=(2 * half // WIDE,),
            in_specs=[
                pl.BlockSpec((tokens, width), lambda j, co: (0, 0)),
                block,
            ]
            + [anywhere()] * len(weight[1]),
            out_specs=block,
            scratch_shapes=[
                pltpu.VMEM((2, width, half), BF),
                pltpu.SemaphoreType.DMA((sem_count(weight),)),
            ],
        ),
        out_shape=jax.ShapeDtypeStruct((tokens, 2 * half), BF),
        compiler_params=params(),
        cost_estimate=cost(4.5, 26 << 20),
    )(co, dkv, active, *weight[1])


def middle_back_kernel(
    co, dkey, drec, middle_ref, dres_ref, lead_ref, vec_ref, *refs, layouts,
):
    key_w, refs = take_refs(refs, layouts[0])
    recept_w, refs = take_refs(refs, layouts[1])
    dmid_ref, dtime_ref, sums_ref, ww, rw, gk_ref, gr_ref, next_ref, sems, sems_r = refs
    i = pl.program_id(0)
    copies = weight_copies(co, key_w, ww, sems, layouts[0])
    recept = weight_copies(co, recept_w, rw, sems_r, layouts[1])

    @pl.when(i == 0)
    def _():
        start_all(recept)
        start_all(copies)
        sums_ref[...] = jnp.zeros_like(sums_ref)
        next_ref[...] = jnp.zeros_like(next_ref)
        for half in (0, 1):
            wait_half(recept, half)
        for half in (0, 1):
            wait_half(copies, half)

    wide, narrow = ww.shape[2], rw.shape[2]
    gk_ref[...] = dot(dkey[:, :wide], ww[0], NT) + dot(dkey[:, wide:], ww[1], NT)
    gr_ref[...] = dot(drec[:, :narrow], rw[0], NT) + dot(drec[:, narrow:], rw[1], NT)
    gain, bias = vec_ref[7:8, :], vec_ref[8:9, :]
    mix_k, mix_r = vec_ref[9:10, :], vec_ref[10:11, :]
    steps = middle_ref.shape[0] // CHUNK

    def step(n, after):
        rows = pl.ds(pl.multiple_of((steps - 1 - n) * CHUNK, CHUNK), CHUNK)
        normed, unit, scaled = norm_rows(middle_ref[rows, :], gain, bias)
        lead = lead_ref[rows, :]
        gk, gr = gk_ref[rows, :], gr_ref[rows, :]
        uk = move_up(gk, after[0]) * lead
        ur = move_up(gr, after[1]) * lead
        grad = gk * mix_k + gr * mix_r + uk * (1.0 - mix_k) + ur * (1.0 - mix_r)
        sums_ref[0] += fold_rows(grad * unit)
        sums_ref[1] += fold_rows(grad)
        sums_ref[2] += fold_rows(normed * (gk - uk))
        sums_ref[3] += fold_rows(normed * (gr - ur))
        dmid = dres_ref[rows, :] + norm_rows_back(grad, unit, scaled, gain)
        dmid_ref[rows, :] = dmid
        dtime_ref[rows, :] = dmid.astype(BF)
        return gk[:1, :], gr[:1, :]

    after = lax.fori_loop(0, steps, step, (next_ref[0:1, :], next_ref[1:2, :]))
    next_ref[0:1, :] = after[0]
    next_ref[1:2, :] = after[1]


def middle_back(co, dkey, drec, middle, dres, lead, vectors, weight, recept):
    tokens, width = middle.shape
    rows = tokens // 4
    wide = weight_width(weight)
    tall = pl.BlockSpec((rows, width), lambda i, co: (3 - i, 0))
    return pl.pallas_call(
        functools.partial(middle_back_kernel, layouts=[weight[0], recept[0]]),
        grid_spec=pltpu.PrefetchScalarGridSpec(
            num_scalar_prefetch=1,
            grid=(4,),
            in_specs=[
                pl.BlockSpec((rows, 2 * wide), lambda i, co: (3 - i, 0)),
                tall,
                tall,
                tall,
                pl.BlockSpec((rows, 1), lambda i, co: (3 - i, 0)),
                pl.BlockSpec(vectors.shape, lambda i, co: (0, 0)),
            ]
            + [anywhere()] * len(arrays_of(weight, recept)),
            out_specs=[tall] * 2 + [pl.BlockSpec((4, 8, width), lambda i, co: (0, 0, 0))],
            scratch_shapes=[
                pltpu.VMEM((2, width, wide), BF),
                pltpu.VMEM((2, width, width // 2), BF),
                pltpu.VMEM((rows, width), F32),
                pltpu.VMEM((rows, width), F32),
                pltpu.VMEM((8, width), F32),
                pltpu.SemaphoreType.DMA((sem_count(weight),)),
                pltpu.SemaphoreType.DMA((sem_count(recept),)),
            ],
        ),
        out_shape=[
            jax.ShapeDtypeStruct((tokens, width), F32),
            jax.ShapeDtypeStruct((tokens, width), BF),
            jax.ShapeDtypeStruct((4, 8, width), F32),
        ],
        compiler_params=params(),
        cost_estimate=cost(8, 36 << 20),
    )(co, dkey, drec, middle, dres, lead, vectors, *arrays_of(weight, recept))


def time_back_kernel(
    co, dtime, key_ref, val_ref, rec_ref, pa_ref, pb_ref, vec, masks, *refs, layout,
):
    arrays, refs = take_refs(refs, layout)
    dkey_ref, dval_ref, drec_ref, sums_ref, ow, dg_ref, sems = refs
    j = pl.program_id(0)
    per_half = ow.shape[2] // TILE
    copies = weight_copies(co, arrays, ow, sems, layout)

    @pl.when(j == 0)
    def _():
        start_all(copies)
        wait_half(copies, 0)

    @pl.when(j == per_half)
    def _():
        wait_half(copies, 1)

    half = co[4] ^ lax.div(j, per_half)
    columns = pl.ds(pl.multiple_of(lax.rem(j, per_half) * TILE, TILE), TILE)
    dg_ref[...] = dot(dtime[...], ow[half, :, columns], NN)

    spread = (8, TILE)
    decay = jnp.broadcast_to(vec[2:3, :], spread)
    first = jnp.broadcast_to(vec[3:4, :], spread)
    r1, r2, r4, r8 = scan_rates(decay)
    left = 7.0 - lax.broadcasted_iota(jnp.int32, spread, 0).astype(F32)
    powers = jnp.exp(-left * jnp.exp(decay))

    def group(start, state):
        rows = pl.ds(start, 8)
        n1, n2, n4, nf, c0, ml = (twice(masks[n, rows, :]) for n in (5, 6, 7, 8, 9, 4))
        key, val, rec, dg = key_ref[rows, :], val_ref[rows, :], rec_ref[rows, :], dg_ref[rows, :]
        pa, pb = pa_ref[rows, :], pb_ref[rows, :]
        power = jnp.exp(key)
        bonus = jnp.exp(first + key)
        inverse = 1.0 / (pb + bonus)
        wkv = (pa + bonus * val) * inverse
        slope = dg * rec * inverse
        drec = dg * wkv * rec * (1.0 - rec)
        c1, c2, c4, cf, cl = n1 * r1, n2 * r2, n4 * r4, nf * powers, ml * r8
        found, starts = [], []
        for local, leaving in ((slope, state[0]), (-slope * wkv, state[1])):
            local = local + c1 * pltpu.roll(local, 7, 0)
            local = local + c2 * pltpu.roll(local, 6, 0)
            local = local + c4 * pltpu.roll(local, 4, 0)
            found.append(n1 * pltpu.roll(local, 7, 0) + cf * leaving)
            starts.append(c0 * jnp.broadcast_to(local[0:1, :], spread) + cl * leaving)
        later_a, later_b = found
        summand = bonus * slope * (val - wkv)
        dkey = power * (later_a * val + later_b) + summand
        dval = power * later_a + bonus * slope
        state = (
            starts[0],
            starts[1],
            state[2] + summand,
            state[3] + later_a * pa + later_b * pb,
        )
        return (dkey, dval, drec), state

    steps = key_ref.shape[0] // CHUNK

    def step(n, state):
        start = pl.multiple_of((steps - 1 - n) * CHUNK, CHUNK)
        lower, state = group(pl.multiple_of(start + 8, 8), state)
        upper, state = group(start, state)
        for up, low, out in zip(upper, lower, (dkey_ref, dval_ref, drec_ref)):
            out[pl.ds(start, CHUNK), :] = jnp.concatenate([up, low], axis=0).astype(BF)
        return state

    zero = jnp.zeros(spread, F32)
    _, _, first_sum, decay_sum = lax.fori_loop(0, steps, step, (zero,) * 4)
    sums_ref[0] = -r1 * jnp.exp(decay) * decay_sum
    sums_ref[1] = first_sum


def time_back(co, dtime, saved, vectors, masks, weight):
    tokens, width = dtime.shape
    half = width // 2
    tile = column_tile(half // TILE)
    block = pl.BlockSpec((tokens, TILE), tile)
    return pl.pallas_call(
        functools.partial(time_back_kernel, layout=weight[0]),
        grid_spec=pltpu.PrefetchScalarGridSpec(
            num_scalar_prefetch=1,
            grid=(width // TILE,),
            in_specs=[pl.BlockSpec((tokens, width), lambda j, co: (0, 0))]
            + [block] * 5
            + [
                pl.BlockSpec((vectors.shape[0], TILE), tile),
                pl.BlockSpec(masks.shape, lambda j, co: (0, 0, 0)),
            ]
            + [anywhere()] * len(weight[1]),
            out_specs=[block] * 3
            + [pl.BlockSpec((2, 8, TILE), lambda j, co: (0,) + tile(j, co))],
            scratch_shapes=[
                pltpu.VMEM((2, width, half), BF),
                pltpu.VMEM((tokens, TILE), F32),
                pltpu.SemaphoreType.DMA((32,)),
            ],
        ),
        out_shape=[jax.ShapeDtypeStruct((tokens, width), BF)] * 3
        + [jax.ShapeDtypeStruct((2, 8, width), F32)],
        compiler_params=params(),
        cost_estimate=cost(9, 34 << 20),
    )(co, dtime, *saved, vectors, masks, *weight[1])


def input_back_kernel(
    co, dkey, dval, drec, x_ref, dmid_ref, lead_ref, vec_ref, *refs, layouts,
):
    key_w, refs = take_refs(refs, layouts[0])
    val_w, refs = take_refs(refs, layouts[1])
    rec_w, refs = take_refs(refs, layouts[2])
    out_ref, sums_ref, kw, vw, rw, gk_ref, gv_ref, gr_ref, next_ref, sems = refs
    i = pl.program_id(0)
    groups = [
        weight_copies(co, arrays, whole, sems.at[n], layout)
        for n, (arrays, whole, layout) in enumerate(zip((key_w, val_w, rec_w), (kw, vw, rw), layouts))
    ]

    @pl.when(i == 0)
    def _():
        for copies in groups:
            start_all(copies)
        sums_ref[...] = jnp.zeros_like(sums_ref)
        next_ref[...] = jnp.zeros_like(next_ref)
        for copies in groups:
            wait_half(copies, 0)
            wait_half(copies, 1)

    half = kw.shape[2]
    for grad, whole, out in ((dkey, kw, gk_ref), (dval, vw, gv_ref), (drec, rw, gr_ref)):
        out[...] = dot(grad[:, :half], whole[0], NT) + dot(grad[:, half:], whole[1], NT)
    gain, bias = vec_ref[0:1, :], vec_ref[1:2, :]
    mixes = [vec_ref[n : n + 1, :] for n in (4, 5, 6)]
    steps = x_ref.shape[0] // CHUNK

    def step(n, after):
        rows = pl.ds(pl.multiple_of((steps - 1 - n) * CHUNK, CHUNK), CHUNK)
        normed, unit, scaled = norm_rows(x_ref[rows, :].astype(F32), gain, bias)
        lead = lead_ref[rows, :]
        total = jnp.zeros_like(normed)
        firsts = []
        for m, (part, mix) in enumerate(zip((gk_ref, gv_ref, gr_ref), mixes)):
            grad = part[rows, :]
            up = move_up(grad, after[m]) * lead
            total = total + grad * mix + up * (1.0 - mix)
            sums_ref[2 + m] += fold_rows(normed * (grad - up))
            firsts.append(grad[:1, :])
        sums_ref[0] += fold_rows(total * unit)
        sums_ref[1] += fold_rows(total)
        out_ref[rows, :] = dmid_ref[rows, :] + norm_rows_back(total, unit, scaled, gain)
        return tuple(firsts)

    after = lax.fori_loop(0, steps, step, tuple(next_ref[m : m + 1, :] for m in range(3)))
    for m in range(3):
        next_ref[m : m + 1, :] = after[m]


def input_back(co, grads, x, dmid, lead, vectors, weights):
    tokens, width = x.shape
    rows = tokens // 4
    tall = pl.BlockSpec((rows, width), lambda i, co: (3 - i, 0))
    return pl.pallas_call(
        functools.partial(input_back_kernel, layouts=[w[0] for w in weights]),
        grid_spec=pltpu.PrefetchScalarGridSpec(
            num_scalar_prefetch=1,
            grid=(4,),
            in_specs=[tall] * 5
            + [
                pl.BlockSpec((rows, 1), lambda i, co: (3 - i, 0)),
                pl.BlockSpec(vectors.shape, lambda i, co: (0, 0)),
            ]
            + [anywhere()] * len(arrays_of(*weights)),
            out_specs=[tall, pl.BlockSpec((5, 8, width), lambda i, co: (0, 0, 0))],
            scratch_shapes=[pltpu.VMEM((2, width, width // 2), BF)] * 3
            + [pltpu.VMEM((rows, width), F32)] * 3
            + [pltpu.VMEM((8, width), F32), pltpu.SemaphoreType.DMA((3, 32))],
        ),
        out_shape=[
            jax.ShapeDtypeStruct((tokens, width), F32),
            jax.ShapeDtypeStruct((5, 8, width), F32),
        ],
        compiler_params=params(),
        cost_estimate=cost(7, 26 << 20),
    )(co, *grads, x, dmid, lead, vectors, *arrays_of(*weights))


def seal(*values):
    return lax.optimization_barrier(values)


def swap(values, axis):
    return lax.ppermute(values, axis, SWAP)


class Gather:
    def __init__(self, shard, order):
        self.order, self.state, self.done = order, (shard,), 0

    def step(self):
        n = self.done
        if n and n < 4:
            self.state = (jnp.stack(self.state),)
        if n < 3:
            self.state += (swap(self.state[0], self.order[n]),)
        elif n == 3:
            near = self.state[0]
            self.state = (near, swap(near, self.order[3]), swap(near, "c"))
        else:
            near, far, near_other = self.state
            self.state = (near, far, near_other, swap(far, "c"))
        self.done += 1

    def part(self, first=0):
        assert self.done == 5
        return ("rel", self.order, first, self.state[0].shape[-1]), self.state


def weight_of(*parts):
    layouts, arrays = zip(*parts)
    return layouts, [array for group in arrays for array in group]


class Reduce:
    def __init__(self, slots, order):
        self.order, self.state, self.done = order, tuple(slots), 0

    def step(self):
        n = self.done
        if n == 0:
            near, far, near_other, far_other = self.state
            self.state = (near, far, swap(far_other, "c"), swap(near_other, "c"))
        elif n == 1:
            near, far, far_got, near_got = self.state
            self.state = (near, near_got, swap(far + far_got, self.order[3]))
        elif n == 2:
            near, near_got, got = (v.astype(F32) for v in self.state)
            held = near + near_got + got
            self.keep(held, 2)
        elif n < 5:
            held = self.state[0] + self.state[1].astype(F32)
            self.keep(held, 4 - n)
        self.done += 1

    def keep(self, held, place):
        self.state = (held[0], swap(held[1].astype(BF), self.order[place]))

    def finish(self):
        assert self.done == 5
        return self.state[0] + self.state[1].astype(F32)


def step_all(*chains):
    for chain in chains:
        chain.step()


def seal_all(chains, *values):
    states, values = seal([chain.state for chain in chains], values)
    for chain, state in zip(chains, states):
        chain.state = tuple(state)
    return values


def gather_plain(shard, first=0):
    whole = lax.all_gather(shard, ("w", "u", "y", "c"), axis=0, tiled=True)
    whole = lax.all_gather(whole, "x", axis=1, tiled=True)
    half = whole.shape[1] // 2
    whole = whole.reshape(16, SLOT, 2, half).transpose(0, 2, 1, 3)
    return ("abs", 0, first, half), (whole,)


def reduce_plain(slots, order):
    table = {}
    for which, index, rel in rel_slots(order):
        block = rel["w"] * 8 + rel["u"] * 4 + rel["y"] * 2 + rel["c"]
        table[block, rel["x"]] = slots[which][index]
    whole = jnp.concatenate(
        [jnp.concatenate([table[b, 0], table[b, 1]], axis=1) for b in range(16)], axis=0
    )
    whole = lax.psum_scatter(whole, ("w", "u", "y", "c"), scatter_dimension=0, tiled=True)
    return lax.psum_scatter(whole, "x", scatter_dimension=1, tiled=True).astype(F32)


def scan_masks(carry):
    c = carry.reshape(-1, 8)
    place = jnp.arange(8)[None, :]

    def behind(values, n):
        return jnp.where(place >= n, jnp.roll(values, n, axis=1), 0.0)

    def ahead(values, n):
        return jnp.where(place < 8 - n, jnp.roll(values, -n, axis=1), 0.0)

    m1 = jnp.where(place >= 1, c, 0.0)
    m2 = m1 * behind(m1, 1)
    m4 = m2 * behind(m2, 2)
    mf = jnp.cumprod(c, axis=1)
    ml = jnp.broadcast_to(mf[:, 7:], c.shape)
    n1 = ahead(c, 1)
    n2 = n1 * ahead(n1, 1)
    n4 = n2 * ahead(n2, 2)
    back = jnp.cumprod(c[:, ::-1], axis=1)[:, ::-1]
    nf = jnp.where(place < 7, jnp.roll(back, -1, axis=1), 1.0)
    c0 = jnp.broadcast_to(c[:, :1], c.shape)
    table = jnp.stack([m1, m2, m4, mf, ml, n1, n2, n4, nf, c0]).reshape(10, -1, 1)
    return jnp.broadcast_to(table, table.shape[:2] + (128,))


def on_device(
    inputs,
    segments,
    teacher,
    first_norm_gain,
    first_norm_bias,
    time_decay,
    time_first,
    time_mix_key,
    time_mix_value,
    time_mix_recept,
    time_key,
    time_value,
    time_recept,
    time_output,
    second_norm_gain,
    second_norm_bias,
    channel_mix_key,
    channel_mix_recept,
    channel_key,
    channel_recept,
    channel_value,
):
    tokens, width = inputs.shape
    sizes = {a: lax.axis_size(a) for a in EVERY}
    devices = math.prod(sizes.values())
    fast = all(size == 2 for size in sizes.values())
    side = lax.axis_index("x")
    if fast:
        co = jnp.stack([lax.axis_index(a) for a in EVERY]).astype(jnp.int32)
    else:
        co = jnp.zeros((5,), jnp.int32)

    ids = lax.dynamic_slice_in_dim(segments, side * tokens, tokens)
    previous = jnp.concatenate([jnp.zeros((1,), jnp.int32), ids[:-1]])
    started = jnp.arange(tokens, dtype=jnp.int32) > 0
    carry = ((ids == previous) & (ids > 0) & started).astype(F32)
    valid = (ids > 0).astype(F32)
    lead = jnp.concatenate([carry[1:], jnp.zeros((1,), F32)])
    masks = scan_masks(carry)
    carry, valid_rows, lead = carry[:, None], valid[:, None], lead[:, None]

    flat = 0
    for axis in EVERY:
        flat = flat * sizes[axis] + lax.axis_index(axis)
    own_vectors = jnp.stack(
        [
            first_norm_gain,
            first_norm_bias,
            time_decay,
            time_first,
            time_mix_key,
            time_mix_value,
            time_mix_recept,
            second_norm_gain,
            second_norm_bias,
            channel_mix_key,
            channel_mix_recept,
        ]
    )
    piece = own_vectors.shape[1]
    spread = jnp.where(
        jnp.arange(width)[None, :] // piece == flat, jnp.tile(own_vectors, (1, width // piece)), 0.0
    )
    counts = jnp.broadcast_to(jnp.sum(valid), (1, width))
    vectors = jnp.concatenate([spread, counts, jnp.zeros((4, width), F32)])
    output_t, value_t = time_output.T, channel_value.T

    if sizes["x"] == 2:
        mine = lax.dynamic_slice_in_dim(teacher, side * tokens, tokens)
        theirs = lax.dynamic_slice_in_dim(teacher, (1 - side) * tokens, tokens)
        theirs = swap(theirs, "x")
        teacher_rows = jnp.where(
            side == 0,
            jnp.concatenate([mine, theirs], axis=1),
            jnp.concatenate([theirs, mine], axis=1),
        )
    else:
        teacher_rows = teacher

    if fast:
        rest = lax.all_gather(jnp.concatenate([value_t, channel_recept], axis=1), EVERY)
        rest = rest.reshape(16, 2, SLOT, rest.shape[-1])
        cols = value_t.shape[1]
        cvalue_w = ((("abs", 0, 0, cols),), [rest])
        crecept_w = ((("abs", cols, 0, width // 2),), [rest])

        key_c, val_c, rec_c = Gather(time_key, "wxuy"), Gather(time_value, "uwyx"), Gather(time_recept, "wyxu")
        out_c = Gather(output_t, "wuyx")
        split = channel_key.shape[1] // 2
        ck_a, ck_b = Gather(channel_key[:, :split], "wxuy"), Gather(channel_key[:, split:], "uwyx")
        three = (key_c, val_c, rec_c)

        step_all(*three)
        got = swap(vectors, "x")
        (vectors, got) = seal_all(three, vectors, got)
        vectors = vectors + got
        step_all(*three, out_c)
        got = swap(vectors, "y")
        (vectors, got) = seal_all((*three, out_c), vectors, got)
        vectors = vectors + got
        step_all(*three, out_c, ck_a, ck_b)
        vectors = vectors + swap(vectors, "c")
        got = swap(vectors, "u")
        (vectors, got) = seal_all((*three, out_c, ck_a, ck_b), vectors, got)
        vectors = vectors + got
        step_all(*three, out_c, ck_a, ck_b)
        vectors = vectors + swap(vectors, "w")
        mixed = first_mix(inputs, carry, vectors)
        (mixed, vectors) = seal_all((*three, out_c, ck_a, ck_b), mixed, vectors)
        step_all(*three, out_c, ck_a, ck_b)
        (mixed,) = seal_all((*three, out_c, ck_a, ck_b), mixed)
        key_w, value_w, recept_w = (weight_of(c.part()) for c in three)
        step_all(out_c, ck_a, ck_b)
    else:
        vectors = lax.psum(vectors, EVERY)
        mixed = first_mix(inputs, carry, vectors)
        key_w, value_w, recept_w, output_w, ckey_w, crecept_w, cvalue_w = (
            weight_of(gather_plain(w))
            for w in (time_key, time_value, time_recept, output_t, channel_key, channel_recept, value_t)
        )
    count = vectors[11, 0]
    scale = (float(tokens * devices) / count).reshape(1)

    *saved, gated = time_forward(co, mixed, (key_w, value_w, recept_w), vectors, masks)
    if fast:
        (gated,) = seal_all((out_c, ck_a, ck_b), gated)
        output_w = weight_of(out_c.part())
        step_all(ck_a, ck_b)
    middle, mixed_k2, mixed_r2 = time_output_step(co, gated, inputs, carry, vectors, output_w)
    if fast:
        (middle, mixed_k2, mixed_r2) = seal_all((ck_a, ck_b), middle, mixed_k2, mixed_r2)
        ckey_w = weight_of(ck_a.part(), ck_b.part(split))
    hidden, active = hidden_step(co, mixed_k2, ckey_w)
    result, dres, dkv, drec2, loss_rows = result_step(
        co, scale, hidden, mixed_r2, middle, teacher_rows, valid_rows, cvalue_w, crecept_w
    )

    half = width // 2
    if fast:
        kept = lax.dynamic_slice_in_dim(result, side * half, half, axis=1)
        sent = lax.dynamic_slice_in_dim(result, (1 - side) * half, half, axis=1)
        arrived = swap(sent, "x")
        split = hidden.shape[1] // 4
        cv_a = Reduce(weight_grad(co, dkv, hidden, "wxuy", 0, split), "wxuy")
        (hidden, dkv) = seal_all((cv_a,), hidden, dkv)
        step_all(cv_a)
        cv_b = Reduce(weight_grad(co, dkv, hidden, "uwyx", split, split), "uwyx")
        (dkv, arrived) = seal_all((cv_a, cv_b), dkv, arrived)
        step_all(cv_a, cv_b)
        dkey2 = hidden_back(co, dkv, active, cvalue_w)
        (dkey2,) = seal_all((cv_b,), dkey2)
        step_all(cv_b)
        ck_a = Reduce(weight_grad(co, mixed_k2, dkey2, "wyxu", 0, split), "wyxu")
        (dkey2,) = seal_all((cv_a, ck_a), dkey2)
        step_all(cv_a, ck_a)
        ck_b = Reduce(weight_grad(co, mixed_k2, dkey2, "wxuy", split, split), "wxuy")
        cr = Reduce(weight_grad(co, mixed_r2, drec2, "uwyx"), "uwyx")
        (dkey2, drec2) = seal_all((ck_a, ck_b, cr), dkey2, drec2)
        step_all(ck_a, ck_b, cr)
        dmid, dtime, sums2 = middle_back(
            co, dkey2, drec2, middle, dres, lead, vectors, ckey_w, crecept_w
        )
        chains = (cv_a, cv_b, ck_a, ck_b, cr)
        (dtime, dmid) = seal_all(chains, dtime, dmid)
        step_all(*chains)
        out_c = Reduce(weight_grad(co, dtime, gated, "wuyx"), "wuyx")
        (dtime,) = seal_all((cv_a, cv_b, ck_a, out_c), dtime)
        step_all(cv_a, cv_b, ck_a, out_c)
        *dmix, sums_t = time_back(co, dtime, saved, vectors, masks, output_w)
        chains = (cv_a, cv_b, ck_a, ck_b, cr, out_c)
        (dmix, dmid) = seal_all(chains, dmix, dmid)
        step_all(cv_b, ck_b, cr, out_c)
        orders = ("wxuy", "uwyx", "wyxu")
        three = []
        pending = [cv_b, ck_b, cr, out_c]
        for m, d, order in zip(mixed, dmix, orders):
            chain = Reduce(weight_grad(co, m, d, order), order)
            (dmix,) = seal_all((*three, chain, *pending), dmix)
            three.append(chain)
            step_all(*three)
            if len(three) == 2:
                step_all(ck_a, ck_b, cr, out_c)
                pending = [ck_a, ck_b, cr, out_c]
        input_grad, sums1 = input_back(
            co, dmix, inputs, dmid, lead, vectors, (key_w, value_w, recept_w)
        )
        (input_grad, sums1) = seal_all((*three, *pending), input_grad, sums1)
        for chain in (ck_b, cr, out_c, *three):
            while chain.done < 5:
                chain.step()
        key_g, val_g, rec_g = (c.finish() for c in three)
        output_g, crecept_g = out_c.finish(), cr.finish()
        cvalue_g = jnp.concatenate([cv_a.finish(), cv_b.finish()], axis=1)
        ckey_g = jnp.concatenate([ck_a.finish(), ck_b.finish()], axis=1)
        outputs = jnp.where(
            side == 0,
            jnp.concatenate([kept, arrived], axis=0),
            jnp.concatenate([arrived, kept], axis=0),
        )
    else:
        order = "wuyx"

        def grad(model, chan):
            return reduce_plain(weight_grad(co, model, chan, order), order)

        if sizes["x"] == 2:
            kept = lax.dynamic_slice_in_dim(result, side * half, half, axis=1)
            arrived = swap(lax.dynamic_slice_in_dim(result, (1 - side) * half, half, axis=1), "x")
            outputs = jnp.where(
                side == 0,
                jnp.concatenate([kept, arrived], axis=0),
                jnp.concatenate([arrived, kept], axis=0),
            )
        else:
            outputs = result
        cvalue_g = grad(dkv, hidden)
        dkey2 = hidden_back(co, dkv, active, cvalue_w)
        ckey_g, crecept_g = grad(mixed_k2, dkey2), grad(mixed_r2, drec2)
        dmid, dtime, sums2 = middle_back(
            co, dkey2, drec2, middle, dres, lead, vectors, ckey_w, crecept_w
        )
        output_g = grad(dtime, gated)
        *dmix, sums_t = time_back(co, dtime, saved, vectors, masks, output_w)
        key_g, val_g, rec_g = (grad(m, d) for m, d in zip(mixed, dmix))
        input_grad, sums1 = input_back(
            co, dmix, inputs, dmid, lead, vectors, (key_w, value_w, recept_w)
        )

    rows = jnp.concatenate([sums1[:2], sums_t, sums1[2:], sums2, loss_rows[None]])
    totals = jnp.sum(rows, axis=1)
    if fast:
        for axis in EVERY:
            totals = totals + swap(totals, axis)
    else:
        totals = lax.psum(totals, EVERY)
    loss = jnp.sum(totals[11]) / (2.0 * count * width)
    vector_g = lax.dynamic_slice_in_dim(totals, flat * piece, piece, axis=1)
    return (
        outputs,
        loss,
        input_grad,
        *[vector_g[n] for n in range(7)],
        key_g,
        val_g,
        rec_g,
        output_g.T,
        *[vector_g[n] for n in range(7, 11)],
        ckey_g,
        crecept_g,
        cvalue_g.T,
    )


def solution(mesh):
    fsdp, tp = mesh.shape["fsdp"], mesh.shape["tp"]
    two = 2 if fsdp % 8 == 0 else 1
    split = Mesh(mesh.devices.reshape(fsdp // two**3, two, two, two, tp), EVERY)
    rows = ("w", "u", "y", "c")
    vector = P(EVERY)
    matrix = P(rows, "x")
    turned = P("x", rows)
    tall = P(EVERY, None)
    return jax.shard_map(
        on_device,
        mesh=split,
        in_specs=(
            (tall, P(rows), matrix)
            + (vector,) * 7
            + (matrix, matrix, matrix, turned)
            + (vector,) * 4
            + (matrix, matrix, turned)
        ),
        out_specs=(
            (matrix, P(), tall)
            + (vector,) * 7
            + (matrix, matrix, matrix, turned)
            + (vector,) * 4
            + (matrix, matrix, turned)
        ),
        check_vma=False,
    )
```

```python
import functools
import itertools
import math

import jax
import jax.numpy as jnp
from jax import lax
from jax.experimental import pallas as pl
from jax.experimental.pallas import tpu as pltpu
from jax.sharding import Mesh
from jax.sharding import PartitionSpec as P

BF = jnp.bfloat16
F32 = jnp.float32
EPSILON = 1e-05
SLOT = 64
CHUNK = 16
VMEM_LIMIT = 58 << 20
EVERY = ("w", "u", "y", "c", "x")
SWAP = [(0, 1), (1, 0)]

NN = (((1,), (0,)), ((), ()))
NT = (((1,), (1,)), ((), ()))
TN = (((0,), (0,)), ((), ()))


def dot(left, right, dims):
    return lax.dot_general(left, right, dims, preferred_element_type=F32)


def rel_slots(order):
    for other_core in (0, 1):
        for last in (0, 1):
            for index in itertools.product((0, 1), repeat=3):
                rel = dict(zip(order[2::-1], index))
                rel[order[3]] = last
                rel["c"] = other_core
                yield other_core * 2 + last, index, rel


def slot_place(co, rel):
    at = {axis: co[n] ^ rel[axis] for n, axis in enumerate(EVERY)}
    block = at["w"] * 8 + at["u"] * 4 + at["y"] * 2 + at["c"]
    return pl.multiple_of(block * SLOT, SLOT), at["x"]


def weight_copies(co, refs, whole, sems, layout):
    copies = []
    refs = list(refs)
    for kind, order, first, columns in layout:
        target = pl.ds(first, columns)
        if kind == "rel":
            order, skip = order
            arrays, refs = refs[:4], refs[4:]
            for which, index, rel in rel_slots(order):
                row, half = slot_place(co, rel)
                copies.append(
                    (
                        rel["x"],
                        pltpu.make_async_copy(
                            arrays[which].at[index + (slice(None), pl.ds(skip, columns))],
                            whole.at[half, pl.ds(row, SLOT), target],
                            sems.at[len(copies)],
                        ),
                    )
                )
        else:
            array, refs = refs[0], refs[1:]
            for rel_x in (0, 1):
                half = co[4] ^ rel_x
                for block in range(16):
                    copies.append(
                        (
                            rel_x,
                            pltpu.make_async_copy(
                                array.at[block, half, :, pl.ds(order, columns)],
                                whole.at[half, pl.ds(block * SLOT, SLOT), target],
                                sems.at[len(copies)],
                            ),
                        )
                    )
    return copies


def take_refs(refs, layout):
    count = sum(4 if part[0] == "rel" else 1 for part in layout)
    return refs[:count], refs[count:]


def arrays_of(*weights):
    return [array for _, arrays in weights for array in arrays]


def both_parts(weights, split):
    (first, arrays_a), (second, arrays_b) = weights
    second = tuple((kind, order, at + split, columns) for kind, order, at, columns in second)
    return tuple(first) + second, list(arrays_a) + list(arrays_b)


def weight_width(weight):
    return sum(part[3] for part in weight[0])


def sem_count(weight):
    return 32 * len(weight[0])


def start_all(copies):
    for _, copy in copies:
        copy.start()


def wait_half(copies, half):
    for which, copy in copies:
        if which == half:
            copy.wait()


ROWS = 32
LANES = 128


def strips(width):
    return [slice(n, n + LANES) for n in range(0, width, LANES)]


def row_parts(ref, row=0):
    return tuple(ref[row : row + 1, strip] for strip in strips(ref.shape[1]))


def chunk_rows(n):
    return pl.ds(pl.multiple_of(n * ROWS, ROWS), ROWS)


def spread_mean(total, width):
    return jnp.broadcast_to(jnp.sum(total, axis=1, keepdims=True) * (1.0 / width), total.shape)


def norm_stats(load, width):
    total = sum(load(strip) for strip in strips(width))
    mean = spread_mean(total, width)
    square = 0.0
    for strip in strips(width):
        centre = load(strip) - mean
        square = square + centre * centre
    return mean, lax.rsqrt(spread_mean(square, width) + EPSILON)


def first_row(shape):
    return lax.broadcasted_iota(jnp.int32, shape, 0) == 0


def last_row(shape):
    return lax.broadcasted_iota(jnp.int32, shape, 0) == shape[0] - 1


def move_down(values, before):
    return jnp.where(first_row(values.shape), before, pltpu.roll(values, 1, 0))


def move_up(values, after):
    return jnp.where(last_row(values.shape), after, pltpu.roll(values, values.shape[0] - 1, 0))


def fold_rows(values):
    return sum(values[n : n + 8] for n in range(0, values.shape[0], 8))


def params(semantics=1):
    return pltpu.CompilerParams(vmem_limit_bytes=VMEM_LIMIT)


def anywhere():
    return pl.BlockSpec(memory_space=pl.ANY)


def cost(units, traffic):
    return pl.CostEstimate(
        flops=int(units * 2 * 1024**3), bytes_accessed=int(traffic), transcendentals=0
    )


def first_mix_kernel(x_ref, carry_ref, vec_ref, mk_ref, mv_ref, mr_ref, last):
    width = x_ref.shape[1]

    def step(n, before):
        rows = chunk_rows(n)
        mean, scaled = norm_stats(lambda strip: x_ref[rows, strip].astype(F32), width)
        carry = carry_ref[rows, :]
        lasts = []
        for strip in strips(width):
            unit = (x_ref[rows, strip].astype(F32) - mean) * scaled
            normed = unit * vec_ref[0:1, strip] + vec_ref[1:2, strip]
            behind = move_down(normed, before[len(lasts)]) * carry
            for m, out in ((4, mk_ref), (5, mv_ref), (6, mr_ref)):
                mix = vec_ref[m : m + 1, strip]
                out[rows, strip] = (normed * mix + behind * (1.0 - mix)).astype(BF)
            lasts.append(normed[ROWS - 1 :, :])
        return tuple(lasts)

    @pl.when(pl.program_id(0) == 0)
    def _():
        last[...] = jnp.zeros_like(last)

    lasts = lax.fori_loop(0, x_ref.shape[0] // ROWS, step, row_parts(last), unroll=2)
    for strip, value in zip(strips(width), lasts):
        last[0:1, strip] = value


def first_mix(x, carry, vectors):
    tokens, width = x.shape
    rows = tokens // 4
    tall = pl.BlockSpec((rows, width), lambda i: (i, 0))
    return pl.pallas_call(
        first_mix_kernel,
        grid=(4,),
        in_specs=[
            tall,
            pl.BlockSpec((rows, LANES), lambda i: (i, 0)),
            pl.BlockSpec(vectors.shape, lambda i: (0, 0)),
        ],
        out_specs=[tall] * 3,
        out_shape=[jax.ShapeDtypeStruct(x.shape, BF)] * 3,
        scratch_shapes=[pltpu.VMEM((8, width), F32)],
        compiler_params=params(),
        cost_estimate=cost(0, 8 << 20),
    )(x, carry, vectors)


TILE = 256


def scan_rates(decay):
    speed = jnp.exp(decay)
    return [jnp.exp(-float(n) * speed) for n in (1, 2, 4, 8)]


def twice(values):
    return jnp.concatenate([values] * (TILE // 128), axis=1)


def time_forward_kernel(
    co, mk, mv, mr, vec, masks, *refs, layouts,
):
    key_w, refs = take_refs(refs, layouts[0])
    val_w, refs = take_refs(refs, layouts[1])
    rec_w, refs = take_refs(refs, layouts[2])
    key_ref, val_ref, rec_ref, pa_ref, pb_ref, gated_ref, kw, vw, rw, sems = refs
    j = pl.program_id(0)
    per_half = kw.shape[2] // TILE
    groups = [
        weight_copies(co, arrays, whole, sems.at[n], layout)
        for n, (arrays, whole, layout) in enumerate(zip((key_w, val_w, rec_w), (kw, vw, rw), layouts))
    ]

    @pl.when(j == 0)
    def _():
        for copies in groups:
            start_all(copies)
        for copies in groups:
            wait_half(copies, 0)

    @pl.when(j == per_half)
    def _():
        for copies in groups:
            wait_half(copies, 1)

    half = co[4] ^ lax.div(j, per_half)
    columns = pl.ds(pl.multiple_of(lax.rem(j, per_half) * TILE, TILE), TILE)
    key_ref[...] = dot(mk[...], kw[half, :, columns], NN)
    val_ref[...] = dot(mv[...], vw[half, :, columns], NN)
    rec_ref[...] = dot(mr[...], rw[half, :, columns], NN)

    spread = (8, TILE)
    decay = jnp.broadcast_to(vec[2:3, :], spread)
    first = jnp.broadcast_to(vec[3:4, :], spread)
    r1, r2, r4, r8 = scan_rates(decay)
    powers = jnp.exp(-lax.broadcasted_iota(jnp.int32, spread, 0).astype(F32) * jnp.exp(decay))

    def group(start, state):
        rows = pl.ds(start, 8)
        key, val, pre = key_ref[rows, :], val_ref[rows, :], rec_ref[rows, :]
        m1, m2, m4, mf, ml = (twice(masks[n, rows, :]) for n in range(5))
        rec = 1.0 / (1.0 + jnp.exp(-pre))
        power = jnp.exp(key)
        bonus = jnp.exp(first + key)
        c1, c2, c4, cf, cl = m1 * r1, m2 * r2, m4 * r4, mf * powers, ml * r8
        priors, ends = [], []
        for local, entering in ((power * val, state[0]), (power, state[1])):
            local = local + c1 * pltpu.roll(local, 1, 0)
            local = local + c2 * pltpu.roll(local, 2, 0)
            local = local + c4 * pltpu.roll(local, 4, 0)
            priors.append(m1 * pltpu.roll(local, 1, 0) + cf * entering)
            ends.append(jnp.broadcast_to(local[7:8, :], spread) + cl * entering)
        wkv = (priors[0] + bonus * val) / (priors[1] + bonus)
        rec_ref[rows, :] = rec
        pa_ref[rows, :] = priors[0]
        pb_ref[rows, :] = priors[1]
        return rec * wkv, tuple(ends)

    def step(i, state):
        start = pl.multiple_of(i * CHUNK, CHUNK)
        upper, state = group(start, state)
        lower, state = group(pl.multiple_of(start + 8, 8), state)
        gated_ref[pl.ds(start, CHUNK), :] = jnp.concatenate([upper, lower], axis=0).astype(BF)
        return state

    zero = jnp.zeros(spread, F32)
    lax.fori_loop(0, key_ref.shape[0] // CHUNK, step, (zero, zero), unroll=2)


def time_forward(co, mixed, weights, vectors, masks):
    tokens, width = mixed[0].shape
    half = width // 2
    per_half = half // TILE

    def tile(j, co):
        return 0, (co[4] ^ lax.div(j, per_half)) * per_half + lax.rem(j, per_half)

    fixed = pl.BlockSpec((tokens, width), lambda j, co: (0, 0))
    block = pl.BlockSpec((tokens, TILE), tile)
    return pl.pallas_call(
        functools.partial(time_forward_kernel, layouts=[w[0] for w in weights]),
        grid_spec=pltpu.PrefetchScalarGridSpec(
            num_scalar_prefetch=1,
            grid=(width // TILE,),
            in_specs=[fixed] * 3
            + [
                pl.BlockSpec((vectors.shape[0], TILE), tile),
                pl.BlockSpec(masks.shape, lambda j, co: (0, 0, 0)),
            ]
            + [anywhere()] * len(arrays_of(*weights)),
            out_specs=[block] * 6,
            scratch_shapes=[pltpu.VMEM((2, width, half), BF)] * 3
            + [pltpu.SemaphoreType.DMA((3, 32))],
        ),
        out_shape=[jax.ShapeDtypeStruct((tokens, width), F32)] * 5
        + [jax.ShapeDtypeStruct((tokens, width), BF)],
        compiler_params=params(),
        cost_estimate=cost(8, 34 << 20),
    )(co, *mixed, vectors, masks, *arrays_of(*weights))


def time_output_kernel(
    co, gated, x_ref, carry_ref, vec_ref, *refs, layout
):
    arrays, refs = take_refs(refs, layout)
    middle_ref, mk_ref, mr_ref, ow, last, sems = refs
    i = pl.program_id(0)
    copies = weight_copies(co, arrays, ow, sems, layout)

    @pl.when(i == 0)
    def _():
        start_all(copies)
        last[...] = jnp.zeros_like(last)
        wait_half(copies, 0)
        wait_half(copies, 1)

    half = ow.shape[2]
    middle_ref[...] = dot(gated[:, :half], ow[0], NT) + dot(gated[:, half:], ow[1], NT)
    width = x_ref.shape[1]

    def step(n, before):
        rows = chunk_rows(n)
        for strip in strips(width):
            middle_ref[rows, strip] += x_ref[rows, strip].astype(F32)
        mean, scaled = norm_stats(lambda strip: middle_ref[rows, strip], width)
        carry = carry_ref[rows, :]
        lasts = []
        for strip in strips(width):
            unit = (middle_ref[rows, strip] - mean) * scaled
            normed = unit * vec_ref[7:8, strip] + vec_ref[8:9, strip]
            behind = move_down(normed, before[len(lasts)]) * carry
            for m, out in ((9, mk_ref), (10, mr_ref)):
                mix = vec_ref[m : m + 1, strip]
                out[rows, strip] = (normed * mix + behind * (1.0 - mix)).astype(BF)
            lasts.append(normed[ROWS - 1 :, :])
        return tuple(lasts)

    lasts = lax.fori_loop(0, x_ref.shape[0] // ROWS, step, row_parts(last), unroll=2)
    for strip, value in zip(strips(width), lasts):
        last[0:1, strip] = value


def time_output_step(co, gated, x, carry, vectors, weight):
    tokens, width = x.shape
    rows = tokens // 4
    tall = pl.BlockSpec((rows, width), lambda i, co: (i, 0))
    return pl.pallas_call(
        functools.partial(time_output_kernel, layout=weight[0]),
        grid_spec=pltpu.PrefetchScalarGridSpec(
            num_scalar_prefetch=1,
            grid=(4,),
            in_specs=[
                tall,
                tall,
                pl.BlockSpec((rows, LANES), lambda i, co: (i, 0)),
                pl.BlockSpec(vectors.shape, lambda i, co: (0, 0)),
            ]
            + [anywhere()] * len(weight[1]),
            out_specs=[tall] * 3,
            scratch_shapes=[
                pltpu.VMEM((2, width, width // 2), BF),
                pltpu.VMEM((8, width), F32),
                pltpu.SemaphoreType.DMA((32,)),
            ],
        ),
        out_shape=[jax.ShapeDtypeStruct((tokens, width), t) for t in (F32, BF, BF)],
        compiler_params=params(),
        cost_estimate=cost(3, 14 << 20),
    )(co, gated, x, carry, vectors, *weight[1])


WIDE = 512


def hidden_kernel(co, mk, *refs, layout):
    arrays, (hidden_ref, active_ref, whole, sems) = take_refs(refs, layout)
    j = pl.program_id(0)
    per_half = whole.shape[2] // WIDE
    copies = weight_copies(co, arrays, whole, sems, layout)

    @pl.when(j == 0)
    def _():
        start_all(copies)
        wait_half(copies, 0)

    @pl.when(j == per_half)
    def _():
        wait_half(copies, 1)

    half = co[4] ^ lax.div(j, per_half)
    columns = pl.ds(pl.multiple_of(lax.rem(j, per_half) * WIDE, WIDE), WIDE)
    active = jnp.maximum(dot(mk[...], whole[half, :, columns], NN), 0.0)
    active_ref[...] = active.astype(BF)
    hidden_ref[...] = (active * active).astype(BF)


def column_tile(per_half):
    return lambda j, co: (0, (co[4] ^ lax.div(j, per_half)) * per_half + lax.rem(j, per_half))


def hidden_step(co, mixed, weight):
    tokens, width = mixed.shape
    half = weight_width(weight)
    block = pl.BlockSpec((tokens, WIDE), column_tile(half // WIDE))
    return pl.pallas_call(
        functools.partial(hidden_kernel, layout=weight[0]),
        grid_spec=pltpu.PrefetchScalarGridSpec(
            num_scalar_prefetch=1,
            grid=(2 * half // WIDE,),
            in_specs=[pl.BlockSpec((tokens, width), lambda j, co: (0, 0))]
            + [anywhere()] * len(weight[1]),
            out_specs=[block] * 2,
            scratch_shapes=[
                pltpu.VMEM((2, width, half), BF),
                pltpu.SemaphoreType.DMA((sem_count(weight),)),
            ],
        ),
        out_shape=[jax.ShapeDtypeStruct((tokens, 2 * half), BF)] * 2,
        compiler_params=params(),
        cost_estimate=cost(4.5, 26 << 20),
    )(co, mixed, *weight[1])


def result_kernel(
    co, scale, hidden, mr, middle_ref, teacher_ref, valid_ref, *refs, layouts,
):
    value_w, refs = take_refs(refs, layouts[0])
    recept_w, refs = take_refs(refs, layouts[1])
    out_ref, dres_ref, dkv_ref, drec_ref, loss_ref, ww, rw, kv_ref, pre_ref, sems, sems_r = refs
    i = pl.program_id(0)
    copies = weight_copies(co, value_w, ww, sems, layouts[0])
    recept = weight_copies(co, recept_w, rw, sems_r, layouts[1])

    @pl.when(i == 0)
    def _():
        start_all(recept)
        start_all(copies)
        loss_ref[...] = jnp.zeros_like(loss_ref)
        for half in (0, 1):
            wait_half(recept, half)
        for half in (0, 1):
            wait_half(copies, half)

    wide, narrow = ww.shape[2], rw.shape[2]
    kv_ref[...] = dot(hidden[:, :wide], ww[0], NT) + dot(hidden[:, wide:], ww[1], NT)
    pre_ref[:, :narrow] = dot(mr[...], rw[0], NN)
    pre_ref[:, narrow:] = dot(mr[...], rw[1], NN)
    factor = scale[0]

    def step(n, _):
        rows = chunk_rows(n)
        valid = valid_ref[rows, :]
        for strip in strips(kv_ref.shape[1]):
            kv = kv_ref[rows, strip]
            rec = 1.0 / (1.0 + jnp.exp(-pre_ref[rows, strip]))
            result = middle_ref[rows, strip] + rec * kv
            out_ref[rows, strip] = result.astype(BF)
            error = (result - teacher_ref[rows, strip].astype(F32)) * valid
            grad = error * factor
            dres_ref[rows, strip] = grad
            dkv = grad * rec
            dkv_ref[rows, strip] = dkv.astype(BF)
            drec_ref[rows, strip] = (dkv * kv * (1.0 - rec)).astype(BF)
            loss_ref[:, strip] += fold_rows(error * error)
        return 0

    lax.fori_loop(0, kv_ref.shape[0] // ROWS, step, 0)


def result_step(co, scale, hidden, mixed, middle, teacher, valid, weight, recept):
    tokens, width = mixed.shape
    rows = tokens // 4
    wide = weight_width(weight)
    tall = pl.BlockSpec((rows, width), lambda i, co, s: (i, 0))
    return pl.pallas_call(
        functools.partial(result_kernel, layouts=[weight[0], recept[0]]),
        grid_spec=pltpu.PrefetchScalarGridSpec(
            num_scalar_prefetch=2,
            grid=(4,),
            in_specs=[
                pl.BlockSpec((rows, 2 * wide), lambda i, co, s: (i, 0)),
                tall,
                tall,
                tall,
                pl.BlockSpec((rows, LANES), lambda i, co, s: (i, 0)),
            ]
            + [anywhere()] * len(arrays_of(weight, recept)),
            out_specs=[tall] * 4 + [pl.BlockSpec((8, width), lambda i, co, s: (0, 0))],
            scratch_shapes=[
                pltpu.VMEM((2, width, wide), BF),
                pltpu.VMEM((2, width, width // 2), BF),
                pltpu.VMEM((rows, width), F32),
                pltpu.VMEM((rows, width), F32),
                pltpu.SemaphoreType.DMA((sem_count(weight),)),
                pltpu.SemaphoreType.DMA((sem_count(recept),)),
            ],
        ),
        out_shape=[jax.ShapeDtypeStruct((tokens, width), t) for t in (BF, F32, BF, BF)]
        + [jax.ShapeDtypeStruct((8, width), F32)],
        compiler_params=params(),
        cost_estimate=cost(7, 38 << 20),
    )(co, scale, hidden, mixed, middle, teacher, valid, *arrays_of(weight, recept))


def grad_copies(co, whole, targets, n, sems, order, piece, merged=False):
    found = ([], [])
    for m, (which, index, rel) in enumerate(rel_slots(order)):
        row, half = slot_place(co, rel)
        found[rel["x"]].append(
            pltpu.make_async_copy(
                whole.at[half, pl.ds(row, SLOT), piece],
                targets[which].at[
                    (index + (n,) if merged else (n,) + index) + (slice(None), piece)
                ],
                sems.at[m],
            )
        )
    return found


def weight_grads_kernel(co, *refs, orders, merged):
    count = len(orders)
    models, chans, refs = refs[:count], refs[count : 2 * count], refs[2 * count :]
    targets, (held, given, whole, sems_in, sems_out) = refs[:4], refs[4:]
    half = whole.shape[3]
    loads = []
    for n in range(count):
        for m, (source, place) in enumerate(((models[n], held), (chans[n], given))):
            loads.append(pltpu.make_async_copy(source, place.at[n], sems_in.at[2 * n + m]))
            loads[-1].start()
    for n, order in enumerate(orders):
        for load in loads[2 * n : 2 * n + 2]:
            load.wait()

        def step(turn, _, n=n, order=order):
            at = co[4] ^ turn
            columns = pl.ds(pl.multiple_of(at * half, half), half)
            whole[n, at] = dot(held[n], given[n, :, columns], TN).astype(BF)
            for which in (0, 1):

                @pl.when(turn == which)
                def _(which=which):
                    copies = grad_copies(
                        co, whole.at[n], targets, n, sems_out.at[n], order, slice(None), merged
                    )
                    for copy in copies[which]:
                        copy.start()

            return 0

        lax.fori_loop(0, 2, step, 0)
    for n, order in enumerate(orders):
        for copies in grad_copies(
            co, whole.at[n], targets, n, sems_out.at[n], order, slice(None), merged
        ):
            for copy in copies:
                copy.wait()


def weight_grads(co, pairs, merged=False):
    models, chans, orders = zip(*pairs)
    tokens, width = models[0].shape
    half = width // 2
    count = len(pairs)
    dims = (2, 2, 2, count) if merged else (count, 2, 2, 2)
    return pl.pallas_call(
        functools.partial(weight_grads_kernel, orders=orders, merged=merged),
        grid_spec=pltpu.PrefetchScalarGridSpec(
            num_scalar_prefetch=1,
            grid=(1,),
            in_specs=[anywhere()] * (2 * count),
            out_specs=[anywhere()] * 4,
            scratch_shapes=[
                pltpu.VMEM((count, tokens, width), BF),
                pltpu.VMEM((count, tokens, width), BF),
                pltpu.VMEM((count, 2, width, half), BF),
                pltpu.SemaphoreType.DMA((2 * count,)),
                pltpu.SemaphoreType.DMA((count, 32)),
            ],
        ),
        out_shape=[jax.ShapeDtypeStruct(dims + (SLOT, half), BF)] * 4,
        compiler_params=params(),
        cost_estimate=cost(count * 1.2, count * (6 << 20)),
    )(co, *models, *chans)


def channel_back_kernel(co, dkv, mixed, hidden, active, *refs, layout, order):
    arrays, (dkey, *refs) = take_refs(refs, layout)
    targets, (whole, grads, sems_in, sems) = refs[:-4], refs[-4:]
    j = pl.program_id(0)
    per_half = grads.shape[4] // WIDE
    columns = pl.ds(pl.multiple_of(lax.rem(j, per_half) * WIDE, WIDE), WIDE)
    turn = lax.div(j, per_half)
    half = co[4] ^ turn
    loads = weight_copies(co, arrays, whole, sems_in, layout)

    @pl.when(j == 0)
    def _():
        start_all(loads)

    def keep(n, values):
        grads[n, half, :, :, columns] = values.astype(BF).reshape(16, SLOT, WIDE)

    keep(0, dot(dkv[...], hidden[...], TN))

    for which in (0, 1):

        @pl.when(j == which * per_half)
        def _(which=which):
            wait_half(loads, which)

    back = dot(dkv[...], whole[half, :, columns], NN)
    back = (2.0 * active[...].astype(F32) * back).astype(BF)
    dkey[...] = back
    keep(1, dot(mixed[...], back, TN))

    if order is None:
        wide = grads.shape[4]

        def copies(turn, piece, size):
            half = co[4] ^ turn
            return [
                pltpu.make_async_copy(
                    grads.at[n, half, :, :, pl.ds(piece, size)],
                    targets[0].at[:, half, :, pl.ds(n * wide + piece, size)],
                    sems.at[n],
                )
                for n in (0, 1)
            ]

        for copy in copies(turn, pl.multiple_of(lax.rem(j, per_half) * WIDE, WIDE), WIDE):
            copy.start()

        @pl.when(j == pl.num_programs(0) - 1)
        def _():
            for which in (0, 1):
                for copy in copies(which, 0, wide):
                    copy.wait()

        return

    def slot_copies(which, piece):
        found = []
        for m, (array, index, rel) in enumerate(rel_slots(order)):
            if rel["x"] != which:
                continue
            row, at = slot_place(co, rel)
            for n in (0, 1):
                found.append(
                    pltpu.make_async_copy(
                        grads.at[n, at, lax.div(row, SLOT), :, piece],
                        targets[array].at[index + (n, slice(None), piece)],
                        sems.at[n * 32 + m],
                    )
                )
        return found

    for which in (0, 1):

        @pl.when(turn == which)
        def _(which=which):
            for copy in slot_copies(which, columns):
                copy.start()

    @pl.when(j == pl.num_programs(0) - 1)
    def _():
        for which in (0, 1):
            for copy in slot_copies(which, slice(None)):
                copy.wait()


def channel_back(co, dkv, mixed, hidden, active, weight, first, half, order):
    tokens, width = dkv.shape
    per_half = half // WIDE
    skip, stride = first // WIDE, hidden.shape[1] // 2 // WIDE

    def tile(j, co):
        return 0, (co[4] ^ lax.div(j, per_half)) * stride + skip + lax.rem(j, per_half)

    fixed = pl.BlockSpec((tokens, width), lambda j, co: (0, 0))
    block = pl.BlockSpec((tokens, WIDE), tile)
    if order is None:
        shapes = [jax.ShapeDtypeStruct((16, 2, SLOT, 2 * half), BF)]
    else:
        shapes = [jax.ShapeDtypeStruct((2, 2, 2, 2, SLOT, half), BF)] * 4
    dkey, *slots = pl.pallas_call(
        functools.partial(channel_back_kernel, layout=weight[0], order=order),
        grid_spec=pltpu.PrefetchScalarGridSpec(
            num_scalar_prefetch=1,
            grid=(2 * per_half,),
            in_specs=[fixed, fixed, block, block] + [anywhere()] * len(weight[1]),
            out_specs=[pl.BlockSpec((tokens, WIDE), column_tile(per_half))]
            + [anywhere()] * len(shapes),
            scratch_shapes=[
                pltpu.VMEM((2, width, half), BF),
                pltpu.VMEM((2, 2, 16, SLOT, half), BF),
                pltpu.SemaphoreType.DMA((sem_count(weight),)),
                pltpu.SemaphoreType.DMA((64,)),
            ],
        ),
        out_shape=[jax.ShapeDtypeStruct((tokens, 2 * half), BF)] + shapes,
        compiler_params=params(),
        cost_estimate=cost(half / 512 * 3.3, half / 512 * (14 << 20)),
    )(co, dkv, mixed, hidden, active, *weight[1])
    return dkey, slots


def middle_back_kernel(
    co, dkey_a, dkey_b, drec, middle_ref, dres_ref, lead_ref, vec_ref, *refs, layouts,
):
    key_w, refs = take_refs(refs, layouts[0])
    recept_w, refs = take_refs(refs, layouts[1])
    dmid_ref, dtime_ref, sums_ref, ww, rw, gk_ref, gr_ref, next_ref, sems, sems_r = refs
    i = pl.program_id(0)
    copies = weight_copies(co, key_w, ww, sems, layouts[0])
    recept = weight_copies(co, recept_w, rw, sems_r, layouts[1])

    @pl.when(i == 0)
    def _():
        start_all(recept)
        start_all(copies)
        sums_ref[...] = jnp.zeros_like(sums_ref)
        next_ref[...] = jnp.zeros_like(next_ref)
        for half in (0, 1):
            wait_half(recept, half)
        for half in (0, 1):
            wait_half(copies, half)

    wide, narrow = dkey_a.shape[1] // 2, rw.shape[2]
    gk_ref[...] = sum(
        dot(part[:, half * wide : (half + 1) * wide], ww[half, :, n * wide : (n + 1) * wide], NT)
        for n, part in enumerate((dkey_a, dkey_b))
        for half in (0, 1)
    )
    gr_ref[...] = dot(drec[:, :narrow], rw[0], NT) + dot(drec[:, narrow:], rw[1], NT)
    steps = middle_ref.shape[0] // ROWS
    width = middle_ref.shape[1]

    def step(n, after):
        rows = chunk_rows(steps - 1 - n)
        mean, scaled = norm_stats(lambda strip: middle_ref[rows, strip], width)
        lead = lead_ref[rows, :]
        firsts = ([], [])
        plain, along = 0.0, 0.0
        for strip in strips(width):
            gain, bias, mix_k, mix_r = (vec_ref[m : m + 1, strip] for m in (7, 8, 9, 10))
            unit = (middle_ref[rows, strip] - mean) * scaled
            normed = unit * gain + bias
            gk, gr = gk_ref[rows, strip], gr_ref[rows, strip]
            uk = move_up(gk, after[0][len(firsts[0])]) * lead
            ur = move_up(gr, after[1][len(firsts[0])]) * lead
            grad = gk * mix_k + gr * mix_r + uk * (1.0 - mix_k) + ur * (1.0 - mix_r)
            sums_ref[0, :, strip] += fold_rows(grad * unit)
            sums_ref[1, :, strip] += fold_rows(grad)
            sums_ref[2, :, strip] += fold_rows(normed * (gk - uk))
            sums_ref[3, :, strip] += fold_rows(normed * (gr - ur))
            firsts[0].append(gk[:1, :])
            firsts[1].append(gr[:1, :])
            weighted = grad * gain
            gk_ref[rows, strip] = weighted
            plain = plain + weighted
            along = along + weighted * unit
        plain, along = spread_mean(plain, width), spread_mean(along, width)
        for strip in strips(width):
            unit = (middle_ref[rows, strip] - mean) * scaled
            dmid = dres_ref[rows, strip] + scaled * (gk_ref[rows, strip] - plain - unit * along)
            dmid_ref[rows, strip] = dmid
            dtime_ref[rows, strip] = dmid.astype(BF)
        return tuple(tuple(f) for f in firsts)

    after = lax.fori_loop(0, steps, step, tuple(row_parts(next_ref, m) for m in (0, 1)), unroll=2)
    for m, values in enumerate(after):
        for strip, value in zip(strips(width), values):
            next_ref[m : m + 1, strip] = value


def middle_back(co, dkeys, drec, middle, dres, lead, vectors, weight, recept):
    tokens, width = middle.shape
    rows = tokens // 4
    wide = weight_width(weight)
    tall = pl.BlockSpec((rows, width), lambda i, co: (3 - i, 0))
    return pl.pallas_call(
        functools.partial(middle_back_kernel, layouts=[weight[0], recept[0]]),
        grid_spec=pltpu.PrefetchScalarGridSpec(
            num_scalar_prefetch=1,
            grid=(4,),
            in_specs=[
                pl.BlockSpec((rows, wide), lambda i, co: (3 - i, 0)),
                pl.BlockSpec((rows, wide), lambda i, co: (3 - i, 0)),
                tall,
                tall,
                tall,
                pl.BlockSpec((rows, LANES), lambda i, co: (3 - i, 0)),
                pl.BlockSpec(vectors.shape, lambda i, co: (0, 0)),
            ]
            + [anywhere()] * len(arrays_of(weight, recept)),
            out_specs=[tall] * 2 + [pl.BlockSpec((4, 8, width), lambda i, co: (0, 0, 0))],
            scratch_shapes=[
                pltpu.VMEM((2, width, wide), BF),
                pltpu.VMEM((2, width, width // 2), BF),
                pltpu.VMEM((rows, width), F32),
                pltpu.VMEM((rows, width), F32),
                pltpu.VMEM((8, width), F32),
                pltpu.SemaphoreType.DMA((sem_count(weight),)),
                pltpu.SemaphoreType.DMA((sem_count(recept),)),
            ],
        ),
        out_shape=[
            jax.ShapeDtypeStruct((tokens, width), F32),
            jax.ShapeDtypeStruct((tokens, width), BF),
            jax.ShapeDtypeStruct((4, 8, width), F32),
        ],
        compiler_params=params(),
        cost_estimate=cost(8, 36 << 20),
    )(co, *dkeys, drec, middle, dres, lead, vectors, *arrays_of(weight, recept))


def time_back_kernel(
    co, dtime, key_ref, val_ref, rec_ref, pa_ref, pb_ref, vec, masks, *refs, layout,
):
    arrays, refs = take_refs(refs, layout)
    dkey_ref, dval_ref, drec_ref, sums_ref, ow, dg_ref, sems = refs
    j = pl.program_id(0)
    per_half = ow.shape[2] // TILE
    copies = weight_copies(co, arrays, ow, sems, layout)

    @pl.when(j == 0)
    def _():
        start_all(copies)
        wait_half(copies, 0)

    @pl.when(j == per_half)
    def _():
        wait_half(copies, 1)

    half = co[4] ^ lax.div(j, per_half)
    columns = pl.ds(pl.multiple_of(lax.rem(j, per_half) * TILE, TILE), TILE)
    dg_ref[...] = dot(dtime[...], ow[half, :, columns], NN)

    spread = (8, TILE)
    decay = jnp.broadcast_to(vec[2:3, :], spread)
    first = jnp.broadcast_to(vec[3:4, :], spread)
    r1, r2, r4, r8 = scan_rates(decay)
    left = 7.0 - lax.broadcasted_iota(jnp.int32, spread, 0).astype(F32)
    powers = jnp.exp(-left * jnp.exp(decay))

    def group(start, state):
        rows = pl.ds(start, 8)
        n1, n2, n4, nf, c0, ml = (twice(masks[n, rows, :]) for n in (0, 1, 2, 3, 4, 5))
        key, val, rec, dg = key_ref[rows, :], val_ref[rows, :], rec_ref[rows, :], dg_ref[rows, :]
        pa, pb = pa_ref[rows, :], pb_ref[rows, :]
        power = jnp.exp(key)
        bonus = jnp.exp(first + key)
        inverse = 1.0 / (pb + bonus)
        wkv = (pa + bonus * val) * inverse
        slope = dg * rec * inverse
        drec = dg * wkv * rec * (1.0 - rec)
        c1, c2, c4, cf, cl = n1 * r1, n2 * r2, n4 * r4, nf * powers, ml * r8
        found, starts = [], []
        for local, leaving in ((slope, state[0]), (-slope * wkv, state[1])):
            local = local + c1 * pltpu.roll(local, 7, 0)
            local = local + c2 * pltpu.roll(local, 6, 0)
            local = local + c4 * pltpu.roll(local, 4, 0)
            found.append(n1 * pltpu.roll(local, 7, 0) + cf * leaving)
            starts.append(c0 * jnp.broadcast_to(local[0:1, :], spread) + cl * leaving)
        later_a, later_b = found
        summand = bonus * slope * (val - wkv)
        dkey = power * (later_a * val + later_b) + summand
        dval = power * later_a + bonus * slope
        state = (
            starts[0],
            starts[1],
            state[2] + summand,
            state[3] + later_a * pa + later_b * pb,
        )
        return (dkey, dval, drec), state

    steps = key_ref.shape[0] // CHUNK

    def step(n, state):
        start = pl.multiple_of((steps - 1 - n) * CHUNK, CHUNK)
        lower, state = group(pl.multiple_of(start + 8, 8), state)
        upper, state = group(start, state)
        for up, low, out in zip(upper, lower, (dkey_ref, dval_ref, drec_ref)):
            out[pl.ds(start, CHUNK), :] = jnp.concatenate([up, low], axis=0).astype(BF)
        return state

    zero = jnp.zeros(spread, F32)
    _, _, first_sum, decay_sum = lax.fori_loop(0, steps, step, (zero,) * 4, unroll=2)
    sums_ref[0] = -r1 * jnp.exp(decay) * decay_sum
    sums_ref[1] = first_sum


def time_back(co, dtime, saved, vectors, masks, weight):
    tokens, width = dtime.shape
    half = width // 2
    tile = column_tile(half // TILE)
    block = pl.BlockSpec((tokens, TILE), tile)
    return pl.pallas_call(
        functools.partial(time_back_kernel, layout=weight[0]),
        grid_spec=pltpu.PrefetchScalarGridSpec(
            num_scalar_prefetch=1,
            grid=(width // TILE,),
            in_specs=[pl.BlockSpec((tokens, width), lambda j, co: (0, 0))]
            + [block] * 5
            + [
                pl.BlockSpec((vectors.shape[0], TILE), tile),
                pl.BlockSpec(masks.shape, lambda j, co: (0, 0, 0)),
            ]
            + [anywhere()] * len(weight[1]),
            out_specs=[block] * 3
            + [pl.BlockSpec((2, 8, TILE), lambda j, co: (0,) + tile(j, co))],
            scratch_shapes=[
                pltpu.VMEM((2, width, half), BF),
                pltpu.VMEM((tokens, TILE), F32),
                pltpu.SemaphoreType.DMA((32,)),
            ],
        ),
        out_shape=[jax.ShapeDtypeStruct((tokens, width), BF)] * 3
        + [jax.ShapeDtypeStruct((2, 8, width), F32)],
        compiler_params=params(),
        cost_estimate=cost(9, 34 << 20),
    )(co, dtime, *saved, vectors, masks, *weight[1])


def input_back_kernel(
    co, dkey, dval, drec, x_ref, dmid_ref, lead_ref, vec_ref, after_ref, _, *refs, layouts,
):
    key_w, refs = take_refs(refs, layouts[0])
    val_w, refs = take_refs(refs, layouts[1])
    rec_w, refs = take_refs(refs, layouts[2])
    out_ref, sums_ref, next_ref, kw, vw, rw, gk_ref, gv_ref, gr_ref, sems = refs
    i = pl.program_id(0)
    groups = [
        weight_copies(co, arrays, whole, sems.at[n], layout)
        for n, (arrays, whole, layout) in enumerate(zip((key_w, val_w, rec_w), (kw, vw, rw), layouts))
    ]

    @pl.when(i == 0)
    def _():
        for copies in groups:
            start_all(copies)
        sums_ref[...] = jnp.zeros_like(sums_ref)
        next_ref[...] = after_ref[...]
        for copies in groups:
            wait_half(copies, 0)
            wait_half(copies, 1)

    half = kw.shape[2]
    for grad, whole, out in ((dkey, kw, gk_ref), (dval, vw, gv_ref), (drec, rw, gr_ref)):
        out[...] = dot(grad[:, :half], whole[0], NT) + dot(grad[:, half:], whole[1], NT)
    steps = x_ref.shape[0] // ROWS
    width = x_ref.shape[1]

    def step(n, after):
        rows = chunk_rows(steps - 1 - n)
        mean, scaled = norm_stats(lambda strip: x_ref[rows, strip].astype(F32), width)
        lead = lead_ref[rows, :]
        firsts = ([], [], [])
        plain, along = 0.0, 0.0
        for strip in strips(width):
            gain, bias = vec_ref[0:1, strip], vec_ref[1:2, strip]
            unit = (x_ref[rows, strip].astype(F32) - mean) * scaled
            normed = unit * gain + bias
            total = 0.0
            for m, part in enumerate((gk_ref, gv_ref, gr_ref)):
                mix = vec_ref[4 + m : 5 + m, strip]
                grad = part[rows, strip]
                up = move_up(grad, after[m][len(firsts[m])]) * lead
                total = total + grad * mix + up * (1.0 - mix)
                sums_ref[2 + m, :, strip] += fold_rows(normed * (grad - up))
                firsts[m].append(grad[:1, :])
            sums_ref[0, :, strip] += fold_rows(total * unit)
            sums_ref[1, :, strip] += fold_rows(total)
            weighted = total * gain
            gk_ref[rows, strip] = weighted
            plain = plain + weighted
            along = along + weighted * unit
        plain, along = spread_mean(plain, width), spread_mean(along, width)
        for strip in strips(width):
            unit = (x_ref[rows, strip].astype(F32) - mean) * scaled
            out_ref[rows, strip] = dmid_ref[rows, strip] + scaled * (
                gk_ref[rows, strip] - plain - unit * along
            )
        return tuple(tuple(f) for f in firsts)

    after = lax.fori_loop(0, steps, step, tuple(row_parts(next_ref, m) for m in range(3)), unroll=2)
    for m, values in enumerate(after):
        for strip, value in zip(strips(width), values):
            next_ref[m : m + 1, strip] = value


def input_back(co, grads, x, dmid, lead, vectors, weights, part, after, found):
    tokens, width = x.shape
    rows = tokens // 4

    def at(i, co):
        return 3 - 2 * part - i, 0

    tall = pl.BlockSpec((rows, width), at)
    edge = pl.BlockSpec((8, width), lambda i, co: (0, 0))
    return pl.pallas_call(
        functools.partial(input_back_kernel, layouts=[w[0] for w in weights]),
        grid_spec=pltpu.PrefetchScalarGridSpec(
            num_scalar_prefetch=1,
            grid=(2,),
            in_specs=[tall] * 5
            + [
                pl.BlockSpec((rows, LANES), at),
                pl.BlockSpec(vectors.shape, lambda i, co: (0, 0)),
                edge,
                anywhere(),
            ]
            + [anywhere()] * len(arrays_of(*weights)),
            out_specs=[
                tall,
                pl.BlockSpec((5, 8, width), lambda i, co: (0, 0, 0)),
                edge,
            ],
            scratch_shapes=[pltpu.VMEM((2, width, width // 2), BF)] * 3
            + [pltpu.VMEM((rows, width), F32)] * 3
            + [pltpu.SemaphoreType.DMA((3, 32))],
        ),
        out_shape=[
            jax.ShapeDtypeStruct((tokens, width), F32),
            jax.ShapeDtypeStruct((5, 8, width), F32),
            jax.ShapeDtypeStruct((8, width), F32),
        ],
        input_output_aliases={9: 0},
        compiler_params=params(),
        cost_estimate=cost(4, 16 << 20),
    )(co, *grads, x, dmid, lead, vectors, after, found, *arrays_of(*weights))


def seal(*values):
    return lax.optimization_barrier(values)


def swap(values, axis):
    return lax.ppermute(values, axis, SWAP)


class Gather:
    def __init__(self, shard, order):
        self.order, self.state, self.done = order, (shard,), 0

    def step(self):
        n = self.done
        if n and n < 4:
            self.state = (jnp.stack(self.state),)
        if n < 3:
            self.state += (swap(self.state[0], self.order[n]),)
        elif n == 3:
            near = self.state[0]
            self.state = (near, swap(near, self.order[3]), swap(near, "c"))
        else:
            near, far, near_other = self.state
            self.state = (near, far, near_other, swap(far, "c"))
        self.done += 1

    def part(self, first=0, skip=0, columns=None):
        assert self.done == 5
        return ("rel", (self.order, skip), first, columns or self.state[0].shape[-1]), self.state


def weight_of(*parts):
    layouts, arrays = zip(*parts)
    return tuple(layouts), [array for group in arrays for array in group]


class Merged:
    def __init__(self, slots, order):
        self.order, self.state, self.done = order, tuple(slots), 0

    def step(self):
        n = self.done
        if n == 0:
            near, far, near_other, far_other = self.state
            self.state = (near, far, swap(far_other, "c"), swap(near_other, "c"))
        elif n == 1:
            near, far, far_got, near_got = self.state
            self.state = (near, near_got, swap(far + far_got, self.order[3]))
        elif n < 5:
            kept, sent = (
                sum(part[place].astype(F32) for part in self.state).astype(BF) for place in (0, 1)
            )
            self.state = (kept, swap(sent, self.order[4 - n]))
        self.done += 1

    def finish(self):
        assert self.done == 5
        return list(self.state[0].astype(F32) + self.state[1].astype(F32))


class Reduce:
    def __init__(self, slots, orders):
        self.orders, self.state, self.done = orders, tuple(slots), 0

    def step(self):
        n = self.done
        if n == 0:
            near, far, near_other, far_other = self.state
            self.state = (near, far, swap(far_other, "c"), swap(near_other, "c"))
        elif n == 1:
            near, far, far_got, near_got = self.state
            got = [swap(far[m] + far_got[m], order[3]) for m, order in enumerate(self.orders)]
            self.state = (near, near_got, *got)
        elif n == 2:
            near, near_got, *got = self.state
            self.keep([(near[m], near_got[m], part) for m, part in enumerate(got)], 2)
        elif n < 5:
            self.keep(self.state, 4 - n)
        self.done += 1

    def keep(self, parts, place):
        kept, sent = (
            [sum(v[at].astype(F32) for v in part).astype(BF) for part in parts] for at in (0, 1)
        )
        if place:
            sent = [swap(v, order[place]) for v, order in zip(sent, self.orders)]
            self.state = tuple(zip(kept, sent))
        else:
            self.state = (*kept, swap(jnp.stack(sent), self.orders[0][0]))

    def finish(self):
        assert self.done == 5
        *kept, got = self.state
        return [v.astype(F32) + got[n].astype(F32) for n, v in enumerate(kept)]


def step_all(*chains):
    for chain in chains:
        chain.step()


def seal_all(chains, *values):
    states, values = seal([chain.state for chain in chains], values)
    for chain, state in zip(chains, states):
        chain.state = tuple(state)
    return values


def pair_up(shard):
    got = swap(shard, "x")
    mine = lax.axis_index("x") == 0
    return jnp.where(mine, jnp.stack([shard, got]), jnp.stack([got, shard]))


def gather_plain(shard):
    whole = lax.all_gather(shard, ("w", "u", "y", "c"), axis=0, tiled=True)
    whole = lax.all_gather(whole, "x", axis=1, tiled=True)
    half = whole.shape[1] // 2
    return whole.reshape(16, SLOT, 2, half).transpose(0, 2, 1, 3)


def all_of(array, skip=0, columns=None):
    return (("abs", skip, 0, columns or array.shape[-1]),), [array]


def gather_vectors(own, first, last):
    for axis in EVERY[::-1][first:last]:
        got = swap(own, axis)
        mine = lax.axis_index(axis) == 0
        own = jnp.where(mine, jnp.concatenate([own, got], axis=1), jnp.concatenate([got, own], axis=1))
    return (own,)


def reduce_plain(slots, orders):
    return [reduce_one([part[n] for part in slots], order) for n, order in enumerate(orders)]


def reduce_merged(slots, order):
    count = slots[0].shape[3]
    return [reduce_one([part[:, :, :, n] for part in slots], order) for n in range(count)]


def scatter_rows(whole):
    whole = whole.reshape(-1, *whole.shape[1:])
    return lax.psum_scatter(whole, ("w", "u", "y", "c"), scatter_dimension=0)


def pair_sum(sums):
    side = lax.axis_index("x")
    sent = lax.dynamic_index_in_dim(sums, 1 - side, keepdims=False)
    kept = lax.dynamic_index_in_dim(sums, side, keepdims=False)
    return kept.astype(F32) + swap(sent, "x").astype(F32)


def reduce_blocks(blocks):
    whole = blocks.transpose(0, 2, 1, 3).reshape(16 * SLOT, -1)
    whole = lax.psum_scatter(whole, ("w", "u", "y", "c"), scatter_dimension=0, tiled=True)
    return lax.psum_scatter(whole, "x", scatter_dimension=1, tiled=True).astype(F32)


def reduce_one(slots, order):
    table = {}
    for which, index, rel in rel_slots(order):
        block = rel["w"] * 8 + rel["u"] * 4 + rel["y"] * 2 + rel["c"]
        table[block, rel["x"]] = slots[which][index]
    whole = jnp.concatenate(
        [jnp.concatenate([table[b, 0], table[b, 1]], axis=1) for b in range(16)], axis=0
    )
    whole = lax.psum_scatter(whole, ("w", "u", "y", "c"), scatter_dimension=0, tiled=True)
    return lax.psum_scatter(whole, "x", scatter_dimension=1, tiled=True).astype(F32)


def scan_masks(carry):
    c = carry.reshape(-1, 8)
    place = jnp.arange(8)[None, :]

    def behind(values, n):
        return jnp.where(place >= n, jnp.roll(values, n, axis=1), 0.0)

    def ahead(values, n):
        return jnp.where(place < 8 - n, jnp.roll(values, -n, axis=1), 0.0)

    m1 = jnp.where(place >= 1, c, 0.0)
    m2 = m1 * behind(m1, 1)
    m4 = m2 * behind(m2, 2)
    mf = jnp.cumprod(c, axis=1)
    ml = jnp.broadcast_to(mf[:, 7:], c.shape)
    n1 = ahead(c, 1)
    n2 = n1 * ahead(n1, 1)
    n4 = n2 * ahead(n2, 2)
    back = jnp.cumprod(c[:, ::-1], axis=1)[:, ::-1]
    nf = jnp.where(place < 7, jnp.roll(back, -1, axis=1), 1.0)
    c0 = jnp.broadcast_to(c[:, :1], c.shape)
    tables = (jnp.stack(t).reshape(len(t), -1, 1) for t in ((m1, m2, m4, mf, ml), (n1, n2, n4, nf, c0, ml)))
    return [jnp.broadcast_to(t, t.shape[:2] + (LANES,)) for t in tables]


def on_device(
    inputs,
    segments,
    teacher,
    first_norm_gain,
    first_norm_bias,
    time_decay,
    time_first,
    time_mix_key,
    time_mix_value,
    time_mix_recept,
    time_key,
    time_value,
    time_recept,
    time_output,
    second_norm_gain,
    second_norm_bias,
    channel_mix_key,
    channel_mix_recept,
    channel_key,
    channel_recept,
    channel_value,
):
    tokens, width = inputs.shape
    sizes = {a: lax.axis_size(a) for a in EVERY}
    devices = math.prod(sizes.values())
    fast = all(size == 2 for size in sizes.values())
    side = lax.axis_index("x")
    if fast:
        co = jnp.stack([lax.axis_index(a) for a in EVERY]).astype(jnp.int32)
    else:
        co = jnp.zeros((5,), jnp.int32)

    ids = lax.dynamic_slice_in_dim(segments, side * tokens, tokens)
    previous = jnp.concatenate([jnp.zeros((1,), jnp.int32), ids[:-1]])
    started = jnp.arange(tokens, dtype=jnp.int32) > 0
    carry = ((ids == previous) & (ids > 0) & started).astype(F32)
    valid = (ids > 0).astype(F32)
    lead = jnp.concatenate([carry[1:], jnp.zeros((1,), F32)])
    masks_down, masks_up = scan_masks(carry)
    carry, valid_rows, lead = (
        jnp.broadcast_to(v[:, None], (tokens, LANES)) for v in (carry, valid, lead)
    )

    flat = 0
    for axis in EVERY:
        flat = flat * sizes[axis] + lax.axis_index(axis)
    own_vectors = jnp.stack(
        [
            first_norm_gain,
            first_norm_bias,
            time_decay,
            time_first,
            time_mix_key,
            time_mix_value,
            time_mix_recept,
            second_norm_gain,
            second_norm_bias,
            channel_mix_key,
            channel_mix_recept,
        ]
    )
    piece = own_vectors.shape[1]
    counts = jnp.where(jnp.arange(piece) == 0, jnp.sum(valid), 0.0)[None, :]
    own_vectors = jnp.concatenate([own_vectors, counts, jnp.zeros((4, piece), F32)])
    output_t, value_t = time_output.T, channel_value.T

    def teacher_rows_of(mine, theirs):
        return jnp.where(
            side == 0,
            jnp.concatenate([mine, theirs], axis=1),
            jnp.concatenate([theirs, mine], axis=1),
        )

    if sizes["x"] == 2:
        mine = lax.dynamic_slice_in_dim(teacher, side * tokens, tokens)
        theirs = lax.dynamic_slice_in_dim(teacher, (1 - side) * tokens, tokens)

    key_order, val_order, rec_order = three_orders = ("wxuy", "wuyx", "wyxu")
    half = width // 2
    if fast:
        wide = channel_key.shape[1]
        split = wide // 2
        keys = [Gather(channel_key[:, :split], "wuyx"), Gather(channel_key[:, split:], "wyux")]
        first = pair_up(jnp.concatenate([time_key, time_value, time_recept, output_t], axis=1))
        late = jnp.concatenate([value_t, channel_recept], axis=1)
        first, late, own_vectors, masks_down, masks_up, mine, theirs = seal_all(
            keys, first, late, own_vectors, masks_down, masks_up, mine, theirs
        )
        first = lax.all_gather(first, ("w", "u", "y", "c"))
        step_all(*keys)
        (vectors,) = gather_vectors(own_vectors, 0, 1)
        late = pair_up(late)
        late, vectors = seal_all(keys, late, vectors)
        step_all(*keys)
        (vectors,) = gather_vectors(vectors, 1, 3)
        (vectors,) = seal_all(keys, vectors)
        step_all(*keys)
        (vectors,) = gather_vectors(vectors, 3, 5)
        (vectors,) = seal_all(keys, vectors)
        step_all(*keys)
        mixed = first_mix(inputs, carry, vectors)
        first, late, mixed, vectors = seal(first, late, mixed, vectors)
        late = lax.all_gather(late, ("w", "u", "y", "c"))
        key_w, value_w, recept_w, output_w = (all_of(first, n * half, half) for n in range(4))
    else:
        early = gather_plain(channel_key)
        wide = early.shape[-1]
        split = wide // 2
        key_w, value_w, recept_w, output_w, crecept_w = (
            all_of(gather_plain(w))
            for w in (time_key, time_value, time_recept, output_t, channel_recept)
        )
        ckey_w = all_of(early)
        late = gather_plain(value_t)
        cvalue_w = [all_of(late, skip, split) for skip in (0, split)]
        vectors = lax.all_gather(own_vectors, EVERY, axis=1, tiled=True)
        mixed = first_mix(inputs, carry, vectors)

    *saved, gated = time_forward(co, mixed, (key_w, value_w, recept_w), vectors, masks_down)
    if fast:
        (gated, theirs) = seal_all(keys, gated, theirs)
        step_all(*keys)
    if sizes["x"] == 2:
        theirs = swap(theirs, "x")
    middle, mixed_k2, mixed_r2 = time_output_step(co, gated, inputs, carry, vectors, output_w)
    if fast:
        middle, mixed_k2, mixed_r2 = seal_all(keys, middle, mixed_k2, mixed_r2)
        ckey_w = weight_of(keys[0].part(), keys[1].part(split))
    hidden, active = hidden_step(co, mixed_k2, ckey_w)
    if fast:
        hidden, theirs, late = seal(hidden, theirs, late)
        cvalue_w = [all_of(late, skip, split) for skip in (0, split)]
        crecept_w = all_of(late, wide, half)
    teacher_rows = teacher_rows_of(mine, theirs) if sizes["x"] == 2 else teacher
    count = jnp.sum(vectors[11])
    scale = (float(tokens * devices) / count).reshape(1)
    result, dres, dkv, drec2, loss_rows = result_step(
        co, scale, hidden, mixed_r2, middle, teacher_rows, valid_rows, both_parts(cvalue_w, split), crecept_w
    )

    kept = lax.dynamic_slice_in_dim(result, side * half, half, axis=1)
    arrived = lax.dynamic_slice_in_dim(result, (1 - side) * half, half, axis=1)
    if sizes["x"] == 2:
        arrived = swap(arrived, "x")

    back = functools.partial(channel_back, co)
    order_b, order_c = "wyux", "wuxy"
    edge = jnp.zeros((8, width), F32)

    def input_back_part(dmix, part, after, found):
        return input_back(
            co, dmix, inputs, dmid, lead, vectors, (key_w, value_w, recept_w), part, after, found
        )

    if fast:
        dkey_b, found = back(dkv, mixed_k2, hidden, active, cvalue_w[1], split, split, order_b)
        group_b = Merged(found, order_b)
        (dkv,) = seal_all((group_b,), dkv)
        group_b.step()
        dkey_a, (blocks,) = back(dkv, mixed_k2, hidden, active, cvalue_w[0], 0, split, None)
        blocks = scatter_rows(blocks)
        (dkey_a, arrived) = seal_all((group_b,), dkey_a, arrived)
        group_b.step()
        dmid, dtime, sums2 = middle_back(
            co, (dkey_a, dkey_b), drec2, middle, dres, lead, vectors, ckey_w, crecept_w
        )
        found = weight_grads(
            co, ((mixed_r2, drec2, order_c), (dtime, gated, order_c)), merged=True
        )
        group_c = Merged(found, order_c)
        (dtime,) = seal_all((group_b, group_c), dtime)
        step_all(group_b, group_c)
        *dmix, sums_t = time_back(co, dtime, saved, vectors, masks_up, output_w)
        (dmix, dmid) = seal_all((group_b, group_c), dmix, dmid)
        step_all(group_b, group_c)
        found = weight_grads(co, [(m, d, order) for m, d, order in zip(mixed, dmix, three_orders)])
        group_t = Reduce(found, three_orders)
        (dmix,) = seal_all((group_b, group_t), dmix)
        step_all(group_b, group_t)
        found, sums_l, edge = input_back_part(dmix, 0, edge, jnp.zeros_like(dmid))
        (dmix, edge, found) = seal_all((group_b, group_c, group_t), dmix, edge, found)
        step_all(group_c, group_t)
        input_grad, sums_u, _ = input_back_part(dmix, 1, edge, found)
    else:
        dkey_b, found = back(dkv, mixed_k2, hidden, active, cvalue_w[1], split, split, order_b)
        cv_b, ck_b = reduce_merged(found, order_b)
        dkey_a, (blocks,) = back(dkv, mixed_k2, hidden, active, cvalue_w[0], 0, split, None)
        cv_a, ck_a = (
            reduce_blocks(blocks[..., n * split : (n + 1) * split]) for n in (0, 1)
        )
        dmid, dtime, sums2 = middle_back(
            co, (dkey_a, dkey_b), drec2, middle, dres, lead, vectors, ckey_w, crecept_w
        )
        found = weight_grads(
            co, ((mixed_r2, drec2, order_c), (dtime, gated, order_c)), merged=True
        )
        crecept_g, output_g = reduce_merged(found, order_c)
        *dmix, sums_t = time_back(co, dtime, saved, vectors, masks_up, output_w)
        found = weight_grads(co, [(m, d, order) for m, d, order in zip(mixed, dmix, three_orders)])
        key_g, val_g, rec_g = reduce_plain(found, three_orders)
        found, sums_l, edge = input_back_part(dmix, 0, edge, jnp.zeros_like(dmid))
        input_grad, sums_u, _ = input_back_part(dmix, 1, edge, found)

    rows = jnp.concatenate([sums_l[:2] + sums_u[:2], sums_t, sums_l[2:] + sums_u[2:], sums2, loss_rows[None]])
    totals = jnp.sum(rows, axis=1)
    if fast:
        (totals,) = seal_all((group_c, group_t), totals)
        for axes in ("xc", "yu", "w"):
            step_all(*[group for group in (group_c, group_t) if group.done < 5])
            for axis in axes:
                totals = totals + swap(totals, axis)
            (totals,) = seal_all((group_c, group_t), totals)
        cv_b, ck_b = group_b.finish()
        cv_a, ck_a = jnp.split(pair_sum(blocks), 2, axis=1)
        crecept_g, output_g = group_c.finish()
        key_g, val_g, rec_g = group_t.finish()
    else:
        totals = lax.psum(totals, EVERY)
    loss = jnp.sum(totals[11]) / (2.0 * count * width)
    vector_g = lax.dynamic_slice_in_dim(totals, flat * piece, piece, axis=1)
    if sizes["x"] == 2:
        cvalue_g = jnp.concatenate([cv_a, cv_b], axis=1)
        ckey_g = jnp.concatenate([ck_a, ck_b], axis=1)
        outputs = jnp.where(
            side == 0,
            jnp.concatenate([kept, arrived], axis=0),
            jnp.concatenate([arrived, kept], axis=0),
        )
    else:
        cvalue_g, ckey_g = (
            jnp.concatenate([a.reshape(-1, 2, split), b.reshape(-1, 2, split)], axis=2).reshape(
                a.shape[0], -1
            )
            for a, b in ((cv_a, cv_b), (ck_a, ck_b))
        )
        outputs = result

    return (
        outputs,
        loss,
        input_grad,
        *[vector_g[n] for n in range(7)],
        key_g,
        val_g,
        rec_g,
        output_g.T,
        *[vector_g[n] for n in range(7, 11)],
        ckey_g,
        crecept_g,
        cvalue_g.T,
    )


def solution(mesh):
    fsdp, tp = mesh.shape["fsdp"], mesh.shape["tp"]
    two = 2 if fsdp % 8 == 0 else 1
    split = Mesh(mesh.devices.reshape(fsdp // two**3, two, two, two, tp), EVERY)
    rows = ("w", "u", "y", "c")
    vector = P(EVERY)
    matrix = P(rows, "x")
    turned = P("x", rows)
    tall = P(EVERY, None)
    return jax.shard_map(
        on_device,
        mesh=split,
        in_specs=(
            (tall, P(rows), matrix)
            + (vector,) * 7
            + (matrix, matrix, matrix, turned)
            + (vector,) * 4
            + (matrix, matrix, turned)
        ),
        out_specs=(
            (matrix, P(), tall)
            + (vector,) * 7
            + (matrix, matrix, matrix, turned)
            + (vector,) * 4
            + (matrix, matrix, turned)
        ),
        check_vma=False,
    )
```

```python
import functools
import itertools
import math

import jax
import jax.numpy as jnp
from jax import lax
from jax.experimental import pallas as pl
from jax.experimental.pallas import tpu as pltpu
from jax.sharding import Mesh
from jax.sharding import PartitionSpec as P

BF = jnp.bfloat16
F32 = jnp.float32
EPSILON = 1e-05
SLOT = 64
CHUNK = 16
VMEM_LIMIT = 58 << 20
EVERY = ("w", "u", "y", "c", "x")
SWAP = [(0, 1), (1, 0)]

NN = (((1,), (0,)), ((), ()))
NT = (((1,), (1,)), ((), ()))
TN = (((0,), (0,)), ((), ()))


def dot(left, right, dims):
    return lax.dot_general(left, right, dims, preferred_element_type=F32)


def rel_slots(order):
    for other_core in (0, 1):
        for last in (0, 1):
            for index in itertools.product((0, 1), repeat=3):
                rel = dict(zip(order[2::-1], index))
                rel[order[3]] = last
                rel["c"] = other_core
                yield other_core * 2 + last, index, rel


def slot_place(co, rel):
    at = {axis: co[n] ^ rel[axis] for n, axis in enumerate(EVERY)}
    block = at["w"] * 8 + at["u"] * 4 + at["y"] * 2 + at["c"]
    return pl.multiple_of(block * SLOT, SLOT), at["x"]


def weight_copies(co, refs, whole, sems, layout):
    copies = []
    refs = list(refs)
    for kind, order, first, columns in layout:
        target = pl.ds(first, columns)
        if kind == "rel":
            order, skip, base = order
            if base is None:
                arrays, refs = refs[:4], refs[4:]
            else:
                arrays, refs = [*refs[:2], refs[2].at[base], refs[2].at[base + 1]], refs[3:]
            for which, index, rel in rel_slots(order):
                row, half = slot_place(co, rel)
                copies.append(
                    (
                        rel["x"],
                        pltpu.make_async_copy(
                            arrays[which].at[index + (slice(None), pl.ds(skip, columns))],
                            whole.at[half, pl.ds(row, SLOT), target],
                            sems.at[len(copies)],
                        ),
                    )
                )
        else:
            array, refs = refs[0], refs[1:]
            for rel_x in (0, 1):
                half = co[4] ^ rel_x
                for block in range(16):
                    copies.append(
                        (
                            rel_x,
                            pltpu.make_async_copy(
                                array.at[block, half, :, pl.ds(order, columns)],
                                whole.at[half, pl.ds(block * SLOT, SLOT), target],
                                sems.at[len(copies)],
                            ),
                        )
                    )
    return copies


def take_refs(refs, layout):
    count = 0
    for kind, order, _, _ in layout:
        count += 1 if kind == "abs" else 4 if order[2] is None else 3
    return refs[:count], refs[count:]


def arrays_of(*weights):
    return [array for _, arrays in weights for array in arrays]


def both_parts(weights, split):
    (first, arrays_a), (second, arrays_b) = weights
    second = tuple((kind, order, at + split, columns) for kind, order, at, columns in second)
    return tuple(first) + second, list(arrays_a) + list(arrays_b)


def weight_width(weight):
    return sum(part[3] for part in weight[0])


def sem_count(weight):
    return 32 * len(weight[0])


def start_all(copies):
    for _, copy in copies:
        copy.start()


def wait_half(copies, half):
    for which, copy in copies:
        if which == half:
            copy.wait()


ROWS = 32
LANES = 128


def strips(width):
    return [slice(n, n + LANES) for n in range(0, width, LANES)]


def row_parts(ref, row=0):
    return tuple(ref[row : row + 1, strip] for strip in strips(ref.shape[1]))


def chunk_rows(n):
    return pl.ds(pl.multiple_of(n * ROWS, ROWS), ROWS)


def spread_mean(total, width):
    return jnp.broadcast_to(jnp.sum(total, axis=1, keepdims=True) * (1.0 / width), total.shape)


def wait_at_first(copies, half):
    @pl.when(pl.program_id(0) == 0)
    def _():
        wait_half(copies, half)


def norm_stats(load, width):
    total = sum(load(strip) for strip in strips(width))
    mean = spread_mean(total, width)
    square = 0.0
    for strip in strips(width):
        centre = load(strip) - mean
        square = square + centre * centre
    return mean, lax.rsqrt(spread_mean(square, width) + EPSILON)


def first_row(shape):
    return lax.broadcasted_iota(jnp.int32, shape, 0) == 0


def last_row(shape):
    return lax.broadcasted_iota(jnp.int32, shape, 0) == shape[0] - 1


def move_down(values, before):
    return jnp.where(first_row(values.shape), before, pltpu.roll(values, 1, 0))


def move_up(values, after):
    return jnp.where(last_row(values.shape), after, pltpu.roll(values, values.shape[0] - 1, 0))


def fold_rows(values):
    return sum(values[n : n + 8] for n in range(0, values.shape[0], 8))


def params(semantics=1):
    return pltpu.CompilerParams(vmem_limit_bytes=VMEM_LIMIT)


def anywhere():
    return pl.BlockSpec(memory_space=pl.ANY)


COST = 0.01


def cost(units, traffic):
    return pl.CostEstimate(
        flops=int(units * 2 * 1024**3 * COST), bytes_accessed=int(traffic * COST), transcendentals=0
    )


def first_mix_kernel(x_ref, carry_ref, vec_ref, mk_ref, mv_ref, mr_ref, last):
    width = x_ref.shape[1]

    def step(n, before):
        rows = chunk_rows(n)
        mean, scaled = norm_stats(lambda strip: x_ref[rows, strip].astype(F32), width)
        carry = carry_ref[rows, :]
        lasts = []
        for strip in strips(width):
            unit = (x_ref[rows, strip].astype(F32) - mean) * scaled
            normed = unit * vec_ref[0:1, strip] + vec_ref[1:2, strip]
            behind = move_down(normed, before[len(lasts)]) * carry
            for m, out in ((4, mk_ref), (5, mv_ref), (6, mr_ref)):
                mix = vec_ref[m : m + 1, strip]
                out[rows, strip] = (normed * mix + behind * (1.0 - mix)).astype(BF)
            lasts.append(normed[ROWS - 1 :, :])
        return tuple(lasts)

    @pl.when(pl.program_id(0) == 0)
    def _():
        last[...] = jnp.zeros_like(last)

    lasts = lax.fori_loop(0, x_ref.shape[0] // ROWS, step, row_parts(last), unroll=2)
    for strip, value in zip(strips(width), lasts):
        last[0:1, strip] = value


def first_mix(x, carry, vectors):
    tokens, width = x.shape
    rows = tokens // 4
    tall = pl.BlockSpec((rows, width), lambda i: (i, 0))
    return pl.pallas_call(
        first_mix_kernel,
        grid=(4,),
        in_specs=[
            tall,
            pl.BlockSpec((rows, LANES), lambda i: (i, 0)),
            pl.BlockSpec(vectors.shape, lambda i: (0, 0)),
        ],
        out_specs=[tall] * 3,
        out_shape=[jax.ShapeDtypeStruct(x.shape, BF)] * 3,
        scratch_shapes=[pltpu.VMEM((8, width), F32)],
        compiler_params=params(),
        cost_estimate=cost(0, 8 << 20),
    )(x, carry, vectors)


TILE = 256


def scan_rates(decay):
    speed = jnp.exp(decay)
    return [jnp.exp(-float(n) * speed) for n in (1, 2, 4, 8)]


def twice(values):
    return jnp.concatenate([values] * (TILE // 128), axis=1)


def time_forward_kernel(
    co, mk, mv, mr, vec, masks, *refs, layouts,
):
    key_w, refs = take_refs(refs, layouts[0])
    val_w, refs = take_refs(refs, layouts[1])
    rec_w, refs = take_refs(refs, layouts[2])
    key_ref, val_ref, rec_ref, pa_ref, pb_ref, gated_ref, kw, vw, rw, sems = refs
    j = pl.program_id(0)
    per_half = kw.shape[2] // TILE
    groups = [
        weight_copies(co, arrays, whole, sems.at[n], layout)
        for n, (arrays, whole, layout) in enumerate(zip((key_w, val_w, rec_w), (kw, vw, rw), layouts))
    ]

    @pl.when(j == 0)
    def _():
        for copies in groups:
            start_all(copies)
        for copies in groups:
            wait_half(copies, 0)

    @pl.when(j == per_half)
    def _():
        for copies in groups:
            wait_half(copies, 1)

    half = co[4] ^ lax.div(j, per_half)
    columns = pl.ds(pl.multiple_of(lax.rem(j, per_half) * TILE, TILE), TILE)
    key_ref[...] = dot(mk[...], kw[half, :, columns], NN)
    val_ref[...] = dot(mv[...], vw[half, :, columns], NN)
    rec_ref[...] = dot(mr[...], rw[half, :, columns], NN)

    spread = (8, TILE)
    decay = jnp.broadcast_to(vec[2:3, :], spread)
    first = jnp.broadcast_to(vec[3:4, :], spread)
    r1, r2, r4, r8 = scan_rates(decay)
    powers = jnp.exp(-lax.broadcasted_iota(jnp.int32, spread, 0).astype(F32) * jnp.exp(decay))

    def group(start, state):
        rows = pl.ds(start, 8)
        key, val, pre = key_ref[rows, :], val_ref[rows, :], rec_ref[rows, :]
        m1, m2, m4, mf, ml = (twice(masks[n, rows, :]) for n in range(5))
        rec = 1.0 / (1.0 + jnp.exp(-pre))
        power = jnp.exp(key)
        bonus = jnp.exp(first + key)
        c1, c2, c4, cf, cl = m1 * r1, m2 * r2, m4 * r4, mf * powers, ml * r8
        priors, ends = [], []
        for local, entering in ((power * val, state[0]), (power, state[1])):
            local = local + c1 * pltpu.roll(local, 1, 0)
            local = local + c2 * pltpu.roll(local, 2, 0)
            local = local + c4 * pltpu.roll(local, 4, 0)
            priors.append(m1 * pltpu.roll(local, 1, 0) + cf * entering)
            ends.append(jnp.broadcast_to(local[7:8, :], spread) + cl * entering)
        wkv = (priors[0] + bonus * val) / (priors[1] + bonus)
        rec_ref[rows, :] = rec
        pa_ref[rows, :] = priors[0]
        pb_ref[rows, :] = priors[1]
        return rec * wkv, tuple(ends)

    def step(i, state):
        start = pl.multiple_of(i * CHUNK, CHUNK)
        upper, state = group(start, state)
        lower, state = group(pl.multiple_of(start + 8, 8), state)
        gated_ref[pl.ds(start, CHUNK), :] = jnp.concatenate([upper, lower], axis=0).astype(BF)
        return state

    zero = jnp.zeros(spread, F32)
    lax.fori_loop(0, key_ref.shape[0] // CHUNK, step, (zero, zero), unroll=2)


def time_forward(co, mixed, weights, vectors, masks):
    tokens, width = mixed[0].shape
    half = width // 2
    per_half = half // TILE

    def tile(j, co):
        return 0, (co[4] ^ lax.div(j, per_half)) * per_half + lax.rem(j, per_half)

    fixed = pl.BlockSpec((tokens, width), lambda j, co: (0, 0))
    block = pl.BlockSpec((tokens, TILE), tile)
    return pl.pallas_call(
        functools.partial(time_forward_kernel, layouts=[w[0] for w in weights]),
        grid_spec=pltpu.PrefetchScalarGridSpec(
            num_scalar_prefetch=1,
            grid=(width // TILE,),
            in_specs=[fixed] * 3
            + [
                pl.BlockSpec((vectors.shape[0], TILE), tile),
                pl.BlockSpec(masks.shape, lambda j, co: (0, 0, 0)),
            ]
            + [anywhere()] * len(arrays_of(*weights)),
            out_specs=[block] * 6,
            scratch_shapes=[pltpu.VMEM((2, width, half), BF)] * 3
            + [pltpu.SemaphoreType.DMA((3, 32))],
        ),
        out_shape=[jax.ShapeDtypeStruct((tokens, width), F32)] * 5
        + [jax.ShapeDtypeStruct((tokens, width), BF)],
        compiler_params=params(),
        cost_estimate=cost(8, 34 << 20),
    )(co, *mixed, vectors, masks, *arrays_of(*weights))


def time_output_kernel(
    co, gated, x_ref, carry_ref, vec_ref, *refs, layout
):
    arrays, refs = take_refs(refs, layout)
    middle_ref, mk_ref, mr_ref, ow, last, sems = refs
    i = pl.program_id(0)
    copies = weight_copies(co, arrays, ow, sems, layout)

    @pl.when(i == 0)
    def _():
        start_all(copies)
        last[...] = jnp.zeros_like(last)
        wait_half(copies, 0)
        wait_half(copies, 1)

    half = ow.shape[2]
    middle_ref[...] = dot(gated[:, :half], ow[0], NT) + dot(gated[:, half:], ow[1], NT)
    width = x_ref.shape[1]

    def step(n, before):
        rows = chunk_rows(n)
        for strip in strips(width):
            middle_ref[rows, strip] += x_ref[rows, strip].astype(F32)
        mean, scaled = norm_stats(lambda strip: middle_ref[rows, strip], width)
        carry = carry_ref[rows, :]
        lasts = []
        for strip in strips(width):
            unit = (middle_ref[rows, strip] - mean) * scaled
            normed = unit * vec_ref[7:8, strip] + vec_ref[8:9, strip]
            behind = move_down(normed, before[len(lasts)]) * carry
            for m, out in ((9, mk_ref), (10, mr_ref)):
                mix = vec_ref[m : m + 1, strip]
                out[rows, strip] = (normed * mix + behind * (1.0 - mix)).astype(BF)
            lasts.append(normed[ROWS - 1 :, :])
        return tuple(lasts)

    lasts = lax.fori_loop(0, x_ref.shape[0] // ROWS, step, row_parts(last), unroll=2)
    for strip, value in zip(strips(width), lasts):
        last[0:1, strip] = value


def time_output_step(co, gated, x, carry, vectors, weight):
    tokens, width = x.shape
    rows = tokens // 4
    tall = pl.BlockSpec((rows, width), lambda i, co: (i, 0))
    return pl.pallas_call(
        functools.partial(time_output_kernel, layout=weight[0]),
        grid_spec=pltpu.PrefetchScalarGridSpec(
            num_scalar_prefetch=1,
            grid=(4,),
            in_specs=[
                tall,
                tall,
                pl.BlockSpec((rows, LANES), lambda i, co: (i, 0)),
                pl.BlockSpec(vectors.shape, lambda i, co: (0, 0)),
            ]
            + [anywhere()] * len(weight[1]),
            out_specs=[tall] * 3,
            scratch_shapes=[
                pltpu.VMEM((2, width, width // 2), BF),
                pltpu.VMEM((8, width), F32),
                pltpu.SemaphoreType.DMA((32,)),
            ],
        ),
        out_shape=[jax.ShapeDtypeStruct((tokens, width), t) for t in (F32, BF, BF)],
        compiler_params=params(),
        cost_estimate=cost(3, 14 << 20),
    )(co, gated, x, carry, vectors, *weight[1])


WIDE = 512


def hidden_kernel(co, mk, *refs, layout):
    arrays, (hidden_ref, active_ref, whole, sems) = take_refs(refs, layout)
    j = pl.program_id(0)
    per_half = whole.shape[2] // WIDE
    copies = weight_copies(co, arrays, whole, sems, layout)

    @pl.when(j == 0)
    def _():
        start_all(copies)
        wait_half(copies, 0)

    @pl.when(j == per_half)
    def _():
        wait_half(copies, 1)

    half = co[4] ^ lax.div(j, per_half)
    columns = pl.ds(pl.multiple_of(lax.rem(j, per_half) * WIDE, WIDE), WIDE)
    active = jnp.maximum(dot(mk[...], whole[half, :, columns], NN), 0.0)
    active_ref[...] = active.astype(BF)
    hidden_ref[...] = (active * active).astype(BF)


def column_tile(per_half):
    return lambda j, co: (0, (co[4] ^ lax.div(j, per_half)) * per_half + lax.rem(j, per_half))


def hidden_step(co, mixed, weight):
    tokens, width = mixed.shape
    half = weight_width(weight)
    block = pl.BlockSpec((tokens, WIDE), column_tile(half // WIDE))
    return pl.pallas_call(
        functools.partial(hidden_kernel, layout=weight[0]),
        grid_spec=pltpu.PrefetchScalarGridSpec(
            num_scalar_prefetch=1,
            grid=(2 * half // WIDE,),
            in_specs=[pl.BlockSpec((tokens, width), lambda j, co: (0, 0))]
            + [anywhere()] * len(weight[1]),
            out_specs=[block] * 2,
            scratch_shapes=[
                pltpu.VMEM((2, width, half), BF),
                pltpu.SemaphoreType.DMA((sem_count(weight),)),
            ],
        ),
        out_shape=[jax.ShapeDtypeStruct((tokens, 2 * half), BF)] * 2,
        compiler_params=params(),
        cost_estimate=cost(4.5, 26 << 20),
    )(co, mixed, *weight[1])


def result_kernel(
    co, scale, hidden, mr, middle_ref, mine_ref, theirs_ref, valid_ref, *refs, layouts,
):
    value_w, refs = take_refs(refs, layouts[0])
    recept_w, refs = take_refs(refs, layouts[1])
    *outs, dres_ref, dkv_ref, drec_ref, loss_ref, ww, rw, kv_ref, pre_ref, sems, sems_r = refs
    i = pl.program_id(0)
    copies = weight_copies(co, value_w, ww, sems, layouts[0])
    recept = weight_copies(co, recept_w, rw, sems_r, layouts[1])

    @pl.when(i == 0)
    def _():
        start_all(recept)
        start_all(copies)
        loss_ref[...] = jnp.zeros_like(loss_ref)
        for half in (0, 1):
            wait_half(recept, half)
            wait_half(copies, half)

    wide, narrow = ww.shape[2], rw.shape[2]
    pre_ref[:, :narrow] = dot(mr[...], rw[0], NN)
    pre_ref[:, narrow:] = dot(mr[...], rw[1], NN)
    kv_ref[...] = dot(hidden[:, :wide], ww[0], NT) + dot(hidden[:, wide:], ww[1], NT)
    factor = scale[0]

    def step(n, _):
        rows = chunk_rows(n)
        valid = valid_ref[rows, :]
        width = kv_ref.shape[1]
        for part, at in itertools.product((0, 1), range(0, width // 2, LANES)):
            first = pl.multiple_of((co[4] ^ part) * (width // 2) + at, LANES)
            strip = pl.ds(first, LANES)
            kv = kv_ref[rows, strip]
            rec = 1.0 / (1.0 + jnp.exp(-pre_ref[rows, strip]))
            result = middle_ref[rows, strip] + rec * kv
            outs[part][rows, at : at + LANES] = result.astype(BF)
            teacher = (mine_ref, theirs_ref)[part][rows, at : at + LANES].astype(F32)
            error = (result - teacher) * valid
            grad = error * factor
            dres_ref[rows, strip] = grad
            dkv = grad * rec
            dkv_ref[rows, strip] = dkv.astype(BF)
            drec_ref[rows, strip] = (dkv * kv * (1.0 - rec)).astype(BF)
            loss_ref[:, strip] += fold_rows(error * error)
        return 0

    lax.fori_loop(0, kv_ref.shape[0] // ROWS, step, 0)


def result_step(co, scale, hidden, mixed, middle, teachers, valid, weight, recept):
    tokens, width = mixed.shape
    rows = tokens // 4
    wide = weight_width(weight)
    tall = pl.BlockSpec((rows, width), lambda i, co, s: (i, 0))
    thin = pl.BlockSpec((rows, width // 2), lambda i, co, s: (i, 0))
    return pl.pallas_call(
        functools.partial(result_kernel, layouts=[weight[0], recept[0]]),
        grid_spec=pltpu.PrefetchScalarGridSpec(
            num_scalar_prefetch=2,
            grid=(4,),
            in_specs=[
                pl.BlockSpec((rows, 2 * wide), lambda i, co, s: (i, 0)),
                tall,
                tall,
                thin,
                thin,
                pl.BlockSpec((rows, LANES), lambda i, co, s: (i, 0)),
            ]
            + [anywhere()] * len(arrays_of(weight, recept)),
            out_specs=[pl.BlockSpec((rows, width // 2), lambda i, co, s: (co[4] * 4 + i, 0)), thin]
            + [tall] * 3
            + [pl.BlockSpec((8, width), lambda i, co, s: (0, 0))],
            scratch_shapes=[
                pltpu.VMEM((2, width, wide), BF),
                pltpu.VMEM((2, width, width // 2), BF),
                pltpu.VMEM((rows, width), F32),
                pltpu.VMEM((rows, width), F32),
                pltpu.SemaphoreType.DMA((sem_count(weight),)),
                pltpu.SemaphoreType.DMA((sem_count(recept),)),
            ],
        ),
        out_shape=[jax.ShapeDtypeStruct((n * tokens, width // 2), BF) for n in (2, 1)]
        + [jax.ShapeDtypeStruct((tokens, width), t) for t in (F32, BF, BF)]
        + [jax.ShapeDtypeStruct((8, width), F32)],
        compiler_params=params(),
        cost_estimate=cost(7, 38 << 20),
    )(co, scale, hidden, mixed, middle, *teachers, valid, *arrays_of(weight, recept))


def grad_copies(co, whole, targets, n, sems, order, piece, merged=False):
    found = ([], [])
    for m, (which, index, rel) in enumerate(rel_slots(order)):
        row, half = slot_place(co, rel)
        found[rel["x"]].append(
            pltpu.make_async_copy(
                whole.at[half, pl.ds(row, SLOT), piece],
                targets[which].at[
                    (index + (n,) if merged else (n,) + index) + (slice(None), piece)
                ],
                sems.at[m],
            )
        )
    return found


def weight_grads_kernel(co, *refs, orders, merged):
    count = len(orders)
    models, chans, refs = refs[:count], refs[count : 2 * count], refs[2 * count :]
    targets, (held, given, whole, sems_in, sems_out) = refs[:4], refs[4:]
    half = whole.shape[3]
    loads = []
    for n in range(count):
        for m, (source, place) in enumerate(((models[n], held), (chans[n], given))):
            loads.append(pltpu.make_async_copy(source, place.at[n], sems_in.at[2 * n + m]))
            loads[-1].start()
    for n, order in enumerate(orders):
        for load in loads[2 * n : 2 * n + 2]:
            load.wait()

        def step(turn, _, n=n, order=order):
            at = co[4] ^ turn
            columns = pl.ds(pl.multiple_of(at * half, half), half)
            whole[n, at] = dot(held[n], given[n, :, columns], TN).astype(BF)
            for which in (0, 1):

                @pl.when(turn == which)
                def _(which=which):
                    copies = grad_copies(
                        co, whole.at[n], targets, n, sems_out.at[n], order, slice(None), merged
                    )
                    for copy in copies[which]:
                        copy.start()

            return 0

        lax.fori_loop(0, 2, step, 0)
    for n, order in enumerate(orders):
        for copies in grad_copies(
            co, whole.at[n], targets, n, sems_out.at[n], order, slice(None), merged
        ):
            for copy in copies:
                copy.wait()


def weight_grads(co, pairs, merged=False):
    models, chans, orders = zip(*pairs)
    tokens, width = models[0].shape
    half = width // 2
    count = len(pairs)
    dims = (2, 2, 2, count) if merged else (count, 2, 2, 2)
    return pl.pallas_call(
        functools.partial(weight_grads_kernel, orders=orders, merged=merged),
        grid_spec=pltpu.PrefetchScalarGridSpec(
            num_scalar_prefetch=1,
            grid=(1,),
            in_specs=[anywhere()] * (2 * count),
            out_specs=[anywhere()] * 4,
            scratch_shapes=[
                pltpu.VMEM((count, tokens, width), BF),
                pltpu.VMEM((count, tokens, width), BF),
                pltpu.VMEM((count, 2, width, half), BF),
                pltpu.SemaphoreType.DMA((2 * count,)),
                pltpu.SemaphoreType.DMA((count, 32)),
            ],
        ),
        out_shape=[jax.ShapeDtypeStruct(dims + (SLOT, half), BF)] * 4,
        compiler_params=params(),
        cost_estimate=cost(count * 1.2, count * (6 << 20)),
    )(co, *models, *chans)


def channel_back_kernel(co, dkv, mixed, hidden, active, *refs, layout, part, order):
    recept, refs = refs[: 2 * (1 - part)], refs[2 * (1 - part) :]
    arrays, refs = take_refs(refs, layout)
    dkey, *targets, whole, grads, narrow, sems_in, sems = refs
    j = pl.program_id(0)
    per_half = grads.shape[4] // WIDE
    columns = pl.ds(pl.multiple_of(lax.rem(j, per_half) * WIDE, WIDE), WIDE)
    turn = lax.div(j, per_half)
    half = co[4] ^ turn
    loads = weight_copies(co, arrays, whole, sems_in, layout)

    @pl.when(j == 0)
    def _():
        start_all(loads)

    def keep(n, values):
        grads[n, half, :, :, columns] = values.astype(BF).reshape(16, SLOT, WIDE)

    keep(0, dot(dkv[...], hidden[...], TN))

    for which in (0, 1):

        @pl.when(j == which * per_half)
        def _(which=which):
            wait_half(loads, which)

    back = dot(dkv[...], whole[half, :, columns], NN)
    back = (2.0 * active[...].astype(F32) * back).astype(BF)
    dkey[...] = back
    keep(1, dot(mixed[...], back, TN))

    wide = grads.shape[4]

    def narrow_copy(turn):
        return pltpu.make_async_copy(
            narrow.at[turn],
            targets[0].at[:, co[4] ^ turn, :, pl.ds(2 * wide, narrow.shape[3])],
            sems.at[2 + turn],
        )

    def block_copies(turn, piece, size):
        half = co[4] ^ turn
        return [
            pltpu.make_async_copy(
                grads.at[n, half, :, :, pl.ds(piece, size)],
                targets[0].at[:, half, :, pl.ds(n * wide + piece, size)],
                sems.at[n],
            )
            for n in (0, 1)
        ]

    def slot_copies(which, piece):
        found = []
        for m, (array, index, rel) in enumerate(rel_slots(order)):
            if rel["x"] == which:
                row, at = slot_place(co, rel)
                for n in (0, 1):
                    found.append(
                        pltpu.make_async_copy(
                            grads.at[n, at, lax.div(row, SLOT), :, piece],
                            targets[array].at[index + (n, slice(None), piece)],
                            sems.at[32 * n + m],
                        )
                    )
        return found

    if part == 0:
        for copy in block_copies(turn, pl.multiple_of(lax.rem(j, per_half) * WIDE, WIDE), WIDE):
            copy.start()

        @pl.when(lax.rem(j, per_half) == 0)
        def _():
            size = narrow.shape[3]
            found = dot(recept[0][...], recept[1][:, pl.ds(pl.multiple_of(half * size, size), size)], TN)
            narrow[turn] = found.astype(BF).reshape(16, SLOT, size)
            narrow_copy(turn).start()

    for which in range(2 * part):

        @pl.when(turn == which)
        def _(which=which):
            for copy in slot_copies(which, columns):
                copy.start()

    @pl.when(j == pl.num_programs(0) - 1)
    def _():
        for which in (0, 1):
            for copy in slot_copies(which, slice(None)) if part else block_copies(which, 0, wide):
                copy.wait()
            if part == 0:
                narrow_copy(which).wait()


def channel_back(co, dkv, mixed, hidden, active, recept, weight, half, part, order):
    tokens, width = dkv.shape
    per_half = half // WIDE
    skip, stride = part * per_half, hidden.shape[1] // 2 // WIDE

    def tile(j, co):
        return 0, (co[4] ^ lax.div(j, per_half)) * stride + skip + lax.rem(j, per_half)

    fixed = pl.BlockSpec((tokens, width), lambda j, co: (0, 0))
    block = pl.BlockSpec((tokens, WIDE), tile)
    return pl.pallas_call(
        functools.partial(channel_back_kernel, layout=weight[0], part=part, order=order),
        grid_spec=pltpu.PrefetchScalarGridSpec(
            num_scalar_prefetch=1,
            grid=(2 * per_half,),
            in_specs=[fixed, fixed, block, block]
            + [fixed] * len(recept)
            + [anywhere()] * len(weight[1]),
            out_specs=[pl.BlockSpec((tokens, WIDE), column_tile(per_half))]
            + [anywhere()] * (1 + 3 * part),
            scratch_shapes=[
                pltpu.VMEM((2, width, half), BF),
                pltpu.VMEM((2, 2, 16, SLOT, half), BF),
                pltpu.VMEM((2, 16, SLOT, width // 2), BF),
                pltpu.SemaphoreType.DMA((sem_count(weight),)),
                pltpu.SemaphoreType.DMA((64,)),
            ],
        ),
        out_shape=[
            jax.ShapeDtypeStruct((tokens, 2 * half), BF),
            *(
                [jax.ShapeDtypeStruct((2, 2, 2, 2, SLOT, half), BF)] * 4
                if part
                else [jax.ShapeDtypeStruct((16, 2, SLOT, 2 * half + width // 2), BF)]
            ),
        ],
        compiler_params=params(),
        cost_estimate=cost(half / 512 * 3.3, half / 512 * (14 << 20)),
    )(co, dkv, mixed, hidden, active, *recept, *weight[1])


def middle_back_kernel(
    co, dkey_a, dkey_b, drec, middle_ref, dres_ref, lead_ref, vec_ref, *refs, layouts,
):
    key_w, refs = take_refs(refs, layouts[0])
    recept_w, refs = take_refs(refs, layouts[1])
    dmid_ref, dtime_ref, sums_ref, ww, rw, gk_ref, gr_ref, next_ref, sems, sems_r = refs
    i = pl.program_id(0)
    copies = weight_copies(co, key_w, ww, sems, layouts[0])
    recept = weight_copies(co, recept_w, rw, sems_r, layouts[1])

    @pl.when(i == 0)
    def _():
        start_all(recept)
        start_all(copies)
        sums_ref[...] = jnp.zeros_like(sums_ref)
        next_ref[...] = jnp.zeros_like(next_ref)
        for half in (0, 1):
            wait_half(recept, half)
            wait_half(copies, half)

    wide, narrow = dkey_a.shape[1] // 2, rw.shape[2]
    gr_ref[...] = dot(drec[:, :narrow], rw[0], NT) + dot(drec[:, narrow:], rw[1], NT)
    gk_ref[...] = sum(
        dot(part[:, half * wide : (half + 1) * wide], ww[half, :, n * wide : (n + 1) * wide], NT)
        for n, part in enumerate((dkey_a, dkey_b))
        for half in (0, 1)
    )
    steps = middle_ref.shape[0] // ROWS
    width = middle_ref.shape[1]

    def step(n, after):
        rows = chunk_rows(steps - 1 - n)
        mean, scaled = norm_stats(lambda strip: middle_ref[rows, strip], width)
        lead = lead_ref[rows, :]
        firsts = ([], [])
        plain, along = 0.0, 0.0
        for strip in strips(width):
            gain, bias, mix_k, mix_r = (vec_ref[m : m + 1, strip] for m in (7, 8, 9, 10))
            unit = (middle_ref[rows, strip] - mean) * scaled
            normed = unit * gain + bias
            gk, gr = gk_ref[rows, strip], gr_ref[rows, strip]
            uk = move_up(gk, after[0][len(firsts[0])]) * lead
            ur = move_up(gr, after[1][len(firsts[0])]) * lead
            grad = gk * mix_k + gr * mix_r + uk * (1.0 - mix_k) + ur * (1.0 - mix_r)
            sums_ref[0, :, strip] += fold_rows(grad * unit)
            sums_ref[1, :, strip] += fold_rows(grad)
            sums_ref[2, :, strip] += fold_rows(normed * (gk - uk))
            sums_ref[3, :, strip] += fold_rows(normed * (gr - ur))
            firsts[0].append(gk[:1, :])
            firsts[1].append(gr[:1, :])
            weighted = grad * gain
            gk_ref[rows, strip] = weighted
            plain = plain + weighted
            along = along + weighted * unit
        plain, along = spread_mean(plain, width), spread_mean(along, width)
        for strip in strips(width):
            unit = (middle_ref[rows, strip] - mean) * scaled
            dmid = dres_ref[rows, strip] + scaled * (gk_ref[rows, strip] - plain - unit * along)
            dmid_ref[rows, strip] = dmid
            dtime_ref[rows, strip] = dmid.astype(BF)
        return tuple(tuple(f) for f in firsts)

    after = lax.fori_loop(0, steps, step, tuple(row_parts(next_ref, m) for m in (0, 1)), unroll=2)
    for m, values in enumerate(after):
        for strip, value in zip(strips(width), values):
            next_ref[m : m + 1, strip] = value


def middle_back(co, dkeys, drec, middle, dres, lead, vectors, weight, recept):
    tokens, width = middle.shape
    rows = tokens // 4
    wide = weight_width(weight)
    tall = pl.BlockSpec((rows, width), lambda i, co: (3 - i, 0))
    return pl.pallas_call(
        functools.partial(middle_back_kernel, layouts=[weight[0], recept[0]]),
        grid_spec=pltpu.PrefetchScalarGridSpec(
            num_scalar_prefetch=1,
            grid=(4,),
            in_specs=[
                pl.BlockSpec((rows, wide), lambda i, co: (3 - i, 0)),
                pl.BlockSpec((rows, wide), lambda i, co: (3 - i, 0)),
                tall,
                tall,
                tall,
                pl.BlockSpec((rows, LANES), lambda i, co: (3 - i, 0)),
                pl.BlockSpec(vectors.shape, lambda i, co: (0, 0)),
            ]
            + [anywhere()] * len(arrays_of(weight, recept)),
            out_specs=[tall] * 2 + [pl.BlockSpec((4, 8, width), lambda i, co: (0, 0, 0))],
            scratch_shapes=[
                pltpu.VMEM((2, width, wide), BF),
                pltpu.VMEM((2, width, width // 2), BF),
                pltpu.VMEM((rows, width), F32),
                pltpu.VMEM((rows, width), F32),
                pltpu.VMEM((8, width), F32),
                pltpu.SemaphoreType.DMA((sem_count(weight),)),
                pltpu.SemaphoreType.DMA((sem_count(recept),)),
            ],
        ),
        out_shape=[
            jax.ShapeDtypeStruct((tokens, width), F32),
            jax.ShapeDtypeStruct((tokens, width), BF),
            jax.ShapeDtypeStruct((4, 8, width), F32),
        ],
        compiler_params=params(),
        cost_estimate=cost(8, 36 << 20),
    )(co, *dkeys, drec, middle, dres, lead, vectors, *arrays_of(weight, recept))


def time_back_kernel(
    co, dtime, key_ref, val_ref, rec_ref, pa_ref, pb_ref, vec, masks, *refs, layout,
):
    arrays, refs = take_refs(refs, layout)
    dkey_ref, dval_ref, drec_ref, sums_ref, ow, dg_ref, sems = refs
    j = pl.program_id(0)
    per_half = ow.shape[2] // TILE
    copies = weight_copies(co, arrays, ow, sems, layout)

    @pl.when(j == 0)
    def _():
        start_all(copies)
        wait_half(copies, 0)

    @pl.when(j == per_half)
    def _():
        wait_half(copies, 1)

    half = co[4] ^ lax.div(j, per_half)
    columns = pl.ds(pl.multiple_of(lax.rem(j, per_half) * TILE, TILE), TILE)
    dg_ref[...] = dot(dtime[...], ow[half, :, columns], NN)

    spread = (8, TILE)
    decay = jnp.broadcast_to(vec[2:3, :], spread)
    first = jnp.broadcast_to(vec[3:4, :], spread)
    r1, r2, r4, r8 = scan_rates(decay)
    left = 7.0 - lax.broadcasted_iota(jnp.int32, spread, 0).astype(F32)
    powers = jnp.exp(-left * jnp.exp(decay))

    def group(start, state):
        rows = pl.ds(start, 8)
        n1, n2, n4, nf, c0, ml = (twice(masks[n, rows, :]) for n in (0, 1, 2, 3, 4, 5))
        key, val, rec, dg = key_ref[rows, :], val_ref[rows, :], rec_ref[rows, :], dg_ref[rows, :]
        pa, pb = pa_ref[rows, :], pb_ref[rows, :]
        power = jnp.exp(key)
        bonus = jnp.exp(first + key)
        inverse = 1.0 / (pb + bonus)
        wkv = (pa + bonus * val) * inverse
        slope = dg * rec * inverse
        drec = dg * wkv * rec * (1.0 - rec)
        c1, c2, c4, cf, cl = n1 * r1, n2 * r2, n4 * r4, nf * powers, ml * r8
        found, starts = [], []
        for local, leaving in ((slope, state[0]), (-slope * wkv, state[1])):
            local = local + c1 * pltpu.roll(local, 7, 0)
            local = local + c2 * pltpu.roll(local, 6, 0)
            local = local + c4 * pltpu.roll(local, 4, 0)
            found.append(n1 * pltpu.roll(local, 7, 0) + cf * leaving)
            starts.append(c0 * jnp.broadcast_to(local[0:1, :], spread) + cl * leaving)
        later_a, later_b = found
        summand = bonus * slope * (val - wkv)
        dkey = power * (later_a * val + later_b) + summand
        dval = power * later_a + bonus * slope
        state = (
            starts[0],
            starts[1],
            state[2] + summand,
            state[3] + later_a * pa + later_b * pb,
        )
        return (dkey, dval, drec), state

    steps = key_ref.shape[0] // CHUNK

    def step(n, state):
        start = pl.multiple_of((steps - 1 - n) * CHUNK, CHUNK)
        lower, state = group(pl.multiple_of(start + 8, 8), state)
        upper, state = group(start, state)
        for up, low, out in zip(upper, lower, (dkey_ref, dval_ref, drec_ref)):
            out[pl.ds(start, CHUNK), :] = jnp.concatenate([up, low], axis=0).astype(BF)
        return state

    zero = jnp.zeros(spread, F32)
    _, _, first_sum, decay_sum = lax.fori_loop(0, steps, step, (zero,) * 4, unroll=2)
    sums_ref[0] = -r1 * jnp.exp(decay) * decay_sum
    sums_ref[1] = first_sum


def time_back(co, dtime, saved, vectors, masks, weight):
    tokens, width = dtime.shape
    half = width // 2
    tile = column_tile(half // TILE)
    block = pl.BlockSpec((tokens, TILE), tile)
    return pl.pallas_call(
        functools.partial(time_back_kernel, layout=weight[0]),
        grid_spec=pltpu.PrefetchScalarGridSpec(
            num_scalar_prefetch=1,
            grid=(width // TILE,),
            in_specs=[pl.BlockSpec((tokens, width), lambda j, co: (0, 0))]
            + [block] * 5
            + [
                pl.BlockSpec((vectors.shape[0], TILE), tile),
                pl.BlockSpec(masks.shape, lambda j, co: (0, 0, 0)),
            ]
            + [anywhere()] * len(weight[1]),
            out_specs=[block] * 3
            + [pl.BlockSpec((2, 8, TILE), lambda j, co: (0,) + tile(j, co))],
            scratch_shapes=[
                pltpu.VMEM((2, width, half), BF),
                pltpu.VMEM((tokens, TILE), F32),
                pltpu.SemaphoreType.DMA((32,)),
            ],
        ),
        out_shape=[jax.ShapeDtypeStruct((tokens, width), BF)] * 3
        + [jax.ShapeDtypeStruct((2, 8, width), F32)],
        compiler_params=params(),
        cost_estimate=cost(9, 34 << 20),
    )(co, dtime, *saved, vectors, masks, *weight[1])


def input_back_kernel(
    co, dkey, dval, drec, x_ref, dmid_ref, lead_ref, vec_ref, after_ref, _, *refs, layouts,
):
    key_w, refs = take_refs(refs, layouts[0])
    val_w, refs = take_refs(refs, layouts[1])
    rec_w, refs = take_refs(refs, layouts[2])
    out_ref, sums_ref, next_ref, kw, vw, rw, gk_ref, gv_ref, gr_ref, sems = refs
    i = pl.program_id(0)
    groups = [
        weight_copies(co, arrays, whole, sems.at[n], layout)
        for n, (arrays, whole, layout) in enumerate(zip((key_w, val_w, rec_w), (kw, vw, rw), layouts))
    ]

    @pl.when(i == 0)
    def _():
        for copies in groups:
            start_all(copies)
        sums_ref[...] = jnp.zeros_like(sums_ref)
        next_ref[...] = after_ref[...]

    half = kw.shape[2]
    for copies, grad, whole, out in zip(
        groups, (dkey, dval, drec), (kw, vw, rw), (gk_ref, gv_ref, gr_ref)
    ):
        wait_at_first(copies, 0)
        wait_at_first(copies, 1)
        out[...] = dot(grad[:, :half], whole[0], NT) + dot(grad[:, half:], whole[1], NT)
    steps = x_ref.shape[0] // ROWS
    width = x_ref.shape[1]

    def step(n, after):
        rows = chunk_rows(steps - 1 - n)
        mean, scaled = norm_stats(lambda strip: x_ref[rows, strip].astype(F32), width)
        lead = lead_ref[rows, :]
        firsts = ([], [], [])
        plain, along = 0.0, 0.0
        for strip in strips(width):
            gain, bias = vec_ref[0:1, strip], vec_ref[1:2, strip]
            unit = (x_ref[rows, strip].astype(F32) - mean) * scaled
            normed = unit * gain + bias
            total = 0.0
            for m, part in enumerate((gk_ref, gv_ref, gr_ref)):
                mix = vec_ref[4 + m : 5 + m, strip]
                grad = part[rows, strip]
                up = move_up(grad, after[m][len(firsts[m])]) * lead
                total = total + grad * mix + up * (1.0 - mix)
                sums_ref[2 + m, :, strip] += fold_rows(normed * (grad - up))
                firsts[m].append(grad[:1, :])
            sums_ref[0, :, strip] += fold_rows(total * unit)
            sums_ref[1, :, strip] += fold_rows(total)
            weighted = total * gain
            gk_ref[rows, strip] = weighted
            plain = plain + weighted
            along = along + weighted * unit
        plain, along = spread_mean(plain, width), spread_mean(along, width)
        for strip in strips(width):
            unit = (x_ref[rows, strip].astype(F32) - mean) * scaled
            out_ref[rows, strip] = dmid_ref[rows, strip] + scaled * (
                gk_ref[rows, strip] - plain - unit * along
            )
        return tuple(tuple(f) for f in firsts)

    after = lax.fori_loop(0, steps, step, tuple(row_parts(next_ref, m) for m in range(3)), unroll=2)
    for m, values in enumerate(after):
        for strip, value in zip(strips(width), values):
            next_ref[m : m + 1, strip] = value


def input_back(co, grads, x, dmid, lead, vectors, weights, part, after, found):
    tokens, width = x.shape
    rows = tokens // 4

    def at(i, co):
        return 3 - 2 * part - i, 0

    tall = pl.BlockSpec((rows, width), at)
    edge = pl.BlockSpec((8, width), lambda i, co: (0, 0))
    return pl.pallas_call(
        functools.partial(input_back_kernel, layouts=[w[0] for w in weights]),
        grid_spec=pltpu.PrefetchScalarGridSpec(
            num_scalar_prefetch=1,
            grid=(2,),
            in_specs=[tall] * 5
            + [
                pl.BlockSpec((rows, LANES), at),
                pl.BlockSpec(vectors.shape, lambda i, co: (0, 0)),
                edge,
                anywhere(),
            ]
            + [anywhere()] * len(arrays_of(*weights)),
            out_specs=[
                tall,
                pl.BlockSpec((5, 8, width), lambda i, co: (0, 0, 0)),
                edge,
            ],
            scratch_shapes=[pltpu.VMEM((2, width, width // 2), BF)] * 3
            + [pltpu.VMEM((rows, width), F32)] * 3
            + [pltpu.SemaphoreType.DMA((3, 32))],
        ),
        out_shape=[
            jax.ShapeDtypeStruct((tokens, width), F32),
            jax.ShapeDtypeStruct((5, 8, width), F32),
            jax.ShapeDtypeStruct((8, width), F32),
        ],
        input_output_aliases={9: 0},
        compiler_params=params(),
        cost_estimate=cost(4, 16 << 20),
    )(co, *grads, x, dmid, lead, vectors, after, found, *arrays_of(*weights))


def seal(*values):
    return lax.optimization_barrier(values)


def swap(values, axis):
    return lax.ppermute(values, axis, SWAP)


class Gather:
    def __init__(self, shard, order, first=None):
        self.order, self.state, self.done = order, (shard,), 0
        if first is not None:
            self.state, self.done = (shard, first), 1

    def step(self):
        n = self.done
        if n and n < 4:
            self.state = (jnp.stack(self.state),)
        if n < 4:
            self.state += (swap(self.state[0], self.order[n]),)
        else:
            near, far = self.state
            self.state = (near, far, swap(near, "c"), swap(far, "c"))
        self.done += 1

    def part(self, first=0, skip=0, columns=None):
        assert self.done == 5
        return ("rel", (self.order, skip, None), first, columns or self.state[0].shape[-1]), self.state

    def part_with(self, others, base):
        assert self.done == 4
        return ("rel", (self.order, 0, base), 0, self.state[0].shape[-1]), (*self.state, others)


def weight_of(*parts):
    layouts, arrays = zip(*parts)
    return tuple(layouts), [array for group in arrays for array in group]


class Merged:
    def __init__(self, slots, order):
        self.order, self.state, self.done = order, tuple(slots), 0

    def step(self):
        n = self.done
        if n == 0:
            near, far, near_other, far_other = self.state
            self.state = (near, far, swap(far_other, "c"), swap(near_other, "c"))
        elif n == 1:
            near, far, far_got, near_got = self.state
            self.state = (near, near_got, swap(far + far_got, self.order[3]))
        elif n < 5:
            kept, sent = (
                sum(part[place].astype(F32) for part in self.state).astype(BF) for place in (0, 1)
            )
            self.state = (kept, swap(sent, self.order[4 - n]))
        self.done += 1

    def finish(self):
        assert self.done == 5
        return list(self.state[0].astype(F32) + self.state[1].astype(F32))


class Reduce:
    def __init__(self, slots, orders):
        self.orders, self.state, self.done = orders, tuple(slots), 0

    def step(self):
        n = self.done
        if n == 0:
            near, far, near_other, far_other = self.state
            self.state = (near, far, swap(far_other, "c"), swap(near_other, "c"))
        elif n == 1:
            near, far, far_got, near_got = self.state
            got = [swap(far[m] + far_got[m], order[3]) for m, order in enumerate(self.orders)]
            self.state = (near, near_got, *got)
        elif n == 2:
            near, near_got, *got = self.state
            self.keep([(near[m], near_got[m], part) for m, part in enumerate(got)], 2)
        elif n < 5:
            self.keep(self.state, 4 - n)
        self.done += 1

    def keep(self, parts, place):
        kept, sent = (
            [sum(v[at].astype(F32) for v in part).astype(BF) for part in parts] for at in (0, 1)
        )
        if place:
            sent = [swap(v, order[place]) for v, order in zip(sent, self.orders)]
            self.state = tuple(zip(kept, sent))
        else:
            self.state = (*kept, swap(jnp.stack(sent), self.orders[0][0]))

    def finish(self):
        assert self.done == 5
        *kept, got = self.state
        return [v.astype(F32) + got[n].astype(F32) for n, v in enumerate(kept)]


def step_all(*chains):
    for chain in chains:
        chain.step()


def seal_all(chains, *values):
    states, values = seal([chain.state for chain in chains], values)
    for chain, state in zip(chains, states):
        chain.state = tuple(state)
    return values


def pair_up(shard):
    got = swap(shard, "x")
    mine = lax.axis_index("x") == 0
    return jnp.where(mine, jnp.stack([shard, got]), jnp.stack([got, shard]))


def gather_plain(shard):
    whole = lax.all_gather(shard, ("w", "u", "y", "c"), axis=0, tiled=True)
    whole = lax.all_gather(whole, "x", axis=1, tiled=True)
    half = whole.shape[1] // 2
    return whole.reshape(16, SLOT, 2, half).transpose(0, 2, 1, 3)


def all_of(array, skip=0, columns=None):
    return (("abs", skip, 0, columns or array.shape[-1]),), [array]


def gather_vectors(own, first, last):
    for axis in EVERY[::-1][first:last]:
        got = swap(own, axis)
        mine = lax.axis_index(axis) == 0
        own = jnp.where(mine, jnp.concatenate([own, got], axis=1), jnp.concatenate([got, own], axis=1))
    return (own,)


def reduce_plain(slots, orders):
    return [reduce_one([part[n] for part in slots], order) for n, order in enumerate(orders)]


def reduce_merged(slots, order):
    count = slots[0].shape[3]
    return [reduce_one([part[:, :, :, n] for part in slots], order) for n in range(count)]


def scatter_rows(whole):
    whole = whole.reshape(-1, *whole.shape[1:])
    return lax.psum_scatter(whole, ("w", "u", "y", "c"), scatter_dimension=0)


def pair_sum(sums):
    side = lax.axis_index("x")
    sent = lax.dynamic_index_in_dim(sums, 1 - side, keepdims=False)
    kept = lax.dynamic_index_in_dim(sums, side, keepdims=False)
    return kept.astype(F32) + swap(sent, "x").astype(F32)


def reduce_blocks(blocks):
    whole = blocks.transpose(0, 2, 1, 3).reshape(16 * SLOT, -1)
    whole = lax.psum_scatter(whole, ("w", "u", "y", "c"), scatter_dimension=0, tiled=True)
    return lax.psum_scatter(whole, "x", scatter_dimension=1, tiled=True).astype(F32)


def reduce_one(slots, order):
    table = {}
    for which, index, rel in rel_slots(order):
        block = rel["w"] * 8 + rel["u"] * 4 + rel["y"] * 2 + rel["c"]
        table[block, rel["x"]] = slots[which][index]
    whole = jnp.concatenate(
        [jnp.concatenate([table[b, 0], table[b, 1]], axis=1) for b in range(16)], axis=0
    )
    whole = lax.psum_scatter(whole, ("w", "u", "y", "c"), scatter_dimension=0, tiled=True)
    return lax.psum_scatter(whole, "x", scatter_dimension=1, tiled=True).astype(F32)


def scan_masks(carry):
    c = carry.reshape(-1, 8)
    place = jnp.arange(8)[None, :]

    def behind(values, n):
        return jnp.where(place >= n, jnp.roll(values, n, axis=1), 0.0)

    def ahead(values, n):
        return jnp.where(place < 8 - n, jnp.roll(values, -n, axis=1), 0.0)

    m1 = jnp.where(place >= 1, c, 0.0)
    m2 = m1 * behind(m1, 1)
    m4 = m2 * behind(m2, 2)
    mf = jnp.cumprod(c, axis=1)
    ml = jnp.broadcast_to(mf[:, 7:], c.shape)
    n1 = ahead(c, 1)
    n2 = n1 * ahead(n1, 1)
    n4 = n2 * ahead(n2, 2)
    back = jnp.cumprod(c[:, ::-1], axis=1)[:, ::-1]
    nf = jnp.where(place < 7, jnp.roll(back, -1, axis=1), 1.0)
    c0 = jnp.broadcast_to(c[:, :1], c.shape)
    tables = (jnp.stack(t).reshape(len(t), -1, 1) for t in ((m1, m2, m4, mf, ml), (n1, n2, n4, nf, c0, ml)))
    return [jnp.broadcast_to(t, t.shape[:2] + (LANES,)) for t in tables]


def on_device(
    inputs,
    segments,
    teacher,
    first_norm_gain,
    first_norm_bias,
    time_decay,
    time_first,
    time_mix_key,
    time_mix_value,
    time_mix_recept,
    time_key,
    time_value,
    time_recept,
    time_output,
    second_norm_gain,
    second_norm_bias,
    channel_mix_key,
    channel_mix_recept,
    channel_key,
    channel_recept,
    channel_value,
):
    tokens, width = inputs.shape
    sizes = {a: lax.axis_size(a) for a in EVERY}
    devices = math.prod(sizes.values())
    fast = all(size == 2 for size in sizes.values())
    side = lax.axis_index("x")
    if fast:
        co = jnp.stack([lax.axis_index(a) for a in EVERY]).astype(jnp.int32)
    else:
        co = jnp.zeros((5,), jnp.int32)

    ids = lax.dynamic_slice_in_dim(segments, side * tokens, tokens)
    previous = jnp.concatenate([jnp.zeros((1,), jnp.int32), ids[:-1]])
    started = jnp.arange(tokens, dtype=jnp.int32) > 0
    carry = ((ids == previous) & (ids > 0) & started).astype(F32)
    valid = (ids > 0).astype(F32)
    lead = jnp.concatenate([carry[1:], jnp.zeros((1,), F32)])
    masks_down, masks_up = scan_masks(carry)
    carry, valid_rows, lead = (
        jnp.broadcast_to(v[:, None], (tokens, LANES)) for v in (carry, valid, lead)
    )

    flat = 0
    for axis in EVERY:
        flat = flat * sizes[axis] + lax.axis_index(axis)
    own_vectors = jnp.stack(
        [
            first_norm_gain,
            first_norm_bias,
            time_decay,
            time_first,
            time_mix_key,
            time_mix_value,
            time_mix_recept,
            second_norm_gain,
            second_norm_bias,
            channel_mix_key,
            channel_mix_recept,
        ]
    )
    piece = own_vectors.shape[1]
    counts = jnp.where(jnp.arange(piece) == 0, jnp.sum(valid), 0.0)[None, :]
    own_vectors = jnp.concatenate([own_vectors, counts, jnp.zeros((4, piece), F32)])
    output_t, value_t = time_output.T, channel_value.T

    if sizes["x"] == 2:
        mine = lax.dynamic_slice_in_dim(teacher, side * tokens, tokens)
        theirs = lax.dynamic_slice_in_dim(teacher, (1 - side) * tokens, tokens)
    else:
        mine, theirs = jnp.split(teacher, 2, axis=1)

    key_order, val_order, rec_order = three_orders = ("wxuy", "wuyx", "wyxu")
    half = width // 2
    if fast:
        wide = channel_key.shape[1]
        split = wide // 2
        chains = keys_a, keys_b, late_b = [
            Gather(channel_key[:, :split], "wuyx"),
            Gather(channel_key[:, split:], "wxuy"),
            Gather(value_t[:, split:], "wyxu"),
        ]
        first = jnp.concatenate([time_key, time_value, time_recept, output_t], axis=1)
        late = jnp.concatenate([value_t[:, :split], channel_recept], axis=1)
        first = lax.all_gather(first, EVERY)
        theirs = swap(theirs, "x")
        step_all(*chains)
        (vectors,) = gather_vectors(own_vectors, 0, 4)
        late, vectors, masks_down, masks_up, mine, theirs, carry, valid_rows, lead = seal_all(
            chains, late, vectors, masks_down, masks_up, mine, theirs, carry, valid_rows, lead
        )
        step_all(*chains)
        (vectors,) = gather_vectors(vectors, 4, 5)
        (vectors,) = seal_all(chains, vectors)
        step_all(*chains)
        mixed = first_mix(inputs, carry, vectors)
        (mixed,) = seal_all(chains, mixed)
        step_all(*chains)
        first, late, mixed = seal(first, late, mixed)
        late = lax.all_gather(late, EVERY).reshape(16, 2, SLOT, -1)
        first = first.reshape(16, 2, SLOT, -1)
        key_w, value_w, recept_w, output_w = (all_of(first, n * half, half) for n in range(4))
    else:
        early = gather_plain(channel_key)
        wide = early.shape[-1]
        split = wide // 2
        key_w, value_w, recept_w, output_w, crecept_w = (
            all_of(gather_plain(w))
            for w in (time_key, time_value, time_recept, output_t, channel_recept)
        )
        ckey_w = all_of(early)
        late = gather_plain(value_t)
        cvalue_w = [all_of(late, skip, split) for skip in (0, split)]
        vectors = lax.all_gather(own_vectors, EVERY, axis=1, tiled=True)
        mixed = first_mix(inputs, carry, vectors)

    *saved, gated = time_forward(co, mixed, (key_w, value_w, recept_w), vectors, masks_down)
    if fast:
        (gated,) = seal_all((keys_a, keys_b), gated)
        step_all(keys_a, keys_b)
    if sizes["x"] == 2 and not fast:
        theirs = swap(theirs, "x")
    middle, mixed_k2, mixed_r2 = time_output_step(co, gated, inputs, carry, vectors, output_w)
    if fast:
        middle, mixed_k2, mixed_r2 = seal_all(chains, middle, mixed_k2, mixed_r2)
        ckey_w = weight_of(keys_a.part(), keys_b.part(split))
        late_b.step()
    hidden, active = hidden_step(co, mixed_k2, ckey_w)
    if fast:
        hidden, late = seal_all((late_b,), hidden, late)
        cvalue_w = [all_of(late, 0, split), weight_of(late_b.part())]
        crecept_w = all_of(late, split, half)
    count = jnp.sum(vectors[11])
    scale = (float(tokens * devices) / count).reshape(1)
    kept, arrived, dres, dkv, drec2, loss_rows = result_step(
        co.at[4].set(side),
        scale,
        hidden,
        mixed_r2,
        middle,
        (mine, theirs),
        valid_rows,
        both_parts(cvalue_w, split),
        crecept_w,
    )

    if sizes["x"] == 2:
        arrived = swap(arrived, "x")

    def outputs_of(kept, arrived):
        return lax.dynamic_update_slice_in_dim(kept, arrived, (1 - side) * tokens, 0)

    back = functools.partial(channel_back, co)
    order_b, order_c = "wuyx", "wuyx"
    edge = jnp.zeros((8, width), F32)

    def input_back_part(dmix, part, after, found):
        return input_back(
            co, dmix, inputs, dmid, lead, vectors, (key_w, value_w, recept_w), part, after, found
        )

    if fast:
        dkey_1, *found = back(dkv, mixed_k2, hidden, active, (), cvalue_w[1], split, 1, order_b)
        group_b = Merged(found, order_b)
        (dkv,) = seal_all((group_b,), dkv)
        group_b.step()
        dkey_0, blocks = back(
            dkv, mixed_k2, hidden, active, (mixed_r2, drec2), cvalue_w[0], split, 0, order_b
        )
        dkey_0, arrived, blocks = seal_all((group_b,), dkey_0, arrived, blocks)
        blocks = scatter_rows(blocks)
        group_b.step()
        outputs = outputs_of(kept, arrived)
        dmid, dtime, sums2 = middle_back(
            co, (dkey_0, dkey_1), drec2, middle, dres, lead, vectors, ckey_w, crecept_w
        )
        found = weight_grads(co, ((dtime, gated, order_c),), merged=True)
        group_c = Merged(found, order_c)
        dtime, outputs = seal_all((group_b, group_c), dtime, outputs)
        step_all(group_b, group_c)
        *dmix, sums_t = time_back(co, dtime, saved, vectors, masks_up, output_w)
        (dmix, dmid) = seal_all((group_c,), dmix, dmid)
        group_c.step()
        found = weight_grads(co, [(m, d, order) for m, d, order in zip(mixed, dmix, three_orders)])
        group_t = Reduce(found, three_orders)
        (dmix,) = seal_all((group_b, group_c, group_t), dmix)
        step_all(group_b, group_c, group_t)
        found, sums_l, edge = input_back_part(dmix, 0, edge, dres)
        (dmix, edge, found) = seal_all((group_b, group_c, group_t), dmix, edge, found)
        step_all(group_b, group_c, group_t)
        input_grad, sums_u, _ = input_back_part(dmix, 1, edge, found)
    else:
        dkey_1, *found = back(dkv, mixed_k2, hidden, active, (), cvalue_w[1], split, 1, order_b)
        dkey_0, blocks = back(
            dkv, mixed_k2, hidden, active, (mixed_r2, drec2), cvalue_w[0], split, 0, order_b
        )
        value_1, ckey_1 = reduce_merged(found, order_b)
        value_0, ckey_0 = (
            reduce_blocks(blocks[..., n * split : (n + 1) * split]) for n in (0, 1)
        )
        crecept_g = reduce_blocks(blocks[..., 2 * split :])
        halves = 2 // sizes["x"]
        cvalue_g, ckey_g = (
            jnp.concatenate(
                [v.reshape(-1, halves, split) for v in pair], axis=2
            ).reshape(pair[0].shape[0], -1)
            for pair in ((value_0, value_1), (ckey_0, ckey_1))
        )
        dmid, dtime, sums2 = middle_back(
            co, (dkey_0, dkey_1), drec2, middle, dres, lead, vectors, ckey_w, crecept_w
        )
        found = weight_grads(co, ((dtime, gated, order_c),), merged=True)
        (output_g,) = reduce_merged(found, order_c)
        *dmix, sums_t = time_back(co, dtime, saved, vectors, masks_up, output_w)
        found = weight_grads(co, [(m, d, order) for m, d, order in zip(mixed, dmix, three_orders)])
        key_g, val_g, rec_g = reduce_plain(found, three_orders)
        found, sums_l, edge = input_back_part(dmix, 0, edge, dres)
        input_grad, sums_u, _ = input_back_part(dmix, 1, edge, found)

    rows = jnp.concatenate([sums_l[:2] + sums_u[:2], sums_t, sums_l[2:] + sums_u[2:], sums2, loss_rows[None]])
    totals = jnp.sum(rows, axis=1)
    if fast:
        (totals,) = seal_all((group_b, group_c, group_t), totals)
        for axes in ("wc", "xy", "u"):
            step_all(*[group for group in (group_c, group_t) if group.done < 5])
            for axis in axes:
                totals = totals + swap(totals, axis)
            totals, blocks = seal_all((group_c, group_t), totals, blocks)
            if axes == "wc":
                blocks = pair_sum(blocks)
        cvalue_g, ckey_g = (
            jnp.concatenate([blocks[:, n * split : (n + 1) * split], found], axis=1)
            for n, found in enumerate(group_b.finish())
        )
        (output_g,) = group_c.finish()
        crecept_g = blocks[:, 2 * split :]
        key_g, val_g, rec_g = group_t.finish()
    else:
        totals = lax.psum(totals, EVERY)
    loss = jnp.sum(totals[11]) / (2.0 * count * width)
    vector_g = lax.dynamic_slice_in_dim(totals, flat * piece, piece, axis=1)
    if not fast:
        outputs = (
            outputs_of(kept, arrived)
            if sizes["x"] == 2
            else jnp.concatenate([kept[:tokens], arrived], axis=1)
        )
    return (
        outputs,
        loss,
        input_grad,
        *[vector_g[n] for n in range(7)],
        key_g,
        val_g,
        rec_g,
        output_g.T,
        *[vector_g[n] for n in range(7, 11)],
        ckey_g,
        crecept_g,
        cvalue_g.T,
    )


def solution(mesh):
    fsdp, tp = mesh.shape["fsdp"], mesh.shape["tp"]
    two = 2 if fsdp % 8 == 0 else 1
    split = Mesh(mesh.devices.reshape(fsdp // two**3, two, two, two, tp), EVERY)
    rows = ("w", "u", "y", "c")
    vector = P(EVERY)
    matrix = P(rows, "x")
    turned = P("x", rows)
    tall = P(EVERY, None)
    return jax.shard_map(
        on_device,
        mesh=split,
        in_specs=(
            (tall, P(rows), matrix)
            + (vector,) * 7
            + (matrix, matrix, matrix, turned)
            + (vector,) * 4
            + (matrix, matrix, turned)
        ),
        out_specs=(
            (matrix, P(), tall)
            + (vector,) * 7
            + (matrix, matrix, matrix, turned)
            + (vector,) * 4
            + (matrix, matrix, turned)
        ),
        check_vma=False,
    )
```

```python
import functools
import itertools
import math

import jax
import jax.numpy as jnp
from jax import lax
from jax.experimental import pallas as pl
from jax.experimental.pallas import tpu as pltpu
from jax.sharding import Mesh
from jax.sharding import PartitionSpec as P

BF = jnp.bfloat16
F32 = jnp.float32
EPSILON = 1e-05
SLOT = 64
CHUNK = 16
VMEM_LIMIT = 58 << 20
EVERY = ("w", "u", "y", "c", "x")
SWAP = [(0, 1), (1, 0)]

NN = (((1,), (0,)), ((), ()))
NT = (((1,), (1,)), ((), ()))
TN = (((0,), (0,)), ((), ()))


def dot(left, right, dims):
    return lax.dot_general(left, right, dims, preferred_element_type=F32)


def rel_slots(order):
    for other_core in (0, 1):
        for last in (0, 1):
            for index in itertools.product((0, 1), repeat=3):
                rel = dict(zip(order[2::-1], index))
                rel[order[3]] = last
                rel["c"] = other_core
                yield other_core * 2 + last, index, rel


def slot_place(co, rel):
    at = {axis: co[n] ^ rel[axis] for n, axis in enumerate(EVERY)}
    return at["w"] * 8 + at["u"] * 4 + at["y"] * 2 + at["c"], at["x"]


def rows_of(whole, half, columns=slice(None)):
    found = whole[half, :, :, columns]
    return found.reshape(found.shape[0] * found.shape[1], found.shape[2])


def start_weight(co, refs, whole, sems, layout, halves=(0, 1)):
    refs = list(refs)
    for n, (kind, order, first, columns) in enumerate(layout):
        target = pl.ds(first, columns)
        if kind == "rel":
            order, skip, base = order
            if base is None:
                arrays, refs = refs[:4], refs[4:]
            else:
                arrays, refs = [*refs[:2], refs[2].at[base], refs[2].at[base + 1]], refs[3:]
            for which, index, rel in sorted(rel_slots(order), key=lambda slot: slot[2]["x"]):
                if rel["x"] in halves:
                    block, half = slot_place(co, rel)
                    pltpu.make_async_copy(
                        arrays[which].at[index + (slice(None), pl.ds(skip, columns))],
                        whole.at[half, block, :, target],
                        sems.at[2 * n + rel["x"]],
                    ).start()
        else:
            array, refs = refs[0], refs[1:]
            for rel_x in halves:
                half = co[4] ^ rel_x
                pltpu.make_async_copy(
                    array.at[:, half, :, pl.ds(order, columns)],
                    whole.at[half, :, :, target],
                    sems.at[2 * n + rel_x],
                ).start()


def wait_weight(co, whole, sems, layout, rel_x):
    for n, (_, _, first, columns) in enumerate(layout):
        held = whole.at[co[4] ^ rel_x, :, :, pl.ds(first, columns)]
        pltpu.make_async_copy(held, held, sems.at[2 * n + rel_x]).wait()


def take_refs(refs, layout):
    count = 0
    for kind, order, _, _ in layout:
        count += 1 if kind == "abs" else 4 if order[2] is None else 3
    return refs[:count], refs[count:]


def arrays_of(*weights):
    return [array for _, arrays in weights for array in arrays]


def both_parts(weights, split):
    (first, arrays_a), (second, arrays_b) = weights
    second = tuple((kind, order, at + split, columns) for kind, order, at, columns in second)
    return tuple(first) + second, list(arrays_a) + list(arrays_b)


def weight_width(weight):
    return sum(part[3] for part in weight[0])


def weight_scratch(*weights):
    return [pltpu.VMEM((2, 16, SLOT, weight_width(w)), BF) for w in weights] + [
        pltpu.SemaphoreType.DMA((2 * len(w[0]),)) for w in weights
    ]


ROWS = 32
LANES = 128


def strips(width):
    return [slice(n, n + LANES) for n in range(0, width, LANES)]


def row_parts(ref, row=0):
    return tuple(ref[row : row + 1, strip] for strip in strips(ref.shape[1]))


def chunk_rows(n):
    return pl.ds(pl.multiple_of(n * ROWS, ROWS), ROWS)


def spread_mean(total, width):
    return jnp.broadcast_to(jnp.sum(total, axis=1, keepdims=True) * (1.0 / width), total.shape)


def norm_stats(load, width):
    total = sum(load(strip) for strip in strips(width))
    mean = spread_mean(total, width)
    square = 0.0
    for strip in strips(width):
        centre = load(strip) - mean
        square = square + centre * centre
    return mean, lax.rsqrt(spread_mean(square, width) + EPSILON)


def first_row(shape):
    return lax.broadcasted_iota(jnp.int32, shape, 0) == 0


def last_row(shape):
    return lax.broadcasted_iota(jnp.int32, shape, 0) == shape[0] - 1


def move_down(values, before):
    return jnp.where(first_row(values.shape), before, pltpu.roll(values, 1, 0))


def move_up(values, after):
    return jnp.where(last_row(values.shape), after, pltpu.roll(values, values.shape[0] - 1, 0))


def fold_rows(values):
    return sum(values[n : n + 8] for n in range(0, values.shape[0], 8))


def params(semantics=1):
    return pltpu.CompilerParams(vmem_limit_bytes=VMEM_LIMIT)


def anywhere():
    return pl.BlockSpec(memory_space=pl.ANY)


COST = 0.01


def cost(units, traffic):
    return pl.CostEstimate(
        flops=int(units * 2 * 1024**3 * COST), bytes_accessed=int(traffic * COST), transcendentals=0
    )


def first_mix_kernel(x_ref, carry_ref, vec_ref, mk_ref, mv_ref, mr_ref, last):
    width = x_ref.shape[1]

    def step(n, before):
        rows = chunk_rows(n)
        mean, scaled = norm_stats(lambda strip: x_ref[rows, strip].astype(F32), width)
        carry = carry_ref[rows, :]
        lasts = []
        for strip in strips(width):
            unit = (x_ref[rows, strip].astype(F32) - mean) * scaled
            normed = unit * vec_ref[0:1, strip] + vec_ref[1:2, strip]
            behind = move_down(normed, before[len(lasts)]) * carry
            for m, out in ((4, mk_ref), (5, mv_ref), (6, mr_ref)):
                mix = vec_ref[m : m + 1, strip]
                out[rows, strip] = (normed * mix + behind * (1.0 - mix)).astype(BF)
            lasts.append(normed[ROWS - 1 :, :])
        return tuple(lasts)

    @pl.when(pl.program_id(0) == 0)
    def _():
        last[...] = jnp.zeros_like(last)

    lasts = lax.fori_loop(0, x_ref.shape[0] // ROWS, step, row_parts(last), unroll=4)
    for strip, value in zip(strips(width), lasts):
        last[0:1, strip] = value


def first_mix(x, carry, vectors):
    tokens, width = x.shape
    rows = tokens // 4
    tall = pl.BlockSpec((rows, width), lambda i: (i, 0))
    return pl.pallas_call(
        first_mix_kernel,
        grid=(4,),
        in_specs=[
            tall,
            pl.BlockSpec((rows, LANES), lambda i: (i, 0)),
            pl.BlockSpec(vectors.shape, lambda i: (0, 0)),
        ],
        out_specs=[tall] * 3,
        out_shape=[jax.ShapeDtypeStruct(x.shape, BF)] * 3,
        scratch_shapes=[pltpu.VMEM((8, width), F32)],
        compiler_params=params(),
        cost_estimate=cost(0, 8 << 20),
    )(x, carry, vectors)


FORWARD_TILE = 512
TILE = 256


def scan_rates(decay):
    speed = jnp.exp(decay)
    return [jnp.exp(-float(n) * speed) for n in (1, 2, 4, 8)]


def repeated(values, size):
    return jnp.concatenate([values] * (size // LANES), axis=1)


def time_forward_kernel(
    co, mk, mv, mr, vec, masks, *refs, layouts,
):
    key_w, refs = take_refs(refs, layouts[0])
    val_w, refs = take_refs(refs, layouts[1])
    rec_w, refs = take_refs(refs, layouts[2])
    key_ref, val_ref, rec_ref, pa_ref, pb_ref, gated_ref, *scratch = refs
    wholes, sems = scratch[:3], scratch[3:]
    j = pl.program_id(0)
    per_half = wholes[0].shape[3] // FORWARD_TILE

    @pl.when(j == 0)
    def _():
        for arrays, whole, sem, layout in zip((key_w, val_w, rec_w), wholes, sems, layouts):
            start_weight(co, arrays, whole, sem, layout)

    for which in (0, 1):

        @pl.when(j == which * per_half)
        def _(which=which):
            for whole, sem, layout in zip(wholes, sems, layouts):
                wait_weight(co, whole, sem, layout, which)

    half = co[4] ^ lax.div(j, per_half)
    columns = pl.ds(pl.multiple_of(lax.rem(j, per_half) * FORWARD_TILE, FORWARD_TILE), FORWARD_TILE)
    for mixed, whole, out in zip((mk, mv, mr), wholes, (key_ref, val_ref, rec_ref)):
        out[...] = dot(mixed[...], rows_of(whole, half, columns), NN)

    spread = (8, FORWARD_TILE)
    decay = jnp.broadcast_to(vec[2:3, :], spread)
    first = jnp.broadcast_to(vec[3:4, :], spread)
    r1, r2, r4, r8 = scan_rates(decay)
    powers = jnp.exp(-lax.broadcasted_iota(jnp.int32, spread, 0).astype(F32) * jnp.exp(decay))

    def group(start, state):
        rows = pl.ds(start, 8)
        key, val, pre = key_ref[rows, :], val_ref[rows, :], rec_ref[rows, :]
        m1, m2, m4, mf, ml = (repeated(masks[n, rows, :], FORWARD_TILE) for n in range(5))
        rec = 1.0 / (1.0 + jnp.exp(-pre))
        power = jnp.exp(key)
        bonus = jnp.exp(first + key)
        c1, c2, c4, cf, cl = m1 * r1, m2 * r2, m4 * r4, mf * powers, ml * r8
        priors, ends = [], []
        for local, entering in ((power * val, state[0]), (power, state[1])):
            local = local + c1 * pltpu.roll(local, 1, 0)
            local = local + c2 * pltpu.roll(local, 2, 0)
            local = local + c4 * pltpu.roll(local, 4, 0)
            priors.append(m1 * pltpu.roll(local, 1, 0) + cf * entering)
            ends.append(jnp.broadcast_to(local[7:8, :], spread) + cl * entering)
        wkv = (priors[0] + bonus * val) / (priors[1] + bonus)
        rec_ref[rows, :] = rec
        pa_ref[rows, :] = priors[0]
        pb_ref[rows, :] = priors[1]
        return rec * wkv, tuple(ends)

    def step(i, state):
        start = pl.multiple_of(i * CHUNK, CHUNK)
        upper, state = group(start, state)
        lower, state = group(pl.multiple_of(start + 8, 8), state)
        gated_ref[pl.ds(start, CHUNK), :] = jnp.concatenate([upper, lower], axis=0).astype(BF)
        return state

    zero = jnp.zeros(spread, F32)
    lax.fori_loop(0, key_ref.shape[0] // CHUNK, step, (zero, zero), unroll=4)


def time_forward(co, mixed, weights, vectors, masks):
    tokens, width = mixed[0].shape
    half = width // 2
    per_half = half // FORWARD_TILE

    def tile(j, co):
        return 0, (co[4] ^ lax.div(j, per_half)) * per_half + lax.rem(j, per_half)

    fixed = pl.BlockSpec((tokens, width), lambda j, co: (0, 0))
    block = pl.BlockSpec((tokens, FORWARD_TILE), tile)
    return pl.pallas_call(
        functools.partial(time_forward_kernel, layouts=[w[0] for w in weights]),
        grid_spec=pltpu.PrefetchScalarGridSpec(
            num_scalar_prefetch=1,
            grid=(width // FORWARD_TILE,),
            in_specs=[fixed] * 3
            + [
                pl.BlockSpec((vectors.shape[0], FORWARD_TILE), tile),
                pl.BlockSpec(masks.shape, lambda j, co: (0, 0, 0)),
            ]
            + [anywhere()] * len(arrays_of(*weights)),
            out_specs=[block] * 6,
            scratch_shapes=weight_scratch(*weights),
        ),
        out_shape=[jax.ShapeDtypeStruct((tokens, width), F32)] * 5
        + [jax.ShapeDtypeStruct((tokens, width), BF)],
        compiler_params=params(),
        cost_estimate=cost(8, 34 << 20),
    )(co, *mixed, vectors, masks, *arrays_of(*weights))


def time_output_kernel(
    co, gated, x_ref, carry_ref, vec_ref, *refs, layout
):
    arrays, refs = take_refs(refs, layout)
    middle_ref, mk_ref, mr_ref, last, ow, sems = refs
    i = pl.program_id(0)

    @pl.when(i == 0)
    def _():
        start_weight(co, arrays, ow, sems, layout)
        last[...] = jnp.zeros_like(last)
        for half in (0, 1):
            wait_weight(co, ow, sems, layout, half)

    half = ow.shape[3]
    middle_ref[...] = dot(gated[:, :half], rows_of(ow, 0), NT) + dot(
        gated[:, half:], rows_of(ow, 1), NT
    )
    width = x_ref.shape[1]

    def step(n, before):
        rows = chunk_rows(n)
        for strip in strips(width):
            middle_ref[rows, strip] += x_ref[rows, strip].astype(F32)
        mean, scaled = norm_stats(lambda strip: middle_ref[rows, strip], width)
        carry = carry_ref[rows, :]
        lasts = []
        for strip in strips(width):
            unit = (middle_ref[rows, strip] - mean) * scaled
            normed = unit * vec_ref[7:8, strip] + vec_ref[8:9, strip]
            behind = move_down(normed, before[len(lasts)]) * carry
            for m, out in ((9, mk_ref), (10, mr_ref)):
                mix = vec_ref[m : m + 1, strip]
                out[rows, strip] = (normed * mix + behind * (1.0 - mix)).astype(BF)
            lasts.append(normed[ROWS - 1 :, :])
        return tuple(lasts)

    lasts = lax.fori_loop(0, x_ref.shape[0] // ROWS, step, row_parts(last), unroll=4)
    for strip, value in zip(strips(width), lasts):
        last[0:1, strip] = value


def time_output_step(co, gated, x, carry, vectors, weight):
    tokens, width = x.shape
    rows = tokens // 4
    tall = pl.BlockSpec((rows, width), lambda i, co: (i, 0))
    return pl.pallas_call(
        functools.partial(time_output_kernel, layout=weight[0]),
        grid_spec=pltpu.PrefetchScalarGridSpec(
            num_scalar_prefetch=1,
            grid=(4,),
            in_specs=[
                tall,
                tall,
                pl.BlockSpec((rows, LANES), lambda i, co: (i, 0)),
                pl.BlockSpec(vectors.shape, lambda i, co: (0, 0)),
            ]
            + [anywhere()] * len(weight[1]),
            out_specs=[tall] * 3,
            scratch_shapes=[pltpu.VMEM((8, width), F32)] + weight_scratch(weight),
        ),
        out_shape=[jax.ShapeDtypeStruct((tokens, width), t) for t in (F32, BF, BF)],
        compiler_params=params(),
        cost_estimate=cost(3, 14 << 20),
    )(co, gated, x, carry, vectors, *weight[1])


WIDE = 512


def hidden_kernel(co, mk, *refs, layout):
    arrays, (hidden_ref, active_ref, whole, sems) = take_refs(refs, layout)
    j = pl.program_id(0)
    per_half = whole.shape[3] // WIDE

    @pl.when(j == 0)
    def _():
        start_weight(co, arrays, whole, sems, layout)

    for which in (0, 1):

        @pl.when(j == which * per_half)
        def _(which=which):
            wait_weight(co, whole, sems, layout, which)

    half = co[4] ^ lax.div(j, per_half)
    columns = pl.ds(pl.multiple_of(lax.rem(j, per_half) * WIDE, WIDE), WIDE)
    active = jnp.maximum(dot(mk[...], rows_of(whole, half, columns), NN), 0.0)
    active_ref[...] = active.astype(BF)
    hidden_ref[...] = (active * active).astype(BF)


def column_tile(per_half):
    return lambda j, co: (0, (co[4] ^ lax.div(j, per_half)) * per_half + lax.rem(j, per_half))


def hidden_step(co, mixed, weight):
    tokens, width = mixed.shape
    half = weight_width(weight)
    block = pl.BlockSpec((tokens, WIDE), column_tile(half // WIDE))
    return pl.pallas_call(
        functools.partial(hidden_kernel, layout=weight[0]),
        grid_spec=pltpu.PrefetchScalarGridSpec(
            num_scalar_prefetch=1,
            grid=(2 * half // WIDE,),
            in_specs=[pl.BlockSpec((tokens, width), lambda j, co: (0, 0))]
            + [anywhere()] * len(weight[1]),
            out_specs=[block] * 2,
            scratch_shapes=weight_scratch(weight),
        ),
        out_shape=[jax.ShapeDtypeStruct((tokens, 2 * half), BF)] * 2,
        compiler_params=params(),
        cost_estimate=cost(4.5, 26 << 20),
    )(co, mixed, *weight[1])


def result_kernel(
    co, scale, hidden, mr, middle_ref, mine_ref, theirs_ref, valid_ref, *refs, layouts,
):
    value_w, refs = take_refs(refs, layouts[0])
    recept_w, refs = take_refs(refs, layouts[1])
    *outs, dres_ref, dkv_ref, drec_ref, loss_ref, kv_ref, pre_ref, ww, rw, sems, sems_r = refs
    i = pl.program_id(0)

    @pl.when(i == 0)
    def _():
        start_weight(co, recept_w, rw, sems_r, layouts[1])
        start_weight(co, value_w, ww, sems, layouts[0])
        loss_ref[...] = jnp.zeros_like(loss_ref)
        for half in (0, 1):
            wait_weight(co, rw, sems_r, layouts[1], half)
            wait_weight(co, ww, sems, layouts[0], half)

    wide, narrow = ww.shape[3], rw.shape[3]
    pre_ref[:, :narrow] = dot(mr[...], rows_of(rw, 0), NN)
    pre_ref[:, narrow:] = dot(mr[...], rows_of(rw, 1), NN)
    kv_ref[...] = dot(hidden[:, :wide], rows_of(ww, 0), NT) + dot(
        hidden[:, wide:], rows_of(ww, 1), NT
    )
    factor = scale[0]

    def step(n, _):
        rows = chunk_rows(n)
        valid = valid_ref[rows, :]
        width = kv_ref.shape[1]
        for part, at in itertools.product((0, 1), range(0, width // 2, LANES)):
            first = pl.multiple_of((co[4] ^ part) * (width // 2) + at, LANES)
            strip = pl.ds(first, LANES)
            kv = kv_ref[rows, strip]
            rec = 1.0 / (1.0 + jnp.exp(-pre_ref[rows, strip]))
            result = middle_ref[rows, strip] + rec * kv
            outs[part][rows, at : at + LANES] = result.astype(BF)
            teacher = (mine_ref, theirs_ref)[part][rows, at : at + LANES].astype(F32)
            error = (result - teacher) * valid
            grad = error * factor
            dres_ref[rows, strip] = grad
            dkv = grad * rec
            dkv_ref[rows, strip] = dkv.astype(BF)
            drec_ref[rows, strip] = (dkv * kv * (1.0 - rec)).astype(BF)
            loss_ref[:, strip] += fold_rows(error * error)
        return 0

    lax.fori_loop(0, kv_ref.shape[0] // ROWS, step, 0, unroll=2)


def result_step(co, scale, hidden, mixed, middle, teachers, valid, weight, recept):
    tokens, width = mixed.shape
    rows = tokens // 4
    wide = weight_width(weight)
    tall = pl.BlockSpec((rows, width), lambda i, co, s: (i, 0))
    thin = pl.BlockSpec((rows, width // 2), lambda i, co, s: (i, 0))
    return pl.pallas_call(
        functools.partial(result_kernel, layouts=[weight[0], recept[0]]),
        grid_spec=pltpu.PrefetchScalarGridSpec(
            num_scalar_prefetch=2,
            grid=(4,),
            in_specs=[
                pl.BlockSpec((rows, 2 * wide), lambda i, co, s: (i, 0)),
                tall,
                tall,
                thin,
                thin,
                pl.BlockSpec((rows, LANES), lambda i, co, s: (i, 0)),
            ]
            + [anywhere()] * len(arrays_of(weight, recept)),
            out_specs=[pl.BlockSpec((rows, width // 2), lambda i, co, s: (co[4] * 4 + i, 0)), thin]
            + [tall] * 3
            + [pl.BlockSpec((8, width), lambda i, co, s: (0, 0))],
            scratch_shapes=[pltpu.VMEM((rows, width), F32)] * 2 + weight_scratch(weight, recept),
        ),
        out_shape=[jax.ShapeDtypeStruct((n * tokens, width // 2), BF) for n in (2, 1)]
        + [jax.ShapeDtypeStruct((tokens, width), t) for t in (F32, BF, BF)]
        + [jax.ShapeDtypeStruct((8, width), F32)],
        compiler_params=params(),
        cost_estimate=cost(7, 38 << 20),
    )(co, scale, hidden, mixed, middle, *teachers, valid, *arrays_of(weight, recept))


def start_grads(co, whole, targets, n, sem, order, which, merged):
    for array, index, rel in rel_slots(order):
        if rel["x"] == which:
            block, half = slot_place(co, rel)
            pltpu.make_async_copy(
                whole.at[half, block],
                targets[array].at[index + (n,) if merged else (n,) + index],
                sem,
            ).start()


def wait_bytes(held, sem):
    pltpu.make_async_copy(held, held, sem).wait()


def weight_grads_kernel(co, *refs, orders, merged):
    count = len(orders)
    models, chans, refs = refs[:count], refs[count : 2 * count], refs[2 * count :]
    targets, (held, given, whole, sems_in, sems_out) = refs[:4], refs[4:]
    half = whole.shape[4]
    loads = []
    for n in range(count):
        for m, (source, place) in enumerate(((models[n], held), (chans[n], given))):
            loads.append(pltpu.make_async_copy(source, place.at[n], sems_in.at[2 * n + m]))
            loads[-1].start()
    for n, order in enumerate(orders):
        for load in loads[2 * n : 2 * n + 2]:
            load.wait()

        def step(turn, _, n=n, order=order):
            at = co[4] ^ turn
            columns = pl.ds(pl.multiple_of(at * half, half), half)
            found = dot(held[n], given[n, :, columns], TN).astype(BF)
            whole[n, at] = found.reshape(16, SLOT, half)
            for which in (0, 1):

                @pl.when(turn == which)
                def _(which=which):
                    start_grads(co, whole.at[n], targets, n, sems_out.at[n], order, which, merged)

            return 0

        lax.fori_loop(0, 2, step, 0)
    for n in range(count):
        wait_bytes(whole.at[n], sems_out.at[n])


def weight_grads(co, pairs, merged=False):
    models, chans, orders = zip(*pairs)
    tokens, width = models[0].shape
    half = width // 2
    count = len(pairs)
    dims = (2, 2, 2, count) if merged else (count, 2, 2, 2)
    return pl.pallas_call(
        functools.partial(weight_grads_kernel, orders=orders, merged=merged),
        grid_spec=pltpu.PrefetchScalarGridSpec(
            num_scalar_prefetch=1,
            grid=(1,),
            in_specs=[anywhere()] * (2 * count),
            out_specs=[anywhere()] * 4,
            scratch_shapes=[
                pltpu.VMEM((count, tokens, width), BF),
                pltpu.VMEM((count, tokens, width), BF),
                pltpu.VMEM((count, 2, 16, SLOT, half), BF),
                pltpu.SemaphoreType.DMA((2 * count,)),
                pltpu.SemaphoreType.DMA((count,)),
            ],
        ),
        out_shape=[jax.ShapeDtypeStruct(dims + (SLOT, half), BF)] * 4,
        compiler_params=params(),
        cost_estimate=cost(count * 1.2, count * (6 << 20)),
    )(co, *models, *chans)


def channel_back_kernel(co, dkv, mixed, hidden, active, *refs, layout, part, order):
    recept, refs = refs[: 2 * (1 - part)], refs[2 * (1 - part) :]
    arrays, refs = take_refs(refs, layout)
    dkey, *targets, grads, narrow, sems, whole, sems_in = refs
    j = pl.program_id(0)
    per_half = grads.shape[4] // WIDE
    columns = pl.ds(pl.multiple_of(lax.rem(j, per_half) * WIDE, WIDE), WIDE)
    turn = lax.div(j, per_half)
    half = co[4] ^ turn

    @pl.when(j == 0)
    def _():
        start_weight(co, arrays, whole, sems_in, layout)

    def keep(n, values):
        grads[n, half, :, :, columns] = values.astype(BF).reshape(16, SLOT, WIDE)

    keep(0, dot(dkv[...], hidden[...], TN))

    for which in (0, 1):

        @pl.when(j == which * per_half)
        def _(which=which):
            wait_weight(co, whole, sems_in, layout, which)

    back = dot(dkv[...], rows_of(whole, half, columns), NN)
    back = (2.0 * active[...].astype(F32) * back).astype(BF)
    dkey[...] = back
    keep(1, dot(mixed[...], back, TN))

    wide = grads.shape[4]

    def narrow_copy(turn):
        return pltpu.make_async_copy(
            narrow.at[turn],
            targets[0].at[:, co[4] ^ turn, :, pl.ds(2 * wide, narrow.shape[3])],
            sems.at[2 + turn],
        )

    if part == 0:
        for n in (0, 1):
            pltpu.make_async_copy(
                grads.at[n, half, :, :, columns],
                targets[0].at[:, half, :, pl.ds(pl.multiple_of(n * wide + columns.start, WIDE), WIDE)],
                sems.at[n],
            ).start()

        @pl.when(lax.rem(j, per_half) == 0)
        def _():
            size = narrow.shape[3]
            found = dot(recept[0][...], recept[1][:, pl.ds(pl.multiple_of(half * size, size), size)], TN)
            narrow[turn] = found.astype(BF).reshape(16, SLOT, size)
            narrow_copy(turn).start()

    for which in range(2 * part):

        @pl.when(turn == which)
        def _(which=which):
            for array, index, rel in rel_slots(order):
                if rel["x"] == which:
                    block, at = slot_place(co, rel)
                    for n in (0, 1):
                        pltpu.make_async_copy(
                            grads.at[n, at, block, :, columns],
                            targets[array].at[index + (n, slice(None), columns)],
                            sems.at[n],
                        ).start()

    @pl.when(j == pl.num_programs(0) - 1)
    def _():
        for n in (0, 1):
            wait_bytes(grads.at[n], sems.at[n])
            if part == 0:
                narrow_copy(n).wait()


def channel_back(co, dkv, mixed, hidden, active, recept, weight, half, part, order):
    tokens, width = dkv.shape
    per_half = half // WIDE
    skip, stride = part * per_half, hidden.shape[1] // 2 // WIDE

    def tile(j, co):
        return 0, (co[4] ^ lax.div(j, per_half)) * stride + skip + lax.rem(j, per_half)

    fixed = pl.BlockSpec((tokens, width), lambda j, co: (0, 0))
    block = pl.BlockSpec((tokens, WIDE), tile)
    return pl.pallas_call(
        functools.partial(channel_back_kernel, layout=weight[0], part=part, order=order),
        grid_spec=pltpu.PrefetchScalarGridSpec(
            num_scalar_prefetch=1,
            grid=(2 * per_half,),
            in_specs=[fixed, fixed, block, block]
            + [fixed] * len(recept)
            + [anywhere()] * len(weight[1]),
            out_specs=[pl.BlockSpec((tokens, WIDE), column_tile(per_half))]
            + [anywhere()] * (1 + 3 * part),
            scratch_shapes=[
                pltpu.VMEM((2, 2, 16, SLOT, half), BF),
                pltpu.VMEM((2, 16, SLOT, width // 2), BF),
                pltpu.SemaphoreType.DMA((4,)),
            ]
            + weight_scratch(weight),
        ),
        out_shape=[
            jax.ShapeDtypeStruct((tokens, 2 * half), BF),
            *(
                [jax.ShapeDtypeStruct((2, 2, 2, 2, SLOT, half), BF)] * 4
                if part
                else [jax.ShapeDtypeStruct((16, 2, SLOT, 2 * half + width // 2), BF)]
            ),
        ],
        compiler_params=params(),
        cost_estimate=cost(half / 512 * 3.3, half / 512 * (14 << 20)),
    )(co, dkv, mixed, hidden, active, *recept, *weight[1])


def middle_back_kernel(
    co, dkey_a, dkey_b, drec, middle_ref, dres_ref, lead_ref, vec_ref, *refs, layouts,
):
    key_w, refs = take_refs(refs, layouts[0])
    recept_w, refs = take_refs(refs, layouts[1])
    dmid_ref, dtime_ref, sums_ref, gk_ref, gr_ref, next_ref, ww, rw, sems, sems_r = refs
    i = pl.program_id(0)

    @pl.when(i == 0)
    def _():
        start_weight(co, recept_w, rw, sems_r, layouts[1])
        start_weight(co, key_w, ww, sems, layouts[0])
        sums_ref[...] = jnp.zeros_like(sums_ref)
        next_ref[...] = jnp.zeros_like(next_ref)
        for half in (0, 1):
            wait_weight(co, rw, sems_r, layouts[1], half)
            wait_weight(co, ww, sems, layouts[0], half)

    wide, narrow = dkey_a.shape[1] // 2, rw.shape[3]
    gr_ref[...] = dot(drec[:, :narrow], rows_of(rw, 0), NT) + dot(
        drec[:, narrow:], rows_of(rw, 1), NT
    )
    gk_ref[...] = sum(
        dot(
            part[:, half * wide : (half + 1) * wide],
            rows_of(ww, half, slice(n * wide, (n + 1) * wide)),
            NT,
        )
        for n, part in enumerate((dkey_a, dkey_b))
        for half in (0, 1)
    )
    steps = middle_ref.shape[0] // ROWS
    width = middle_ref.shape[1]

    def step(n, after):
        rows = chunk_rows(steps - 1 - n)
        mean, scaled = norm_stats(lambda strip: middle_ref[rows, strip], width)
        lead = lead_ref[rows, :]
        firsts = ([], [])
        plain, along = 0.0, 0.0
        for strip in strips(width):
            gain, bias, mix_k, mix_r = (vec_ref[m : m + 1, strip] for m in (7, 8, 9, 10))
            unit = (middle_ref[rows, strip] - mean) * scaled
            normed = unit * gain + bias
            gk, gr = gk_ref[rows, strip], gr_ref[rows, strip]
            uk = move_up(gk, after[0][len(firsts[0])]) * lead
            ur = move_up(gr, after[1][len(firsts[0])]) * lead
            grad = gk * mix_k + gr * mix_r + uk * (1.0 - mix_k) + ur * (1.0 - mix_r)
            sums_ref[0, :, strip] += fold_rows(grad * unit)
            sums_ref[1, :, strip] += fold_rows(grad)
            sums_ref[2, :, strip] += fold_rows(normed * (gk - uk))
            sums_ref[3, :, strip] += fold_rows(normed * (gr - ur))
            firsts[0].append(gk[:1, :])
            firsts[1].append(gr[:1, :])
            weighted = grad * gain
            gk_ref[rows, strip] = weighted
            plain = plain + weighted
            along = along + weighted * unit
        plain, along = spread_mean(plain, width), spread_mean(along, width)
        for strip in strips(width):
            unit = (middle_ref[rows, strip] - mean) * scaled
            dmid = dres_ref[rows, strip] + scaled * (gk_ref[rows, strip] - plain - unit * along)
            dmid_ref[rows, strip] = dmid
            dtime_ref[rows, strip] = dmid.astype(BF)
        return tuple(tuple(f) for f in firsts)

    after = lax.fori_loop(0, steps, step, tuple(row_parts(next_ref, m) for m in (0, 1)), unroll=4)
    for m, values in enumerate(after):
        for strip, value in zip(strips(width), values):
            next_ref[m : m + 1, strip] = value


def middle_back(co, dkeys, drec, middle, dres, lead, vectors, weight, recept):
    tokens, width = middle.shape
    rows = tokens // 4
    wide = weight_width(weight)
    tall = pl.BlockSpec((rows, width), lambda i, co: (3 - i, 0))
    return pl.pallas_call(
        functools.partial(middle_back_kernel, layouts=[weight[0], recept[0]]),
        grid_spec=pltpu.PrefetchScalarGridSpec(
            num_scalar_prefetch=1,
            grid=(4,),
            in_specs=[
                pl.BlockSpec((rows, wide), lambda i, co: (3 - i, 0)),
                pl.BlockSpec((rows, wide), lambda i, co: (3 - i, 0)),
                tall,
                tall,
                tall,
                pl.BlockSpec((rows, LANES), lambda i, co: (3 - i, 0)),
                pl.BlockSpec(vectors.shape, lambda i, co: (0, 0)),
            ]
            + [anywhere()] * len(arrays_of(weight, recept)),
            out_specs=[tall] * 2 + [pl.BlockSpec((4, 8, width), lambda i, co: (0, 0, 0))],
            scratch_shapes=[pltpu.VMEM((rows, width), F32)] * 2
            + [pltpu.VMEM((8, width), F32)]
            + weight_scratch(weight, recept),
        ),
        out_shape=[
            jax.ShapeDtypeStruct((tokens, width), F32),
            jax.ShapeDtypeStruct((tokens, width), BF),
            jax.ShapeDtypeStruct((4, 8, width), F32),
        ],
        compiler_params=params(),
        cost_estimate=cost(8, 36 << 20),
    )(co, *dkeys, drec, middle, dres, lead, vectors, *arrays_of(weight, recept))


def time_back_kernel(
    co, dtime, key_ref, val_ref, rec_ref, pa_ref, pb_ref, vec, masks, *refs, layout,
):
    arrays, refs = take_refs(refs, layout)
    dkey_ref, dval_ref, drec_ref, sums_ref, dg_ref, ow, sems = refs
    j = pl.program_id(0)
    per_half = ow.shape[3] // TILE

    @pl.when(j == 0)
    def _():
        start_weight(co, arrays, ow, sems, layout)

    for which in (0, 1):

        @pl.when(j == which * per_half)
        def _(which=which):
            wait_weight(co, ow, sems, layout, which)

    half = co[4] ^ lax.div(j, per_half)
    columns = pl.ds(pl.multiple_of(lax.rem(j, per_half) * TILE, TILE), TILE)
    dg_ref[...] = dot(dtime[...], rows_of(ow, half, columns), NN)

    spread = (8, TILE)
    decay = jnp.broadcast_to(vec[2:3, :], spread)
    first = jnp.broadcast_to(vec[3:4, :], spread)
    r1, r2, r4, r8 = scan_rates(decay)
    left = 7.0 - lax.broadcasted_iota(jnp.int32, spread, 0).astype(F32)
    powers = jnp.exp(-left * jnp.exp(decay))

    def group(start, state):
        rows = pl.ds(start, 8)
        n1, n2, n4, nf, c0, ml = (repeated(masks[n, rows, :], TILE) for n in (0, 1, 2, 3, 4, 5))
        key, val, rec, dg = key_ref[rows, :], val_ref[rows, :], rec_ref[rows, :], dg_ref[rows, :]
        pa, pb = pa_ref[rows, :], pb_ref[rows, :]
        power = jnp.exp(key)
        bonus = jnp.exp(first + key)
        inverse = 1.0 / (pb + bonus)
        wkv = (pa + bonus * val) * inverse
        slope = dg * rec * inverse
        drec = dg * wkv * rec * (1.0 - rec)
        c1, c2, c4, cf, cl = n1 * r1, n2 * r2, n4 * r4, nf * powers, ml * r8
        found, starts = [], []
        for local, leaving in ((slope, state[0]), (-slope * wkv, state[1])):
            local = local + c1 * pltpu.roll(local, 7, 0)
            local = local + c2 * pltpu.roll(local, 6, 0)
            local = local + c4 * pltpu.roll(local, 4, 0)
            found.append(n1 * pltpu.roll(local, 7, 0) + cf * leaving)
            starts.append(c0 * jnp.broadcast_to(local[0:1, :], spread) + cl * leaving)
        later_a, later_b = found
        summand = bonus * slope * (val - wkv)
        dkey = power * (later_a * val + later_b) + summand
        dval = power * later_a + bonus * slope
        state = (
            starts[0],
            starts[1],
            state[2] + summand,
            state[3] + later_a * pa + later_b * pb,
        )
        return (dkey, dval, drec), state

    steps = key_ref.shape[0] // CHUNK

    def step(n, state):
        start = pl.multiple_of((steps - 1 - n) * CHUNK, CHUNK)
        lower, state = group(pl.multiple_of(start + 8, 8), state)
        upper, state = group(start, state)
        for up, low, out in zip(upper, lower, (dkey_ref, dval_ref, drec_ref)):
            out[pl.ds(start, CHUNK), :] = jnp.concatenate([up, low], axis=0).astype(BF)
        return state

    zero = jnp.zeros(spread, F32)
    _, _, first_sum, decay_sum = lax.fori_loop(0, steps, step, (zero,) * 4, unroll=4)
    sums_ref[0] = -r1 * jnp.exp(decay) * decay_sum
    sums_ref[1] = first_sum


def time_back(co, dtime, saved, vectors, masks, weight):
    tokens, width = dtime.shape
    half = width // 2
    tile = column_tile(half // TILE)
    block = pl.BlockSpec((tokens, TILE), tile)
    return pl.pallas_call(
        functools.partial(time_back_kernel, layout=weight[0]),
        grid_spec=pltpu.PrefetchScalarGridSpec(
            num_scalar_prefetch=1,
            grid=(width // TILE,),
            in_specs=[pl.BlockSpec((tokens, width), lambda j, co: (0, 0))]
            + [block] * 5
            + [
                pl.BlockSpec((vectors.shape[0], TILE), tile),
                pl.BlockSpec(masks.shape, lambda j, co: (0, 0, 0)),
            ]
            + [anywhere()] * len(weight[1]),
            out_specs=[block] * 3
            + [pl.BlockSpec((2, 8, TILE), lambda j, co: (0,) + tile(j, co))],
            scratch_shapes=[pltpu.VMEM((tokens, TILE), F32)] + weight_scratch(weight),
        ),
        out_shape=[jax.ShapeDtypeStruct((tokens, width), BF)] * 3
        + [jax.ShapeDtypeStruct((2, 8, width), F32)],
        compiler_params=params(),
        cost_estimate=cost(9, 34 << 20),
    )(co, dtime, *saved, vectors, masks, *weight[1])


def input_back_kernel(
    co, dkey, dval, drec, x_ref, dmid_ref, lead_ref, vec_ref, after_ref, *refs, layouts, part,
):
    count = 1 if part else 3
    before, refs = refs[:count], refs[count + 1 :]
    key_w, refs = take_refs(refs, layouts[0])
    val_w, refs = take_refs(refs, layouts[1])
    rec_w, refs = take_refs(refs, layouts[2])
    out_ref, totals_ref, next_ref, sums_ref, gk_ref, gv_ref, gr_ref, *scratch = refs
    wholes, sems = scratch[:3], scratch[3:]
    i = pl.program_id(0)

    @pl.when(i == 0)
    def _():
        for arrays, whole, sem, layout in zip((key_w, val_w, rec_w), wholes, sems, layouts):
            start_weight(co, arrays, whole, sem, layout)
        sums_ref[...] = jnp.zeros_like(sums_ref)
        next_ref[...] = after_ref[...]

    half = wholes[0].shape[3]
    for n, (grad, out) in enumerate(((dkey, gk_ref), (dval, gv_ref), (drec, gr_ref))):

        @pl.when(i == 0)
        def _(n=n):
            for which in (0, 1):
                wait_weight(co, wholes[n], sems[n], layouts[n], which)

        out[...] = dot(grad[:, :half], rows_of(wholes[n], 0), NT) + dot(
            grad[:, half:], rows_of(wholes[n], 1), NT
        )
    steps = x_ref.shape[0] // ROWS
    width = x_ref.shape[1]

    def step(n, after):
        rows = chunk_rows(steps - 1 - n)
        mean, scaled = norm_stats(lambda strip: x_ref[rows, strip].astype(F32), width)
        lead = lead_ref[rows, :]
        firsts = ([], [], [])
        plain, along = 0.0, 0.0
        for strip in strips(width):
            gain, bias = vec_ref[0:1, strip], vec_ref[1:2, strip]
            unit = (x_ref[rows, strip].astype(F32) - mean) * scaled
            normed = unit * gain + bias
            total = 0.0
            for m, part in enumerate((gk_ref, gv_ref, gr_ref)):
                mix = vec_ref[4 + m : 5 + m, strip]
                grad = part[rows, strip]
                up = move_up(grad, after[m][len(firsts[m])]) * lead
                total = total + grad * mix + up * (1.0 - mix)
                sums_ref[2 + m, :, strip] += fold_rows(normed * (grad - up))
                firsts[m].append(grad[:1, :])
            sums_ref[0, :, strip] += fold_rows(total * unit)
            sums_ref[1, :, strip] += fold_rows(total)
            weighted = total * gain
            gk_ref[rows, strip] = weighted
            plain = plain + weighted
            along = along + weighted * unit
        plain, along = spread_mean(plain, width), spread_mean(along, width)
        for strip in strips(width):
            unit = (x_ref[rows, strip].astype(F32) - mean) * scaled
            out_ref[rows, strip] = dmid_ref[rows, strip] + scaled * (
                gk_ref[rows, strip] - plain - unit * along
            )
        return tuple(tuple(f) for f in firsts)

    after = lax.fori_loop(0, steps, step, tuple(row_parts(next_ref, m) for m in range(3)), unroll=4)
    for m, values in enumerate(after):
        for strip, value in zip(strips(width), values):
            next_ref[m : m + 1, strip] = value

    @pl.when(i == pl.num_programs(0) - 1)
    def _():
        if part:
            totals_ref[...] = before[0][...]
        else:
            time_sums, channel_sums, loss_sums = before
            totals_ref[...] = jnp.zeros_like(totals_ref)
            for n in range(2):
                totals_ref[2 + n : 3 + n, :] = jnp.sum(time_sums[n], axis=0, keepdims=True)
            for n in range(4):
                totals_ref[7 + n : 8 + n, :] = jnp.sum(channel_sums[n], axis=0, keepdims=True)
            totals_ref[11:12, :] = jnp.sum(loss_sums[...], axis=0, keepdims=True)
        for n, row in enumerate((0, 1, 4, 5, 6)):
            totals_ref[row : row + 1, :] += jnp.sum(sums_ref[n], axis=0, keepdims=True)


def input_back(co, grads, x, dmid, lead, vectors, weights, part, after, before, found):
    tokens, width = x.shape
    rows = tokens // 4

    def at(i, co):
        return 3 - 2 * part - i, 0

    tall = pl.BlockSpec((rows, width), at)
    edge = pl.BlockSpec((8, width), lambda i, co: (0, 0))
    return pl.pallas_call(
        functools.partial(input_back_kernel, layouts=[w[0] for w in weights], part=part),
        grid_spec=pltpu.PrefetchScalarGridSpec(
            num_scalar_prefetch=1,
            grid=(2,),
            in_specs=[tall] * 5
            + [
                pl.BlockSpec((rows, LANES), at),
                pl.BlockSpec(vectors.shape, lambda i, co: (0, 0)),
                edge,
                *(
                    pl.BlockSpec(sums.shape, lambda i, co, dims=sums.ndim: (0,) * dims)
                    for sums in before
                ),
                anywhere(),
            ]
            + [anywhere()] * len(arrays_of(*weights)),
            out_specs=[tall, pl.BlockSpec((12, width), lambda i, co: (0, 0)), edge],
            scratch_shapes=[pltpu.VMEM((5, 8, width), F32)]
            + [pltpu.VMEM((rows, width), F32)] * 3 + weight_scratch(*weights),
        ),
        out_shape=[
            jax.ShapeDtypeStruct((tokens, width), F32),
            jax.ShapeDtypeStruct((12, width), F32),
            jax.ShapeDtypeStruct((8, width), F32),
        ],
        input_output_aliases={9 + len(before): 0},
        compiler_params=params(),
        cost_estimate=cost(4, 16 << 20),
    )(co, *grads, x, dmid, lead, vectors, after, *before, found, *arrays_of(*weights))


def seal(*values):
    return lax.optimization_barrier(values)


def swap(values, axis):
    return lax.ppermute(values, axis, SWAP)


class Gather:
    def __init__(self, shard, order, first=None):
        self.order, self.state, self.done = order, (shard,), 0
        if first is not None:
            self.state, self.done = (shard, first), 1

    def step(self):
        n = self.done
        if n and n < 4:
            self.state = (jnp.stack(self.state),)
        if n < 4:
            self.state += (swap(self.state[0], self.order[n]),)
        else:
            near, far = self.state
            self.state = (near, far, swap(near, "c"), swap(far, "c"))
        self.done += 1

    def part(self, first=0, skip=0, columns=None):
        assert self.done == 5
        return ("rel", (self.order, skip, None), first, columns or self.state[0].shape[-1]), self.state

    def part_with(self, others, base):
        assert self.done == 4
        return ("rel", (self.order, 0, base), 0, self.state[0].shape[-1]), (*self.state, others)


def weight_of(*parts):
    layouts, arrays = zip(*parts)
    return tuple(layouts), [array for group in arrays for array in group]


class Merged:
    def __init__(self, slots, order):
        self.order, self.state, self.done = order, tuple(slots), 0

    def step(self):
        n = self.done
        if n == 0:
            near, far, near_other, far_other = self.state
            self.state = (near, far, swap(far_other, "c"), swap(near_other, "c"))
        elif n == 1:
            near, far, far_got, near_got = self.state
            self.state = (near, near_got, swap(far + far_got, self.order[3]))
        elif n < 5:
            kept, sent = (
                sum(part[place].astype(F32) for part in self.state).astype(BF) for place in (0, 1)
            )
            self.state = (kept, swap(sent, self.order[4 - n]))
        self.done += 1

    def finish(self):
        assert self.done == 5
        return list(self.state[0].astype(F32) + self.state[1].astype(F32))


class Reduce:
    def __init__(self, slots, orders):
        self.orders, self.state, self.done = orders, tuple(slots), 0

    def step(self):
        n = self.done
        if n == 0:
            near, far, near_other, far_other = self.state
            self.state = (near, far, swap(far_other, "c"), swap(near_other, "c"))
        elif n == 1:
            near, far, far_got, near_got = self.state
            got = [swap(far[m] + far_got[m], order[3]) for m, order in enumerate(self.orders)]
            self.state = (near, near_got, *got)
        elif n == 2:
            near, near_got, *got = self.state
            self.keep([(near[m], near_got[m], part) for m, part in enumerate(got)], 2)
        elif n < 5:
            self.keep(self.state, 4 - n)
        self.done += 1

    def keep(self, parts, place):
        kept, sent = (
            [sum(v[at].astype(F32) for v in part).astype(BF) for part in parts] for at in (0, 1)
        )
        if place:
            sent = [swap(v, order[place]) for v, order in zip(sent, self.orders)]
            self.state = tuple(zip(kept, sent))
        else:
            self.state = (*kept, swap(jnp.stack(sent), self.orders[0][0]))

    def finish(self):
        assert self.done == 5
        *kept, got = self.state
        return [v.astype(F32) + got[n].astype(F32) for n, v in enumerate(kept)]


def step_all(*chains):
    for chain in chains:
        chain.step()


def seal_all(chains, *values):
    states, values = seal([chain.state for chain in chains], values)
    for chain, state in zip(chains, states):
        chain.state = tuple(state)
    return values


def pair_up(shard):
    got = swap(shard, "x")
    mine = lax.axis_index("x") == 0
    return jnp.where(mine, jnp.stack([shard, got]), jnp.stack([got, shard]))


def gather_plain(shard):
    whole = lax.all_gather(shard, ("w", "u", "y", "c"), axis=0, tiled=True)
    whole = lax.all_gather(whole, "x", axis=1, tiled=True)
    half = whole.shape[1] // 2
    return whole.reshape(16, SLOT, 2, half).transpose(0, 2, 1, 3)


def all_of(array, skip=0, columns=None):
    return (("abs", skip, 0, columns or array.shape[-1]),), [array]


def gather_vectors(own, first, last):
    for axis in EVERY[::-1][first:last]:
        got = swap(own, axis)
        mine = lax.axis_index(axis) == 0
        own = jnp.where(mine, jnp.concatenate([own, got], axis=1), jnp.concatenate([got, own], axis=1))
    return (own,)


def reduce_plain(slots, orders):
    return [reduce_one([part[n] for part in slots], order) for n, order in enumerate(orders)]


def reduce_merged(slots, order):
    count = slots[0].shape[3]
    return [reduce_one([part[:, :, :, n] for part in slots], order) for n in range(count)]


def scatter_rows(whole):
    whole = whole.reshape(-1, *whole.shape[1:])
    return lax.psum_scatter(whole, ("w", "u", "y", "c"), scatter_dimension=0)


def pair_sum(sums):
    side = lax.axis_index("x")
    sent = lax.dynamic_index_in_dim(sums, 1 - side, keepdims=False)
    kept = lax.dynamic_index_in_dim(sums, side, keepdims=False)
    return kept.astype(F32) + swap(sent, "x").astype(F32)


def reduce_blocks(blocks):
    whole = blocks.transpose(0, 2, 1, 3).reshape(16 * SLOT, -1)
    whole = lax.psum_scatter(whole, ("w", "u", "y", "c"), scatter_dimension=0, tiled=True)
    return lax.psum_scatter(whole, "x", scatter_dimension=1, tiled=True).astype(F32)


def reduce_one(slots, order):
    table = {}
    for which, index, rel in rel_slots(order):
        block = rel["w"] * 8 + rel["u"] * 4 + rel["y"] * 2 + rel["c"]
        table[block, rel["x"]] = slots[which][index]
    whole = jnp.concatenate(
        [jnp.concatenate([table[b, 0], table[b, 1]], axis=1) for b in range(16)], axis=0
    )
    whole = lax.psum_scatter(whole, ("w", "u", "y", "c"), scatter_dimension=0, tiled=True)
    return lax.psum_scatter(whole, "x", scatter_dimension=1, tiled=True).astype(F32)


def scan_masks(carry):
    c = carry.reshape(-1, 8)
    place = jnp.arange(8)[None, :]

    def behind(values, n):
        return jnp.where(place >= n, jnp.roll(values, n, axis=1), 0.0)

    def ahead(values, n):
        return jnp.where(place < 8 - n, jnp.roll(values, -n, axis=1), 0.0)

    m1 = jnp.where(place >= 1, c, 0.0)
    m2 = m1 * behind(m1, 1)
    m4 = m2 * behind(m2, 2)
    mf = jnp.cumprod(c, axis=1)
    ml = jnp.broadcast_to(mf[:, 7:], c.shape)
    n1 = ahead(c, 1)
    n2 = n1 * ahead(n1, 1)
    n4 = n2 * ahead(n2, 2)
    back = jnp.cumprod(c[:, ::-1], axis=1)[:, ::-1]
    nf = jnp.where(place < 7, jnp.roll(back, -1, axis=1), 1.0)
    c0 = jnp.broadcast_to(c[:, :1], c.shape)
    tables = (jnp.stack(t).reshape(len(t), -1, 1) for t in ((m1, m2, m4, mf, ml), (n1, n2, n4, nf, c0, ml)))
    return [jnp.broadcast_to(t, t.shape[:2] + (LANES,)) for t in tables]


def on_device(
    inputs,
    segments,
    teacher,
    first_norm_gain,
    first_norm_bias,
    time_decay,
    time_first,
    time_mix_key,
    time_mix_value,
    time_mix_recept,
    time_key,
    time_value,
    time_recept,
    time_output,
    second_norm_gain,
    second_norm_bias,
    channel_mix_key,
    channel_mix_recept,
    channel_key,
    channel_recept,
    channel_value,
):
    tokens, width = inputs.shape
    sizes = {a: lax.axis_size(a) for a in EVERY}
    devices = math.prod(sizes.values())
    fast = all(size == 2 for size in sizes.values())
    side = lax.axis_index("x")
    if fast:
        co = jnp.stack([lax.axis_index(a) for a in EVERY]).astype(jnp.int32)
    else:
        co = jnp.zeros((5,), jnp.int32)

    ids = lax.dynamic_slice_in_dim(segments, side * tokens, tokens)
    previous = jnp.concatenate([jnp.zeros((1,), jnp.int32), ids[:-1]])
    started = jnp.arange(tokens, dtype=jnp.int32) > 0
    carry = ((ids == previous) & (ids > 0) & started).astype(F32)
    valid = (ids > 0).astype(F32)
    lead = jnp.concatenate([carry[1:], jnp.zeros((1,), F32)])
    masks_down, masks_up = scan_masks(carry)
    carry, valid_rows, lead = (
        jnp.broadcast_to(v[:, None], (tokens, LANES)) for v in (carry, valid, lead)
    )

    flat = 0
    for axis in EVERY:
        flat = flat * sizes[axis] + lax.axis_index(axis)
    own_vectors = jnp.stack(
        [
            first_norm_gain,
            first_norm_bias,
            time_decay,
            time_first,
            time_mix_key,
            time_mix_value,
            time_mix_recept,
            second_norm_gain,
            second_norm_bias,
            channel_mix_key,
            channel_mix_recept,
        ]
    )
    piece = own_vectors.shape[1]
    counts = jnp.where(jnp.arange(piece) == 0, jnp.sum(valid), 0.0)[None, :]
    own_vectors = jnp.concatenate([own_vectors, counts, jnp.zeros((4, piece), F32)])
    output_t, value_t = time_output.T, channel_value.T

    if sizes["x"] == 2:
        mine = lax.dynamic_slice_in_dim(teacher, side * tokens, tokens)
        theirs = lax.dynamic_slice_in_dim(teacher, (1 - side) * tokens, tokens)
    else:
        mine, theirs = jnp.split(teacher, 2, axis=1)

    key_order, val_order, rec_order = three_orders = ("wxuy", "wuyx", "wyxu")
    half = width // 2
    if fast:
        wide = channel_key.shape[1]
        split = wide // 2
        chains = keys_a, keys_b, late_b = [
            Gather(channel_key[:, :split], "wuyx"),
            Gather(channel_key[:, split:], "wxuy"),
            Gather(value_t[:, split:], "wyxu"),
        ]
        first = jnp.concatenate([time_key, time_value, time_recept, output_t], axis=1)
        late = jnp.concatenate([value_t[:, :split], channel_recept], axis=1)
        first = lax.all_gather(first, EVERY)
        theirs = swap(theirs, "x")
        step_all(*chains)
        (vectors,) = gather_vectors(own_vectors, 0, 4)
        late, vectors, masks_down, masks_up, mine, theirs, carry, valid_rows, lead = seal_all(
            chains, late, vectors, masks_down, masks_up, mine, theirs, carry, valid_rows, lead
        )
        step_all(*chains)
        (vectors,) = gather_vectors(vectors, 4, 5)
        (vectors,) = seal_all(chains, vectors)
        step_all(*chains)
        mixed = first_mix(inputs, carry, vectors)
        (mixed,) = seal_all(chains, mixed)
        step_all(*chains)
        first, late, mixed = seal(first, late, mixed)
        late = lax.all_gather(late, EVERY).reshape(16, 2, SLOT, -1)
        first = first.reshape(16, 2, SLOT, -1)
        key_w, value_w, recept_w, output_w = (all_of(first, n * half, half) for n in range(4))
    else:
        early = gather_plain(channel_key)
        wide = early.shape[-1]
        split = wide // 2
        key_w, value_w, recept_w, output_w, crecept_w = (
            all_of(gather_plain(w))
            for w in (time_key, time_value, time_recept, output_t, channel_recept)
        )
        ckey_w = all_of(early)
        late = gather_plain(value_t)
        cvalue_w = [all_of(late, skip, split) for skip in (0, split)]
        vectors = lax.all_gather(own_vectors, EVERY, axis=1, tiled=True)
        mixed = first_mix(inputs, carry, vectors)

    *saved, gated = time_forward(co, mixed, (key_w, value_w, recept_w), vectors, masks_down)
    if fast:
        (gated,) = seal_all((keys_a, keys_b), gated)
        step_all(keys_a, keys_b)
    if sizes["x"] == 2 and not fast:
        theirs = swap(theirs, "x")
    middle, mixed_k2, mixed_r2 = time_output_step(co, gated, inputs, carry, vectors, output_w)
    if fast:
        middle, mixed_k2, mixed_r2 = seal_all(chains, middle, mixed_k2, mixed_r2)
        ckey_w = weight_of(keys_a.part(), keys_b.part(split))
        late_b.step()
    hidden, active = hidden_step(co, mixed_k2, ckey_w)
    if fast:
        hidden, late = seal_all((late_b,), hidden, late)
        cvalue_w = [all_of(late, 0, split), weight_of(late_b.part())]
        crecept_w = all_of(late, split, half)
    count = jnp.sum(vectors[11])
    scale = (float(tokens * devices) / count).reshape(1)
    kept, arrived, dres, dkv, drec2, loss_rows = result_step(
        co.at[4].set(side),
        scale,
        hidden,
        mixed_r2,
        middle,
        (mine, theirs),
        valid_rows,
        both_parts(cvalue_w, split),
        crecept_w,
    )

    if sizes["x"] == 2:
        arrived = swap(arrived, "x")

    def outputs_of(kept, arrived):
        return lax.dynamic_update_slice_in_dim(kept, arrived, (1 - side) * tokens, 0)

    back = functools.partial(channel_back, co)
    order_b, order_c = "wuyx", "wuyx"
    edge = jnp.zeros((8, width), F32)

    def input_back_part(dmix, part, after, before, found):
        return input_back(
            co, dmix, inputs, dmid, lead, vectors, (key_w, value_w, recept_w), part, after, before, found
        )

    if fast:
        dkey_1, *found = back(dkv, mixed_k2, hidden, active, (), cvalue_w[1], split, 1, order_b)
        group_b = Merged(found, order_b)
        (dkv,) = seal_all((group_b,), dkv)
        group_b.step()
        dkey_0, blocks = back(
            dkv, mixed_k2, hidden, active, (mixed_r2, drec2), cvalue_w[0], split, 0, order_b
        )
        dkey_0, arrived, blocks = seal_all((group_b,), dkey_0, arrived, blocks)
        blocks = scatter_rows(blocks)
        group_b.step()
        outputs = outputs_of(kept, arrived)
        dmid, dtime, sums2 = middle_back(
            co, (dkey_0, dkey_1), drec2, middle, dres, lead, vectors, ckey_w, crecept_w
        )
        found = weight_grads(co, ((dtime, gated, order_c),), merged=True)
        group_c = Merged(found, order_c)
        dtime, outputs = seal_all((group_b, group_c), dtime, outputs)
        step_all(group_b, group_c)
        *dmix, sums_t = time_back(co, dtime, saved, vectors, masks_up, output_w)
        (dmix, dmid) = seal_all((group_c,), dmix, dmid)
        group_c.step()
        found = weight_grads(co, [(m, d, order) for m, d, order in zip(mixed, dmix, three_orders)])
        group_t = Reduce(found, three_orders)
        (dmix,) = seal_all((group_b, group_c, group_t), dmix)
        step_all(group_b, group_c, group_t)
        found, totals, edge = input_back_part(dmix, 0, edge, (sums_t, sums2, loss_rows), dres)
        (dmix, edge, found) = seal_all((group_c, group_t), dmix, edge, found)
        step_all(group_c, group_t)
        input_grad, totals, _ = input_back_part(dmix, 1, edge, (totals,), found)
    else:
        dkey_1, *found = back(dkv, mixed_k2, hidden, active, (), cvalue_w[1], split, 1, order_b)
        dkey_0, blocks = back(
            dkv, mixed_k2, hidden, active, (mixed_r2, drec2), cvalue_w[0], split, 0, order_b
        )
        value_1, ckey_1 = reduce_merged(found, order_b)
        value_0, ckey_0 = (
            reduce_blocks(blocks[..., n * split : (n + 1) * split]) for n in (0, 1)
        )
        crecept_g = reduce_blocks(blocks[..., 2 * split :])
        halves = 2 // sizes["x"]
        cvalue_g, ckey_g = (
            jnp.concatenate(
                [v.reshape(-1, halves, split) for v in pair], axis=2
            ).reshape(pair[0].shape[0], -1)
            for pair in ((value_0, value_1), (ckey_0, ckey_1))
        )
        dmid, dtime, sums2 = middle_back(
            co, (dkey_0, dkey_1), drec2, middle, dres, lead, vectors, ckey_w, crecept_w
        )
        found = weight_grads(co, ((dtime, gated, order_c),), merged=True)
        (output_g,) = reduce_merged(found, order_c)
        *dmix, sums_t = time_back(co, dtime, saved, vectors, masks_up, output_w)
        found = weight_grads(co, [(m, d, order) for m, d, order in zip(mixed, dmix, three_orders)])
        key_g, val_g, rec_g = reduce_plain(found, three_orders)
        found, totals, edge = input_back_part(dmix, 0, edge, (sums_t, sums2, loss_rows), dres)
        input_grad, totals, _ = input_back_part(dmix, 1, edge, (totals,), found)

    if fast:
        (totals,) = seal_all((group_b, group_c, group_t), totals)
        for axes in ("wc", "y", "xu"):
            step_all(*[group for group in (group_t, group_c, group_b) if group.done < 5])
            for axis in axes:
                totals = totals + swap(totals, axis)
            if axes == "y":
                blocks = pair_sum(blocks)
                totals, blocks = seal_all((group_b, group_c, group_t), totals, blocks)
                cvalue_g, ckey_g = (
                    jnp.concatenate([blocks[:, n * split : (n + 1) * split], found], axis=1)
                    for n, found in enumerate(group_b.finish())
                )
                cvalue_g = cvalue_g.T
            elif axes == "wc":
                totals, blocks = seal_all((group_c, group_t), totals, blocks)
        totals, cvalue_g, ckey_g = seal_all((group_t,), totals, cvalue_g, ckey_g)
        cvalue_g = cvalue_g.T
        (output_g,) = group_c.finish()
        crecept_g = blocks[:, 2 * split :]
        key_g, val_g, rec_g = group_t.finish()
    else:
        totals = lax.psum(totals, EVERY)
    loss = jnp.sum(totals[11]) / (2.0 * count * width)
    vector_g = lax.dynamic_slice_in_dim(totals, flat * piece, piece, axis=1)
    if not fast:
        outputs = (
            outputs_of(kept, arrived)
            if sizes["x"] == 2
            else jnp.concatenate([kept[:tokens], arrived], axis=1)
        )
    return (
        outputs,
        loss,
        input_grad,
        *[vector_g[n] for n in range(7)],
        key_g,
        val_g,
        rec_g,
        output_g.T,
        *[vector_g[n] for n in range(7, 11)],
        ckey_g,
        crecept_g,
        cvalue_g.T,
    )


def solution(mesh):
    fsdp, tp = mesh.shape["fsdp"], mesh.shape["tp"]
    two = 2 if fsdp % 8 == 0 else 1
    split = Mesh(mesh.devices.reshape(fsdp // two**3, two, two, two, tp), EVERY)
    rows = ("w", "u", "y", "c")
    vector = P(EVERY)
    matrix = P(rows, "x")
    turned = P("x", rows)
    tall = P(EVERY, None)
    return jax.shard_map(
        on_device,
        mesh=split,
        in_specs=(
            (tall, P(rows), matrix)
            + (vector,) * 7
            + (matrix, matrix, matrix, turned)
            + (vector,) * 4
            + (matrix, matrix, turned)
        ),
        out_specs=(
            (matrix, P(), tall)
            + (vector,) * 7
            + (matrix, matrix, matrix, turned)
            + (vector,) * 4
            + (matrix, matrix, turned)
        ),
        check_vma=False,
    )
```

```python
import functools
import itertools
import math

import jax
import jax.numpy as jnp
from jax import lax
from jax.experimental import pallas as pl
from jax.experimental.pallas import tpu as pltpu
from jax.sharding import Mesh
from jax.sharding import PartitionSpec as P

BF = jnp.bfloat16
F32 = jnp.float32
EPSILON = 1e-05
SLOT = 64
CHUNK = 16
VMEM_LIMIT = 58 << 20
EVERY = ("w", "u", "y", "c", "x")
SWAP = [(0, 1), (1, 0)]

NN = (((1,), (0,)), ((), ()))
NT = (((1,), (1,)), ((), ()))
TN = (((0,), (0,)), ((), ()))


def dot(left, right, dims):
    return lax.dot_general(left, right, dims, preferred_element_type=F32)


def rel_slots(order):
    for other_core in (0, 1):
        for last in (0, 1):
            for index in itertools.product((0, 1), repeat=3):
                rel = dict(zip(order[2::-1], index))
                rel[order[3]] = last
                rel["c"] = other_core
                yield other_core * 2 + last, index, rel


def slot_place(co, rel):
    at = {axis: co[n] ^ rel[axis] for n, axis in enumerate(EVERY)}
    return at["w"] * 8 + at["u"] * 4 + at["y"] * 2 + at["c"], at["x"]


def rows_of(whole, half, columns=slice(None)):
    found = whole[half, :, :, columns]
    return found.reshape(found.shape[0] * found.shape[1], found.shape[2])


def start_weight(co, refs, whole, sems, layout, halves=(0, 1)):
    refs = list(refs)
    for n, (kind, order, first, columns) in enumerate(layout):
        target = pl.ds(first, columns)
        if kind == "rel":
            order, skip, base = order
            if base is None:
                arrays, refs = refs[:4], refs[4:]
            else:
                arrays, refs = [*refs[:2], refs[2].at[base], refs[2].at[base + 1]], refs[3:]
            for which, index, rel in sorted(rel_slots(order), key=lambda slot: slot[2]["x"]):
                if rel["x"] in halves:
                    block, half = slot_place(co, rel)
                    pltpu.make_async_copy(
                        arrays[which].at[index + (slice(None), pl.ds(skip, columns))],
                        whole.at[half, block, :, target],
                        sems.at[2 * n + rel["x"]],
                    ).start()
        else:
            array, refs = refs[0], refs[1:]
            for rel_x in halves:
                half = co[4] ^ rel_x
                pltpu.make_async_copy(
                    array.at[:, half, :, pl.ds(order, columns)],
                    whole.at[half, :, :, target],
                    sems.at[2 * n + rel_x],
                ).start()


def wait_weight(co, whole, sems, layout, rel_x):
    for n, (_, _, first, columns) in enumerate(layout):
        held = whole.at[co[4] ^ rel_x, :, :, pl.ds(first, columns)]
        pltpu.make_async_copy(held, held, sems.at[2 * n + rel_x]).wait()


def take_refs(refs, layout):
    count = 0
    for kind, order, _, _ in layout:
        count += 1 if kind == "abs" else 4 if order[2] is None else 3
    return refs[:count], refs[count:]


def arrays_of(*weights):
    return [array for _, arrays in weights for array in arrays]


def both_parts(weights, split):
    (first, arrays_a), (second, arrays_b) = weights
    second = tuple((kind, order, at + split, columns) for kind, order, at, columns in second)
    return tuple(first) + second, list(arrays_a) + list(arrays_b)


def weight_width(weight):
    return sum(part[3] for part in weight[0])


def weight_scratch(*weights):
    return [pltpu.VMEM((2, 16, SLOT, weight_width(w)), BF) for w in weights] + [
        pltpu.SemaphoreType.DMA((2 * len(w[0]),)) for w in weights
    ]


ROWS = 32
LANES = 128


def strips(width):
    return [slice(n, n + LANES) for n in range(0, width, LANES)]


def row_parts(ref, row=0):
    return tuple(ref[row : row + 1, strip] for strip in strips(ref.shape[1]))


def chunk_rows(n):
    return pl.ds(pl.multiple_of(n * ROWS, ROWS), ROWS)


def spread_mean(total, width):
    return jnp.broadcast_to(jnp.sum(total, axis=1, keepdims=True) * (1.0 / width), total.shape)


def norm_stats(load, width):
    total = sum(load(strip) for strip in strips(width))
    mean = spread_mean(total, width)
    square = 0.0
    for strip in strips(width):
        centre = load(strip) - mean
        square = square + centre * centre
    return mean, lax.rsqrt(spread_mean(square, width) + EPSILON)


def first_row(shape):
    return lax.broadcasted_iota(jnp.int32, shape, 0) == 0


def last_row(shape):
    return lax.broadcasted_iota(jnp.int32, shape, 0) == shape[0] - 1


def move_down(values, before):
    return jnp.where(first_row(values.shape), before, pltpu.roll(values, 1, 0))


def move_up(values, after):
    return jnp.where(last_row(values.shape), after, pltpu.roll(values, values.shape[0] - 1, 0))


def fold_rows(values):
    return sum(values[n : n + 8] for n in range(0, values.shape[0], 8))


def params(semantics=1):
    return pltpu.CompilerParams(vmem_limit_bytes=VMEM_LIMIT)


def anywhere():
    return pl.BlockSpec(memory_space=pl.ANY)


COST = 0.01


def cost(units, traffic):
    return pl.CostEstimate(
        flops=int(units * 2 * 1024**3 * COST), bytes_accessed=int(traffic * COST), transcendentals=0
    )


def first_mix_kernel(x_ref, carry_ref, vec_ref, mk_ref, mv_ref, mr_ref, last):
    width = x_ref.shape[1]

    def step(n, before):
        rows = chunk_rows(n)
        mean, scaled = norm_stats(lambda strip: x_ref[rows, strip].astype(F32), width)
        carry = carry_ref[rows, :]
        lasts = []
        for strip in strips(width):
            unit = (x_ref[rows, strip].astype(F32) - mean) * scaled
            normed = unit * vec_ref[0:1, strip] + vec_ref[1:2, strip]
            behind = move_down(normed, before[len(lasts)]) * carry
            for m, out in ((4, mk_ref), (5, mv_ref), (6, mr_ref)):
                mix = vec_ref[m : m + 1, strip]
                out[rows, strip] = (normed * mix + behind * (1.0 - mix)).astype(BF)
            lasts.append(normed[ROWS - 1 :, :])
        return tuple(lasts)

    @pl.when(pl.program_id(0) == 0)
    def _():
        last[...] = jnp.zeros_like(last)

    lasts = lax.fori_loop(0, x_ref.shape[0] // ROWS, step, row_parts(last), unroll=4)
    for strip, value in zip(strips(width), lasts):
        last[0:1, strip] = value


def first_mix(x, carry, vectors):
    tokens, width = x.shape
    rows = tokens // 4
    tall = pl.BlockSpec((rows, width), lambda i: (i, 0))
    return pl.pallas_call(
        first_mix_kernel,
        grid=(4,),
        in_specs=[
            tall,
            pl.BlockSpec((rows, LANES), lambda i: (i, 0)),
            pl.BlockSpec(vectors.shape, lambda i: (0, 0)),
        ],
        out_specs=[tall] * 3,
        out_shape=[jax.ShapeDtypeStruct(x.shape, BF)] * 3,
        scratch_shapes=[pltpu.VMEM((8, width), F32)],
        compiler_params=params(),
        cost_estimate=cost(0, 8 << 20),
    )(x, carry, vectors)


FORWARD_TILE = 512
TILE = 256


def scan_rates(decay):
    speed = jnp.exp(decay)
    return [jnp.exp(-float(n) * speed) for n in (1, 2, 4, 8)]


def repeated(values, size):
    return jnp.concatenate([values] * (size // LANES), axis=1)


def time_forward_kernel(
    co, mk, mv, mr, vec, masks, *refs, layouts,
):
    key_w, refs = take_refs(refs, layouts[0])
    val_w, refs = take_refs(refs, layouts[1])
    rec_w, refs = take_refs(refs, layouts[2])
    key_ref, val_ref, rec_ref, pa_ref, pb_ref, gated_ref, *scratch = refs
    wholes, sems = scratch[:3], scratch[3:]
    j = pl.program_id(0)
    per_half = wholes[0].shape[3] // FORWARD_TILE

    @pl.when(j == 0)
    def _():
        for arrays, whole, sem, layout in zip((key_w, val_w, rec_w), wholes, sems, layouts):
            start_weight(co, arrays, whole, sem, layout)

    for which in (0, 1):

        @pl.when(j == which * per_half)
        def _(which=which):
            for whole, sem, layout in zip(wholes, sems, layouts):
                wait_weight(co, whole, sem, layout, which)

    half = co[4] ^ lax.div(j, per_half)
    columns = pl.ds(pl.multiple_of(lax.rem(j, per_half) * FORWARD_TILE, FORWARD_TILE), FORWARD_TILE)
    for mixed, whole, out in zip((mk, mv, mr), wholes, (key_ref, val_ref, rec_ref)):
        out[...] = dot(mixed[...], rows_of(whole, half, columns), NN)

    spread = (8, FORWARD_TILE)
    decay = jnp.broadcast_to(vec[2:3, :], spread)
    first = jnp.broadcast_to(vec[3:4, :], spread)
    r1, r2, r4, r8 = scan_rates(decay)
    powers = jnp.exp(-lax.broadcasted_iota(jnp.int32, spread, 0).astype(F32) * jnp.exp(decay))

    def group(start, state):
        rows = pl.ds(start, 8)
        key, val, pre = key_ref[rows, :], val_ref[rows, :], rec_ref[rows, :]
        m1, m2, m4, mf, ml = (repeated(masks[n, rows, :], FORWARD_TILE) for n in range(5))
        rec = 1.0 / (1.0 + jnp.exp(-pre))
        power = jnp.exp(key)
        bonus = jnp.exp(first + key)
        c1, c2, c4, cf, cl = m1 * r1, m2 * r2, m4 * r4, mf * powers, ml * r8
        priors, ends = [], []
        for local, entering in ((power * val, state[0]), (power, state[1])):
            local = local + c1 * pltpu.roll(local, 1, 0)
            local = local + c2 * pltpu.roll(local, 2, 0)
            local = local + c4 * pltpu.roll(local, 4, 0)
            priors.append(m1 * pltpu.roll(local, 1, 0) + cf * entering)
            ends.append(jnp.broadcast_to(local[7:8, :], spread) + cl * entering)
        wkv = (priors[0] + bonus * val) / (priors[1] + bonus)
        rec_ref[rows, :] = rec
        pa_ref[rows, :] = priors[0]
        pb_ref[rows, :] = priors[1]
        return rec * wkv, tuple(ends)

    def step(i, state):
        start = pl.multiple_of(i * CHUNK, CHUNK)
        upper, state = group(start, state)
        lower, state = group(pl.multiple_of(start + 8, 8), state)
        gated_ref[pl.ds(start, CHUNK), :] = jnp.concatenate([upper, lower], axis=0).astype(BF)
        return state

    zero = jnp.zeros(spread, F32)
    lax.fori_loop(0, key_ref.shape[0] // CHUNK, step, (zero, zero), unroll=4)


def time_forward(co, mixed, weights, vectors, masks):
    tokens, width = mixed[0].shape
    half = width // 2
    per_half = half // FORWARD_TILE

    def tile(j, co):
        return 0, (co[4] ^ lax.div(j, per_half)) * per_half + lax.rem(j, per_half)

    fixed = pl.BlockSpec((tokens, width), lambda j, co: (0, 0))
    block = pl.BlockSpec((tokens, FORWARD_TILE), tile)
    return pl.pallas_call(
        functools.partial(time_forward_kernel, layouts=[w[0] for w in weights]),
        grid_spec=pltpu.PrefetchScalarGridSpec(
            num_scalar_prefetch=1,
            grid=(width // FORWARD_TILE,),
            in_specs=[fixed] * 3
            + [
                pl.BlockSpec((vectors.shape[0], FORWARD_TILE), tile),
                pl.BlockSpec(masks.shape, lambda j, co: (0, 0, 0)),
            ]
            + [anywhere()] * len(arrays_of(*weights)),
            out_specs=[block] * 6,
            scratch_shapes=weight_scratch(*weights),
        ),
        out_shape=[jax.ShapeDtypeStruct((tokens, width), F32)] * 5
        + [jax.ShapeDtypeStruct((tokens, width), BF)],
        compiler_params=params(),
        cost_estimate=cost(8, 34 << 20),
    )(co, *mixed, vectors, masks, *arrays_of(*weights))


def time_output_kernel(
    co, gated, x_ref, carry_ref, vec_ref, *refs, layout
):
    arrays, refs = take_refs(refs, layout)
    middle_ref, mk_ref, mr_ref, last, ow, sems = refs
    i = pl.program_id(0)

    @pl.when(i == 0)
    def _():
        start_weight(co, arrays, ow, sems, layout)
        last[...] = jnp.zeros_like(last)
        for half in (0, 1):
            wait_weight(co, ow, sems, layout, half)

    half = ow.shape[3]
    middle_ref[...] = dot(gated[:, :half], rows_of(ow, 0), NT) + dot(
        gated[:, half:], rows_of(ow, 1), NT
    )
    width = x_ref.shape[1]

    def step(n, before):
        rows = chunk_rows(n)
        for strip in strips(width):
            middle_ref[rows, strip] += x_ref[rows, strip].astype(F32)
        mean, scaled = norm_stats(lambda strip: middle_ref[rows, strip], width)
        carry = carry_ref[rows, :]
        lasts = []
        for strip in strips(width):
            unit = (middle_ref[rows, strip] - mean) * scaled
            normed = unit * vec_ref[7:8, strip] + vec_ref[8:9, strip]
            behind = move_down(normed, before[len(lasts)]) * carry
            for m, out in ((9, mk_ref), (10, mr_ref)):
                mix = vec_ref[m : m + 1, strip]
                out[rows, strip] = (normed * mix + behind * (1.0 - mix)).astype(BF)
            lasts.append(normed[ROWS - 1 :, :])
        return tuple(lasts)

    lasts = lax.fori_loop(0, x_ref.shape[0] // ROWS, step, row_parts(last), unroll=4)
    for strip, value in zip(strips(width), lasts):
        last[0:1, strip] = value


def time_output_step(co, gated, x, carry, vectors, weight):
    tokens, width = x.shape
    rows = tokens // 4
    tall = pl.BlockSpec((rows, width), lambda i, co: (i, 0))
    return pl.pallas_call(
        functools.partial(time_output_kernel, layout=weight[0]),
        grid_spec=pltpu.PrefetchScalarGridSpec(
            num_scalar_prefetch=1,
            grid=(4,),
            in_specs=[
                tall,
                tall,
                pl.BlockSpec((rows, LANES), lambda i, co: (i, 0)),
                pl.BlockSpec(vectors.shape, lambda i, co: (0, 0)),
            ]
            + [anywhere()] * len(weight[1]),
            out_specs=[tall] * 3,
            scratch_shapes=[pltpu.VMEM((8, width), F32)] + weight_scratch(weight),
        ),
        out_shape=[jax.ShapeDtypeStruct((tokens, width), t) for t in (F32, BF, BF)],
        compiler_params=params(),
        cost_estimate=cost(3, 14 << 20),
    )(co, gated, x, carry, vectors, *weight[1])


WIDE = 512


def hidden_kernel(co, mk, *refs, layout):
    arrays, (hidden_ref, active_ref, whole, sems) = take_refs(refs, layout)
    j = pl.program_id(0)
    per_half = whole.shape[3] // WIDE

    @pl.when(j == 0)
    def _():
        start_weight(co, arrays, whole, sems, layout)

    for which in (0, 1):

        @pl.when(j == which * per_half)
        def _(which=which):
            wait_weight(co, whole, sems, layout, which)

    half = co[4] ^ lax.div(j, per_half)
    columns = pl.ds(pl.multiple_of(lax.rem(j, per_half) * WIDE, WIDE), WIDE)
    active = jnp.maximum(dot(mk[...], rows_of(whole, half, columns), NN), 0.0)
    active_ref[...] = active.astype(BF)
    hidden_ref[...] = (active * active).astype(BF)


def column_tile(per_half):
    return lambda j, co: (0, (co[4] ^ lax.div(j, per_half)) * per_half + lax.rem(j, per_half))


def hidden_step(co, mixed, weight):
    tokens, width = mixed.shape
    half = weight_width(weight)
    block = pl.BlockSpec((tokens, WIDE), column_tile(half // WIDE))
    return pl.pallas_call(
        functools.partial(hidden_kernel, layout=weight[0]),
        grid_spec=pltpu.PrefetchScalarGridSpec(
            num_scalar_prefetch=1,
            grid=(2 * half // WIDE,),
            in_specs=[pl.BlockSpec((tokens, width), lambda j, co: (0, 0))]
            + [anywhere()] * len(weight[1]),
            out_specs=[block] * 2,
            scratch_shapes=weight_scratch(weight),
        ),
        out_shape=[jax.ShapeDtypeStruct((tokens, 2 * half), BF)] * 2,
        compiler_params=params(),
        cost_estimate=cost(4.5, 26 << 20),
    )(co, mixed, *weight[1])


def result_kernel(
    co, scale, hidden, mr, middle_ref, mine_ref, theirs_ref, valid_ref, *refs, layouts,
):
    value_w, refs = take_refs(refs, layouts[0])
    recept_w, refs = take_refs(refs, layouts[1])
    *outs, dres_ref, dkv_ref, drec_ref, loss_ref, kv_ref, pre_ref, ww, rw, sems, sems_r = refs
    i = pl.program_id(0)

    @pl.when(i == 0)
    def _():
        start_weight(co, recept_w, rw, sems_r, layouts[1])
        start_weight(co, value_w, ww, sems, layouts[0])
        loss_ref[...] = jnp.zeros_like(loss_ref)
        for half in (0, 1):
            wait_weight(co, rw, sems_r, layouts[1], half)
            wait_weight(co, ww, sems, layouts[0], half)

    wide, narrow = ww.shape[3], rw.shape[3]
    pre_ref[:, :narrow] = dot(mr[...], rows_of(rw, 0), NN)
    pre_ref[:, narrow:] = dot(mr[...], rows_of(rw, 1), NN)
    kv_ref[...] = dot(hidden[:, :wide], rows_of(ww, 0), NT) + dot(
        hidden[:, wide:], rows_of(ww, 1), NT
    )
    factor = scale[0]

    def step(n, _):
        rows = chunk_rows(n)
        valid = valid_ref[rows, :]
        width = kv_ref.shape[1]
        for part, at in itertools.product((0, 1), range(0, width // 2, LANES)):
            first = pl.multiple_of((co[4] ^ part) * (width // 2) + at, LANES)
            strip = pl.ds(first, LANES)
            kv = kv_ref[rows, strip]
            rec = 1.0 / (1.0 + jnp.exp(-pre_ref[rows, strip]))
            result = middle_ref[rows, strip] + rec * kv
            outs[part][rows, at : at + LANES] = result.astype(BF)
            teacher = (mine_ref, theirs_ref)[part][rows, at : at + LANES].astype(F32)
            error = (result - teacher) * valid
            grad = error * factor
            dres_ref[rows, strip] = grad
            dkv = grad * rec
            dkv_ref[rows, strip] = dkv.astype(BF)
            drec_ref[rows, strip] = (dkv * kv * (1.0 - rec)).astype(BF)
            loss_ref[:, strip] += fold_rows(error * error)
        return 0

    lax.fori_loop(0, kv_ref.shape[0] // ROWS, step, 0, unroll=2)


def result_step(co, scale, hidden, mixed, middle, teachers, valid, weight, recept):
    tokens, width = mixed.shape
    rows = tokens // 4
    wide = weight_width(weight)
    tall = pl.BlockSpec((rows, width), lambda i, co, s: (i, 0))
    thin = pl.BlockSpec((rows, width // 2), lambda i, co, s: (i, 0))
    return pl.pallas_call(
        functools.partial(result_kernel, layouts=[weight[0], recept[0]]),
        grid_spec=pltpu.PrefetchScalarGridSpec(
            num_scalar_prefetch=2,
            grid=(4,),
            in_specs=[
                pl.BlockSpec((rows, 2 * wide), lambda i, co, s: (i, 0)),
                tall,
                tall,
                thin,
                thin,
                pl.BlockSpec((rows, LANES), lambda i, co, s: (i, 0)),
            ]
            + [anywhere()] * len(arrays_of(weight, recept)),
            out_specs=[pl.BlockSpec((rows, width // 2), lambda i, co, s: (co[4] * 4 + i, 0)), thin]
            + [tall] * 3
            + [pl.BlockSpec((8, width), lambda i, co, s: (0, 0))],
            scratch_shapes=[pltpu.VMEM((rows, width), F32)] * 2 + weight_scratch(weight, recept),
        ),
        out_shape=[jax.ShapeDtypeStruct((n * tokens, width // 2), BF) for n in (2, 1)]
        + [jax.ShapeDtypeStruct((tokens, width), t) for t in (F32, BF, BF)]
        + [jax.ShapeDtypeStruct((8, width), F32)],
        compiler_params=params(),
        cost_estimate=cost(7, 38 << 20),
    )(co, scale, hidden, mixed, middle, *teachers, valid, *arrays_of(weight, recept))


def start_grads(co, whole, targets, n, sem, order, which, merged):
    for array, index, rel in rel_slots(order):
        if rel["x"] == which:
            block, half = slot_place(co, rel)
            pltpu.make_async_copy(
                whole.at[half, block],
                targets[array].at[index + (n,) if merged else (n,) + index],
                sem,
            ).start()


def wait_bytes(held, sem):
    pltpu.make_async_copy(held, held, sem).wait()


def weight_grads_kernel(co, *refs, orders, merged):
    count = len(orders)
    models, chans, refs = refs[:count], refs[count : 2 * count], refs[2 * count :]
    targets, (held, given, whole, sems_in, sems_out) = refs[:4], refs[4:]
    half = whole.shape[4]
    loads = []
    for n in range(count):
        for m, (source, place) in enumerate(((models[n], held), (chans[n], given))):
            loads.append(pltpu.make_async_copy(source, place.at[n], sems_in.at[2 * n + m]))
            loads[-1].start()
    for n, order in enumerate(orders):
        for load in loads[2 * n : 2 * n + 2]:
            load.wait()

        def step(turn, _, n=n, order=order):
            at = co[4] ^ turn
            columns = pl.ds(pl.multiple_of(at * half, half), half)
            found = dot(held[n], given[n, :, columns], TN).astype(BF)
            whole[n, at] = found.reshape(16, SLOT, half)
            for which in (0, 1):

                @pl.when(turn == which)
                def _(which=which):
                    start_grads(co, whole.at[n], targets, n, sems_out.at[n], order, which, merged)

            return 0

        lax.fori_loop(0, 2, step, 0)
    for n in range(count):
        wait_bytes(whole.at[n], sems_out.at[n])


def weight_grads(co, pairs, merged=False):
    models, chans, orders = zip(*pairs)
    tokens, width = models[0].shape
    half = width // 2
    count = len(pairs)
    dims = (2, 2, 2, count) if merged else (count, 2, 2, 2)
    return pl.pallas_call(
        functools.partial(weight_grads_kernel, orders=orders, merged=merged),
        grid_spec=pltpu.PrefetchScalarGridSpec(
            num_scalar_prefetch=1,
            grid=(1,),
            in_specs=[anywhere()] * (2 * count),
            out_specs=[anywhere()] * 4,
            scratch_shapes=[
                pltpu.VMEM((count, tokens, width), BF),
                pltpu.VMEM((count, tokens, width), BF),
                pltpu.VMEM((count, 2, 16, SLOT, half), BF),
                pltpu.SemaphoreType.DMA((2 * count,)),
                pltpu.SemaphoreType.DMA((count,)),
            ],
        ),
        out_shape=[jax.ShapeDtypeStruct(dims + (SLOT, half), BF)] * 4,
        compiler_params=params(),
        cost_estimate=cost(count * 1.2, count * (6 << 20)),
    )(co, *models, *chans)


def channel_back_kernel(co, dkv, mixed, hidden, active, *refs, layout, part, order):
    recept, refs = refs[: 2 * (1 - part)], refs[2 * (1 - part) :]
    arrays, refs = take_refs(refs, layout)
    dkey, *targets, grads, narrow, sems, whole, sems_in = refs
    j = pl.program_id(0)
    per_half = grads.shape[4] // WIDE
    columns = pl.ds(pl.multiple_of(lax.rem(j, per_half) * WIDE, WIDE), WIDE)
    turn = lax.div(j, per_half)
    half = co[4] ^ turn

    @pl.when(j == 0)
    def _():
        start_weight(co, arrays, whole, sems_in, layout)

    def keep(n, values):
        grads[n, half, :, :, columns] = values.astype(BF).reshape(16, SLOT, WIDE)

    keep(0, dot(dkv[...], hidden[...], TN))

    for which in (0, 1):

        @pl.when(j == which * per_half)
        def _(which=which):
            wait_weight(co, whole, sems_in, layout, which)

    back = dot(dkv[...], rows_of(whole, half, columns), NN)
    back = (2.0 * active[...].astype(F32) * back).astype(BF)
    dkey[...] = back
    keep(1, dot(mixed[...], back, TN))

    wide = grads.shape[4]

    def narrow_copy(turn):
        return pltpu.make_async_copy(
            narrow.at[turn],
            targets[0].at[:, co[4] ^ turn, :, pl.ds(2 * wide, narrow.shape[3])],
            sems.at[2 + turn],
        )

    if part == 0:
        for n in (0, 1):
            pltpu.make_async_copy(
                grads.at[n, half, :, :, columns],
                targets[0].at[:, half, :, pl.ds(pl.multiple_of(n * wide + columns.start, WIDE), WIDE)],
                sems.at[n],
            ).start()

        @pl.when(lax.rem(j, per_half) == 0)
        def _():
            size = narrow.shape[3]
            found = dot(recept[0][...], recept[1][:, pl.ds(pl.multiple_of(half * size, size), size)], TN)
            narrow[turn] = found.astype(BF).reshape(16, SLOT, size)
            narrow_copy(turn).start()

    for which in range(2 * part):

        @pl.when(turn == which)
        def _(which=which):
            for array, index, rel in rel_slots(order):
                if rel["x"] == which:
                    block, at = slot_place(co, rel)
                    for n in (0, 1):
                        pltpu.make_async_copy(
                            grads.at[n, at, block, :, columns],
                            targets[array].at[index + (n, slice(None), columns)],
                            sems.at[n],
                        ).start()

    @pl.when(j == pl.num_programs(0) - 1)
    def _():
        for n in (0, 1):
            wait_bytes(grads.at[n], sems.at[n])
            if part == 0:
                narrow_copy(n).wait()


def channel_back(co, dkv, mixed, hidden, active, recept, weight, half, part, order):
    tokens, width = dkv.shape
    per_half = half // WIDE
    skip, stride = part * per_half, hidden.shape[1] // 2 // WIDE

    def tile(j, co):
        return 0, (co[4] ^ lax.div(j, per_half)) * stride + skip + lax.rem(j, per_half)

    fixed = pl.BlockSpec((tokens, width), lambda j, co: (0, 0))
    block = pl.BlockSpec((tokens, WIDE), tile)
    return pl.pallas_call(
        functools.partial(channel_back_kernel, layout=weight[0], part=part, order=order),
        grid_spec=pltpu.PrefetchScalarGridSpec(
            num_scalar_prefetch=1,
            grid=(2 * per_half,),
            in_specs=[fixed, fixed, block, block]
            + [fixed] * len(recept)
            + [anywhere()] * len(weight[1]),
            out_specs=[pl.BlockSpec((tokens, WIDE), column_tile(per_half))]
            + [anywhere()] * (1 + 3 * part),
            scratch_shapes=[
                pltpu.VMEM((2, 2, 16, SLOT, half), BF),
                pltpu.VMEM((2, 16, SLOT, width // 2), BF),
                pltpu.SemaphoreType.DMA((4,)),
            ]
            + weight_scratch(weight),
        ),
        out_shape=[
            jax.ShapeDtypeStruct((tokens, 2 * half), BF),
            *(
                [jax.ShapeDtypeStruct((2, 2, 2, 2, SLOT, half), BF)] * 4
                if part
                else [jax.ShapeDtypeStruct((16, 2, SLOT, 2 * half + width // 2), BF)]
            ),
        ],
        compiler_params=params(),
        cost_estimate=cost(half / 512 * 3.3, half / 512 * (14 << 20)),
    )(co, dkv, mixed, hidden, active, *recept, *weight[1])


def middle_back_kernel(
    co, dkey_a, dkey_b, drec, middle_ref, dres_ref, lead_ref, vec_ref, *refs, layouts,
):
    key_w, refs = take_refs(refs, layouts[0])
    recept_w, refs = take_refs(refs, layouts[1])
    dmid_ref, dtime_ref, sums_ref, gk_ref, gr_ref, next_ref, ww, rw, sems, sems_r = refs
    i = pl.program_id(0)

    @pl.when(i == 0)
    def _():
        start_weight(co, recept_w, rw, sems_r, layouts[1])
        start_weight(co, key_w, ww, sems, layouts[0])
        sums_ref[...] = jnp.zeros_like(sums_ref)
        next_ref[...] = jnp.zeros_like(next_ref)
        for half in (0, 1):
            wait_weight(co, rw, sems_r, layouts[1], half)
            wait_weight(co, ww, sems, layouts[0], half)

    wide, narrow = dkey_a.shape[1] // 2, rw.shape[3]
    gr_ref[...] = dot(drec[:, :narrow], rows_of(rw, 0), NT) + dot(
        drec[:, narrow:], rows_of(rw, 1), NT
    )
    gk_ref[...] = sum(
        dot(
            part[:, half * wide : (half + 1) * wide],
            rows_of(ww, half, slice(n * wide, (n + 1) * wide)),
            NT,
        )
        for n, part in enumerate((dkey_a, dkey_b))
        for half in (0, 1)
    )
    steps = middle_ref.shape[0] // ROWS
    width = middle_ref.shape[1]

    def step(n, after):
        rows = chunk_rows(steps - 1 - n)
        mean, scaled = norm_stats(lambda strip: middle_ref[rows, strip], width)
        lead = lead_ref[rows, :]
        firsts = ([], [])
        plain, along = 0.0, 0.0
        for strip in strips(width):
            gain, bias, mix_k, mix_r = (vec_ref[m : m + 1, strip] for m in (7, 8, 9, 10))
            unit = (middle_ref[rows, strip] - mean) * scaled
            normed = unit * gain + bias
            gk, gr = gk_ref[rows, strip], gr_ref[rows, strip]
            uk = move_up(gk, after[0][len(firsts[0])]) * lead
            ur = move_up(gr, after[1][len(firsts[0])]) * lead
            grad = gk * mix_k + gr * mix_r + uk * (1.0 - mix_k) + ur * (1.0 - mix_r)
            sums_ref[0, :, strip] += fold_rows(grad * unit)
            sums_ref[1, :, strip] += fold_rows(grad)
            sums_ref[2, :, strip] += fold_rows(normed * (gk - uk))
            sums_ref[3, :, strip] += fold_rows(normed * (gr - ur))
            firsts[0].append(gk[:1, :])
            firsts[1].append(gr[:1, :])
            weighted = grad * gain
            gk_ref[rows, strip] = weighted
            plain = plain + weighted
            along = along + weighted * unit
        plain, along = spread_mean(plain, width), spread_mean(along, width)
        for strip in strips(width):
            unit = (middle_ref[rows, strip] - mean) * scaled
            dmid = dres_ref[rows, strip] + scaled * (gk_ref[rows, strip] - plain - unit * along)
            dmid_ref[rows, strip] = dmid
            dtime_ref[rows, strip] = dmid.astype(BF)
        return tuple(tuple(f) for f in firsts)

    after = lax.fori_loop(0, steps, step, tuple(row_parts(next_ref, m) for m in (0, 1)), unroll=4)
    for m, values in enumerate(after):
        for strip, value in zip(strips(width), values):
            next_ref[m : m + 1, strip] = value


def middle_back(co, dkeys, drec, middle, dres, lead, vectors, weight, recept):
    tokens, width = middle.shape
    rows = tokens // 4
    wide = weight_width(weight)
    tall = pl.BlockSpec((rows, width), lambda i, co: (3 - i, 0))
    return pl.pallas_call(
        functools.partial(middle_back_kernel, layouts=[weight[0], recept[0]]),
        grid_spec=pltpu.PrefetchScalarGridSpec(
            num_scalar_prefetch=1,
            grid=(4,),
            in_specs=[
                pl.BlockSpec((rows, wide), lambda i, co: (3 - i, 0)),
                pl.BlockSpec((rows, wide), lambda i, co: (3 - i, 0)),
                tall,
                tall,
                tall,
                pl.BlockSpec((rows, LANES), lambda i, co: (3 - i, 0)),
                pl.BlockSpec(vectors.shape, lambda i, co: (0, 0)),
            ]
            + [anywhere()] * len(arrays_of(weight, recept)),
            out_specs=[tall] * 2 + [pl.BlockSpec((4, 8, width), lambda i, co: (0, 0, 0))],
            scratch_shapes=[pltpu.VMEM((rows, width), F32)] * 2
            + [pltpu.VMEM((8, width), F32)]
            + weight_scratch(weight, recept),
        ),
        out_shape=[
            jax.ShapeDtypeStruct((tokens, width), F32),
            jax.ShapeDtypeStruct((tokens, width), BF),
            jax.ShapeDtypeStruct((4, 8, width), F32),
        ],
        compiler_params=params(),
        cost_estimate=cost(8, 36 << 20),
    )(co, *dkeys, drec, middle, dres, lead, vectors, *arrays_of(weight, recept))


def time_back_kernel(
    co, dtime, key_ref, val_ref, rec_ref, pa_ref, pb_ref, vec, masks, *refs, layout,
):
    arrays, refs = take_refs(refs, layout)
    dkey_ref, dval_ref, drec_ref, sums_ref, dg_ref, ow, sems = refs
    j = pl.program_id(0)
    per_half = ow.shape[3] // TILE

    @pl.when(j == 0)
    def _():
        start_weight(co, arrays, ow, sems, layout)

    for which in (0, 1):

        @pl.when(j == which * per_half)
        def _(which=which):
            wait_weight(co, ow, sems, layout, which)

    half = co[4] ^ lax.div(j, per_half)
    columns = pl.ds(pl.multiple_of(lax.rem(j, per_half) * TILE, TILE), TILE)
    dg_ref[...] = dot(dtime[...], rows_of(ow, half, columns), NN)

    spread = (8, TILE)
    decay = jnp.broadcast_to(vec[2:3, :], spread)
    first = jnp.broadcast_to(vec[3:4, :], spread)
    r1, r2, r4, r8 = scan_rates(decay)
    left = 7.0 - lax.broadcasted_iota(jnp.int32, spread, 0).astype(F32)
    powers = jnp.exp(-left * jnp.exp(decay))

    def group(start, state):
        rows = pl.ds(start, 8)
        n1, n2, n4, nf, c0, ml = (repeated(masks[n, rows, :], TILE) for n in (0, 1, 2, 3, 4, 5))
        key, val, rec, dg = key_ref[rows, :], val_ref[rows, :], rec_ref[rows, :], dg_ref[rows, :]
        pa, pb = pa_ref[rows, :], pb_ref[rows, :]
        power = jnp.exp(key)
        bonus = jnp.exp(first + key)
        inverse = 1.0 / (pb + bonus)
        wkv = (pa + bonus * val) * inverse
        slope = dg * rec * inverse
        drec = dg * wkv * rec * (1.0 - rec)
        c1, c2, c4, cf, cl = n1 * r1, n2 * r2, n4 * r4, nf * powers, ml * r8
        found, starts = [], []
        for local, leaving in ((slope, state[0]), (-slope * wkv, state[1])):
            local = local + c1 * pltpu.roll(local, 7, 0)
            local = local + c2 * pltpu.roll(local, 6, 0)
            local = local + c4 * pltpu.roll(local, 4, 0)
            found.append(n1 * pltpu.roll(local, 7, 0) + cf * leaving)
            starts.append(c0 * jnp.broadcast_to(local[0:1, :], spread) + cl * leaving)
        later_a, later_b = found
        summand = bonus * slope * (val - wkv)
        dkey = power * (later_a * val + later_b) + summand
        dval = power * later_a + bonus * slope
        state = (
            starts[0],
            starts[1],
            state[2] + summand,
            state[3] + later_a * pa + later_b * pb,
        )
        return (dkey, dval, drec), state

    steps = key_ref.shape[0] // CHUNK

    def step(n, state):
        start = pl.multiple_of((steps - 1 - n) * CHUNK, CHUNK)
        lower, state = group(pl.multiple_of(start + 8, 8), state)
        upper, state = group(start, state)
        for up, low, out in zip(upper, lower, (dkey_ref, dval_ref, drec_ref)):
            out[pl.ds(start, CHUNK), :] = jnp.concatenate([up, low], axis=0).astype(BF)
        return state

    zero = jnp.zeros(spread, F32)
    _, _, first_sum, decay_sum = lax.fori_loop(0, steps, step, (zero,) * 4, unroll=4)
    sums_ref[0] = -r1 * jnp.exp(decay) * decay_sum
    sums_ref[1] = first_sum


def time_back(co, dtime, saved, vectors, masks, weight):
    tokens, width = dtime.shape
    half = width // 2
    tile = column_tile(half // TILE)
    block = pl.BlockSpec((tokens, TILE), tile)
    return pl.pallas_call(
        functools.partial(time_back_kernel, layout=weight[0]),
        grid_spec=pltpu.PrefetchScalarGridSpec(
            num_scalar_prefetch=1,
            grid=(width // TILE,),
            in_specs=[pl.BlockSpec((tokens, width), lambda j, co: (0, 0))]
            + [block] * 5
            + [
                pl.BlockSpec((vectors.shape[0], TILE), tile),
                pl.BlockSpec(masks.shape, lambda j, co: (0, 0, 0)),
            ]
            + [anywhere()] * len(weight[1]),
            out_specs=[block] * 3
            + [pl.BlockSpec((2, 8, TILE), lambda j, co: (0,) + tile(j, co))],
            scratch_shapes=[pltpu.VMEM((tokens, TILE), F32)] + weight_scratch(weight),
        ),
        out_shape=[jax.ShapeDtypeStruct((tokens, width), BF)] * 3
        + [jax.ShapeDtypeStruct((2, 8, width), F32)],
        compiler_params=params(),
        cost_estimate=cost(9, 34 << 20),
    )(co, dtime, *saved, vectors, masks, *weight[1])


def input_back_kernel(
    co, dkey, dval, drec, x_ref, dmid_ref, lead_ref, vec_ref, after_ref, *refs, layouts, part,
):
    count = 1 if part else 3
    before, refs = refs[:count], refs[count + 1 :]
    key_w, refs = take_refs(refs, layouts[0])
    val_w, refs = take_refs(refs, layouts[1])
    rec_w, refs = take_refs(refs, layouts[2])
    out_ref, totals_ref, next_ref, sums_ref, gk_ref, gv_ref, gr_ref, *scratch = refs
    wholes, sems = scratch[:3], scratch[3:]
    i = pl.program_id(0)

    @pl.when(i == 0)
    def _():
        for arrays, whole, sem, layout in zip((key_w, val_w, rec_w), wholes, sems, layouts):
            start_weight(co, arrays, whole, sem, layout)
        sums_ref[...] = jnp.zeros_like(sums_ref)
        next_ref[...] = after_ref[...]

    half = wholes[0].shape[3]
    for n, (grad, out) in enumerate(((dkey, gk_ref), (dval, gv_ref), (drec, gr_ref))):

        @pl.when(i == 0)
        def _(n=n):
            for which in (0, 1):
                wait_weight(co, wholes[n], sems[n], layouts[n], which)

        out[...] = dot(grad[:, :half], rows_of(wholes[n], 0), NT) + dot(
            grad[:, half:], rows_of(wholes[n], 1), NT
        )
    steps = x_ref.shape[0] // ROWS
    width = x_ref.shape[1]

    def step(n, after):
        rows = chunk_rows(steps - 1 - n)
        mean, scaled = norm_stats(lambda strip: x_ref[rows, strip].astype(F32), width)
        lead = lead_ref[rows, :]
        firsts = ([], [], [])
        plain, along = 0.0, 0.0
        for strip in strips(width):
            gain, bias = vec_ref[0:1, strip], vec_ref[1:2, strip]
            unit = (x_ref[rows, strip].astype(F32) - mean) * scaled
            normed = unit * gain + bias
            total = 0.0
            for m, part in enumerate((gk_ref, gv_ref, gr_ref)):
                mix = vec_ref[4 + m : 5 + m, strip]
                grad = part[rows, strip]
                up = move_up(grad, after[m][len(firsts[m])]) * lead
                total = total + grad * mix + up * (1.0 - mix)
                sums_ref[2 + m, :, strip] += fold_rows(normed * (grad - up))
                firsts[m].append(grad[:1, :])
            sums_ref[0, :, strip] += fold_rows(total * unit)
            sums_ref[1, :, strip] += fold_rows(total)
            weighted = total * gain
            gk_ref[rows, strip] = weighted
            plain = plain + weighted
            along = along + weighted * unit
        plain, along = spread_mean(plain, width), spread_mean(along, width)
        for strip in strips(width):
            unit = (x_ref[rows, strip].astype(F32) - mean) * scaled
            out_ref[rows, strip] = dmid_ref[rows, strip] + scaled * (
                gk_ref[rows, strip] - plain - unit * along
            )
        return tuple(tuple(f) for f in firsts)

    after = lax.fori_loop(0, steps, step, tuple(row_parts(next_ref, m) for m in range(3)), unroll=4)
    for m, values in enumerate(after):
        for strip, value in zip(strips(width), values):
            next_ref[m : m + 1, strip] = value

    @pl.when(i == pl.num_programs(0) - 1)
    def _():
        if part:
            totals_ref[...] = before[0][...]
        else:
            time_sums, channel_sums, loss_sums = before
            totals_ref[...] = jnp.zeros_like(totals_ref)
            for n in range(2):
                totals_ref[2 + n : 3 + n, :] = jnp.sum(time_sums[n], axis=0, keepdims=True)
            for n in range(4):
                totals_ref[7 + n : 8 + n, :] = jnp.sum(channel_sums[n], axis=0, keepdims=True)
            totals_ref[11:12, :] = jnp.sum(loss_sums[...], axis=0, keepdims=True)
        for n, row in enumerate((0, 1, 4, 5, 6)):
            totals_ref[row : row + 1, :] += jnp.sum(sums_ref[n], axis=0, keepdims=True)


def input_back(co, grads, x, dmid, lead, vectors, weights, part, after, before, found):
    tokens, width = x.shape
    rows = tokens // 4

    def at(i, co):
        return 3 - 2 * part - i, 0

    tall = pl.BlockSpec((rows, width), at)
    edge = pl.BlockSpec((8, width), lambda i, co: (0, 0))
    return pl.pallas_call(
        functools.partial(input_back_kernel, layouts=[w[0] for w in weights], part=part),
        grid_spec=pltpu.PrefetchScalarGridSpec(
            num_scalar_prefetch=1,
            grid=(2,),
            in_specs=[tall] * 5
            + [
                pl.BlockSpec((rows, LANES), at),
                pl.BlockSpec(vectors.shape, lambda i, co: (0, 0)),
                edge,
                *(
                    pl.BlockSpec(sums.shape, lambda i, co, dims=sums.ndim: (0,) * dims)
                    for sums in before
                ),
                anywhere(),
            ]
            + [anywhere()] * len(arrays_of(*weights)),
            out_specs=[tall, pl.BlockSpec((12, width), lambda i, co: (0, 0)), edge],
            scratch_shapes=[pltpu.VMEM((5, 8, width), F32)]
            + [pltpu.VMEM((rows, width), F32)] * 3 + weight_scratch(*weights),
        ),
        out_shape=[
            jax.ShapeDtypeStruct((tokens, width), F32),
            jax.ShapeDtypeStruct((12, width), F32),
            jax.ShapeDtypeStruct((8, width), F32),
        ],
        input_output_aliases={9 + len(before): 0},
        compiler_params=params(),
        cost_estimate=cost(4, 16 << 20),
    )(co, *grads, x, dmid, lead, vectors, after, *before, found, *arrays_of(*weights))


def seal(*values):
    return lax.optimization_barrier(values)


def swap(values, axis):
    return lax.ppermute(values, axis, SWAP)


class Gather:
    def __init__(self, shard, order, first=None):
        self.order, self.state, self.done = order, (shard,), 0
        if first is not None:
            self.state, self.done = (shard, first), 1

    def step(self):
        n = self.done
        if n and n < 4:
            self.state = (jnp.stack(self.state),)
        if n < 4:
            self.state += (swap(self.state[0], self.order[n]),)
        else:
            near, far = self.state
            self.state = (near, far, swap(near, "c"), swap(far, "c"))
        self.done += 1

    def part(self, first=0, skip=0, columns=None):
        assert self.done == 5
        return ("rel", (self.order, skip, None), first, columns or self.state[0].shape[-1]), self.state

    def part_with(self, others, base):
        assert self.done == 4
        return ("rel", (self.order, 0, base), 0, self.state[0].shape[-1]), (*self.state, others)


def weight_of(*parts):
    layouts, arrays = zip(*parts)
    return tuple(layouts), [array for group in arrays for array in group]


class Merged:
    def __init__(self, slots, order):
        self.order, self.state, self.done = order, tuple(slots), 0

    def step(self):
        n = self.done
        if n == 0:
            near, far, near_other, far_other = self.state
            self.state = (near, far, swap(far_other, "c"), swap(near_other, "c"))
        elif n == 1:
            near, far, far_got, near_got = self.state
            self.state = (near, near_got, swap(far + far_got, self.order[3]))
        elif n < 5:
            kept, sent = (
                sum(part[place].astype(F32) for part in self.state).astype(BF) for place in (0, 1)
            )
            self.state = (kept, swap(sent, self.order[4 - n]))
        self.done += 1

    def finish(self):
        assert self.done == 5
        return list(self.state[0].astype(F32) + self.state[1].astype(F32))


class Reduce:
    def __init__(self, slots, orders):
        self.orders, self.state, self.done = orders, tuple(slots), 0

    def step(self):
        n = self.done
        if n == 0:
            near, far, near_other, far_other = self.state
            self.state = (near, far, swap(far_other, "c"), swap(near_other, "c"))
        elif n == 1:
            near, far, far_got, near_got = self.state
            got = [swap(far[m] + far_got[m], order[3]) for m, order in enumerate(self.orders)]
            self.state = (near, near_got, *got)
        elif n == 2:
            near, near_got, *got = self.state
            self.keep([(near[m], near_got[m], part) for m, part in enumerate(got)], 2)
        elif n < 5:
            self.keep(self.state, 4 - n)
        self.done += 1

    def keep(self, parts, place):
        kept, sent = (
            [sum(v[at].astype(F32) for v in part).astype(BF) for part in parts] for at in (0, 1)
        )
        if place:
            sent = [swap(v, order[place]) for v, order in zip(sent, self.orders)]
            self.state = tuple(zip(kept, sent))
        else:
            self.state = (*kept, swap(jnp.stack(sent), self.orders[0][0]))

    def finish(self):
        assert self.done == 5
        *kept, got = self.state
        return [v.astype(F32) + got[n].astype(F32) for n, v in enumerate(kept)]


def step_all(*chains):
    for chain in chains:
        chain.step()


def seal_all(chains, *values):
    states, values = seal([chain.state for chain in chains], values)
    for chain, state in zip(chains, states):
        chain.state = tuple(state)
    return values


def pair_up(shard):
    got = swap(shard, "x")
    mine = lax.axis_index("x") == 0
    return jnp.where(mine, jnp.stack([shard, got]), jnp.stack([got, shard]))


def gather_plain(shard):
    whole = lax.all_gather(shard, ("w", "u", "y", "c"), axis=0, tiled=True)
    whole = lax.all_gather(whole, "x", axis=1, tiled=True)
    half = whole.shape[1] // 2
    return whole.reshape(16, SLOT, 2, half).transpose(0, 2, 1, 3)


def all_of(array, skip=0, columns=None):
    return (("abs", skip, 0, columns or array.shape[-1]),), [array]


def gather_vectors(own, first, last):
    for axis in EVERY[::-1][first:last]:
        got = swap(own, axis)
        mine = lax.axis_index(axis) == 0
        own = jnp.where(mine, jnp.concatenate([own, got], axis=1), jnp.concatenate([got, own], axis=1))
    return (own,)


def reduce_plain(slots, orders):
    return [reduce_one([part[n] for part in slots], order) for n, order in enumerate(orders)]


def reduce_merged(slots, order):
    count = slots[0].shape[3]
    return [reduce_one([part[:, :, :, n] for part in slots], order) for n in range(count)]


def scatter_rows(whole):
    whole = whole.reshape(-1, *whole.shape[1:])
    return lax.psum_scatter(whole, ("w", "u", "y", "c"), scatter_dimension=0)


def pair_sum(sums):
    side = lax.axis_index("x")
    sent = lax.dynamic_index_in_dim(sums, 1 - side, keepdims=False)
    kept = lax.dynamic_index_in_dim(sums, side, keepdims=False)
    return kept.astype(F32) + swap(sent, "x").astype(F32)


def reduce_blocks(blocks):
    whole = blocks.transpose(0, 2, 1, 3).reshape(16 * SLOT, -1)
    whole = lax.psum_scatter(whole, ("w", "u", "y", "c"), scatter_dimension=0, tiled=True)
    return lax.psum_scatter(whole, "x", scatter_dimension=1, tiled=True).astype(F32)


def reduce_one(slots, order):
    table = {}
    for which, index, rel in rel_slots(order):
        block = rel["w"] * 8 + rel["u"] * 4 + rel["y"] * 2 + rel["c"]
        table[block, rel["x"]] = slots[which][index]
    whole = jnp.concatenate(
        [jnp.concatenate([table[b, 0], table[b, 1]], axis=1) for b in range(16)], axis=0
    )
    whole = lax.psum_scatter(whole, ("w", "u", "y", "c"), scatter_dimension=0, tiled=True)
    return lax.psum_scatter(whole, "x", scatter_dimension=1, tiled=True).astype(F32)


def scan_masks(carry):
    c = carry.reshape(-1, 8)
    place = jnp.arange(8)[None, :]

    def behind(values, n):
        return jnp.where(place >= n, jnp.roll(values, n, axis=1), 0.0)

    def ahead(values, n):
        return jnp.where(place < 8 - n, jnp.roll(values, -n, axis=1), 0.0)

    m1 = jnp.where(place >= 1, c, 0.0)
    m2 = m1 * behind(m1, 1)
    m4 = m2 * behind(m2, 2)
    mf = jnp.cumprod(c, axis=1)
    ml = jnp.broadcast_to(mf[:, 7:], c.shape)
    n1 = ahead(c, 1)
    n2 = n1 * ahead(n1, 1)
    n4 = n2 * ahead(n2, 2)
    back = jnp.cumprod(c[:, ::-1], axis=1)[:, ::-1]
    nf = jnp.where(place < 7, jnp.roll(back, -1, axis=1), 1.0)
    c0 = jnp.broadcast_to(c[:, :1], c.shape)
    tables = (jnp.stack(t).reshape(len(t), -1, 1) for t in ((m1, m2, m4, mf, ml), (n1, n2, n4, nf, c0, ml)))
    return [jnp.broadcast_to(t, t.shape[:2] + (LANES,)) for t in tables]


def on_device(
    inputs,
    segments,
    teacher,
    first_norm_gain,
    first_norm_bias,
    time_decay,
    time_first,
    time_mix_key,
    time_mix_value,
    time_mix_recept,
    time_key,
    time_value,
    time_recept,
    time_output,
    second_norm_gain,
    second_norm_bias,
    channel_mix_key,
    channel_mix_recept,
    channel_key,
    channel_recept,
    channel_value,
):
    tokens, width = inputs.shape
    sizes = {a: lax.axis_size(a) for a in EVERY}
    devices = math.prod(sizes.values())
    fast = all(size == 2 for size in sizes.values())
    side = lax.axis_index("x")
    if fast:
        co = jnp.stack([lax.axis_index(a) for a in EVERY]).astype(jnp.int32)
    else:
        co = jnp.zeros((5,), jnp.int32)

    ids = lax.dynamic_slice_in_dim(segments, side * tokens, tokens)
    previous = jnp.concatenate([jnp.zeros((1,), jnp.int32), ids[:-1]])
    started = jnp.arange(tokens, dtype=jnp.int32) > 0
    carry = ((ids == previous) & (ids > 0) & started).astype(F32)
    valid = (ids > 0).astype(F32)
    lead = jnp.concatenate([carry[1:], jnp.zeros((1,), F32)])
    masks_down, masks_up = scan_masks(carry)
    carry, valid_rows, lead = (
        jnp.broadcast_to(v[:, None], (tokens, LANES)) for v in (carry, valid, lead)
    )

    flat = 0
    for axis in EVERY:
        flat = flat * sizes[axis] + lax.axis_index(axis)
    own_vectors = jnp.stack(
        [
            first_norm_gain,
            first_norm_bias,
            time_decay,
            time_first,
            time_mix_key,
            time_mix_value,
            time_mix_recept,
            second_norm_gain,
            second_norm_bias,
            channel_mix_key,
            channel_mix_recept,
        ]
    )
    piece = own_vectors.shape[1]
    counts = jnp.where(jnp.arange(piece) == 0, jnp.sum(valid), 0.0)[None, :]
    own_vectors = jnp.concatenate([own_vectors, counts, jnp.zeros((4, piece), F32)])
    output_t, value_t = time_output.T, channel_value.T

    if sizes["x"] == 2:
        mine = lax.dynamic_slice_in_dim(teacher, side * tokens, tokens)
        theirs = lax.dynamic_slice_in_dim(teacher, (1 - side) * tokens, tokens)
    else:
        mine, theirs = jnp.split(teacher, 2, axis=1)

    key_order, val_order, rec_order = three_orders = ("wxuy", "wuyx", "wyxu")
    half = width // 2
    if fast:
        wide = channel_key.shape[1]
        split = wide // 2
        chains = keys_a, keys_b, late_b = [
            Gather(channel_key[:, :split], "wuyx"),
            Gather(channel_key[:, split:], "wxuy"),
            Gather(value_t[:, split:], "wyxu"),
        ]
        first = jnp.concatenate([time_key, time_value, time_recept, output_t], axis=1)
        late = jnp.concatenate([value_t[:, :split], channel_recept], axis=1)
        first = lax.all_gather(first, EVERY)
        theirs = swap(theirs, "x")
        step_all(*chains)
        (vectors,) = gather_vectors(own_vectors, 0, 4)
        late, vectors, masks_down, masks_up, mine, theirs, carry, valid_rows, lead = seal_all(
            chains, late, vectors, masks_down, masks_up, mine, theirs, carry, valid_rows, lead
        )
        step_all(*chains)
        (vectors,) = gather_vectors(vectors, 4, 5)
        (vectors,) = seal_all(chains, vectors)
        step_all(*chains)
        mixed = first_mix(inputs, carry, vectors)
        (mixed,) = seal_all(chains, mixed)
        step_all(*chains)
        first, late, mixed = seal(first, late, mixed)
        late = lax.all_gather(late, EVERY).reshape(16, 2, SLOT, -1)
        first = first.reshape(16, 2, SLOT, -1)
        key_w, value_w, recept_w, output_w = (all_of(first, n * half, half) for n in range(4))
    else:
        early = gather_plain(channel_key)
        wide = early.shape[-1]
        split = wide // 2
        key_w, value_w, recept_w, output_w, crecept_w = (
            all_of(gather_plain(w))
            for w in (time_key, time_value, time_recept, output_t, channel_recept)
        )
        ckey_w = all_of(early)
        late = gather_plain(value_t)
        cvalue_w = [all_of(late, skip, split) for skip in (0, split)]
        vectors = lax.all_gather(own_vectors, EVERY, axis=1, tiled=True)
        mixed = first_mix(inputs, carry, vectors)

    *saved, gated = time_forward(co, mixed, (key_w, value_w, recept_w), vectors, masks_down)
    if fast:
        (gated,) = seal_all((keys_a, keys_b), gated)
        step_all(keys_a, keys_b)
    if sizes["x"] == 2 and not fast:
        theirs = swap(theirs, "x")
    middle, mixed_k2, mixed_r2 = time_output_step(co, gated, inputs, carry, vectors, output_w)
    if fast:
        middle, mixed_k2, mixed_r2 = seal_all(chains, middle, mixed_k2, mixed_r2)
        ckey_w = weight_of(keys_a.part(), keys_b.part(split))
        late_b.step()
    hidden, active = hidden_step(co, mixed_k2, ckey_w)
    if fast:
        hidden, late = seal_all((late_b,), hidden, late)
        cvalue_w = [all_of(late, 0, split), weight_of(late_b.part())]
        crecept_w = all_of(late, split, half)
    count = jnp.sum(vectors[11])
    scale = (float(tokens * devices) / count).reshape(1)
    kept, arrived, dres, dkv, drec2, loss_rows = result_step(
        co.at[4].set(side),
        scale,
        hidden,
        mixed_r2,
        middle,
        (mine, theirs),
        valid_rows,
        both_parts(cvalue_w, split),
        crecept_w,
    )

    if sizes["x"] == 2:
        arrived = swap(arrived, "x")

    def outputs_of(kept, arrived):
        return lax.dynamic_update_slice_in_dim(kept, arrived, (1 - side) * tokens, 0)

    back = functools.partial(channel_back, co)
    order_b, order_c = "wuyx", "wuxy"
    edge = jnp.zeros((8, width), F32)

    def input_back_part(dmix, part, after, before, found):
        return input_back(
            co, dmix, inputs, dmid, lead, vectors, (key_w, value_w, recept_w), part, after, before, found
        )

    if fast:
        dkey_0, blocks = back(
            dkv, mixed_k2, hidden, active, (mixed_r2, drec2), cvalue_w[0], split, 0, order_b
        )
        dkv, arrived, blocks = seal(dkv, arrived, blocks)
        blocks = scatter_rows(blocks)
        dkey_1, *found = back(dkv, mixed_k2, hidden, active, (), cvalue_w[1], split, 1, order_b)
        group_b = Merged(found, order_b)
        (dkey_1,) = seal_all((group_b,), dkey_1)
        group_b.step()
        outputs = outputs_of(kept, arrived)
        dmid, dtime, sums2 = middle_back(
            co, (dkey_0, dkey_1), drec2, middle, dres, lead, vectors, ckey_w, crecept_w
        )
        (dtime,) = seal_all((group_b,), dtime)
        group_b.step()
        found = weight_grads(co, ((dtime, gated, order_c),), merged=True)
        group_c = Merged(found, order_c)
        dtime, outputs = seal_all((group_c,), dtime, outputs)
        group_c.step()
        *dmix, sums_t = time_back(co, dtime, saved, vectors, masks_up, output_w)
        (dmix, dmid) = seal_all((group_c,), dmix, dmid)
        group_c.step()
        found = weight_grads(co, [(m, d, order) for m, d, order in zip(mixed, dmix, three_orders)])
        group_t = Reduce(found, three_orders)
        (dmix,) = seal_all((group_b, group_c, group_t), dmix)
        step_all(group_b, group_c, group_t)
        found, totals, edge = input_back_part(dmix, 0, edge, (sums_t, sums2, loss_rows), dres)
        (dmix, edge, found) = seal_all((group_c, group_t), dmix, edge, found)
        step_all(group_c, group_t)
        input_grad, totals, _ = input_back_part(dmix, 1, edge, (totals,), found)
    else:
        dkey_1, *found = back(dkv, mixed_k2, hidden, active, (), cvalue_w[1], split, 1, order_b)
        dkey_0, blocks = back(
            dkv, mixed_k2, hidden, active, (mixed_r2, drec2), cvalue_w[0], split, 0, order_b
        )
        value_1, ckey_1 = reduce_merged(found, order_b)
        value_0, ckey_0 = (
            reduce_blocks(blocks[..., n * split : (n + 1) * split]) for n in (0, 1)
        )
        crecept_g = reduce_blocks(blocks[..., 2 * split :])
        halves = 2 // sizes["x"]
        cvalue_g, ckey_g = (
            jnp.concatenate(
                [v.reshape(-1, halves, split) for v in pair], axis=2
            ).reshape(pair[0].shape[0], -1)
            for pair in ((value_0, value_1), (ckey_0, ckey_1))
        )
        dmid, dtime, sums2 = middle_back(
            co, (dkey_0, dkey_1), drec2, middle, dres, lead, vectors, ckey_w, crecept_w
        )
        found = weight_grads(co, ((dtime, gated, order_c),), merged=True)
        (output_g,) = reduce_merged(found, order_c)
        *dmix, sums_t = time_back(co, dtime, saved, vectors, masks_up, output_w)
        found = weight_grads(co, [(m, d, order) for m, d, order in zip(mixed, dmix, three_orders)])
        key_g, val_g, rec_g = reduce_plain(found, three_orders)
        found, totals, edge = input_back_part(dmix, 0, edge, (sums_t, sums2, loss_rows), dres)
        input_grad, totals, _ = input_back_part(dmix, 1, edge, (totals,), found)

    if fast:
        (totals,) = seal_all((group_b, group_c, group_t), totals)
        for axes in ("wc", "y", "xu"):
            step_all(*[group for group in (group_t, group_c, group_b) if group.done < 5])
            for axis in axes:
                totals = totals + swap(totals, axis)
            if axes == "y":
                blocks = pair_sum(blocks)
                totals, blocks = seal_all((group_b, group_c, group_t), totals, blocks)
                cvalue_g, ckey_g = (
                    jnp.concatenate([blocks[:, n * split : (n + 1) * split], found], axis=1)
                    for n, found in enumerate(group_b.finish())
                )
                cvalue_g = cvalue_g.T
            elif axes == "wc":
                totals, blocks = seal_all((group_c, group_t), totals, blocks)
        totals, cvalue_g, ckey_g = seal_all((group_t,), totals, cvalue_g, ckey_g)
        cvalue_g = cvalue_g.T
        (output_g,) = group_c.finish()
        crecept_g = blocks[:, 2 * split :]
        key_g, val_g, rec_g = group_t.finish()
    else:
        totals = lax.psum(totals, EVERY)
    loss = jnp.sum(totals[11]) / (2.0 * count * width)
    vector_g = lax.dynamic_slice_in_dim(totals, flat * piece, piece, axis=1)
    if not fast:
        outputs = (
            outputs_of(kept, arrived)
            if sizes["x"] == 2
            else jnp.concatenate([kept[:tokens], arrived], axis=1)
        )
    return (
        outputs,
        loss,
        input_grad,
        *[vector_g[n] for n in range(7)],
        key_g,
        val_g,
        rec_g,
        output_g.T,
        *[vector_g[n] for n in range(7, 11)],
        ckey_g,
        crecept_g,
        cvalue_g.T,
    )


def solution(mesh):
    fsdp, tp = mesh.shape["fsdp"], mesh.shape["tp"]
    two = 2 if fsdp % 8 == 0 else 1
    split = Mesh(mesh.devices.reshape(fsdp // two**3, two, two, two, tp), EVERY)
    rows = ("w", "u", "y", "c")
    vector = P(EVERY)
    matrix = P(rows, "x")
    turned = P("x", rows)
    tall = P(EVERY, None)
    return jax.shard_map(
        on_device,
        mesh=split,
        in_specs=(
            (tall, P(rows), matrix)
            + (vector,) * 7
            + (matrix, matrix, matrix, turned)
            + (vector,) * 4
            + (matrix, matrix, turned)
        ),
        out_specs=(
            (matrix, P(), tall)
            + (vector,) * 7
            + (matrix, matrix, matrix, turned)
            + (vector,) * 4
            + (matrix, matrix, turned)
        ),
        check_vma=False,
    )
```

```python
import functools
import itertools
import math

import jax
import jax.numpy as jnp
from jax import lax
from jax.experimental import pallas as pl
from jax.experimental.pallas import tpu as pltpu
from jax.sharding import Mesh
from jax.sharding import PartitionSpec as P

BF = jnp.bfloat16
F32 = jnp.float32
EPSILON = 1e-05
SLOT = 64
CHUNK = 16
VMEM_LIMIT = 58 << 20
EVERY = ("w", "u", "y", "c", "x")
SWAP = [(0, 1), (1, 0)]

NN = (((1,), (0,)), ((), ()))
NT = (((1,), (1,)), ((), ()))
TN = (((0,), (0,)), ((), ()))


def dot(left, right, dims):
    return lax.dot_general(left, right, dims, preferred_element_type=F32)


def rel_slots(order):
    for other_core in (0, 1):
        for last in (0, 1):
            for index in itertools.product((0, 1), repeat=3):
                rel = dict(zip(order[2::-1], index))
                rel[order[3]] = last
                rel["c"] = other_core
                yield other_core * 2 + last, index, rel


def slot_place(co, rel):
    at = {axis: co[n] ^ rel[axis] for n, axis in enumerate(EVERY)}
    return at["w"] * 8 + at["u"] * 4 + at["y"] * 2 + at["c"], at["x"]


def rows_of(whole, half, columns=slice(None)):
    found = whole[half, :, :, columns]
    return found.reshape(found.shape[0] * found.shape[1], found.shape[2])


def start_weight(co, refs, whole, sems, layout, halves=(0, 1)):
    refs = list(refs)
    for n, (kind, order, first, columns) in enumerate(layout):
        target = pl.ds(first, columns)
        if kind == "rel":
            order, skip, base = order
            if base is None:
                arrays, refs = refs[:4], refs[4:]
            else:
                arrays, refs = [*refs[:2], refs[2].at[base], refs[2].at[base + 1]], refs[3:]
            for which, index, rel in sorted(rel_slots(order), key=lambda slot: slot[2]["x"]):
                if rel["x"] in halves:
                    block, half = slot_place(co, rel)
                    pltpu.make_async_copy(
                        arrays[which].at[index + (slice(None), pl.ds(skip, columns))],
                        whole.at[half, block, :, target],
                        sems.at[2 * n + rel["x"]],
                    ).start()
        else:
            array, refs = refs[0], refs[1:]
            for rel_x in halves:
                half = co[4] ^ rel_x
                pltpu.make_async_copy(
                    array.at[:, half, :, pl.ds(order, columns)],
                    whole.at[half, :, :, target],
                    sems.at[2 * n + rel_x],
                ).start()


def wait_weight(co, whole, sems, layout, rel_x):
    for n, (_, _, first, columns) in enumerate(layout):
        held = whole.at[co[4] ^ rel_x, :, :, pl.ds(first, columns)]
        pltpu.make_async_copy(held, held, sems.at[2 * n + rel_x]).wait()


def take_refs(refs, layout):
    count = 0
    for kind, order, _, _ in layout:
        count += 1 if kind == "abs" else 4 if order[2] is None else 3
    return refs[:count], refs[count:]


def arrays_of(*weights):
    return [array for _, arrays in weights for array in arrays]


def both_parts(weights, split):
    (first, arrays_a), (second, arrays_b) = weights
    second = tuple((kind, order, at + split, columns) for kind, order, at, columns in second)
    return tuple(first) + second, list(arrays_a) + list(arrays_b)


def weight_width(weight):
    return sum(part[3] for part in weight[0])


def weight_scratch(*weights):
    return [pltpu.VMEM((2, 16, SLOT, weight_width(w)), BF) for w in weights] + [
        pltpu.SemaphoreType.DMA((2 * len(w[0]),)) for w in weights
    ]


ROWS = 32
LANES = 128


def strips(width):
    return [slice(n, n + LANES) for n in range(0, width, LANES)]


def row_parts(ref, row=0):
    return tuple(ref[row : row + 1, strip] for strip in strips(ref.shape[1]))


def chunk_rows(n):
    return pl.ds(pl.multiple_of(n * ROWS, ROWS), ROWS)


def spread_mean(total, width):
    return jnp.broadcast_to(jnp.sum(total, axis=1, keepdims=True) * (1.0 / width), total.shape)


def norm_stats(load, width):
    total = sum(load(strip) for strip in strips(width))
    mean = spread_mean(total, width)
    square = 0.0
    for strip in strips(width):
        centre = load(strip) - mean
        square = square + centre * centre
    return mean, lax.rsqrt(spread_mean(square, width) + EPSILON)


def first_row(shape):
    return lax.broadcasted_iota(jnp.int32, shape, 0) == 0


def last_row(shape):
    return lax.broadcasted_iota(jnp.int32, shape, 0) == shape[0] - 1


def move_down(values, before):
    return jnp.where(first_row(values.shape), before, pltpu.roll(values, 1, 0))


def move_up(values, after):
    return jnp.where(last_row(values.shape), after, pltpu.roll(values, values.shape[0] - 1, 0))


def fold_rows(values):
    return sum(values[n : n + 8] for n in range(0, values.shape[0], 8))


def params(semantics=1):
    return pltpu.CompilerParams(vmem_limit_bytes=VMEM_LIMIT)


def anywhere():
    return pl.BlockSpec(memory_space=pl.ANY)


COST = 0.01


def cost(units, traffic):
    return pl.CostEstimate(
        flops=int(units * 2 * 1024**3 * COST), bytes_accessed=int(traffic * COST), transcendentals=0
    )


def first_mix_kernel(x_ref, carry_ref, vec_ref, mk_ref, mv_ref, mr_ref, last):
    width = x_ref.shape[1]

    def step(n, before):
        rows = chunk_rows(n)
        mean, scaled = norm_stats(lambda strip: x_ref[rows, strip].astype(F32), width)
        carry = carry_ref[rows, :]
        lasts = []
        for strip in strips(width):
            unit = (x_ref[rows, strip].astype(F32) - mean) * scaled
            normed = unit * vec_ref[0:1, strip] + vec_ref[1:2, strip]
            behind = move_down(normed, before[len(lasts)]) * carry
            for m, out in ((4, mk_ref), (5, mv_ref), (6, mr_ref)):
                mix = vec_ref[m : m + 1, strip]
                out[rows, strip] = (normed * mix + behind * (1.0 - mix)).astype(BF)
            lasts.append(normed[ROWS - 1 :, :])
        return tuple(lasts)

    @pl.when(pl.program_id(0) == 0)
    def _():
        last[...] = jnp.zeros_like(last)

    lasts = lax.fori_loop(0, x_ref.shape[0] // ROWS, step, row_parts(last), unroll=4)
    for strip, value in zip(strips(width), lasts):
        last[0:1, strip] = value


def first_mix(x, carry, vectors):
    tokens, width = x.shape
    rows = tokens // 4
    tall = pl.BlockSpec((rows, width), lambda i: (i, 0))
    return pl.pallas_call(
        first_mix_kernel,
        grid=(4,),
        in_specs=[
            tall,
            pl.BlockSpec((rows, LANES), lambda i: (i, 0)),
            pl.BlockSpec(vectors.shape, lambda i: (0, 0)),
        ],
        out_specs=[tall] * 3,
        out_shape=[jax.ShapeDtypeStruct(x.shape, BF)] * 3,
        scratch_shapes=[pltpu.VMEM((8, width), F32)],
        compiler_params=params(),
        cost_estimate=cost(0, 8 << 20),
    )(x, carry, vectors)


FORWARD_TILE = 512
TILE = 256


def scan_rates(decay):
    speed = jnp.exp(decay)
    return [jnp.exp(-float(n) * speed) for n in (1, 2, 4, 8)]


def repeated(values, size):
    return jnp.concatenate([values] * (size // LANES), axis=1)


def time_forward_kernel(
    co, mk, mv, mr, vec, masks, *refs, layouts,
):
    key_w, refs = take_refs(refs, layouts[0])
    val_w, refs = take_refs(refs, layouts[1])
    rec_w, refs = take_refs(refs, layouts[2])
    key_ref, val_ref, rec_ref, pa_ref, pb_ref, gated_ref, *scratch = refs
    wholes, sems = scratch[:3], scratch[3:]
    j = pl.program_id(0)
    per_half = wholes[0].shape[3] // FORWARD_TILE

    @pl.when(j == 0)
    def _():
        for arrays, whole, sem, layout in zip((key_w, val_w, rec_w), wholes, sems, layouts):
            start_weight(co, arrays, whole, sem, layout)

    for which in (0, 1):

        @pl.when(j == which * per_half)
        def _(which=which):
            for whole, sem, layout in zip(wholes, sems, layouts):
                wait_weight(co, whole, sem, layout, which)

    half = co[4] ^ lax.div(j, per_half)
    columns = pl.ds(pl.multiple_of(lax.rem(j, per_half) * FORWARD_TILE, FORWARD_TILE), FORWARD_TILE)
    for mixed, whole, out in zip((mk, mv, mr), wholes, (key_ref, val_ref, rec_ref)):
        out[...] = dot(mixed[...], rows_of(whole, half, columns), NN)

    spread = (8, FORWARD_TILE)
    decay = jnp.broadcast_to(vec[2:3, :], spread)
    first = jnp.broadcast_to(vec[3:4, :], spread)
    r1, r2, r4, r8 = scan_rates(decay)
    powers = jnp.exp(-lax.broadcasted_iota(jnp.int32, spread, 0).astype(F32) * jnp.exp(decay))

    def group(start, state):
        rows = pl.ds(start, 8)
        key, val, pre = key_ref[rows, :], val_ref[rows, :], rec_ref[rows, :]
        m1, m2, m4, mf, ml = (repeated(masks[n, rows, :], FORWARD_TILE) for n in range(5))
        rec = 1.0 / (1.0 + jnp.exp(-pre))
        power = jnp.exp(key)
        bonus = jnp.exp(first + key)
        c1, c2, c4, cf, cl = m1 * r1, m2 * r2, m4 * r4, mf * powers, ml * r8
        priors, ends = [], []
        for local, entering in ((power * val, state[0]), (power, state[1])):
            local = local + c1 * pltpu.roll(local, 1, 0)
            local = local + c2 * pltpu.roll(local, 2, 0)
            local = local + c4 * pltpu.roll(local, 4, 0)
            priors.append(m1 * pltpu.roll(local, 1, 0) + cf * entering)
            ends.append(jnp.broadcast_to(local[7:8, :], spread) + cl * entering)
        wkv = (priors[0] + bonus * val) / (priors[1] + bonus)
        rec_ref[rows, :] = rec
        pa_ref[rows, :] = priors[0]
        pb_ref[rows, :] = priors[1]
        return rec * wkv, tuple(ends)

    def step(i, state):
        start = pl.multiple_of(i * CHUNK, CHUNK)
        upper, state = group(start, state)
        lower, state = group(pl.multiple_of(start + 8, 8), state)
        gated_ref[pl.ds(start, CHUNK), :] = jnp.concatenate([upper, lower], axis=0).astype(BF)
        return state

    zero = jnp.zeros(spread, F32)
    lax.fori_loop(0, key_ref.shape[0] // CHUNK, step, (zero, zero), unroll=4)


def time_forward(co, mixed, weights, vectors, masks):
    tokens, width = mixed[0].shape
    half = width // 2
    per_half = half // FORWARD_TILE

    def tile(j, co):
        return 0, (co[4] ^ lax.div(j, per_half)) * per_half + lax.rem(j, per_half)

    fixed = pl.BlockSpec((tokens, width), lambda j, co: (0, 0))
    block = pl.BlockSpec((tokens, FORWARD_TILE), tile)
    return pl.pallas_call(
        functools.partial(time_forward_kernel, layouts=[w[0] for w in weights]),
        grid_spec=pltpu.PrefetchScalarGridSpec(
            num_scalar_prefetch=1,
            grid=(width // FORWARD_TILE,),
            in_specs=[fixed] * 3
            + [
                pl.BlockSpec((vectors.shape[0], FORWARD_TILE), tile),
                pl.BlockSpec(masks.shape, lambda j, co: (0, 0, 0)),
            ]
            + [anywhere()] * len(arrays_of(*weights)),
            out_specs=[block] * 6,
            scratch_shapes=weight_scratch(*weights),
        ),
        out_shape=[jax.ShapeDtypeStruct((tokens, width), F32)] * 5
        + [jax.ShapeDtypeStruct((tokens, width), BF)],
        compiler_params=params(),
        cost_estimate=cost(8, 34 << 20),
    )(co, *mixed, vectors, masks, *arrays_of(*weights))


def time_output_kernel(
    co, gated, x_ref, carry_ref, vec_ref, *refs, layout
):
    arrays, refs = take_refs(refs, layout)
    middle_ref, mk_ref, mr_ref, last, ow, sems = refs
    i = pl.program_id(0)

    @pl.when(i == 0)
    def _():
        start_weight(co, arrays, ow, sems, layout)
        last[...] = jnp.zeros_like(last)
        for half in (0, 1):
            wait_weight(co, ow, sems, layout, half)

    half = ow.shape[3]
    middle_ref[...] = dot(gated[:, :half], rows_of(ow, 0), NT) + dot(
        gated[:, half:], rows_of(ow, 1), NT
    )
    width = x_ref.shape[1]

    def step(n, before):
        rows = chunk_rows(n)
        for strip in strips(width):
            middle_ref[rows, strip] += x_ref[rows, strip].astype(F32)
        mean, scaled = norm_stats(lambda strip: middle_ref[rows, strip], width)
        carry = carry_ref[rows, :]
        lasts = []
        for strip in strips(width):
            unit = (middle_ref[rows, strip] - mean) * scaled
            normed = unit * vec_ref[7:8, strip] + vec_ref[8:9, strip]
            behind = move_down(normed, before[len(lasts)]) * carry
            for m, out in ((9, mk_ref), (10, mr_ref)):
                mix = vec_ref[m : m + 1, strip]
                out[rows, strip] = (normed * mix + behind * (1.0 - mix)).astype(BF)
            lasts.append(normed[ROWS - 1 :, :])
        return tuple(lasts)

    lasts = lax.fori_loop(0, x_ref.shape[0] // ROWS, step, row_parts(last), unroll=4)
    for strip, value in zip(strips(width), lasts):
        last[0:1, strip] = value


def time_output_step(co, gated, x, carry, vectors, weight):
    tokens, width = x.shape
    rows = tokens // 4
    tall = pl.BlockSpec((rows, width), lambda i, co: (i, 0))
    return pl.pallas_call(
        functools.partial(time_output_kernel, layout=weight[0]),
        grid_spec=pltpu.PrefetchScalarGridSpec(
            num_scalar_prefetch=1,
            grid=(4,),
            in_specs=[
                tall,
                tall,
                pl.BlockSpec((rows, LANES), lambda i, co: (i, 0)),
                pl.BlockSpec(vectors.shape, lambda i, co: (0, 0)),
            ]
            + [anywhere()] * len(weight[1]),
            out_specs=[tall] * 3,
            scratch_shapes=[pltpu.VMEM((8, width), F32)] + weight_scratch(weight),
        ),
        out_shape=[jax.ShapeDtypeStruct((tokens, width), t) for t in (F32, BF, BF)],
        compiler_params=params(),
        cost_estimate=cost(3, 14 << 20),
    )(co, gated, x, carry, vectors, *weight[1])


WIDE = 512


def hidden_kernel(co, mk, *refs, layout):
    arrays, (hidden_ref, active_ref, whole, sems) = take_refs(refs, layout)
    j = pl.program_id(0)
    per_half = whole.shape[3] // WIDE

    @pl.when(j == 0)
    def _():
        start_weight(co, arrays, whole, sems, layout)

    for which in (0, 1):

        @pl.when(j == which * per_half)
        def _(which=which):
            wait_weight(co, whole, sems, layout, which)

    half = co[4] ^ lax.div(j, per_half)
    columns = pl.ds(pl.multiple_of(lax.rem(j, per_half) * WIDE, WIDE), WIDE)
    active = jnp.maximum(dot(mk[...], rows_of(whole, half, columns), NN), 0.0)
    active_ref[...] = active.astype(BF)
    hidden_ref[...] = (active * active).astype(BF)


def column_tile(per_half):
    return lambda j, co: (0, (co[4] ^ lax.div(j, per_half)) * per_half + lax.rem(j, per_half))


def hidden_step(co, mixed, weight):
    tokens, width = mixed.shape
    half = weight_width(weight)
    block = pl.BlockSpec((tokens, WIDE), column_tile(half // WIDE))
    return pl.pallas_call(
        functools.partial(hidden_kernel, layout=weight[0]),
        grid_spec=pltpu.PrefetchScalarGridSpec(
            num_scalar_prefetch=1,
            grid=(2 * half // WIDE,),
            in_specs=[pl.BlockSpec((tokens, width), lambda j, co: (0, 0))]
            + [anywhere()] * len(weight[1]),
            out_specs=[block] * 2,
            scratch_shapes=weight_scratch(weight),
        ),
        out_shape=[jax.ShapeDtypeStruct((tokens, 2 * half), BF)] * 2,
        compiler_params=params(),
        cost_estimate=cost(4.5, 26 << 20),
    )(co, mixed, *weight[1])


def result_kernel(
    co, scale, hidden, mr, middle_ref, mine_ref, theirs_ref, valid_ref, *refs, layouts,
):
    value_w, refs = take_refs(refs, layouts[0])
    recept_w, refs = take_refs(refs, layouts[1])
    *outs, dres_ref, dkv_ref, drec_ref, loss_ref, kv_ref, pre_ref, ww, rw, sems, sems_r = refs
    i = pl.program_id(0)

    @pl.when(i == 0)
    def _():
        start_weight(co, recept_w, rw, sems_r, layouts[1])
        start_weight(co, value_w, ww, sems, layouts[0])
        loss_ref[...] = jnp.zeros_like(loss_ref)
        for half in (0, 1):
            wait_weight(co, rw, sems_r, layouts[1], half)
            wait_weight(co, ww, sems, layouts[0], half)

    wide, narrow = ww.shape[3], rw.shape[3]
    pre_ref[:, :narrow] = dot(mr[...], rows_of(rw, 0), NN)
    pre_ref[:, narrow:] = dot(mr[...], rows_of(rw, 1), NN)
    kv_ref[...] = dot(hidden[:, :wide], rows_of(ww, 0), NT) + dot(
        hidden[:, wide:], rows_of(ww, 1), NT
    )
    factor = scale[0]

    def step(n, _):
        rows = chunk_rows(n)
        valid = valid_ref[rows, :]
        width = kv_ref.shape[1]
        for part, at in itertools.product((0, 1), range(0, width // 2, LANES)):
            first = pl.multiple_of((co[4] ^ part) * (width // 2) + at, LANES)
            strip = pl.ds(first, LANES)
            kv = kv_ref[rows, strip]
            rec = 1.0 / (1.0 + jnp.exp(-pre_ref[rows, strip]))
            result = middle_ref[rows, strip] + rec * kv
            outs[part][rows, at : at + LANES] = result.astype(BF)
            teacher = (mine_ref, theirs_ref)[part][rows, at : at + LANES].astype(F32)
            error = (result - teacher) * valid
            grad = error * factor
            dres_ref[rows, strip] = grad
            dkv = grad * rec
            dkv_ref[rows, strip] = dkv.astype(BF)
            drec_ref[rows, strip] = (dkv * kv * (1.0 - rec)).astype(BF)
            loss_ref[:, strip] += fold_rows(error * error)
        return 0

    lax.fori_loop(0, kv_ref.shape[0] // ROWS, step, 0, unroll=2)


def result_step(co, scale, hidden, mixed, middle, teachers, valid, weight, recept):
    tokens, width = mixed.shape
    rows = tokens // 4
    wide = weight_width(weight)
    tall = pl.BlockSpec((rows, width), lambda i, co, s: (i, 0))
    thin = pl.BlockSpec((rows, width // 2), lambda i, co, s: (i, 0))
    return pl.pallas_call(
        functools.partial(result_kernel, layouts=[weight[0], recept[0]]),
        grid_spec=pltpu.PrefetchScalarGridSpec(
            num_scalar_prefetch=2,
            grid=(4,),
            in_specs=[
                pl.BlockSpec((rows, 2 * wide), lambda i, co, s: (i, 0)),
                tall,
                tall,
                thin,
                thin,
                pl.BlockSpec((rows, LANES), lambda i, co, s: (i, 0)),
            ]
            + [anywhere()] * len(arrays_of(weight, recept)),
            out_specs=[pl.BlockSpec((rows, width // 2), lambda i, co, s: (co[4] * 4 + i, 0)), thin]
            + [tall] * 3
            + [pl.BlockSpec((8, width), lambda i, co, s: (0, 0))],
            scratch_shapes=[pltpu.VMEM((rows, width), F32)] * 2 + weight_scratch(weight, recept),
        ),
        out_shape=[jax.ShapeDtypeStruct((n * tokens, width // 2), BF) for n in (2, 1)]
        + [jax.ShapeDtypeStruct((tokens, width), t) for t in (F32, BF, BF)]
        + [jax.ShapeDtypeStruct((8, width), F32)],
        compiler_params=params(),
        cost_estimate=cost(7, 38 << 20),
    )(co, scale, hidden, mixed, middle, *teachers, valid, *arrays_of(weight, recept))


def start_grads(co, whole, targets, n, sem, order, which, merged):
    for array, index, rel in rel_slots(order):
        if rel["x"] == which:
            block, half = slot_place(co, rel)
            pltpu.make_async_copy(
                whole.at[half, block],
                targets[array].at[index + (n,) if merged else (n,) + index],
                sem,
            ).start()


def wait_bytes(held, sem):
    pltpu.make_async_copy(held, held, sem).wait()


def weight_grads_kernel(co, *refs, orders, merged):
    count = len(orders)
    models, chans, refs = refs[:count], refs[count : 2 * count], refs[2 * count :]
    targets, (held, given, whole, sems_in, sems_out) = refs[:4], refs[4:]
    half = whole.shape[4]
    loads = []
    for n in range(count):
        for m, (source, place) in enumerate(((models[n], held), (chans[n], given))):
            loads.append(pltpu.make_async_copy(source, place.at[n], sems_in.at[2 * n + m]))
            loads[-1].start()
    for n, order in enumerate(orders):
        for load in loads[2 * n : 2 * n + 2]:
            load.wait()

        def step(turn, _, n=n, order=order):
            at = co[4] ^ turn
            columns = pl.ds(pl.multiple_of(at * half, half), half)
            found = dot(held[n], given[n, :, columns], TN).astype(BF)
            whole[n, at] = found.reshape(16, SLOT, half)
            for which in (0, 1):

                @pl.when(turn == which)
                def _(which=which):
                    start_grads(co, whole.at[n], targets, n, sems_out.at[n], order, which, merged)

            return 0

        lax.fori_loop(0, 2, step, 0)
    for n in range(count):
        wait_bytes(whole.at[n], sems_out.at[n])


def weight_grads(co, pairs, merged=False):
    models, chans, orders = zip(*pairs)
    tokens, width = models[0].shape
    half = width // 2
    count = len(pairs)
    dims = (2, 2, 2, count) if merged else (count, 2, 2, 2)
    return pl.pallas_call(
        functools.partial(weight_grads_kernel, orders=orders, merged=merged),
        grid_spec=pltpu.PrefetchScalarGridSpec(
            num_scalar_prefetch=1,
            grid=(1,),
            in_specs=[anywhere()] * (2 * count),
            out_specs=[anywhere()] * 4,
            scratch_shapes=[
                pltpu.VMEM((count, tokens, width), BF),
                pltpu.VMEM((count, tokens, width), BF),
                pltpu.VMEM((count, 2, 16, SLOT, half), BF),
                pltpu.SemaphoreType.DMA((2 * count,)),
                pltpu.SemaphoreType.DMA((count,)),
            ],
        ),
        out_shape=[jax.ShapeDtypeStruct(dims + (SLOT, half), BF)] * 4,
        compiler_params=params(),
        cost_estimate=cost(count * 1.2, count * (6 << 20)),
    )(co, *models, *chans)


def channel_back_kernel(co, dkv, mixed, active, *refs, layout, part, order):
    if part == 0:
        (hidden, hidden_1, *recept), refs = refs[:4], refs[4:]
    arrays, refs = take_refs(refs, layout)
    dkey, targets, refs = refs[0], refs[1:5], refs[5:]
    if part == 0:
        blocks, *refs = refs
        grads, narrow, *refs = refs
    other, sems, whole, sems_in = refs
    j = pl.program_id(0)
    wide = other.shape[3]
    per_half = wide // WIDE
    columns = pl.ds(pl.multiple_of(lax.rem(j, per_half) * WIDE, WIDE), WIDE)
    turn = lax.div(j, per_half)
    half = co[4] ^ turn

    @pl.when(j == 0)
    def _():
        start_weight(co, arrays, whole, sems_in, layout)

    def cut(values):
        return values.astype(BF).reshape(16, SLOT, WIDE)

    if part == 0:
        other[half, :, :, columns] = cut(dot(dkv[...], hidden_1[...], TN))
        grads[0, half, :, :, columns] = cut(dot(dkv[...], hidden[...], TN))

    for which in (0, 1):

        @pl.when(j == which * per_half)
        def _(which=which):
            wait_weight(co, whole, sems_in, layout, which)

    back = dot(dkv[...], rows_of(whole, half, columns), NN)
    back = (2.0 * active[...].astype(F32) * back).astype(BF)
    dkey[...] = back
    found = cut(dot(mixed[...], back, TN))
    if part == 0:
        grads[1, half, :, :, columns] = found
    else:
        other[half, :, :, columns] = found

    for which in (0, 1):

        @pl.when(j == (which + 1) * per_half - 1)
        def _(which=which):
            start_grads(co, other, targets, 0, sems.at[0], order, which, True)

    if part == 0:

        def narrow_copy(turn):
            return pltpu.make_async_copy(
                narrow.at[turn],
                blocks.at[:, co[4] ^ turn, :, pl.ds(2 * wide, narrow.shape[3])],
                sems.at[3 + turn],
            )

        for n in (0, 1):
            pltpu.make_async_copy(
                grads.at[n, half, :, :, columns],
                blocks.at[:, half, :, pl.ds(pl.multiple_of(n * wide + columns.start, WIDE), WIDE)],
                sems.at[1 + n],
            ).start()

        @pl.when(lax.rem(j, per_half) == 0)
        def _():
            size = narrow.shape[3]
            found = dot(recept[0][...], recept[1][:, pl.ds(pl.multiple_of(half * size, size), size)], TN)
            narrow[turn] = found.astype(BF).reshape(16, SLOT, size)
            narrow_copy(turn).start()

    @pl.when(j == pl.num_programs(0) - 1)
    def _():
        wait_bytes(other, sems.at[0])
        if part == 0:
            for n in (0, 1):
                wait_bytes(grads.at[n], sems.at[1 + n])
                narrow_copy(n).wait()


def channel_back(co, dkv, mixed, hidden, active, recept, weight, half, part, order):
    tokens, width = dkv.shape
    per_half = half // WIDE
    stride = active.shape[1] // 2 // WIDE

    def tile_of(skip):
        return lambda j, co: (
            0,
            (co[4] ^ lax.div(j, per_half)) * stride + skip + lax.rem(j, per_half),
        )

    fixed = pl.BlockSpec((tokens, width), lambda j, co: (0, 0))
    own, other = (pl.BlockSpec((tokens, WIDE), tile_of(n * per_half)) for n in (part, 1 - part))
    first = part == 0
    return pl.pallas_call(
        functools.partial(channel_back_kernel, layout=weight[0], part=part, order=order),
        grid_spec=pltpu.PrefetchScalarGridSpec(
            num_scalar_prefetch=1,
            grid=(2 * per_half,),
            in_specs=[fixed, fixed, own]
            + [own, other, fixed, fixed] * first
            + [anywhere()] * len(weight[1]),
            out_specs=[pl.BlockSpec((tokens, WIDE), column_tile(per_half))]
            + [anywhere()] * (4 + first),
            scratch_shapes=[
                pltpu.VMEM((2, 2, 16, SLOT, half), BF),
                pltpu.VMEM((2, 16, SLOT, width // 2), BF),
            ]
            * first
            + [pltpu.VMEM((2, 16, SLOT, half), BF), pltpu.SemaphoreType.DMA((5,))]
            + weight_scratch(weight),
        ),
        out_shape=[jax.ShapeDtypeStruct((tokens, 2 * half), BF)]
        + [jax.ShapeDtypeStruct((2, 2, 2, 1, SLOT, half), BF)] * 4
        + [jax.ShapeDtypeStruct((16, 2, SLOT, 2 * half + width // 2), BF)] * first,
        compiler_params=params(),
        cost_estimate=cost(half / 512 * 3.3, half / 512 * (14 << 20)),
    )(co, dkv, mixed, active, *(hidden, hidden, *recept)[: 4 * first], *weight[1])


def middle_back_kernel(
    co, dkey_a, dkey_b, drec, middle_ref, dres_ref, lead_ref, vec_ref, *refs, layouts,
):
    key_w, refs = take_refs(refs, layouts[0])
    recept_w, refs = take_refs(refs, layouts[1])
    dmid_ref, dtime_ref, sums_ref, gk_ref, gr_ref, next_ref, ww, rw, sems, sems_r = refs
    i = pl.program_id(0)

    @pl.when(i == 0)
    def _():
        start_weight(co, recept_w, rw, sems_r, layouts[1])
        start_weight(co, key_w, ww, sems, layouts[0])
        sums_ref[...] = jnp.zeros_like(sums_ref)
        next_ref[...] = jnp.zeros_like(next_ref)
        for half in (0, 1):
            wait_weight(co, rw, sems_r, layouts[1], half)
            wait_weight(co, ww, sems, layouts[0], half)

    wide, narrow = dkey_a.shape[1] // 2, rw.shape[3]
    gr_ref[...] = dot(drec[:, :narrow], rows_of(rw, 0), NT) + dot(
        drec[:, narrow:], rows_of(rw, 1), NT
    )
    gk_ref[...] = sum(
        dot(
            part[:, half * wide : (half + 1) * wide],
            rows_of(ww, half, slice(n * wide, (n + 1) * wide)),
            NT,
        )
        for n, part in enumerate((dkey_a, dkey_b))
        for half in (0, 1)
    )
    steps = middle_ref.shape[0] // ROWS
    width = middle_ref.shape[1]

    def step(n, after):
        rows = chunk_rows(steps - 1 - n)
        mean, scaled = norm_stats(lambda strip: middle_ref[rows, strip], width)
        lead = lead_ref[rows, :]
        firsts = ([], [])
        plain, along = 0.0, 0.0
        for strip in strips(width):
            gain, bias, mix_k, mix_r = (vec_ref[m : m + 1, strip] for m in (7, 8, 9, 10))
            unit = (middle_ref[rows, strip] - mean) * scaled
            normed = unit * gain + bias
            gk, gr = gk_ref[rows, strip], gr_ref[rows, strip]
            uk = move_up(gk, after[0][len(firsts[0])]) * lead
            ur = move_up(gr, after[1][len(firsts[0])]) * lead
            grad = gk * mix_k + gr * mix_r + uk * (1.0 - mix_k) + ur * (1.0 - mix_r)
            sums_ref[0, :, strip] += fold_rows(grad * unit)
            sums_ref[1, :, strip] += fold_rows(grad)
            sums_ref[2, :, strip] += fold_rows(normed * (gk - uk))
            sums_ref[3, :, strip] += fold_rows(normed * (gr - ur))
            firsts[0].append(gk[:1, :])
            firsts[1].append(gr[:1, :])
            weighted = grad * gain
            gk_ref[rows, strip] = weighted
            plain = plain + weighted
            along = along + weighted * unit
        plain, along = spread_mean(plain, width), spread_mean(along, width)
        for strip in strips(width):
            unit = (middle_ref[rows, strip] - mean) * scaled
            dmid = dres_ref[rows, strip] + scaled * (gk_ref[rows, strip] - plain - unit * along)
            dmid_ref[rows, strip] = dmid
            dtime_ref[rows, strip] = dmid.astype(BF)
        return tuple(tuple(f) for f in firsts)

    after = lax.fori_loop(0, steps, step, tuple(row_parts(next_ref, m) for m in (0, 1)), unroll=4)
    for m, values in enumerate(after):
        for strip, value in zip(strips(width), values):
            next_ref[m : m + 1, strip] = value


def middle_back(co, dkeys, drec, middle, dres, lead, vectors, weight, recept):
    tokens, width = middle.shape
    rows = tokens // 4
    wide = weight_width(weight)
    tall = pl.BlockSpec((rows, width), lambda i, co: (3 - i, 0))
    return pl.pallas_call(
        functools.partial(middle_back_kernel, layouts=[weight[0], recept[0]]),
        grid_spec=pltpu.PrefetchScalarGridSpec(
            num_scalar_prefetch=1,
            grid=(4,),
            in_specs=[
                pl.BlockSpec((rows, wide), lambda i, co: (3 - i, 0)),
                pl.BlockSpec((rows, wide), lambda i, co: (3 - i, 0)),
                tall,
                tall,
                tall,
                pl.BlockSpec((rows, LANES), lambda i, co: (3 - i, 0)),
                pl.BlockSpec(vectors.shape, lambda i, co: (0, 0)),
            ]
            + [anywhere()] * len(arrays_of(weight, recept)),
            out_specs=[tall] * 2 + [pl.BlockSpec((4, 8, width), lambda i, co: (0, 0, 0))],
            scratch_shapes=[pltpu.VMEM((rows, width), F32)] * 2
            + [pltpu.VMEM((8, width), F32)]
            + weight_scratch(weight, recept),
        ),
        out_shape=[
            jax.ShapeDtypeStruct((tokens, width), F32),
            jax.ShapeDtypeStruct((tokens, width), BF),
            jax.ShapeDtypeStruct((4, 8, width), F32),
        ],
        compiler_params=params(),
        cost_estimate=cost(8, 36 << 20),
    )(co, *dkeys, drec, middle, dres, lead, vectors, *arrays_of(weight, recept))


def time_back_kernel(
    co, dtime, key_ref, val_ref, rec_ref, pa_ref, pb_ref, vec, masks, *refs, layout,
):
    arrays, refs = take_refs(refs, layout)
    dkey_ref, dval_ref, drec_ref, sums_ref, dg_ref, ow, sems = refs
    j = pl.program_id(0)
    per_half = ow.shape[3] // TILE

    @pl.when(j == 0)
    def _():
        start_weight(co, arrays, ow, sems, layout)

    for which in (0, 1):

        @pl.when(j == which * per_half)
        def _(which=which):
            wait_weight(co, ow, sems, layout, which)

    half = co[4] ^ lax.div(j, per_half)
    columns = pl.ds(pl.multiple_of(lax.rem(j, per_half) * TILE, TILE), TILE)
    dg_ref[...] = dot(dtime[...], rows_of(ow, half, columns), NN)

    spread = (8, TILE)
    decay = jnp.broadcast_to(vec[2:3, :], spread)
    first = jnp.broadcast_to(vec[3:4, :], spread)
    r1, r2, r4, r8 = scan_rates(decay)
    left = 7.0 - lax.broadcasted_iota(jnp.int32, spread, 0).astype(F32)
    powers = jnp.exp(-left * jnp.exp(decay))

    def group(start, state):
        rows = pl.ds(start, 8)
        n1, n2, n4, nf, c0, ml = (repeated(masks[n, rows, :], TILE) for n in (0, 1, 2, 3, 4, 5))
        key, val, rec, dg = key_ref[rows, :], val_ref[rows, :], rec_ref[rows, :], dg_ref[rows, :]
        pa, pb = pa_ref[rows, :], pb_ref[rows, :]
        power = jnp.exp(key)
        bonus = jnp.exp(first + key)
        inverse = 1.0 / (pb + bonus)
        wkv = (pa + bonus * val) * inverse
        slope = dg * rec * inverse
        drec = dg * wkv * rec * (1.0 - rec)
        c1, c2, c4, cf, cl = n1 * r1, n2 * r2, n4 * r4, nf * powers, ml * r8
        found, starts = [], []
        for local, leaving in ((slope, state[0]), (-slope * wkv, state[1])):
            local = local + c1 * pltpu.roll(local, 7, 0)
            local = local + c2 * pltpu.roll(local, 6, 0)
            local = local + c4 * pltpu.roll(local, 4, 0)
            found.append(n1 * pltpu.roll(local, 7, 0) + cf * leaving)
            starts.append(c0 * jnp.broadcast_to(local[0:1, :], spread) + cl * leaving)
        later_a, later_b = found
        summand = bonus * slope * (val - wkv)
        dkey = power * (later_a * val + later_b) + summand
        dval = power * later_a + bonus * slope
        state = (
            starts[0],
            starts[1],
            state[2] + summand,
            state[3] + later_a * pa + later_b * pb,
        )
        return (dkey, dval, drec), state

    steps = key_ref.shape[0] // CHUNK

    def step(n, state):
        start = pl.multiple_of((steps - 1 - n) * CHUNK, CHUNK)
        lower, state = group(pl.multiple_of(start + 8, 8), state)
        upper, state = group(start, state)
        for up, low, out in zip(upper, lower, (dkey_ref, dval_ref, drec_ref)):
            out[pl.ds(start, CHUNK), :] = jnp.concatenate([up, low], axis=0).astype(BF)
        return state

    zero = jnp.zeros(spread, F32)
    _, _, first_sum, decay_sum = lax.fori_loop(0, steps, step, (zero,) * 4, unroll=4)
    sums_ref[0] = -r1 * jnp.exp(decay) * decay_sum
    sums_ref[1] = first_sum


def time_back(co, dtime, saved, vectors, masks, weight):
    tokens, width = dtime.shape
    half = width // 2
    tile = column_tile(half // TILE)
    block = pl.BlockSpec((tokens, TILE), tile)
    return pl.pallas_call(
        functools.partial(time_back_kernel, layout=weight[0]),
        grid_spec=pltpu.PrefetchScalarGridSpec(
            num_scalar_prefetch=1,
            grid=(width // TILE,),
            in_specs=[pl.BlockSpec((tokens, width), lambda j, co: (0, 0))]
            + [block] * 5
            + [
                pl.BlockSpec((vectors.shape[0], TILE), tile),
                pl.BlockSpec(masks.shape, lambda j, co: (0, 0, 0)),
            ]
            + [anywhere()] * len(weight[1]),
            out_specs=[block] * 3
            + [pl.BlockSpec((2, 8, TILE), lambda j, co: (0,) + tile(j, co))],
            scratch_shapes=[pltpu.VMEM((tokens, TILE), F32)] + weight_scratch(weight),
        ),
        out_shape=[jax.ShapeDtypeStruct((tokens, width), BF)] * 3
        + [jax.ShapeDtypeStruct((2, 8, width), F32)],
        compiler_params=params(),
        cost_estimate=cost(9, 34 << 20),
    )(co, dtime, *saved, vectors, masks, *weight[1])


def input_back_kernel(
    co, dkey, dval, drec, x_ref, dmid_ref, lead_ref, vec_ref, after_ref, *refs, layouts, part,
):
    count = 1 if part else 3
    before, refs = refs[:count], refs[count + 1 :]
    key_w, refs = take_refs(refs, layouts[0])
    val_w, refs = take_refs(refs, layouts[1])
    rec_w, refs = take_refs(refs, layouts[2])
    out_ref, totals_ref, next_ref, sums_ref, gk_ref, gv_ref, gr_ref, *scratch = refs
    wholes, sems = scratch[:3], scratch[3:]
    i = pl.program_id(0)

    @pl.when(i == 0)
    def _():
        for arrays, whole, sem, layout in zip((key_w, val_w, rec_w), wholes, sems, layouts):
            start_weight(co, arrays, whole, sem, layout)
        sums_ref[...] = jnp.zeros_like(sums_ref)
        next_ref[...] = after_ref[...]

    half = wholes[0].shape[3]
    for n, (grad, out) in enumerate(((dkey, gk_ref), (dval, gv_ref), (drec, gr_ref))):

        @pl.when(i == 0)
        def _(n=n):
            for which in (0, 1):
                wait_weight(co, wholes[n], sems[n], layouts[n], which)

        out[...] = dot(grad[:, :half], rows_of(wholes[n], 0), NT) + dot(
            grad[:, half:], rows_of(wholes[n], 1), NT
        )
    steps = x_ref.shape[0] // ROWS
    width = x_ref.shape[1]

    def step(n, after):
        rows = chunk_rows(steps - 1 - n)
        mean, scaled = norm_stats(lambda strip: x_ref[rows, strip].astype(F32), width)
        lead = lead_ref[rows, :]
        firsts = ([], [], [])
        plain, along = 0.0, 0.0
        for strip in strips(width):
            gain, bias = vec_ref[0:1, strip], vec_ref[1:2, strip]
            unit = (x_ref[rows, strip].astype(F32) - mean) * scaled
            normed = unit * gain + bias
            total = 0.0
            for m, part in enumerate((gk_ref, gv_ref, gr_ref)):
                mix = vec_ref[4 + m : 5 + m, strip]
                grad = part[rows, strip]
                up = move_up(grad, after[m][len(firsts[m])]) * lead
                total = total + grad * mix + up * (1.0 - mix)
                sums_ref[2 + m, :, strip] += fold_rows(normed * (grad - up))
                firsts[m].append(grad[:1, :])
            sums_ref[0, :, strip] += fold_rows(total * unit)
            sums_ref[1, :, strip] += fold_rows(total)
            weighted = total * gain
            gk_ref[rows, strip] = weighted
            plain = plain + weighted
            along = along + weighted * unit
        plain, along = spread_mean(plain, width), spread_mean(along, width)
        for strip in strips(width):
            unit = (x_ref[rows, strip].astype(F32) - mean) * scaled
            out_ref[rows, strip] = dmid_ref[rows, strip] + scaled * (
                gk_ref[rows, strip] - plain - unit * along
            )
        return tuple(tuple(f) for f in firsts)

    after = lax.fori_loop(0, steps, step, tuple(row_parts(next_ref, m) for m in range(3)), unroll=4)
    for m, values in enumerate(after):
        for strip, value in zip(strips(width), values):
            next_ref[m : m + 1, strip] = value

    @pl.when(i == pl.num_programs(0) - 1)
    def _():
        if part:
            totals_ref[...] = before[0][...]
        else:
            time_sums, channel_sums, loss_sums = before
            totals_ref[...] = jnp.zeros_like(totals_ref)
            for n in range(2):
                totals_ref[2 + n : 3 + n, :] = jnp.sum(time_sums[n], axis=0, keepdims=True)
            for n in range(4):
                totals_ref[7 + n : 8 + n, :] = jnp.sum(channel_sums[n], axis=0, keepdims=True)
            totals_ref[11:12, :] = jnp.sum(loss_sums[...], axis=0, keepdims=True)
        for n, row in enumerate((0, 1, 4, 5, 6)):
            totals_ref[row : row + 1, :] += jnp.sum(sums_ref[n], axis=0, keepdims=True)


def input_back(co, grads, x, dmid, lead, vectors, weights, part, after, before, found):
    tokens, width = x.shape
    rows = tokens // 4

    def at(i, co):
        return 3 - 2 * part - i, 0

    tall = pl.BlockSpec((rows, width), at)
    edge = pl.BlockSpec((8, width), lambda i, co: (0, 0))
    return pl.pallas_call(
        functools.partial(input_back_kernel, layouts=[w[0] for w in weights], part=part),
        grid_spec=pltpu.PrefetchScalarGridSpec(
            num_scalar_prefetch=1,
            grid=(2,),
            in_specs=[tall] * 5
            + [
                pl.BlockSpec((rows, LANES), at),
                pl.BlockSpec(vectors.shape, lambda i, co: (0, 0)),
                edge,
                *(
                    pl.BlockSpec(sums.shape, lambda i, co, dims=sums.ndim: (0,) * dims)
                    for sums in before
                ),
                anywhere(),
            ]
            + [anywhere()] * len(arrays_of(*weights)),
            out_specs=[tall, pl.BlockSpec((12, width), lambda i, co: (0, 0)), edge],
            scratch_shapes=[pltpu.VMEM((5, 8, width), F32)]
            + [pltpu.VMEM((rows, width), F32)] * 3 + weight_scratch(*weights),
        ),
        out_shape=[
            jax.ShapeDtypeStruct((tokens, width), F32),
            jax.ShapeDtypeStruct((12, width), F32),
            jax.ShapeDtypeStruct((8, width), F32),
        ],
        input_output_aliases={9 + len(before): 0},
        compiler_params=params(),
        cost_estimate=cost(4, 16 << 20),
    )(co, *grads, x, dmid, lead, vectors, after, *before, found, *arrays_of(*weights))


def seal(*values):
    return lax.optimization_barrier(values)


def swap(values, axis):
    return lax.ppermute(values, axis, SWAP)


class Gather:
    def __init__(self, shard, order, first=None):
        self.order, self.state, self.done = order, (shard,), 0
        if first is not None:
            self.state, self.done = (shard, first), 1

    def step(self):
        n = self.done
        if n and n < 4:
            self.state = (jnp.stack(self.state),)
        if n < 4:
            self.state += (swap(self.state[0], self.order[n]),)
        else:
            near, far = self.state
            self.state = (near, far, swap(near, "c"), swap(far, "c"))
        self.done += 1

    def part(self, first=0, skip=0, columns=None):
        assert self.done == 5
        return ("rel", (self.order, skip, None), first, columns or self.state[0].shape[-1]), self.state

    def part_with(self, others, base):
        assert self.done == 4
        return ("rel", (self.order, 0, base), 0, self.state[0].shape[-1]), (*self.state, others)


def weight_of(*parts):
    layouts, arrays = zip(*parts)
    return tuple(layouts), [array for group in arrays for array in group]


class Merged:
    def __init__(self, slots, order):
        self.order, self.state, self.done = order, tuple(slots), 0

    def step(self):
        n = self.done
        if n == 0:
            near, far, near_other, far_other = self.state
            self.state = (near, far, swap(far_other, "c"), swap(near_other, "c"))
        elif n == 1:
            near, far, far_got, near_got = self.state
            self.state = (near, near_got, swap(far + far_got, self.order[3]))
        elif n < 5:
            kept, sent = (
                sum(part[place].astype(F32) for part in self.state).astype(BF) for place in (0, 1)
            )
            self.state = (kept, swap(sent, self.order[4 - n]))
        self.done += 1

    def finish(self):
        assert self.done == 5
        return list(self.state[0].astype(F32) + self.state[1].astype(F32))


class Reduce:
    def __init__(self, slots, orders):
        self.orders, self.state, self.done = orders, tuple(slots), 0

    def step(self):
        n = self.done
        if n == 0:
            near, far, near_other, far_other = self.state
            self.state = (near, far, swap(far_other, "c"), swap(near_other, "c"))
        elif n == 1:
            near, far, far_got, near_got = self.state
            got = [swap(far[m] + far_got[m], order[3]) for m, order in enumerate(self.orders)]
            self.state = (near, near_got, *got)
        elif n == 2:
            near, near_got, *got = self.state
            self.keep([(near[m], near_got[m], part) for m, part in enumerate(got)], 2)
        elif n < 5:
            self.keep(self.state, 4 - n)
        self.done += 1

    def keep(self, parts, place):
        kept, sent = (
            [sum(v[at].astype(F32) for v in part).astype(BF) for part in parts] for at in (0, 1)
        )
        if place:
            sent = [swap(v, order[place]) for v, order in zip(sent, self.orders)]
            self.state = tuple(zip(kept, sent))
        else:
            self.state = (*kept, swap(jnp.stack(sent), self.orders[0][0]))

    def finish(self):
        assert self.done == 5
        *kept, got = self.state
        return [v.astype(F32) + got[n].astype(F32) for n, v in enumerate(kept)]


def step_all(*chains):
    for chain in chains:
        chain.step()


def seal_all(chains, *values):
    states, values = seal([chain.state for chain in chains], values)
    for chain, state in zip(chains, states):
        chain.state = tuple(state)
    return values


def pair_up(shard):
    got = swap(shard, "x")
    mine = lax.axis_index("x") == 0
    return jnp.where(mine, jnp.stack([shard, got]), jnp.stack([got, shard]))


def gather_plain(shard):
    whole = lax.all_gather(shard, ("w", "u", "y", "c"), axis=0, tiled=True)
    whole = lax.all_gather(whole, "x", axis=1, tiled=True)
    half = whole.shape[1] // 2
    return whole.reshape(16, SLOT, 2, half).transpose(0, 2, 1, 3)


def all_of(array, skip=0, columns=None):
    return (("abs", skip, 0, columns or array.shape[-1]),), [array]


def gather_vectors(own, first, last):
    for axis in EVERY[::-1][first:last]:
        got = swap(own, axis)
        mine = lax.axis_index(axis) == 0
        own = jnp.where(mine, jnp.concatenate([own, got], axis=1), jnp.concatenate([got, own], axis=1))
    return (own,)


def reduce_plain(slots, orders):
    return [reduce_one([part[n] for part in slots], order) for n, order in enumerate(orders)]


def reduce_merged(slots, order):
    count = slots[0].shape[3]
    return [reduce_one([part[:, :, :, n] for part in slots], order) for n in range(count)]


def scatter_rows(whole):
    whole = whole.reshape(-1, *whole.shape[1:])
    return lax.psum_scatter(whole, ("w", "u", "y", "c"), scatter_dimension=0)


def pair_sum(sums):
    side = lax.axis_index("x")
    sent = lax.dynamic_index_in_dim(sums, 1 - side, keepdims=False)
    kept = lax.dynamic_index_in_dim(sums, side, keepdims=False)
    return kept.astype(F32) + swap(sent, "x").astype(F32)


def reduce_blocks(blocks):
    whole = blocks.transpose(0, 2, 1, 3).reshape(16 * SLOT, -1)
    whole = lax.psum_scatter(whole, ("w", "u", "y", "c"), scatter_dimension=0, tiled=True)
    return lax.psum_scatter(whole, "x", scatter_dimension=1, tiled=True).astype(F32)


def reduce_one(slots, order):
    table = {}
    for which, index, rel in rel_slots(order):
        block = rel["w"] * 8 + rel["u"] * 4 + rel["y"] * 2 + rel["c"]
        table[block, rel["x"]] = slots[which][index]
    whole = jnp.concatenate(
        [jnp.concatenate([table[b, 0], table[b, 1]], axis=1) for b in range(16)], axis=0
    )
    whole = lax.psum_scatter(whole, ("w", "u", "y", "c"), scatter_dimension=0, tiled=True)
    return lax.psum_scatter(whole, "x", scatter_dimension=1, tiled=True).astype(F32)


def scan_masks(carry):
    c = carry.reshape(-1, 8)
    place = jnp.arange(8)[None, :]

    def behind(values, n):
        return jnp.where(place >= n, jnp.roll(values, n, axis=1), 0.0)

    def ahead(values, n):
        return jnp.where(place < 8 - n, jnp.roll(values, -n, axis=1), 0.0)

    m1 = jnp.where(place >= 1, c, 0.0)
    m2 = m1 * behind(m1, 1)
    m4 = m2 * behind(m2, 2)
    mf = jnp.cumprod(c, axis=1)
    ml = jnp.broadcast_to(mf[:, 7:], c.shape)
    n1 = ahead(c, 1)
    n2 = n1 * ahead(n1, 1)
    n4 = n2 * ahead(n2, 2)
    back = jnp.cumprod(c[:, ::-1], axis=1)[:, ::-1]
    nf = jnp.where(place < 7, jnp.roll(back, -1, axis=1), 1.0)
    c0 = jnp.broadcast_to(c[:, :1], c.shape)
    tables = (jnp.stack(t).reshape(len(t), -1, 1) for t in ((m1, m2, m4, mf, ml), (n1, n2, n4, nf, c0, ml)))
    return [jnp.broadcast_to(t, t.shape[:2] + (LANES,)) for t in tables]


def on_device(
    inputs,
    segments,
    teacher,
    first_norm_gain,
    first_norm_bias,
    time_decay,
    time_first,
    time_mix_key,
    time_mix_value,
    time_mix_recept,
    time_key,
    time_value,
    time_recept,
    time_output,
    second_norm_gain,
    second_norm_bias,
    channel_mix_key,
    channel_mix_recept,
    channel_key,
    channel_recept,
    channel_value,
):
    tokens, width = inputs.shape
    sizes = {a: lax.axis_size(a) for a in EVERY}
    devices = math.prod(sizes.values())
    fast = all(size == 2 for size in sizes.values())
    side = lax.axis_index("x")
    if fast:
        co = jnp.stack([lax.axis_index(a) for a in EVERY]).astype(jnp.int32)
    else:
        co = jnp.zeros((5,), jnp.int32)

    ids = lax.dynamic_slice_in_dim(segments, side * tokens, tokens)
    previous = jnp.concatenate([jnp.zeros((1,), jnp.int32), ids[:-1]])
    started = jnp.arange(tokens, dtype=jnp.int32) > 0
    carry = ((ids == previous) & (ids > 0) & started).astype(F32)
    valid = (ids > 0).astype(F32)
    lead = jnp.concatenate([carry[1:], jnp.zeros((1,), F32)])
    masks_down, masks_up = scan_masks(carry)
    carry, valid_rows, lead = (
        jnp.broadcast_to(v[:, None], (tokens, LANES)) for v in (carry, valid, lead)
    )

    flat = 0
    for axis in EVERY:
        flat = flat * sizes[axis] + lax.axis_index(axis)
    own_vectors = jnp.stack(
        [
            first_norm_gain,
            first_norm_bias,
            time_decay,
            time_first,
            time_mix_key,
            time_mix_value,
            time_mix_recept,
            second_norm_gain,
            second_norm_bias,
            channel_mix_key,
            channel_mix_recept,
        ]
    )
    piece = own_vectors.shape[1]
    counts = jnp.where(jnp.arange(piece) == 0, jnp.sum(valid), 0.0)[None, :]
    own_vectors = jnp.concatenate([own_vectors, counts, jnp.zeros((4, piece), F32)])
    output_t, value_t = time_output.T, channel_value.T

    if sizes["x"] == 2:
        mine = lax.dynamic_slice_in_dim(teacher, side * tokens, tokens)
        theirs = lax.dynamic_slice_in_dim(teacher, (1 - side) * tokens, tokens)
    else:
        mine, theirs = jnp.split(teacher, 2, axis=1)

    key_order, val_order, rec_order = three_orders = ("wxuy", "wuyx", "wyxu")
    half = width // 2
    if fast:
        wide = channel_key.shape[1]
        split = wide // 2
        chains = keys_a, keys_b, late_b = [
            Gather(channel_key[:, :split], "wuyx"),
            Gather(channel_key[:, split:], "wxuy"),
            Gather(value_t[:, split:], "wyxu"),
        ]
        first = jnp.concatenate([time_key, time_value, time_recept, output_t], axis=1)
        late = jnp.concatenate([value_t[:, :split], channel_recept], axis=1)
        first = lax.all_gather(first, EVERY)
        theirs = swap(theirs, "x")
        step_all(*chains)
        (vectors,) = gather_vectors(own_vectors, 0, 4)
        late, vectors, masks_down, masks_up, mine, theirs, carry, valid_rows, lead = seal_all(
            chains, late, vectors, masks_down, masks_up, mine, theirs, carry, valid_rows, lead
        )
        step_all(*chains)
        (vectors,) = gather_vectors(vectors, 4, 5)
        (vectors,) = seal_all(chains, vectors)
        step_all(*chains)
        mixed = first_mix(inputs, carry, vectors)
        (mixed,) = seal_all(chains, mixed)
        step_all(*chains)
        first, late, mixed = seal(first, late, mixed)
        late = lax.all_gather(late, EVERY).reshape(16, 2, SLOT, -1)
        first = first.reshape(16, 2, SLOT, -1)
        key_w, value_w, recept_w, output_w = (all_of(first, n * half, half) for n in range(4))
    else:
        early = gather_plain(channel_key)
        wide = early.shape[-1]
        split = wide // 2
        key_w, value_w, recept_w, output_w, crecept_w = (
            all_of(gather_plain(w))
            for w in (time_key, time_value, time_recept, output_t, channel_recept)
        )
        ckey_w = all_of(early)
        late = gather_plain(value_t)
        cvalue_w = [all_of(late, skip, split) for skip in (0, split)]
        vectors = lax.all_gather(own_vectors, EVERY, axis=1, tiled=True)
        mixed = first_mix(inputs, carry, vectors)

    *saved, gated = time_forward(co, mixed, (key_w, value_w, recept_w), vectors, masks_down)
    if fast:
        (gated,) = seal_all((keys_a, keys_b), gated)
        step_all(keys_a, keys_b)
    if sizes["x"] == 2 and not fast:
        theirs = swap(theirs, "x")
    middle, mixed_k2, mixed_r2 = time_output_step(co, gated, inputs, carry, vectors, output_w)
    if fast:
        middle, mixed_k2, mixed_r2 = seal_all(chains, middle, mixed_k2, mixed_r2)
        ckey_w = weight_of(keys_a.part(), keys_b.part(split))
        late_b.step()
    hidden, active = hidden_step(co, mixed_k2, ckey_w)
    if fast:
        hidden, late = seal_all((late_b,), hidden, late)
        cvalue_w = [all_of(late, 0, split), weight_of(late_b.part())]
        crecept_w = all_of(late, split, half)
    count = jnp.sum(vectors[11])
    scale = (float(tokens * devices) / count).reshape(1)
    kept, arrived, dres, dkv, drec2, loss_rows = result_step(
        co.at[4].set(side),
        scale,
        hidden,
        mixed_r2,
        middle,
        (mine, theirs),
        valid_rows,
        both_parts(cvalue_w, split),
        crecept_w,
    )

    if sizes["x"] == 2:
        arrived = swap(arrived, "x")

    def outputs_of(kept, arrived):
        return lax.dynamic_update_slice_in_dim(kept, arrived, (1 - side) * tokens, 0)

    back = functools.partial(channel_back, co)
    order_b, order_c = "wuyx", "wuyx"
    edge = jnp.zeros((8, width), F32)

    def input_back_part(dmix, part, after, before, found):
        return input_back(
            co, dmix, inputs, dmid, lead, vectors, (key_w, value_w, recept_w), part, after, before, found
        )

    if fast:
        dkey_0, *found, blocks = back(
            dkv, mixed_k2, hidden, active, (mixed_r2, drec2), cvalue_w[0], split, 0, order_b
        )
        group_v = Merged(found, order_b)
        dkv, arrived, blocks = seal_all((group_v,), dkv, arrived, blocks)
        blocks = scatter_rows(blocks)
        group_v.step()
        dkey_1, *found = back(dkv, mixed_k2, None, active, (), cvalue_w[1], split, 1, order_b)
        group_b = Merged(found, order_b)
        (dkey_1,) = seal_all((group_v, group_b), dkey_1)
        step_all(group_v, group_b)
        outputs = outputs_of(kept, arrived)
        dmid, dtime, sums2 = middle_back(
            co, (dkey_0, dkey_1), drec2, middle, dres, lead, vectors, ckey_w, crecept_w
        )
        (dtime,) = seal_all((group_v, group_b), dtime)
        step_all(group_v, group_b)
        found = weight_grads(co, ((dtime, gated, order_c),), merged=True)
        group_c = Merged(found, order_c)
        dtime, outputs = seal_all((group_c,), dtime, outputs)
        group_c.step()
        *dmix, sums_t = time_back(co, dtime, saved, vectors, masks_up, output_w)
        (dmix, dmid) = seal_all((group_v, group_b, group_c), dmix, dmid)
        step_all(group_v, group_b, group_c)
        found = weight_grads(co, [(m, d, order) for m, d, order in zip(mixed, dmix, three_orders)])
        group_t = Reduce(found, three_orders)
        (dmix,) = seal_all((group_v, group_b, group_c, group_t), dmix)
        step_all(group_v, group_b, group_c, group_t)
        found, totals, edge = input_back_part(dmix, 0, edge, (sums_t, sums2, loss_rows), dres)
        (dmix, edge, found) = seal_all((group_v, group_b, group_c, group_t), dmix, edge, found)
        step_all(group_b, group_c, group_t)
        input_grad, totals, _ = input_back_part(dmix, 1, edge, (totals,), found)
    else:
        dkey_0, *found, blocks = back(
            dkv, mixed_k2, hidden, active, (mixed_r2, drec2), cvalue_w[0], split, 0, order_b
        )
        (value_1,) = reduce_merged(found, order_b)
        dkey_1, *found = back(dkv, mixed_k2, None, active, (), cvalue_w[1], split, 1, order_b)
        (ckey_1,) = reduce_merged(found, order_b)
        value_0, ckey_0 = (
            reduce_blocks(blocks[..., n * split : (n + 1) * split]) for n in (0, 1)
        )
        crecept_g = reduce_blocks(blocks[..., 2 * split :])
        halves = 2 // sizes["x"]
        cvalue_g, ckey_g = (
            jnp.concatenate(
                [v.reshape(-1, halves, split) for v in pair], axis=2
            ).reshape(pair[0].shape[0], -1)
            for pair in ((value_0, value_1), (ckey_0, ckey_1))
        )
        dmid, dtime, sums2 = middle_back(
            co, (dkey_0, dkey_1), drec2, middle, dres, lead, vectors, ckey_w, crecept_w
        )
        found = weight_grads(co, ((dtime, gated, order_c),), merged=True)
        (output_g,) = reduce_merged(found, order_c)
        *dmix, sums_t = time_back(co, dtime, saved, vectors, masks_up, output_w)
        found = weight_grads(co, [(m, d, order) for m, d, order in zip(mixed, dmix, three_orders)])
        key_g, val_g, rec_g = reduce_plain(found, three_orders)
        found, totals, edge = input_back_part(dmix, 0, edge, (sums_t, sums2, loss_rows), dres)
        input_grad, totals, _ = input_back_part(dmix, 1, edge, (totals,), found)

    if fast:
        (totals,) = seal_all((group_b, group_c, group_t), totals)
        for axes in ("wc", "y", "xu"):
            step_all(*[group for group in (group_t, group_c, group_b) if group.done < 5])
            for axis in axes:
                totals = totals + swap(totals, axis)
            if axes == "y":
                blocks = pair_sum(blocks)
                totals, blocks = seal_all((group_b, group_c, group_t), totals, blocks)
                cvalue_g, ckey_g = (
                    jnp.concatenate([blocks[:, n * split : (n + 1) * split], found], axis=1)
                    for n, found in enumerate(group_v.finish() + group_b.finish())
                )
                cvalue_g = cvalue_g.T
            elif axes == "wc":
                totals, blocks = seal_all((group_c, group_t), totals, blocks)
        totals, cvalue_g, ckey_g = seal_all((group_t,), totals, cvalue_g, ckey_g)
        cvalue_g = cvalue_g.T
        (output_g,) = group_c.finish()
        crecept_g = blocks[:, 2 * split :]
        key_g, val_g, rec_g = group_t.finish()
    else:
        totals = lax.psum(totals, EVERY)
    loss = jnp.sum(totals[11]) / (2.0 * count * width)
    vector_g = lax.dynamic_slice_in_dim(totals, flat * piece, piece, axis=1)
    if not fast:
        outputs = (
            outputs_of(kept, arrived)
            if sizes["x"] == 2
            else jnp.concatenate([kept[:tokens], arrived], axis=1)
        )
    return (
        outputs,
        loss,
        input_grad,
        *[vector_g[n] for n in range(7)],
        key_g,
        val_g,
        rec_g,
        output_g.T,
        *[vector_g[n] for n in range(7, 11)],
        ckey_g,
        crecept_g,
        cvalue_g.T,
    )


def solution(mesh):
    fsdp, tp = mesh.shape["fsdp"], mesh.shape["tp"]
    two = 2 if fsdp % 8 == 0 else 1
    split = Mesh(mesh.devices.reshape(fsdp // two**3, two, two, two, tp), EVERY)
    rows = ("w", "u", "y", "c")
    vector = P(EVERY)
    matrix = P(rows, "x")
    turned = P("x", rows)
    tall = P(EVERY, None)
    return jax.shard_map(
        on_device,
        mesh=split,
        in_specs=(
            (tall, P(rows), matrix)
            + (vector,) * 7
            + (matrix, matrix, matrix, turned)
            + (vector,) * 4
            + (matrix, matrix, turned)
        ),
        out_specs=(
            (matrix, P(), tall)
            + (vector,) * 7
            + (matrix, matrix, matrix, turned)
            + (vector,) * 4
            + (matrix, matrix, turned)
        ),
        check_vma=False,
    )
```

```python
import functools
import itertools
import math

import jax
import jax.numpy as jnp
from jax import lax
from jax.experimental import pallas as pl
from jax.experimental.pallas import tpu as pltpu
from jax.sharding import Mesh
from jax.sharding import PartitionSpec as P

BF = jnp.bfloat16
F32 = jnp.float32
EPSILON = 1e-05
SLOT = 64
CHUNK = 16
VMEM_LIMIT = 58 << 20
EVERY = ("w", "u", "y", "c", "x")
SWAP = [(0, 1), (1, 0)]

NN = (((1,), (0,)), ((), ()))
NT = (((1,), (1,)), ((), ()))
TN = (((0,), (0,)), ((), ()))


def dot(left, right, dims):
    return lax.dot_general(left, right, dims, preferred_element_type=F32)


def rel_slots(order):
    for other_core in (0, 1):
        for last in (0, 1):
            for index in itertools.product((0, 1), repeat=3):
                rel = dict(zip(order[2::-1], index))
                rel[order[3]] = last
                rel["c"] = other_core
                yield other_core * 2 + last, index, rel


def slot_place(co, rel):
    at = {axis: co[n] ^ rel[axis] for n, axis in enumerate(EVERY)}
    return at["w"] * 8 + at["u"] * 4 + at["y"] * 2 + at["c"], at["x"]


def rows_of(whole, half, columns=slice(None)):
    found = whole[half, :, :, columns]
    return found.reshape(found.shape[0] * found.shape[1], found.shape[2])


def start_weight(co, refs, whole, sems, layout, halves=(0, 1)):
    refs = list(refs)
    for n, (kind, order, first, columns) in enumerate(layout):
        target = pl.ds(first, columns)
        if kind == "rel":
            order, skip, base = order
            if base is None:
                arrays, refs = refs[:4], refs[4:]
            else:
                arrays, refs = [*refs[:2], refs[2].at[base], refs[2].at[base + 1]], refs[3:]
            for which, index, rel in sorted(rel_slots(order), key=lambda slot: slot[2]["x"]):
                if rel["x"] in halves:
                    block, half = slot_place(co, rel)
                    pltpu.make_async_copy(
                        arrays[which].at[index + (slice(None), pl.ds(skip, columns))],
                        whole.at[half, block, :, target],
                        sems.at[2 * n + rel["x"]],
                    ).start()
        else:
            array, refs = refs[0], refs[1:]
            for rel_x in halves:
                half = co[4] ^ rel_x
                pltpu.make_async_copy(
                    array.at[:, half, :, pl.ds(order, columns)],
                    whole.at[half, :, :, target],
                    sems.at[2 * n + rel_x],
                ).start()


def wait_weight(co, whole, sems, layout, rel_x):
    for n, (_, _, first, columns) in enumerate(layout):
        held = whole.at[co[4] ^ rel_x, :, :, pl.ds(first, columns)]
        pltpu.make_async_copy(held, held, sems.at[2 * n + rel_x]).wait()


def take_refs(refs, layout):
    count = 0
    for kind, order, _, _ in layout:
        count += 1 if kind == "abs" else 4 if order[2] is None else 3
    return refs[:count], refs[count:]


def arrays_of(*weights):
    return [array for _, arrays in weights for array in arrays]


def both_parts(weights, split):
    (first, arrays_a), (second, arrays_b) = weights
    second = tuple((kind, order, at + split, columns) for kind, order, at, columns in second)
    return tuple(first) + second, list(arrays_a) + list(arrays_b)


def weight_width(weight):
    return sum(part[3] for part in weight[0])


def weight_scratch(*weights):
    return [pltpu.VMEM((2, 16, SLOT, weight_width(w)), BF) for w in weights] + [
        pltpu.SemaphoreType.DMA((2 * len(w[0]),)) for w in weights
    ]


ROWS = 32
LANES = 128


def strips(width):
    return [slice(n, n + LANES) for n in range(0, width, LANES)]


def row_parts(ref, row=0):
    return tuple(ref[row : row + 1, strip] for strip in strips(ref.shape[1]))


def chunk_rows(n):
    return pl.ds(pl.multiple_of(n * ROWS, ROWS), ROWS)


def spread_mean(total, width):
    return jnp.broadcast_to(jnp.sum(total, axis=1, keepdims=True) * (1.0 / width), total.shape)


def norm_stats(load, width):
    total = sum(load(strip) for strip in strips(width))
    mean = spread_mean(total, width)
    square = 0.0
    for strip in strips(width):
        centre = load(strip) - mean
        square = square + centre * centre
    return mean, lax.rsqrt(spread_mean(square, width) + EPSILON)


def first_row(shape):
    return lax.broadcasted_iota(jnp.int32, shape, 0) == 0


def last_row(shape):
    return lax.broadcasted_iota(jnp.int32, shape, 0) == shape[0] - 1


def move_down(values, before):
    return jnp.where(first_row(values.shape), before, pltpu.roll(values, 1, 0))


def move_up(values, after):
    return jnp.where(last_row(values.shape), after, pltpu.roll(values, values.shape[0] - 1, 0))


def fold_rows(values):
    return sum(values[n : n + 8] for n in range(0, values.shape[0], 8))


def params(semantics=1):
    return pltpu.CompilerParams(vmem_limit_bytes=VMEM_LIMIT)


def anywhere():
    return pl.BlockSpec(memory_space=pl.ANY)


COST = 0.01


def cost(units, traffic):
    return pl.CostEstimate(
        flops=int(units * 2 * 1024**3 * COST), bytes_accessed=int(traffic * COST), transcendentals=0
    )


def first_mix_kernel(x_ref, carry_ref, vec_ref, mk_ref, mv_ref, mr_ref, last):
    width = x_ref.shape[1]

    def step(n, before):
        rows = chunk_rows(n)
        mean, scaled = norm_stats(lambda strip: x_ref[rows, strip].astype(F32), width)
        carry = carry_ref[rows, :]
        lasts = []
        for strip in strips(width):
            unit = (x_ref[rows, strip].astype(F32) - mean) * scaled
            normed = unit * vec_ref[0:1, strip] + vec_ref[1:2, strip]
            behind = move_down(normed, before[len(lasts)]) * carry
            for m, out in ((4, mk_ref), (5, mv_ref), (6, mr_ref)):
                mix = vec_ref[m : m + 1, strip]
                out[rows, strip] = (normed * mix + behind * (1.0 - mix)).astype(BF)
            lasts.append(normed[ROWS - 1 :, :])
        return tuple(lasts)

    @pl.when(pl.program_id(0) == 0)
    def _():
        last[...] = jnp.zeros_like(last)

    lasts = lax.fori_loop(0, x_ref.shape[0] // ROWS, step, row_parts(last), unroll=4)
    for strip, value in zip(strips(width), lasts):
        last[0:1, strip] = value


def first_mix(x, carry, vectors):
    tokens, width = x.shape
    rows = tokens // 4
    tall = pl.BlockSpec((rows, width), lambda i: (i, 0))
    return pl.pallas_call(
        first_mix_kernel,
        grid=(4,),
        in_specs=[
            tall,
            pl.BlockSpec((rows, LANES), lambda i: (i, 0)),
            pl.BlockSpec(vectors.shape, lambda i: (0, 0)),
        ],
        out_specs=[tall] * 3,
        out_shape=[jax.ShapeDtypeStruct(x.shape, BF)] * 3,
        scratch_shapes=[pltpu.VMEM((8, width), F32)],
        compiler_params=params(),
        cost_estimate=cost(0, 8 << 20),
    )(x, carry, vectors)


FORWARD_TILE = 512
TILE = 256


def scan_rates(decay):
    speed = jnp.exp(decay)
    return [jnp.exp(-float(n) * speed) for n in (1, 2, 4, 8)]


def repeated(values, size):
    return jnp.concatenate([values] * (size // LANES), axis=1)


def time_forward_kernel(
    co, mk, mv, mr, vec, masks, *refs, layouts,
):
    key_w, refs = take_refs(refs, layouts[0])
    val_w, refs = take_refs(refs, layouts[1])
    rec_w, refs = take_refs(refs, layouts[2])
    key_ref, val_ref, rec_ref, pa_ref, pb_ref, gated_ref, *scratch = refs
    wholes, sems = scratch[:3], scratch[3:]
    j = pl.program_id(0)
    per_half = wholes[0].shape[3] // FORWARD_TILE

    @pl.when(j == 0)
    def _():
        for arrays, whole, sem, layout in zip((key_w, val_w, rec_w), wholes, sems, layouts):
            start_weight(co, arrays, whole, sem, layout)

    for which in (0, 1):

        @pl.when(j == which * per_half)
        def _(which=which):
            for whole, sem, layout in zip(wholes, sems, layouts):
                wait_weight(co, whole, sem, layout, which)

    half = co[4] ^ lax.div(j, per_half)
    columns = pl.ds(pl.multiple_of(lax.rem(j, per_half) * FORWARD_TILE, FORWARD_TILE), FORWARD_TILE)
    for mixed, whole, out in zip((mk, mv, mr), wholes, (key_ref, val_ref, rec_ref)):
        out[...] = dot(mixed[...], rows_of(whole, half, columns), NN)

    spread = (8, FORWARD_TILE)
    decay = jnp.broadcast_to(vec[2:3, :], spread)
    first = jnp.broadcast_to(vec[3:4, :], spread)
    r1, r2, r4, r8 = scan_rates(decay)
    powers = jnp.exp(-lax.broadcasted_iota(jnp.int32, spread, 0).astype(F32) * jnp.exp(decay))

    def group(start, state):
        rows = pl.ds(start, 8)
        key, val, pre = key_ref[rows, :], val_ref[rows, :], rec_ref[rows, :]
        m1, m2, m4, mf, ml = (repeated(masks[n, rows, :], FORWARD_TILE) for n in range(5))
        rec = 1.0 / (1.0 + jnp.exp(-pre))
        power = jnp.exp(key)
        bonus = jnp.exp(first + key)
        c1, c2, c4, cf, cl = m1 * r1, m2 * r2, m4 * r4, mf * powers, ml * r8
        priors, ends = [], []
        for local, entering in ((power * val, state[0]), (power, state[1])):
            local = local + c1 * pltpu.roll(local, 1, 0)
            local = local + c2 * pltpu.roll(local, 2, 0)
            local = local + c4 * pltpu.roll(local, 4, 0)
            priors.append(m1 * pltpu.roll(local, 1, 0) + cf * entering)
            ends.append(jnp.broadcast_to(local[7:8, :], spread) + cl * entering)
        wkv = (priors[0] + bonus * val) / (priors[1] + bonus)
        rec_ref[rows, :] = rec
        pa_ref[rows, :] = priors[0]
        pb_ref[rows, :] = priors[1]
        return rec * wkv, tuple(ends)

    def step(i, state):
        start = pl.multiple_of(i * CHUNK, CHUNK)
        upper, state = group(start, state)
        lower, state = group(pl.multiple_of(start + 8, 8), state)
        gated_ref[pl.ds(start, CHUNK), :] = jnp.concatenate([upper, lower], axis=0).astype(BF)
        return state

    zero = jnp.zeros(spread, F32)
    lax.fori_loop(0, key_ref.shape[0] // CHUNK, step, (zero, zero), unroll=4)


def time_forward(co, mixed, weights, vectors, masks):
    tokens, width = mixed[0].shape
    half = width // 2
    per_half = half // FORWARD_TILE

    def tile(j, co):
        return 0, (co[4] ^ lax.div(j, per_half)) * per_half + lax.rem(j, per_half)

    fixed = pl.BlockSpec((tokens, width), lambda j, co: (0, 0))
    block = pl.BlockSpec((tokens, FORWARD_TILE), tile)
    return pl.pallas_call(
        functools.partial(time_forward_kernel, layouts=[w[0] for w in weights]),
        grid_spec=pltpu.PrefetchScalarGridSpec(
            num_scalar_prefetch=1,
            grid=(width // FORWARD_TILE,),
            in_specs=[fixed] * 3
            + [
                pl.BlockSpec((vectors.shape[0], FORWARD_TILE), tile),
                pl.BlockSpec(masks.shape, lambda j, co: (0, 0, 0)),
            ]
            + [anywhere()] * len(arrays_of(*weights)),
            out_specs=[block] * 6,
            scratch_shapes=weight_scratch(*weights),
        ),
        out_shape=[jax.ShapeDtypeStruct((tokens, width), F32)] * 5
        + [jax.ShapeDtypeStruct((tokens, width), BF)],
        compiler_params=params(),
        cost_estimate=cost(8, 34 << 20),
    )(co, *mixed, vectors, masks, *arrays_of(*weights))


def time_output_kernel(
    co, gated, x_ref, carry_ref, vec_ref, *refs, layout
):
    arrays, refs = take_refs(refs, layout)
    middle_ref, mk_ref, mr_ref, last, ow, sems = refs
    i = pl.program_id(0)

    @pl.when(i == 0)
    def _():
        start_weight(co, arrays, ow, sems, layout)
        last[...] = jnp.zeros_like(last)
        for half in (0, 1):
            wait_weight(co, ow, sems, layout, half)

    half = ow.shape[3]
    middle_ref[...] = dot(gated[:, :half], rows_of(ow, 0), NT) + dot(
        gated[:, half:], rows_of(ow, 1), NT
    )
    width = x_ref.shape[1]

    def step(n, before):
        rows = chunk_rows(n)
        for strip in strips(width):
            middle_ref[rows, strip] += x_ref[rows, strip].astype(F32)
        mean, scaled = norm_stats(lambda strip: middle_ref[rows, strip], width)
        carry = carry_ref[rows, :]
        lasts = []
        for strip in strips(width):
            unit = (middle_ref[rows, strip] - mean) * scaled
            normed = unit * vec_ref[7:8, strip] + vec_ref[8:9, strip]
            behind = move_down(normed, before[len(lasts)]) * carry
            for m, out in ((9, mk_ref), (10, mr_ref)):
                mix = vec_ref[m : m + 1, strip]
                out[rows, strip] = (normed * mix + behind * (1.0 - mix)).astype(BF)
            lasts.append(normed[ROWS - 1 :, :])
        return tuple(lasts)

    lasts = lax.fori_loop(0, x_ref.shape[0] // ROWS, step, row_parts(last), unroll=4)
    for strip, value in zip(strips(width), lasts):
        last[0:1, strip] = value


def time_output_step(co, gated, x, carry, vectors, weight):
    tokens, width = x.shape
    rows = tokens // 4
    tall = pl.BlockSpec((rows, width), lambda i, co: (i, 0))
    return pl.pallas_call(
        functools.partial(time_output_kernel, layout=weight[0]),
        grid_spec=pltpu.PrefetchScalarGridSpec(
            num_scalar_prefetch=1,
            grid=(4,),
            in_specs=[
                tall,
                tall,
                pl.BlockSpec((rows, LANES), lambda i, co: (i, 0)),
                pl.BlockSpec(vectors.shape, lambda i, co: (0, 0)),
            ]
            + [anywhere()] * len(weight[1]),
            out_specs=[tall] * 3,
            scratch_shapes=[pltpu.VMEM((8, width), F32)] + weight_scratch(weight),
        ),
        out_shape=[jax.ShapeDtypeStruct((tokens, width), t) for t in (F32, BF, BF)],
        compiler_params=params(),
        cost_estimate=cost(3, 14 << 20),
    )(co, gated, x, carry, vectors, *weight[1])


WIDE = 512


def hidden_kernel(co, mk, *refs, layout):
    arrays, (hidden_ref, active_ref, whole, sems) = take_refs(refs, layout)
    j = pl.program_id(0)
    per_half = whole.shape[3] // WIDE

    @pl.when(j == 0)
    def _():
        start_weight(co, arrays, whole, sems, layout)

    for which in (0, 1):

        @pl.when(j == which * per_half)
        def _(which=which):
            wait_weight(co, whole, sems, layout, which)

    half = co[4] ^ lax.div(j, per_half)
    columns = pl.ds(pl.multiple_of(lax.rem(j, per_half) * WIDE, WIDE), WIDE)
    active = jnp.maximum(dot(mk[...], rows_of(whole, half, columns), NN), 0.0)
    active_ref[...] = active.astype(BF)
    hidden_ref[...] = (active * active).astype(BF)


def column_tile(per_half):
    return lambda j, co: (0, (co[4] ^ lax.div(j, per_half)) * per_half + lax.rem(j, per_half))


def hidden_step(co, mixed, weight):
    tokens, width = mixed.shape
    half = weight_width(weight)
    block = pl.BlockSpec((tokens, WIDE), column_tile(half // WIDE))
    return pl.pallas_call(
        functools.partial(hidden_kernel, layout=weight[0]),
        grid_spec=pltpu.PrefetchScalarGridSpec(
            num_scalar_prefetch=1,
            grid=(2 * half // WIDE,),
            in_specs=[pl.BlockSpec((tokens, width), lambda j, co: (0, 0))]
            + [anywhere()] * len(weight[1]),
            out_specs=[block] * 2,
            scratch_shapes=weight_scratch(weight),
        ),
        out_shape=[jax.ShapeDtypeStruct((tokens, 2 * half), BF)] * 2,
        compiler_params=params(),
        cost_estimate=cost(4.5, 26 << 20),
    )(co, mixed, *weight[1])


def result_kernel(
    co, scale, hidden, mr, middle_ref, mine_ref, theirs_ref, valid_ref, *refs, layouts,
):
    value_w, refs = take_refs(refs, layouts[0])
    recept_w, refs = take_refs(refs, layouts[1])
    *outs, dres_ref, dkv_ref, drec_ref, loss_ref, kv_ref, pre_ref, ww, rw, sems, sems_r = refs
    i = pl.program_id(0)

    @pl.when(i == 0)
    def _():
        start_weight(co, recept_w, rw, sems_r, layouts[1])
        start_weight(co, value_w, ww, sems, layouts[0])
        loss_ref[...] = jnp.zeros_like(loss_ref)
        for half in (0, 1):
            wait_weight(co, rw, sems_r, layouts[1], half)
            wait_weight(co, ww, sems, layouts[0], half)

    wide, narrow = ww.shape[3], rw.shape[3]
    pre_ref[:, :narrow] = dot(mr[...], rows_of(rw, 0), NN)
    pre_ref[:, narrow:] = dot(mr[...], rows_of(rw, 1), NN)
    kv_ref[...] = dot(hidden[:, :wide], rows_of(ww, 0), NT) + dot(
        hidden[:, wide:], rows_of(ww, 1), NT
    )
    factor = scale[0]

    def step(n, _):
        rows = chunk_rows(n)
        valid = valid_ref[rows, :]
        width = kv_ref.shape[1]
        for part, at in itertools.product((0, 1), range(0, width // 2, LANES)):
            first = pl.multiple_of((co[4] ^ part) * (width // 2) + at, LANES)
            strip = pl.ds(first, LANES)
            kv = kv_ref[rows, strip]
            rec = 1.0 / (1.0 + jnp.exp(-pre_ref[rows, strip]))
            result = middle_ref[rows, strip] + rec * kv
            outs[part][rows, at : at + LANES] = result.astype(BF)
            teacher = (mine_ref, theirs_ref)[part][rows, at : at + LANES].astype(F32)
            error = (result - teacher) * valid
            grad = error * factor
            dres_ref[rows, strip] = grad
            dkv = grad * rec
            dkv_ref[rows, strip] = dkv.astype(BF)
            drec_ref[rows, strip] = (dkv * kv * (1.0 - rec)).astype(BF)
            loss_ref[:, strip] += fold_rows(error * error)
        return 0

    lax.fori_loop(0, kv_ref.shape[0] // ROWS, step, 0, unroll=2)


def result_step(co, scale, hidden, mixed, middle, teachers, valid, weight, recept):
    tokens, width = mixed.shape
    rows = tokens // 4
    wide = weight_width(weight)
    tall = pl.BlockSpec((rows, width), lambda i, co, s: (i, 0))
    thin = pl.BlockSpec((rows, width // 2), lambda i, co, s: (i, 0))
    return pl.pallas_call(
        functools.partial(result_kernel, layouts=[weight[0], recept[0]]),
        grid_spec=pltpu.PrefetchScalarGridSpec(
            num_scalar_prefetch=2,
            grid=(4,),
            in_specs=[
                pl.BlockSpec((rows, 2 * wide), lambda i, co, s: (i, 0)),
                tall,
                tall,
                thin,
                thin,
                pl.BlockSpec((rows, LANES), lambda i, co, s: (i, 0)),
            ]
            + [anywhere()] * len(arrays_of(weight, recept)),
            out_specs=[pl.BlockSpec((rows, width // 2), lambda i, co, s: (co[4] * 4 + i, 0)), thin]
            + [tall] * 3
            + [pl.BlockSpec((8, width), lambda i, co, s: (0, 0))],
            scratch_shapes=[pltpu.VMEM((rows, width), F32)] * 2 + weight_scratch(weight, recept),
        ),
        out_shape=[jax.ShapeDtypeStruct((n * tokens, width // 2), BF) for n in (2, 1)]
        + [jax.ShapeDtypeStruct((tokens, width), t) for t in (F32, BF, BF)]
        + [jax.ShapeDtypeStruct((8, width), F32)],
        compiler_params=params(),
        cost_estimate=cost(7, 38 << 20),
    )(co, scale, hidden, mixed, middle, *teachers, valid, *arrays_of(weight, recept))


def start_grads(co, whole, targets, n, sem, order, which, merged):
    for array, index, rel in rel_slots(order):
        if rel["x"] == which:
            block, half = slot_place(co, rel)
            pltpu.make_async_copy(
                whole.at[half, block],
                targets[array].at[index + (n,) if merged else (n,) + index],
                sem,
            ).start()


def wait_bytes(held, sem):
    pltpu.make_async_copy(held, held, sem).wait()


def weight_grads_kernel(co, *refs, orders, merged):
    count = len(orders)
    models, chans, refs = refs[:count], refs[count : 2 * count], refs[2 * count :]
    targets, (held, given, whole, sems_in, sems_out) = refs[:4], refs[4:]
    half = whole.shape[4]
    loads = []
    for n in range(count):
        for m, (source, place) in enumerate(((models[n], held), (chans[n], given))):
            loads.append(pltpu.make_async_copy(source, place.at[n], sems_in.at[2 * n + m]))
            loads[-1].start()
    for n, order in enumerate(orders):
        for load in loads[2 * n : 2 * n + 2]:
            load.wait()

        def step(turn, _, n=n, order=order):
            at = co[4] ^ turn
            columns = pl.ds(pl.multiple_of(at * half, half), half)
            found = dot(held[n], given[n, :, columns], TN).astype(BF)
            whole[n, at] = found.reshape(16, SLOT, half)
            for which in (0, 1):

                @pl.when(turn == which)
                def _(which=which):
                    start_grads(co, whole.at[n], targets, n, sems_out.at[n], order, which, merged)

            return 0

        lax.fori_loop(0, 2, step, 0)
    for n in range(count):
        wait_bytes(whole.at[n], sems_out.at[n])


def weight_grads(co, pairs, merged=False):
    models, chans, orders = zip(*pairs)
    tokens, width = models[0].shape
    half = width // 2
    count = len(pairs)
    dims = (2, 2, 2, count) if merged else (count, 2, 2, 2)
    return pl.pallas_call(
        functools.partial(weight_grads_kernel, orders=orders, merged=merged),
        grid_spec=pltpu.PrefetchScalarGridSpec(
            num_scalar_prefetch=1,
            grid=(1,),
            in_specs=[anywhere()] * (2 * count),
            out_specs=[anywhere()] * 4,
            scratch_shapes=[
                pltpu.VMEM((count, tokens, width), BF),
                pltpu.VMEM((count, tokens, width), BF),
                pltpu.VMEM((count, 2, 16, SLOT, half), BF),
                pltpu.SemaphoreType.DMA((2 * count,)),
                pltpu.SemaphoreType.DMA((count,)),
            ],
        ),
        out_shape=[jax.ShapeDtypeStruct(dims + (SLOT, half), BF)] * 4,
        compiler_params=params(),
        cost_estimate=cost(count * 1.2, count * (6 << 20)),
    )(co, *models, *chans)


def channel_back_kernel(co, dkv, mixed, active, *refs, layout, part, order):
    if part == 0:
        (hidden, hidden_1, *recept), refs = refs[:4], refs[4:]
    arrays, refs = take_refs(refs, layout)
    dkey, targets, refs = refs[0], refs[1:5], refs[5:]
    if part == 0:
        blocks, *refs = refs
        grads, narrow, held, sems_held, *refs = refs
    other, sems, whole, sems_in = refs
    j = pl.program_id(0)
    wide = other.shape[3]
    per_half = wide // WIDE
    columns = pl.ds(pl.multiple_of(lax.rem(j, per_half) * WIDE, WIDE), WIDE)
    turn = lax.div(j, per_half)
    half = co[4] ^ turn

    @pl.when(j == 0)
    def _():
        start_weight(co, arrays, whole, sems_in, layout)
        if part == 0:
            for n in (0, 1):
                pltpu.make_async_copy(recept[n], held.at[n], sems_held.at[n]).start()

    def cut(values):
        return values.astype(BF).reshape(16, SLOT, WIDE)

    if part == 0:
        other[half, :, :, columns] = cut(dot(dkv[...], hidden_1[...], TN))
        grads[0, half, :, :, columns] = cut(dot(dkv[...], hidden[...], TN))

    for which in (0, 1):

        @pl.when(j == which * per_half)
        def _(which=which):
            wait_weight(co, whole, sems_in, layout, which)

    back = dot(dkv[...], rows_of(whole, half, columns), NN)
    back = (2.0 * active[...].astype(F32) * back).astype(BF)
    dkey[...] = back
    found = cut(dot(mixed[...], back, TN))
    if part == 0:
        grads[1, half, :, :, columns] = found
    else:
        other[half, :, :, columns] = found

    for which in (0, 1):

        @pl.when(j == (which + 1) * per_half - 1)
        def _(which=which):
            start_grads(co, other, targets, 0, sems.at[0], order, which, True)

    if part == 0:

        def narrow_copy(turn):
            return pltpu.make_async_copy(
                narrow.at[turn],
                blocks.at[:, co[4] ^ turn, :, pl.ds(2 * wide, narrow.shape[3])],
                sems.at[3 + turn],
            )

        for n in (0, 1):
            pltpu.make_async_copy(
                grads.at[n, half, :, :, columns],
                blocks.at[:, half, :, pl.ds(pl.multiple_of(n * wide + columns.start, WIDE), WIDE)],
                sems.at[1 + n],
            ).start()

        @pl.when(j == per_half - 1)
        def _():
            for n in (0, 1):
                pltpu.make_async_copy(recept[n], held.at[n], sems_held.at[n]).wait()

        @pl.when(lax.rem(j, per_half) == per_half - 1)
        def _():
            size = narrow.shape[3]
            found = dot(held[0], held[1, :, pl.ds(pl.multiple_of(half * size, size), size)], TN)
            narrow[turn] = found.astype(BF).reshape(16, SLOT, size)
            narrow_copy(turn).start()

    @pl.when(j == pl.num_programs(0) - 1)
    def _():
        wait_bytes(other, sems.at[0])
        if part == 0:
            for n in (0, 1):
                wait_bytes(grads.at[n], sems.at[1 + n])
                narrow_copy(n).wait()


def channel_back(co, dkv, mixed, hidden, active, recept, weight, half, part, order):
    tokens, width = dkv.shape
    per_half = half // WIDE
    stride = active.shape[1] // 2 // WIDE

    def tile_of(skip):
        return lambda j, co: (
            0,
            (co[4] ^ lax.div(j, per_half)) * stride + skip + lax.rem(j, per_half),
        )

    fixed = pl.BlockSpec((tokens, width), lambda j, co: (0, 0))
    own, other = (pl.BlockSpec((tokens, WIDE), tile_of(n * per_half)) for n in (part, 1 - part))
    first = part == 0
    return pl.pallas_call(
        functools.partial(channel_back_kernel, layout=weight[0], part=part, order=order),
        grid_spec=pltpu.PrefetchScalarGridSpec(
            num_scalar_prefetch=1,
            grid=(2 * per_half,),
            in_specs=[fixed, fixed, own]
            + [own, other, anywhere(), anywhere()] * first
            + [anywhere()] * len(weight[1]),
            out_specs=[pl.BlockSpec((tokens, WIDE), column_tile(per_half))]
            + [anywhere()] * (4 + first),
            scratch_shapes=[
                pltpu.VMEM((2, 2, 16, SLOT, half), BF),
                pltpu.VMEM((2, 16, SLOT, width // 2), BF),
                pltpu.VMEM((2, tokens, width), BF),
                pltpu.SemaphoreType.DMA((2,)),
            ]
            * first
            + [pltpu.VMEM((2, 16, SLOT, half), BF), pltpu.SemaphoreType.DMA((5,))]
            + weight_scratch(weight),
        ),
        out_shape=[jax.ShapeDtypeStruct((tokens, 2 * half), BF)]
        + [jax.ShapeDtypeStruct((2, 2, 2, 1, SLOT, half), BF)] * 4
        + [jax.ShapeDtypeStruct((16, 2, SLOT, 2 * half + width // 2), BF)] * first,
        compiler_params=params(),
        cost_estimate=cost(half / 512 * 3.3, half / 512 * (14 << 20)),
    )(co, dkv, mixed, active, *(hidden, hidden, *recept)[: 4 * first], *weight[1])


def middle_back_kernel(
    co, dkey_a, dkey_b, drec, middle_ref, dres_ref, lead_ref, vec_ref, *refs, layouts,
):
    key_w, refs = take_refs(refs, layouts[0])
    recept_w, refs = take_refs(refs, layouts[1])
    dmid_ref, dtime_ref, sums_ref, gk_ref, gr_ref, next_ref, ww, rw, sems, sems_r = refs
    i = pl.program_id(0)

    @pl.when(i == 0)
    def _():
        start_weight(co, recept_w, rw, sems_r, layouts[1])
        start_weight(co, key_w, ww, sems, layouts[0])
        sums_ref[...] = jnp.zeros_like(sums_ref)
        next_ref[...] = jnp.zeros_like(next_ref)
        for half in (0, 1):
            wait_weight(co, rw, sems_r, layouts[1], half)
            wait_weight(co, ww, sems, layouts[0], half)

    wide, narrow = dkey_a.shape[1] // 2, rw.shape[3]
    gr_ref[...] = dot(drec[:, :narrow], rows_of(rw, 0), NT) + dot(
        drec[:, narrow:], rows_of(rw, 1), NT
    )
    gk_ref[...] = sum(
        dot(
            part[:, half * wide : (half + 1) * wide],
            rows_of(ww, half, slice(n * wide, (n + 1) * wide)),
            NT,
        )
        for n, part in enumerate((dkey_a, dkey_b))
        for half in (0, 1)
    )
    steps = middle_ref.shape[0] // ROWS
    width = middle_ref.shape[1]

    def step(n, after):
        rows = chunk_rows(steps - 1 - n)
        mean, scaled = norm_stats(lambda strip: middle_ref[rows, strip], width)
        lead = lead_ref[rows, :]
        firsts = ([], [])
        plain, along = 0.0, 0.0
        for strip in strips(width):
            gain, bias, mix_k, mix_r = (vec_ref[m : m + 1, strip] for m in (7, 8, 9, 10))
            unit = (middle_ref[rows, strip] - mean) * scaled
            normed = unit * gain + bias
            gk, gr = gk_ref[rows, strip], gr_ref[rows, strip]
            uk = move_up(gk, after[0][len(firsts[0])]) * lead
            ur = move_up(gr, after[1][len(firsts[0])]) * lead
            grad = gk * mix_k + gr * mix_r + uk * (1.0 - mix_k) + ur * (1.0 - mix_r)
            sums_ref[0, :, strip] += fold_rows(grad * unit)
            sums_ref[1, :, strip] += fold_rows(grad)
            sums_ref[2, :, strip] += fold_rows(normed * (gk - uk))
            sums_ref[3, :, strip] += fold_rows(normed * (gr - ur))
            firsts[0].append(gk[:1, :])
            firsts[1].append(gr[:1, :])
            weighted = grad * gain
            gk_ref[rows, strip] = weighted
            plain = plain + weighted
            along = along + weighted * unit
        plain, along = spread_mean(plain, width), spread_mean(along, width)
        for strip in strips(width):
            unit = (middle_ref[rows, strip] - mean) * scaled
            dmid = dres_ref[rows, strip] + scaled * (gk_ref[rows, strip] - plain - unit * along)
            dmid_ref[rows, strip] = dmid
            dtime_ref[rows, strip] = dmid.astype(BF)
        return tuple(tuple(f) for f in firsts)

    after = lax.fori_loop(0, steps, step, tuple(row_parts(next_ref, m) for m in (0, 1)), unroll=4)
    for m, values in enumerate(after):
        for strip, value in zip(strips(width), values):
            next_ref[m : m + 1, strip] = value


def middle_back(co, dkeys, drec, middle, dres, lead, vectors, weight, recept):
    tokens, width = middle.shape
    rows = tokens // 4
    wide = weight_width(weight)
    tall = pl.BlockSpec((rows, width), lambda i, co: (3 - i, 0))
    return pl.pallas_call(
        functools.partial(middle_back_kernel, layouts=[weight[0], recept[0]]),
        grid_spec=pltpu.PrefetchScalarGridSpec(
            num_scalar_prefetch=1,
            grid=(4,),
            in_specs=[
                pl.BlockSpec((rows, wide), lambda i, co: (3 - i, 0)),
                pl.BlockSpec((rows, wide), lambda i, co: (3 - i, 0)),
                tall,
                tall,
                tall,
                pl.BlockSpec((rows, LANES), lambda i, co: (3 - i, 0)),
                pl.BlockSpec(vectors.shape, lambda i, co: (0, 0)),
            ]
            + [anywhere()] * len(arrays_of(weight, recept)),
            out_specs=[tall] * 2 + [pl.BlockSpec((4, 8, width), lambda i, co: (0, 0, 0))],
            scratch_shapes=[pltpu.VMEM((rows, width), F32)] * 2
            + [pltpu.VMEM((8, width), F32)]
            + weight_scratch(weight, recept),
        ),
        out_shape=[
            jax.ShapeDtypeStruct((tokens, width), F32),
            jax.ShapeDtypeStruct((tokens, width), BF),
            jax.ShapeDtypeStruct((4, 8, width), F32),
        ],
        compiler_params=params(),
        cost_estimate=cost(8, 36 << 20),
    )(co, *dkeys, drec, middle, dres, lead, vectors, *arrays_of(weight, recept))


def time_back_kernel(
    co, dtime, key_ref, val_ref, rec_ref, pa_ref, pb_ref, vec, masks, *refs, layout,
):
    arrays, refs = take_refs(refs, layout)
    dkey_ref, dval_ref, drec_ref, sums_ref, dg_ref, ow, sems = refs
    j = pl.program_id(0)
    per_half = ow.shape[3] // TILE

    @pl.when(j == 0)
    def _():
        start_weight(co, arrays, ow, sems, layout)

    for which in (0, 1):

        @pl.when(j == which * per_half)
        def _(which=which):
            wait_weight(co, ow, sems, layout, which)

    half = co[4] ^ lax.div(j, per_half)
    columns = pl.ds(pl.multiple_of(lax.rem(j, per_half) * TILE, TILE), TILE)
    dg_ref[...] = dot(dtime[...], rows_of(ow, half, columns), NN)

    spread = (8, TILE)
    decay = jnp.broadcast_to(vec[2:3, :], spread)
    first = jnp.broadcast_to(vec[3:4, :], spread)
    r1, r2, r4, r8 = scan_rates(decay)
    left = 7.0 - lax.broadcasted_iota(jnp.int32, spread, 0).astype(F32)
    powers = jnp.exp(-left * jnp.exp(decay))

    def group(start, state):
        rows = pl.ds(start, 8)
        n1, n2, n4, nf, c0, ml = (repeated(masks[n, rows, :], TILE) for n in (0, 1, 2, 3, 4, 5))
        key, val, rec, dg = key_ref[rows, :], val_ref[rows, :], rec_ref[rows, :], dg_ref[rows, :]
        pa, pb = pa_ref[rows, :], pb_ref[rows, :]
        power = jnp.exp(key)
        bonus = jnp.exp(first + key)
        inverse = 1.0 / (pb + bonus)
        wkv = (pa + bonus * val) * inverse
        slope = dg * rec * inverse
        drec = dg * wkv * rec * (1.0 - rec)
        c1, c2, c4, cf, cl = n1 * r1, n2 * r2, n4 * r4, nf * powers, ml * r8
        found, starts = [], []
        for local, leaving in ((slope, state[0]), (-slope * wkv, state[1])):
            local = local + c1 * pltpu.roll(local, 7, 0)
            local = local + c2 * pltpu.roll(local, 6, 0)
            local = local + c4 * pltpu.roll(local, 4, 0)
            found.append(n1 * pltpu.roll(local, 7, 0) + cf * leaving)
            starts.append(c0 * jnp.broadcast_to(local[0:1, :], spread) + cl * leaving)
        later_a, later_b = found
        summand = bonus * slope * (val - wkv)
        dkey = power * (later_a * val + later_b) + summand
        dval = power * later_a + bonus * slope
        state = (
            starts[0],
            starts[1],
            state[2] + summand,
            state[3] + later_a * pa + later_b * pb,
        )
        return (dkey, dval, drec), state

    steps = key_ref.shape[0] // CHUNK

    def step(n, state):
        start = pl.multiple_of((steps - 1 - n) * CHUNK, CHUNK)
        lower, state = group(pl.multiple_of(start + 8, 8), state)
        upper, state = group(start, state)
        for up, low, out in zip(upper, lower, (dkey_ref, dval_ref, drec_ref)):
            out[pl.ds(start, CHUNK), :] = jnp.concatenate([up, low], axis=0).astype(BF)
        return state

    zero = jnp.zeros(spread, F32)
    _, _, first_sum, decay_sum = lax.fori_loop(0, steps, step, (zero,) * 4, unroll=4)
    sums_ref[0] = -r1 * jnp.exp(decay) * decay_sum
    sums_ref[1] = first_sum


def time_back(co, dtime, saved, vectors, masks, weight):
    tokens, width = dtime.shape
    half = width // 2
    tile = column_tile(half // TILE)
    block = pl.BlockSpec((tokens, TILE), tile)
    return pl.pallas_call(
        functools.partial(time_back_kernel, layout=weight[0]),
        grid_spec=pltpu.PrefetchScalarGridSpec(
            num_scalar_prefetch=1,
            grid=(width // TILE,),
            in_specs=[pl.BlockSpec((tokens, width), lambda j, co: (0, 0))]
            + [block] * 5
            + [
                pl.BlockSpec((vectors.shape[0], TILE), tile),
                pl.BlockSpec(masks.shape, lambda j, co: (0, 0, 0)),
            ]
            + [anywhere()] * len(weight[1]),
            out_specs=[block] * 3
            + [pl.BlockSpec((2, 8, TILE), lambda j, co: (0,) + tile(j, co))],
            scratch_shapes=[pltpu.VMEM((tokens, TILE), F32)] + weight_scratch(weight),
        ),
        out_shape=[jax.ShapeDtypeStruct((tokens, width), BF)] * 3
        + [jax.ShapeDtypeStruct((2, 8, width), F32)],
        compiler_params=params(),
        cost_estimate=cost(9, 34 << 20),
    )(co, dtime, *saved, vectors, masks, *weight[1])


def input_back_kernel(
    co, dkey, dval, drec, x_ref, dmid_ref, lead_ref, vec_ref, after_ref, *refs, layouts, part,
):
    count = 1 if part else 3
    before, refs = refs[:count], refs[count + 1 :]
    key_w, refs = take_refs(refs, layouts[0])
    val_w, refs = take_refs(refs, layouts[1])
    rec_w, refs = take_refs(refs, layouts[2])
    out_ref, totals_ref, next_ref, sums_ref, gk_ref, gv_ref, gr_ref, *scratch = refs
    wholes, sems = scratch[:3], scratch[3:]
    i = pl.program_id(0)

    @pl.when(i == 0)
    def _():
        for arrays, whole, sem, layout in zip((key_w, val_w, rec_w), wholes, sems, layouts):
            start_weight(co, arrays, whole, sem, layout)
        sums_ref[...] = jnp.zeros_like(sums_ref)
        next_ref[...] = after_ref[...]

    half = wholes[0].shape[3]
    for n, (grad, out) in enumerate(((dkey, gk_ref), (dval, gv_ref), (drec, gr_ref))):

        @pl.when(i == 0)
        def _(n=n):
            for which in (0, 1):
                wait_weight(co, wholes[n], sems[n], layouts[n], which)

        out[...] = dot(grad[:, :half], rows_of(wholes[n], 0), NT) + dot(
            grad[:, half:], rows_of(wholes[n], 1), NT
        )
    steps = x_ref.shape[0] // ROWS
    width = x_ref.shape[1]

    def step(n, after):
        rows = chunk_rows(steps - 1 - n)
        mean, scaled = norm_stats(lambda strip: x_ref[rows, strip].astype(F32), width)
        lead = lead_ref[rows, :]
        firsts = ([], [], [])
        plain, along = 0.0, 0.0
        for strip in strips(width):
            gain, bias = vec_ref[0:1, strip], vec_ref[1:2, strip]
            unit = (x_ref[rows, strip].astype(F32) - mean) * scaled
            normed = unit * gain + bias
            total = 0.0
            for m, part in enumerate((gk_ref, gv_ref, gr_ref)):
                mix = vec_ref[4 + m : 5 + m, strip]
                grad = part[rows, strip]
                up = move_up(grad, after[m][len(firsts[m])]) * lead
                total = total + grad * mix + up * (1.0 - mix)
                sums_ref[2 + m, :, strip] += fold_rows(normed * (grad - up))
                firsts[m].append(grad[:1, :])
            sums_ref[0, :, strip] += fold_rows(total * unit)
            sums_ref[1, :, strip] += fold_rows(total)
            weighted = total * gain
            gk_ref[rows, strip] = weighted
            plain = plain + weighted
            along = along + weighted * unit
        plain, along = spread_mean(plain, width), spread_mean(along, width)
        for strip in strips(width):
            unit = (x_ref[rows, strip].astype(F32) - mean) * scaled
            out_ref[rows, strip] = dmid_ref[rows, strip] + scaled * (
                gk_ref[rows, strip] - plain - unit * along
            )
        return tuple(tuple(f) for f in firsts)

    after = lax.fori_loop(0, steps, step, tuple(row_parts(next_ref, m) for m in range(3)), unroll=4)
    for m, values in enumerate(after):
        for strip, value in zip(strips(width), values):
            next_ref[m : m + 1, strip] = value

    @pl.when(i == pl.num_programs(0) - 1)
    def _():
        if part:
            totals_ref[...] = before[0][...]
        else:
            time_sums, channel_sums, loss_sums = before
            totals_ref[...] = jnp.zeros_like(totals_ref)
            for n in range(2):
                totals_ref[2 + n : 3 + n, :] = jnp.sum(time_sums[n], axis=0, keepdims=True)
            for n in range(4):
                totals_ref[7 + n : 8 + n, :] = jnp.sum(channel_sums[n], axis=0, keepdims=True)
            totals_ref[11:12, :] = jnp.sum(loss_sums[...], axis=0, keepdims=True)
        for n, row in enumerate((0, 1, 4, 5, 6)):
            totals_ref[row : row + 1, :] += jnp.sum(sums_ref[n], axis=0, keepdims=True)


def input_back(co, grads, x, dmid, lead, vectors, weights, part, after, before, found):
    tokens, width = x.shape
    rows = tokens // 4

    def at(i, co):
        return 3 - 2 * part - i, 0

    tall = pl.BlockSpec((rows, width), at)
    edge = pl.BlockSpec((8, width), lambda i, co: (0, 0))
    return pl.pallas_call(
        functools.partial(input_back_kernel, layouts=[w[0] for w in weights], part=part),
        grid_spec=pltpu.PrefetchScalarGridSpec(
            num_scalar_prefetch=1,
            grid=(2,),
            in_specs=[tall] * 5
            + [
                pl.BlockSpec((rows, LANES), at),
                pl.BlockSpec(vectors.shape, lambda i, co: (0, 0)),
                edge,
                *(
                    pl.BlockSpec(sums.shape, lambda i, co, dims=sums.ndim: (0,) * dims)
                    for sums in before
                ),
                anywhere(),
            ]
            + [anywhere()] * len(arrays_of(*weights)),
            out_specs=[tall, pl.BlockSpec((12, width), lambda i, co: (0, 0)), edge],
            scratch_shapes=[pltpu.VMEM((5, 8, width), F32)]
            + [pltpu.VMEM((rows, width), F32)] * 3 + weight_scratch(*weights),
        ),
        out_shape=[
            jax.ShapeDtypeStruct((tokens, width), F32),
            jax.ShapeDtypeStruct((12, width), F32),
            jax.ShapeDtypeStruct((8, width), F32),
        ],
        input_output_aliases={9 + len(before): 0},
        compiler_params=params(),
        cost_estimate=cost(4, 16 << 20),
    )(co, *grads, x, dmid, lead, vectors, after, *before, found, *arrays_of(*weights))


def seal(*values):
    return lax.optimization_barrier(values)


def swap(values, axis):
    return lax.ppermute(values, axis, SWAP)


class Gather:
    def __init__(self, shard, order, first=None):
        self.order, self.state, self.done = order, (shard,), 0
        if first is not None:
            self.state, self.done = (shard, first), 1

    def step(self):
        n = self.done
        if n and n < 4:
            self.state = (jnp.stack(self.state),)
        if n < 4:
            self.state += (swap(self.state[0], self.order[n]),)
        else:
            near, far = self.state
            self.state = (near, far, swap(near, "c"), swap(far, "c"))
        self.done += 1

    def part(self, first=0, skip=0, columns=None):
        assert self.done == 5
        return ("rel", (self.order, skip, None), first, columns or self.state[0].shape[-1]), self.state

    def part_with(self, others, base):
        assert self.done == 4
        return ("rel", (self.order, 0, base), 0, self.state[0].shape[-1]), (*self.state, others)


def weight_of(*parts):
    layouts, arrays = zip(*parts)
    return tuple(layouts), [array for group in arrays for array in group]


class Merged:
    def __init__(self, slots, order):
        self.order, self.state, self.done = order, tuple(slots), 0

    def step(self):
        n = self.done
        if n == 0:
            near, far, near_other, far_other = self.state
            self.state = (near, far, swap(far_other, "c"), swap(near_other, "c"))
        elif n == 1:
            near, far, far_got, near_got = self.state
            self.state = (near, near_got, swap(far + far_got, self.order[3]))
        elif n < 5:
            kept, sent = (
                sum(part[place].astype(F32) for part in self.state).astype(BF) for place in (0, 1)
            )
            self.state = (kept, swap(sent, self.order[4 - n]))
        self.done += 1

    def finish(self):
        assert self.done == 5
        return list(self.state[0].astype(F32) + self.state[1].astype(F32))


class Reduce:
    def __init__(self, slots, orders):
        self.orders, self.state, self.done = orders, tuple(slots), 0

    def step(self):
        n = self.done
        if n == 0:
            near, far, near_other, far_other = self.state
            self.state = (near, far, swap(far_other, "c"), swap(near_other, "c"))
        elif n == 1:
            near, far, far_got, near_got = self.state
            got = [swap(far[m] + far_got[m], order[3]) for m, order in enumerate(self.orders)]
            self.state = (near, near_got, *got)
        elif n == 2:
            near, near_got, *got = self.state
            self.keep([(near[m], near_got[m], part) for m, part in enumerate(got)], 2)
        elif n < 5:
            self.keep(self.state, 4 - n)
        self.done += 1

    def keep(self, parts, place):
        kept, sent = (
            [sum(v[at].astype(F32) for v in part).astype(BF) for part in parts] for at in (0, 1)
        )
        if place:
            sent = [swap(v, order[place]) for v, order in zip(sent, self.orders)]
            self.state = tuple(zip(kept, sent))
        else:
            self.state = (*kept, swap(jnp.stack(sent), self.orders[0][0]))

    def finish(self):
        assert self.done == 5
        *kept, got = self.state
        return [v.astype(F32) + got[n].astype(F32) for n, v in enumerate(kept)]


def step_all(*chains):
    for chain in chains:
        chain.step()


def seal_all(chains, *values):
    states, values = seal([chain.state for chain in chains], values)
    for chain, state in zip(chains, states):
        chain.state = tuple(state)
    return values


def pair_up(shard):
    got = swap(shard, "x")
    mine = lax.axis_index("x") == 0
    return jnp.where(mine, jnp.stack([shard, got]), jnp.stack([got, shard]))


def gather_plain(shard):
    whole = lax.all_gather(shard, ("w", "u", "y", "c"), axis=0, tiled=True)
    whole = lax.all_gather(whole, "x", axis=1, tiled=True)
    half = whole.shape[1] // 2
    return whole.reshape(16, SLOT, 2, half).transpose(0, 2, 1, 3)


def all_of(array, skip=0, columns=None):
    return (("abs", skip, 0, columns or array.shape[-1]),), [array]


def gather_vectors(own, first, last):
    for axis in EVERY[::-1][first:last]:
        got = swap(own, axis)
        mine = lax.axis_index(axis) == 0
        own = jnp.where(mine, jnp.concatenate([own, got], axis=1), jnp.concatenate([got, own], axis=1))
    return (own,)


def reduce_plain(slots, orders):
    return [reduce_one([part[n] for part in slots], order) for n, order in enumerate(orders)]


def reduce_merged(slots, order):
    count = slots[0].shape[3]
    return [reduce_one([part[:, :, :, n] for part in slots], order) for n in range(count)]


def scatter_rows(whole):
    whole = whole.reshape(-1, *whole.shape[1:])
    return lax.psum_scatter(whole, ("w", "u", "y", "c"), scatter_dimension=0)


def pair_sum(sums):
    side = lax.axis_index("x")
    sent = lax.dynamic_index_in_dim(sums, 1 - side, keepdims=False)
    kept = lax.dynamic_index_in_dim(sums, side, keepdims=False)
    return kept.astype(F32) + swap(sent, "x").astype(F32)


def reduce_blocks(blocks):
    whole = blocks.transpose(0, 2, 1, 3).reshape(16 * SLOT, -1)
    whole = lax.psum_scatter(whole, ("w", "u", "y", "c"), scatter_dimension=0, tiled=True)
    return lax.psum_scatter(whole, "x", scatter_dimension=1, tiled=True).astype(F32)


def reduce_one(slots, order):
    table = {}
    for which, index, rel in rel_slots(order):
        block = rel["w"] * 8 + rel["u"] * 4 + rel["y"] * 2 + rel["c"]
        table[block, rel["x"]] = slots[which][index]
    whole = jnp.concatenate(
        [jnp.concatenate([table[b, 0], table[b, 1]], axis=1) for b in range(16)], axis=0
    )
    whole = lax.psum_scatter(whole, ("w", "u", "y", "c"), scatter_dimension=0, tiled=True)
    return lax.psum_scatter(whole, "x", scatter_dimension=1, tiled=True).astype(F32)


def scan_masks(carry):
    c = carry.reshape(-1, 8)
    place = jnp.arange(8)[None, :]

    def behind(values, n):
        return jnp.where(place >= n, jnp.roll(values, n, axis=1), 0.0)

    def ahead(values, n):
        return jnp.where(place < 8 - n, jnp.roll(values, -n, axis=1), 0.0)

    m1 = jnp.where(place >= 1, c, 0.0)
    m2 = m1 * behind(m1, 1)
    m4 = m2 * behind(m2, 2)
    mf = jnp.cumprod(c, axis=1)
    ml = jnp.broadcast_to(mf[:, 7:], c.shape)
    n1 = ahead(c, 1)
    n2 = n1 * ahead(n1, 1)
    n4 = n2 * ahead(n2, 2)
    back = jnp.cumprod(c[:, ::-1], axis=1)[:, ::-1]
    nf = jnp.where(place < 7, jnp.roll(back, -1, axis=1), 1.0)
    c0 = jnp.broadcast_to(c[:, :1], c.shape)
    tables = (jnp.stack(t).reshape(len(t), -1, 1) for t in ((m1, m2, m4, mf, ml), (n1, n2, n4, nf, c0, ml)))
    return [jnp.broadcast_to(t, t.shape[:2] + (LANES,)) for t in tables]


def on_device(
    inputs,
    segments,
    teacher,
    first_norm_gain,
    first_norm_bias,
    time_decay,
    time_first,
    time_mix_key,
    time_mix_value,
    time_mix_recept,
    time_key,
    time_value,
    time_recept,
    time_output,
    second_norm_gain,
    second_norm_bias,
    channel_mix_key,
    channel_mix_recept,
    channel_key,
    channel_recept,
    channel_value,
):
    tokens, width = inputs.shape
    sizes = {a: lax.axis_size(a) for a in EVERY}
    devices = math.prod(sizes.values())
    fast = all(size == 2 for size in sizes.values())
    side = lax.axis_index("x")
    if fast:
        co = jnp.stack([lax.axis_index(a) for a in EVERY]).astype(jnp.int32)
    else:
        co = jnp.zeros((5,), jnp.int32)

    ids = lax.dynamic_slice_in_dim(segments, side * tokens, tokens)
    previous = jnp.concatenate([jnp.zeros((1,), jnp.int32), ids[:-1]])
    started = jnp.arange(tokens, dtype=jnp.int32) > 0
    carry = ((ids == previous) & (ids > 0) & started).astype(F32)
    valid = (ids > 0).astype(F32)
    lead = jnp.concatenate([carry[1:], jnp.zeros((1,), F32)])
    masks_down, masks_up = scan_masks(carry)
    carry, valid_rows, lead = (
        jnp.broadcast_to(v[:, None], (tokens, LANES)) for v in (carry, valid, lead)
    )

    flat = 0
    for axis in EVERY:
        flat = flat * sizes[axis] + lax.axis_index(axis)
    own_vectors = jnp.stack(
        [
            first_norm_gain,
            first_norm_bias,
            time_decay,
            time_first,
            time_mix_key,
            time_mix_value,
            time_mix_recept,
            second_norm_gain,
            second_norm_bias,
            channel_mix_key,
            channel_mix_recept,
        ]
    )
    piece = own_vectors.shape[1]
    counts = jnp.where(jnp.arange(piece) == 0, jnp.sum(valid), 0.0)[None, :]
    own_vectors = jnp.concatenate([own_vectors, counts, jnp.zeros((4, piece), F32)])
    output_t, value_t = time_output.T, channel_value.T

    if sizes["x"] == 2:
        mine = lax.dynamic_slice_in_dim(teacher, side * tokens, tokens)
        theirs = lax.dynamic_slice_in_dim(teacher, (1 - side) * tokens, tokens)
    else:
        mine, theirs = jnp.split(teacher, 2, axis=1)

    key_order, val_order, rec_order = three_orders = ("wxuy", "wuyx", "wyxu")
    half = width // 2
    if fast:
        wide = channel_key.shape[1]
        split = wide // 2
        chains = keys_a, keys_b, late_b = [
            Gather(channel_key[:, :split], "wuyx"),
            Gather(channel_key[:, split:], "wxuy"),
            Gather(value_t[:, split:], "wyxu"),
        ]
        first = jnp.concatenate([time_key, time_value, time_recept, output_t], axis=1)
        late = jnp.concatenate([value_t[:, :split], channel_recept], axis=1)
        first = lax.all_gather(first, EVERY)
        theirs = swap(theirs, "x")
        step_all(*chains)
        (vectors,) = gather_vectors(own_vectors, 0, 4)
        late, vectors, masks_down, masks_up, mine, theirs, carry, valid_rows, lead = seal_all(
            chains, late, vectors, masks_down, masks_up, mine, theirs, carry, valid_rows, lead
        )
        step_all(*chains)
        (vectors,) = gather_vectors(vectors, 4, 5)
        (vectors,) = seal_all(chains, vectors)
        step_all(*chains)
        mixed = first_mix(inputs, carry, vectors)
        (mixed,) = seal_all(chains, mixed)
        step_all(*chains)
        first, late, mixed = seal(first, late, mixed)
        late = lax.all_gather(late, EVERY).reshape(16, 2, SLOT, -1)
        first = first.reshape(16, 2, SLOT, -1)
        key_w, value_w, recept_w, output_w = (all_of(first, n * half, half) for n in range(4))
    else:
        early = gather_plain(channel_key)
        wide = early.shape[-1]
        split = wide // 2
        key_w, value_w, recept_w, output_w, crecept_w = (
            all_of(gather_plain(w))
            for w in (time_key, time_value, time_recept, output_t, channel_recept)
        )
        ckey_w = all_of(early)
        late = gather_plain(value_t)
        cvalue_w = [all_of(late, skip, split) for skip in (0, split)]
        vectors = lax.all_gather(own_vectors, EVERY, axis=1, tiled=True)
        mixed = first_mix(inputs, carry, vectors)

    *saved, gated = time_forward(co, mixed, (key_w, value_w, recept_w), vectors, masks_down)
    if fast:
        (gated,) = seal_all((keys_a, keys_b), gated)
        step_all(keys_a, keys_b)
    if sizes["x"] == 2 and not fast:
        theirs = swap(theirs, "x")
    middle, mixed_k2, mixed_r2 = time_output_step(co, gated, inputs, carry, vectors, output_w)
    if fast:
        middle, mixed_k2, mixed_r2 = seal_all(chains, middle, mixed_k2, mixed_r2)
        ckey_w = weight_of(keys_a.part(), keys_b.part(split))
        late_b.step()
    hidden, active = hidden_step(co, mixed_k2, ckey_w)
    if fast:
        hidden, late = seal_all((late_b,), hidden, late)
        cvalue_w = [all_of(late, 0, split), weight_of(late_b.part())]
        crecept_w = all_of(late, split, half)
    count = jnp.sum(vectors[11])
    scale = (float(tokens * devices) / count).reshape(1)
    kept, arrived, dres, dkv, drec2, loss_rows = result_step(
        co.at[4].set(side),
        scale,
        hidden,
        mixed_r2,
        middle,
        (mine, theirs),
        valid_rows,
        both_parts(cvalue_w, split),
        crecept_w,
    )

    if sizes["x"] == 2:
        arrived = swap(arrived, "x")

    def outputs_of(kept, arrived):
        return lax.dynamic_update_slice_in_dim(kept, arrived, (1 - side) * tokens, 0)

    back = functools.partial(channel_back, co)
    order_b, order_c = "wuyx", "wuyx"
    edge = jnp.zeros((8, width), F32)

    def input_back_part(dmix, part, after, before, found):
        return input_back(
            co, dmix, inputs, dmid, lead, vectors, (key_w, value_w, recept_w), part, after, before, found
        )

    if fast:
        dkey_0, *found, blocks = back(
            dkv, mixed_k2, hidden, active, (mixed_r2, drec2), cvalue_w[0], split, 0, order_b
        )
        group_v = Merged(found, order_b)
        dkv, arrived, blocks = seal_all((group_v,), dkv, arrived, blocks)
        blocks = scatter_rows(blocks)
        group_v.step()
        dkey_1, *found = back(dkv, mixed_k2, None, active, (), cvalue_w[1], split, 1, order_b)
        group_b = Merged(found, order_b)
        (dkey_1,) = seal_all((group_v, group_b), dkey_1)
        step_all(group_v, group_b)
        outputs = outputs_of(kept, arrived)
        dmid, dtime, sums2 = middle_back(
            co, (dkey_0, dkey_1), drec2, middle, dres, lead, vectors, ckey_w, crecept_w
        )
        (dtime,) = seal_all((group_v, group_b), dtime)
        step_all(group_v, group_b)
        found = weight_grads(co, ((dtime, gated, order_c),), merged=True)
        group_c = Merged(found, order_c)
        dtime, outputs = seal_all((group_c,), dtime, outputs)
        group_c.step()
        *dmix, sums_t = time_back(co, dtime, saved, vectors, masks_up, output_w)
        (dmix, dmid) = seal_all((group_v, group_b, group_c), dmix, dmid)
        step_all(group_v, group_b, group_c)
        found = weight_grads(co, [(m, d, order) for m, d, order in zip(mixed, dmix, three_orders)])
        group_t = Reduce(found, three_orders)
        (dmix,) = seal_all((group_v, group_b, group_c, group_t), dmix)
        step_all(group_v, group_b, group_c, group_t)
        found, totals, edge = input_back_part(dmix, 0, edge, (sums_t, sums2, loss_rows), dres)
        (dmix, edge, found) = seal_all((group_v, group_b, group_c, group_t), dmix, edge, found)
        step_all(group_b, group_c, group_t)
        input_grad, totals, _ = input_back_part(dmix, 1, edge, (totals,), found)
    else:
        dkey_0, *found, blocks = back(
            dkv, mixed_k2, hidden, active, (mixed_r2, drec2), cvalue_w[0], split, 0, order_b
        )
        (value_1,) = reduce_merged(found, order_b)
        dkey_1, *found = back(dkv, mixed_k2, None, active, (), cvalue_w[1], split, 1, order_b)
        (ckey_1,) = reduce_merged(found, order_b)
        value_0, ckey_0 = (
            reduce_blocks(blocks[..., n * split : (n + 1) * split]) for n in (0, 1)
        )
        crecept_g = reduce_blocks(blocks[..., 2 * split :])
        halves = 2 // sizes["x"]
        cvalue_g, ckey_g = (
            jnp.concatenate(
                [v.reshape(-1, halves, split) for v in pair], axis=2
            ).reshape(pair[0].shape[0], -1)
            for pair in ((value_0, value_1), (ckey_0, ckey_1))
        )
        dmid, dtime, sums2 = middle_back(
            co, (dkey_0, dkey_1), drec2, middle, dres, lead, vectors, ckey_w, crecept_w
        )
        found = weight_grads(co, ((dtime, gated, order_c),), merged=True)
        (output_g,) = reduce_merged(found, order_c)
        *dmix, sums_t = time_back(co, dtime, saved, vectors, masks_up, output_w)
        found = weight_grads(co, [(m, d, order) for m, d, order in zip(mixed, dmix, three_orders)])
        key_g, val_g, rec_g = reduce_plain(found, three_orders)
        found, totals, edge = input_back_part(dmix, 0, edge, (sums_t, sums2, loss_rows), dres)
        input_grad, totals, _ = input_back_part(dmix, 1, edge, (totals,), found)

    if fast:
        (totals,) = seal_all((group_b, group_c, group_t), totals)
        for axes in ("wc", "y", "xu"):
            step_all(*[group for group in (group_t, group_c, group_b) if group.done < 5])
            for axis in axes:
                totals = totals + swap(totals, axis)
            if axes == "y":
                blocks = pair_sum(blocks)
                totals, blocks = seal_all((group_b, group_c, group_t), totals, blocks)
                cvalue_g, ckey_g = (
                    jnp.concatenate([blocks[:, n * split : (n + 1) * split], found], axis=1)
                    for n, found in enumerate(group_v.finish() + group_b.finish())
                )
                cvalue_g = cvalue_g.T
            elif axes == "wc":
                totals, blocks = seal_all((group_c, group_t), totals, blocks)
        totals, cvalue_g, ckey_g = seal_all((group_t,), totals, cvalue_g, ckey_g)
        cvalue_g = cvalue_g.T
        (output_g,) = group_c.finish()
        crecept_g = blocks[:, 2 * split :]
        key_g, val_g, rec_g = group_t.finish()
    else:
        totals = lax.psum(totals, EVERY)
    loss = jnp.sum(totals[11]) / (2.0 * count * width)
    vector_g = lax.dynamic_slice_in_dim(totals, flat * piece, piece, axis=1)
    if not fast:
        outputs = (
            outputs_of(kept, arrived)
            if sizes["x"] == 2
            else jnp.concatenate([kept[:tokens], arrived], axis=1)
        )
    return (
        outputs,
        loss,
        input_grad,
        *[vector_g[n] for n in range(7)],
        key_g,
        val_g,
        rec_g,
        output_g.T,
        *[vector_g[n] for n in range(7, 11)],
        ckey_g,
        crecept_g,
        cvalue_g.T,
    )


def solution(mesh):
    fsdp, tp = mesh.shape["fsdp"], mesh.shape["tp"]
    two = 2 if fsdp % 8 == 0 else 1
    split = Mesh(mesh.devices.reshape(fsdp // two**3, two, two, two, tp), EVERY)
    rows = ("w", "u", "y", "c")
    vector = P(EVERY)
    matrix = P(rows, "x")
    turned = P("x", rows)
    tall = P(EVERY, None)
    return jax.shard_map(
        on_device,
        mesh=split,
        in_specs=(
            (tall, P(rows), matrix)
            + (vector,) * 7
            + (matrix, matrix, matrix, turned)
            + (vector,) * 4
            + (matrix, matrix, turned)
        ),
        out_specs=(
            (matrix, P(), tall)
            + (vector,) * 7
            + (matrix, matrix, matrix, turned)
            + (vector,) * 4
            + (matrix, matrix, turned)
        ),
        check_vma=False,
    )
```
